32 devices in a mesh: depth: 4 (over x, core), sx: 4 (over z), sy: 2 (over y).
Axes of the slice: x: 2, y: 2, z: 4, core: 2. Of those that a mesh axis runs over, the one named last changes fastest.
Arguments:
- density: float32 [128, 64, 1024], P('sx', 'sy', 'depth'), may hold values from -6 to 6
- kernel_taps: bfloat16 [2, 33], replicated, may hold values from 0.099609375 to 0.3984375
- tf_centre: float32 [8, 4], replicated, may hold values from -2 to 2
- tf_width: float32 [8, 4], replicated, may hold values from 0.4 to 1.5
- tf_color: float32 [8, 4, 3], replicated, may hold values from 0.05 to 1
- tf_opacity: float32 [8, 4], replicated, may hold values from 0.0005 to 0.004
- brick_tf: int32 [8, 4, 8], P('sx', 'sy', 'depth'), may hold values from 0 to 7
- view_order: int32 [8, 4], P('sx', 'sy'), may hold values from 0 to 1
Outputs:
- picture: float32 [4, 4, 4, 8, 64], P(None, 'sx', 'depth', None, 'sy')
The draws below stay inside these ranges and needn't reach their ends.
Inputs may be any that keep to these rules, and one draw needn't show every extreme that they name: `view_order`: 0: the viewer of that column of bricks faces z = 0; 1: it faces z = 1023.
All inputs are finite; a program needn't handle non-finite values.
Results may differ from the reference program's by a relative error of at most 0.0003.
Values may be sent and summed in bfloat16 or wider, within the bound.
No kernel may reach another device: no remote copies, remote signals or barrier semaphores. Data moves between devices by JAX's collectives and lax.ppermute only.
A program may use at most 64 MiB of HBM per device.

```python
import math
import jax
import jax.numpy as jnp
from jax import lax

CX = 32
CY = 32
TAPS = 33
NTF = 8
NBUMP = 4
BRICKS = 2
NX = 128
NY = 64
NZ = 1024
NBX = 8
NBY = 4
NBZ = 8
N_DEPTH = 4
N_SX = 4


def with_ends(array, rng, least, largest):
    longest = array.shape.index(max(array.shape))
    spots = []
    for shift in (0, 1):
        where = [jax.random.randint(jax.random.fold_in(rng, axis), (), 0, length) for axis, length in enumerate(array.shape)]
        where[longest] = (where[longest] + shift) % array.shape[longest]
        spots.append(tuple(where))
    return array.at[spots[0]].set(least).at[spots[1]].set(largest)


def levels(key, shape, cuts, low, high):
    level, own = 1.0, jax.random.fold_in(key, 6)
    for axis_at, blocks in cuts:
        heights = jnp.exp(jax.random.uniform(jax.random.fold_in(own, axis_at), (blocks,), jnp.float32, low / len(cuts), high / len(cuts)))
        level = level * jnp.repeat(heights, shape[axis_at] // blocks).reshape([-1 if axis == axis_at else 1 for axis in range(len(shape))])
    return level


def bell_draw(stream_key, shape, width, limit, cuts=(), held_as=jnp.bfloat16):
    drawn = jax.random.normal(stream_key, shape, jnp.float32) * width
    if len(cuts) > 0:
        drawn = levels(stream_key, shape, cuts, -0.22, 0.18) * drawn
    return jnp.clip(drawn, min=-limit, max=limit).astype(held_as)


def setup_inputs(seed: int = 0) -> dict:
    arg_keys = jax.random.split(jax.random.key(seed), 9)
    density = bell_draw(arg_keys[0], (NX, NY, NZ), 1.0, 6.0, ((0, 4), (1, 2), (2, 4)), jnp.float32)
    kernel_taps = jnp.clip(jax.random.uniform(arg_keys[1], (2, TAPS), jnp.float32, 0.099609375, 0.3984375), 0.099609375, 0.3984375).astype(jnp.bfloat16)
    tf_centre = jnp.clip(jax.random.uniform(arg_keys[2], (NTF, NBUMP), jnp.float32, -2.0, 2.0), -2.0, 2.0)
    tf_width = jnp.clip(jnp.exp(jax.random.uniform(arg_keys[3], (NTF, NBUMP), jnp.float32, math.log(0.4), math.log(1.5))), 0.4, 1.5)
    tf_color = jnp.clip(jax.random.uniform(arg_keys[4], (NTF, NBUMP, 3), jnp.float32, 0.05, 1.0), 0.05, 1.0)
    tf_opacity = jnp.clip(jnp.exp(jax.random.uniform(arg_keys[5], (NTF, NBUMP), jnp.float32, math.log(0.0005), math.log(0.004))), 0.0005, 0.004)
    brick_tf = with_ends(jax.random.randint(arg_keys[6], (NBX, NBY, NBZ), 0, NTF), jax.random.fold_in(arg_keys[6], 1), 0, NTF - 1).astype(jnp.int32)
    view_order = with_ends(jax.random.randint(arg_keys[7], (NBX, NBY), 0, 2), jax.random.fold_in(arg_keys[7], 1), 0, 1).astype(jnp.int32)
    return dict(density=density, kernel_taps=kernel_taps, tf_centre=tf_centre, tf_width=tf_width, tf_color=tf_color, tf_opacity=tf_opacity, brick_tf=brick_tf, view_order=view_order)


def expand_table(table):
    return jnp.repeat(jnp.repeat(table, CX // BRICKS, 0), CY // BRICKS, 1)


def reference(density, kernel_taps, tf_centre, tf_width, tf_color, tf_opacity, brick_tf, view_order):
    thick = NZ // NBZ
    rim_width = (TAPS - 1) // 2
    taps_wide = kernel_taps.astype(jnp.float32)
    highest = lax.Precision.HIGHEST
    reverse_map = expand_table(view_order)

    def slab_image(index):
        cells = lax.dynamic_slice_in_dim(density, index * thick, thick, 2)
        coarse = cells.astype(jnp.bfloat16)
        padded = jnp.pad(coarse, ((rim_width, rim_width), (rim_width, rim_width), (0, 0))).astype(jnp.float32)
        across = jnp.zeros((NX, NY + 2 * rim_width, thick), jnp.float32)
        for offset in range(TAPS):
            across = across + taps_wide[0, offset] * padded[offset:offset + NX]
        across = lax.optimization_barrier(across.astype(jnp.bfloat16)).astype(jnp.float32)
        occlusion = jnp.zeros((NX, NY, thick), jnp.float32)
        for offset in range(TAPS):
            occlusion = occlusion + taps_wide[1, offset] * across[:, offset:offset + NY]
        shading = jax.nn.sigmoid(-occlusion)
        chosen = lax.dynamic_slice_in_dim(brick_tf, index, 1, 2)[:, :, 0]
        onehot = (chosen[:, :, None] == jnp.arange(NTF, dtype=jnp.int32)).astype(jnp.float32)
        centre = expand_table(jnp.einsum("abt,tj->abj", onehot, tf_centre, precision=highest))
        spread = expand_table(jnp.einsum("abt,tj->abj", onehot, tf_width, precision=highest))
        opacity = expand_table(jnp.einsum("abt,tj->abj", onehot, tf_opacity, precision=highest))
        colour_table = expand_table(jnp.einsum("abt,tjc->abjc", onehot, tf_color, precision=highest))
        optical = jnp.zeros((NX, NY, thick), jnp.float32)
        emission = [jnp.zeros((NX, NY, thick), jnp.float32) for channel in range(3)]
        for bump_index in range(NBUMP):
            bump_value = jnp.exp(-jnp.square((cells - centre[:, :, bump_index, None]) / spread[:, :, bump_index, None]))
            optical = optical + opacity[:, :, bump_index, None] * bump_value
            for channel in range(3):
                emission[channel] = emission[channel] + colour_table[:, :, bump_index, channel, None] * bump_value
        running = jnp.cumsum(optical, axis=2)
        summed = running[:, :, -1:]
        preceding = jnp.where(reverse_map[:, :, None] == 1, summed - running, running - optical)
        weights = jnp.exp(-preceding) * (1.0 - jnp.exp(-optical))
        colours = [jnp.sum(weights * (shading * emission[channel]), axis=2) for channel in range(3)]
        transmit = jnp.exp(-summed[:, :, 0])
        return jnp.stack(colours + [transmit])

    images = lax.map(slab_image, jnp.arange(NBZ, dtype=jnp.int32))

    def advance(carry, part_image):
        colour = carry[:3] + carry[3:] * part_image[:3]
        return jnp.concatenate([colour, carry[3:] * part_image[3:]]), None

    start = jnp.concatenate([jnp.zeros((3, NX, NY), jnp.float32), jnp.ones((1, NX, NY), jnp.float32)])
    forward, unused = lax.scan(advance, start, images)
    backward, unused_back = lax.scan(advance, start, images, reverse=True)
    final = jnp.where(reverse_map[None] == 1, backward, forward)
    picture = jnp.concatenate([final[:3], 1.0 - final[3:]])
    return picture.reshape(4, N_SX, N_DEPTH, CX // N_DEPTH, NY)
```

```python
import functools
import math
import jax
import jax.numpy as jnp
from jax import lax
from jax.experimental import pallas as pl
from jax.experimental.pallas import tpu as pltpu
from jax.sharding import PartitionSpec as P

LOG2E = math.log2(math.e)
VMEM = pl.BlockSpec(memory_space=pltpu.VMEM)
SMEM = pl.BlockSpec(memory_space=pltpu.SMEM)
ANY = pl.BlockSpec(memory_space=pl.ANY)
VMEM_LIMIT = 40 * 1024 * 1024


def swap_rounds(count):
    rounds = []
    for first in (0, 1):
        pairs = [(i, i + 1) for i in range(first, count - 1, 2)]
        if pairs:
            rounds.append([(a, b) for a, b in pairs] + [(b, a) for a, b in pairs])
    return rounds


def strips_kernel(rim, y_rounds, x_parity, y_parity, density, xs1, xs2, *ys):
    px, py = x_parity(), y_parity()
    first = pl.ds(rim * (1 - px), rim)
    second = pl.ds(rim * px, rim)
    for r in range(y_rounds):
        group = pl.ds(pl.multiple_of(rim * (1 - py if r == 0 else py), rim), rim)
        ys[2 * r][...] = density[first, group, :].astype(jnp.bfloat16)
        ys[2 * r + 1][...] = density[second, group, :].astype(jnp.bfloat16)
    xs1[...] = density[first].astype(jnp.bfloat16)
    xs2[...] = density[second].astype(jnp.bfloat16)


def iota(shape, dim):
    return lax.broadcasted_iota(jnp.int32, shape, dim)


def toeplitz(taps, rim):
    return pltpu.roll(jnp.broadcast_to(taps, (rim, 128)), 0, 1, stride=1, stride_axis=0)


def blur_matrices(rim, taps):
    size = rim * rim
    f32, bf16 = jnp.float32, jnp.bfloat16
    row_hi = iota((size, rim), 0) // rim == iota((size, rim), 1)
    row_lo = iota((size, rim), 0) % rim == iota((size, rim), 1)
    col = iota((128, 3 * size), 1)
    src = iota((128, 3 * size), 0)
    col_x = col // rim == src
    col_y = (col // size) * rim + col % rim == src
    tx = toeplitz(taps[0:1], rim).astype(bf16)
    ty = toeplitz(taps[1:2] * 0.5, rim).astype(bf16)
    wide_x = jnp.dot(tx, col_x.astype(f32).astype(bf16), preferred_element_type=f32).astype(bf16)
    wide_y = jnp.dot(ty, col_y.astype(f32).astype(bf16), preferred_element_type=f32).astype(bf16)
    full_x = jnp.dot(row_hi.astype(f32).astype(bf16), wide_x, preferred_element_type=f32)
    full_y = jnp.dot(row_lo.astype(f32).astype(bf16), wide_y, preferred_element_type=f32)
    r, c = iota((size, 3 * size), 0), iota((size, 3 * size), 1)
    dd = jnp.where(r % rim == c % rim, full_x, 0.0)
    ee = jnp.where(r // rim == (c // rim) % rim, full_y, 0.0)
    return dd.astype(bf16), ee.astype(bf16)


def cells_kernel(
    rim, bumps, taps, centre, width, colour, opacity, brick_tf, view_order, density,
    coarse, g0, g1, g2, total, dd, ee, optical_s, e0, e1, e2
):
    by, bx = pl.program_id(0), pl.program_id(1)
    bricks = brick_tf.shape[2]
    rows_x, rows_y, rows_z = density.shape
    depth = rows_z // bricks
    f32, bf16 = jnp.float32, jnp.bfloat16

    @pl.when(jnp.logical_and(by == 0, bx == 0))
    def _():
        dd_v, ee_v = blur_matrices(rim, taps[...])
        dd[...] = dd_v
        ee[...] = ee_v

    emitted = (e0, e1, e2)
    coarse[...] = density[...].astype(bf16)
    for bz in range(bricks):
        zs = slice(bz * depth, (bz + 1) * depth)
        k = brick_tf[bx, by, bz]
        cen, neg, opa, col = [], [], [], []
        for j in range(bumps):
            cen.append(centre[k, j])
            wide = jnp.full((8, depth), width[k, j], f32)
            neg.append((-LOG2E / (wide * wide))[None])
            opa.append(opacity[k, j] * (-LOG2E))
            col.append([colour[k, 3 * j + c] * 0.5 for c in range(3)])
        for x in range(rows_x):
            d = density[x, :, zs].reshape(rows_y // 8, 8, depth)
            opt, em = None, [None] * 3
            for j in range(bumps):
                w = d - cen[j]
                b = jnp.exp2((w * w) * neg[j])
                opt = opa[j] * b if opt is None else opt + opa[j] * b
                for c in range(3):
                    em[c] = col[j][c] * b if em[c] is None else em[c] + col[j][c] * b
            rows = slice(x * rows_y, (x + 1) * rows_y)
            optical_s[rows, zs] = opt.reshape(rows_y, depth)
            for c in range(3):
                emitted[c][rows, zs] = em[c].reshape(rows_y, depth)
    order = view_order[bx, by]
    zr, zc = iota((rows_z, rows_z), 0), iota((rows_z, rows_z), 1)
    sign = 1 - 2 * order
    tri = jnp.where((zc - zr) * sign > 0, 1.0, 0.0).astype(bf16)
    opt = optical_s[...]
    hi = opt.astype(bf16)
    lo = (opt - hi.astype(f32)).astype(bf16)
    ahead = jnp.dot(hi, tri, preferred_element_type=f32) + jnp.dot(lo, tri, preferred_element_type=f32)
    weight = jnp.exp2(ahead) * (1.0 - jnp.exp2(opt))
    for c, out in enumerate((g0, g1, g2)):
        out[...] = (weight * emitted[c][...]).reshape(rows_x, rows_y, rows_z)
    folded = opt[:, :depth]
    for bz in range(1, bricks):
        folded = folded + opt[:, bz * depth:(bz + 1) * depth]
    summed = jnp.sum(folded.reshape(rows_x, rows_y, depth), axis=2, keepdims=True)
    lane = iota((rows_y, 128), 1)
    acc = jnp.zeros((rows_y, 128), f32)
    for x in range(rows_x):
        acc = jnp.where(lane == bx * rows_x + x, summed[x], acc)

    @pl.when(bx == 0)
    def _():
        total[...] = acc

    @pl.when(bx > 0)
    def _():
        total[...] += acc


def image_kernel(
    rim, depth_count, x_rounds, y_rounds, x_parity, y_parity, depth_index, *refs
):
    refs = list(refs)
    coarse, g0, g1, g2, total, dd, ee = refs[:7]
    refs = refs[7:]
    xr = refs[:x_rounds]
    refs = refs[x_rounds:]
    strips = refs[:2 * y_rounds]
    refs = refs[2 * y_rounds:]
    corners = refs[:x_rounds * y_rounds]
    refs = refs[x_rounds * y_rounds:]
    outs = refs[:depth_count]
    cx, ac, img, sems = refs[depth_count:]
    f32, bf16 = jnp.float32, jnp.bfloat16
    px, py, me = x_parity(), y_parity(), depth_index()
    rows_x, rows_y, rows_z = coarse.shape
    half = rows_x // rim
    groups = rows_y // rim

    def y_cols(r):
        return slice(rows_y + r * rim, rows_y + (r + 1) * rim)

    copies = [(coarse, cx.at[rim:rim + rows_x, 0:rows_y])]
    for n in range(x_rounds):
        at = (rows_x + rim) * ((1 - px) if n == 0 else px)
        copies.append((xr[n], cx.at[pl.ds(at, rim), 0:rows_y]))
    for r in range(y_rounds):
        for n in range(2):
            at = rim + rim * ((1 - px) if n == 0 else px)
            copies.append((strips[2 * r + n], cx.at[pl.ds(at, rim), y_cols(r)]))
        for n in range(x_rounds):
            at = (rows_x + rim) * ((1 - px) if n == 0 else px)
            copies.append((corners[r * x_rounds + n], cx.at[pl.ds(at, rim), y_cols(r)]))
    started = []
    for i, (src, dst) in enumerate(copies):
        copy = pltpu.make_async_copy(src, dst, sems.at[i])
        copy.start()
        started.append(copy)
    if x_rounds < 2:
        for n in range(x_rounds, 2):
            at = (rows_x + rim) * ((1 - px) if n == 0 else px)
            cx[pl.ds(at, rim)] = jnp.zeros((rim,) + cx.shape[1:], bf16)
    for r in range(y_rounds, 2):
        slot = (groups + 1) * ((1 - py) if r == 0 else py)
        ac[pl.ds(slot, 1)] = jnp.zeros((1,) + ac.shape[1:], bf16)
    for copy in started:
        copy.wait()
    for g in range(groups + y_rounds):
        if g < groups:
            slot = g + 1
        else:
            slot = (groups + 1) * ((1 - py) if g == groups else py)
        for h in range(half):
            rhs = cx[h * rim:(h + 3) * rim, g * rim:(g + 1) * rim, :].reshape(3 * rim * rim, rows_z)
            across = jnp.dot(dd[...], rhs, preferred_element_type=f32).astype(bf16)
            ac[slot, h * rim:(h + 1) * rim] = across.reshape(rim, rim, rows_z)
    lane = iota((rim, 128), 1)
    for g in range(groups):
        accs = [jnp.zeros((rim, 128), f32) for c in range(3)]
        for h in range(half):
            rhs = ac[g:g + 3, h * rim:(h + 1) * rim].reshape(3 * rim * rim, rows_z)
            occ = jnp.dot(ee[...], rhs, preferred_element_type=f32)
            shade = (1.0 - jnp.tanh(occ)).reshape(rim, rim, rows_z)
            for c, gref in enumerate((g0, g1, g2)):
                v = shade * gref[h * rim:(h + 1) * rim, g * rim:(g + 1) * rim, :]
                folded = v[:, :, :128]
                for z in range(128, rows_z, 128):
                    folded = folded + v[:, :, z:z + 128]
                summed = jnp.sum(folded, axis=2, keepdims=True)
                for x in range(rim):
                    accs[c] = jnp.where(lane == h * rim + x, summed[x], accs[c])
        for c in range(3):
            img[c, g * rim:(g + 1) * rim, :] = accs[c]
    img[3] = jnp.exp2(total[...])
    for c in range(4):
        img[4 + c, 0:rows_x, 0:rows_y] = img[c].T[:rows_x, :]
    block = rows_x // depth_count
    for k in range(depth_count):
        at = pl.multiple_of((me ^ k) * block, block)
        outs[k][...] = img[4:8, pl.ds(at, block), 0:rows_y]


def picture_kernel(rim, depth_count, block, depth_index, view_order, *refs):
    parts = [ref[...] for ref in refs[:depth_count]]
    out = refs[depth_count]
    me = depth_index()
    shape = parts[0].shape[1:]
    brick = (me * block) // rim
    order = jnp.zeros(shape, jnp.int32)
    for y in range(view_order.shape[1]):
        order = jnp.where(iota(shape, 1) // rim == y, view_order[brick, y], order)
    bit = 0
    while len(parts) > 1:
        mine = (me >> bit & 1) == order
        merged = []
        for a, b in zip(parts[::2], parts[1::2]):
            front = jnp.where(mine[None], a, b)
            back = jnp.where(mine[None], b, a)
            merged.append(
                jnp.concatenate([front[:3] + front[3:] * back[:3], front[3:] * back[3:]])
            )
        parts = merged
        bit += 1
    final = jnp.concatenate([parts[0][:3], 1.0 - parts[0][3:]])
    out[...] = final.reshape(out.shape)


def per_device(
    density, kernel_taps, tf_centre, tf_width, tf_color, tf_opacity, brick_tf, view_order
):
    f32, bf16 = jnp.float32, jnp.bfloat16
    rows_x, rows_y, rows_z = density.shape
    rim = (kernel_taps.shape[1] - 1) // 2
    bumps = tf_centre.shape[1]
    bricks = brick_tf.shape
    depth_count = lax.axis_size("depth")
    x_swaps = swap_rounds(lax.axis_size("sx"))
    y_swaps = swap_rounds(lax.axis_size("sy"))
    x_parity = lambda: lax.rem(lax.axis_index("sx"), 2)
    y_parity = lambda: lax.rem(lax.axis_index("sy"), 2)
    depth_index = lambda: lax.axis_index("depth")
    params = pltpu.CompilerParams(vmem_limit_bytes=VMEM_LIMIT)
    struct = jax.ShapeDtypeStruct

    sends = pl.pallas_call(
        functools.partial(strips_kernel, rim, len(y_swaps), x_parity, y_parity),
        out_shape=[struct((rim, rows_y, rows_z), bf16)] * 2
        + [struct((rim, rim, rows_z), bf16)] * (2 * len(y_swaps)),
        in_specs=[VMEM],
        out_specs=[VMEM] * (2 + 2 * len(y_swaps)),
        compiler_params=params,
        name="strips",
    )(density)
    strips = [
        lax.ppermute(piece, "sy", y_swaps[i // 2]) for i, piece in enumerate(sends[2:])
    ]
    x_halos = [lax.ppermute(piece, "sx", swaps) for piece, swaps in zip(sends[:2], x_swaps)]
    corners = [
        lax.ppermute(strips[2 * r + n], "sx", swaps)
        for r in range(len(y_swaps))
        for n, swaps in enumerate(x_swaps)
    ]

    size = rim * rim
    taps = jnp.pad(kernel_taps.astype(f32), ((0, 0), (0, 128 - kernel_taps.shape[1])))
    cell_block = pl.BlockSpec((rows_x // bricks[0], rows_y // bricks[1], rows_z), lambda y, x: (x, y, 0))
    whole = lambda shape: pl.BlockSpec(shape, lambda y, x: (0,) * len(shape))
    group_rows = (rows_x // bricks[0]) * (rows_y // bricks[1])
    coarse, g0, g1, g2, total, dd, ee = pl.pallas_call(
        functools.partial(cells_kernel, rim, bumps),
        grid=(bricks[1], bricks[0]),
        out_shape=[struct(density.shape, bf16)]
        + [struct(density.shape, f32)] * 3
        + [struct((rows_y, 128), f32)]
        + [struct((size, 3 * size), bf16)] * 2,
        in_specs=[whole((2, 128))] + [SMEM] * 6 + [cell_block],
        out_specs=[cell_block] * 4
        + [pl.BlockSpec((rows_y // bricks[1], 128), lambda y, x: (y, 0))]
        + [whole((size, 3 * size))] * 2,
        scratch_shapes=[pltpu.VMEM((group_rows, rows_z), f32)] * 4,
        compiler_params=params,
        cost_estimate=pl.CostEstimate(flops=density.size * 60, bytes_accessed=density.size * 20, transcendentals=density.size * 6),
        name="cells",
    )(taps, tf_centre, tf_width, tf_color.reshape(tf_color.shape[0], -1), tf_opacity, brick_tf, view_order, density)

    block = rows_x // depth_count
    n_copies = 1 + len(x_swaps) + 2 * len(y_swaps) + len(corners)
    parts = pl.pallas_call(
        functools.partial(
            image_kernel, rim, depth_count, len(x_swaps), len(y_swaps), x_parity, y_parity, depth_index
        ),
        out_shape=[struct((4, block, rows_y), f32)] * depth_count,
        in_specs=[ANY] + [VMEM] * 6 + [ANY] * (n_copies - 1),
        out_specs=[VMEM] * depth_count,
        scratch_shapes=[
            pltpu.VMEM((rows_x + 2 * rim, rows_y + rim * len(y_swaps), rows_z), bf16),
            pltpu.VMEM((rows_y // rim + 2, rows_x, rim, rows_z), bf16),
            pltpu.VMEM((8, rows_y, 128), f32),
            pltpu.SemaphoreType.DMA((n_copies,)),
        ],
        compiler_params=params,
        name="image",
    )(coarse, g0, g1, g2, total, dd, ee, *x_halos, *strips, *corners)
    pieces = [parts[0]] + [
        lax.ppermute(parts[k], "depth", [(i, i ^ k) for i in range(depth_count)])
        for k in range(1, depth_count)
    ]
    return pl.pallas_call(
        functools.partial(picture_kernel, rim, depth_count, block, depth_index),
        out_shape=struct((4, 1, 1, block, rows_y), f32),
        in_specs=[SMEM] + [VMEM] * depth_count,
        out_specs=VMEM,
        name="picture",
    )(view_order, *pieces)


def solution(mesh):
    return jax.shard_map(
        per_device,
        mesh=mesh,
        in_specs=(
            P("sx", "sy", "depth"),
            P(),
            P(),
            P(),
            P(),
            P(),
            P("sx", "sy", "depth"),
            P("sx", "sy"),
        ),
        out_specs=P(None, "sx", "depth", None, "sy"),
        check_vma=False,
    )
```

```python
import functools
import math
import jax
import jax.numpy as jnp
from jax import lax
from jax.experimental import pallas as pl
from jax.experimental.pallas import tpu as pltpu
from jax.sharding import PartitionSpec as P

LOG2E = math.log2(math.e)
VMEM = pl.BlockSpec(memory_space=pltpu.VMEM)
SMEM = pl.BlockSpec(memory_space=pltpu.SMEM)
ANY = pl.BlockSpec(memory_space=pl.ANY)
VMEM_LIMIT = 40 * 1024 * 1024


def swap_rounds(count):
    rounds = []
    for first in (0, 1):
        pairs = [(i, i + 1) for i in range(first, count - 1, 2)]
        if pairs:
            rounds.append([(a, b) for a, b in pairs] + [(b, a) for a, b in pairs])
    return rounds


def strips_kernel(rim, y_rounds, x_parity, y_parity, density, xs1, xs2, *ys):
    px, py = x_parity(), y_parity()
    first = pl.ds(rim * (1 - px), rim)
    second = pl.ds(rim * px, rim)
    for r in range(y_rounds):
        group = pl.ds(pl.multiple_of(rim * (1 - py if r == 0 else py), rim), rim)
        ys[2 * r][...] = density[first, group, :].astype(jnp.bfloat16)
        ys[2 * r + 1][...] = density[second, group, :].astype(jnp.bfloat16)
    xs1[...] = density[first].astype(jnp.bfloat16)
    xs2[...] = density[second].astype(jnp.bfloat16)


def iota(shape, dim):
    return lax.broadcasted_iota(jnp.int32, shape, dim)


def toeplitz(taps, rim):
    return pltpu.roll(jnp.broadcast_to(taps, (rim, 128)), 0, 1, stride=1, stride_axis=0)


def blur_matrices(rim, taps):
    size = rim * rim
    f32, bf16 = jnp.float32, jnp.bfloat16
    row_hi = iota((size, rim), 0) // rim == iota((size, rim), 1)
    row_lo = iota((size, rim), 0) % rim == iota((size, rim), 1)
    col = iota((128, 3 * size), 1)
    src = iota((128, 3 * size), 0)
    col_x = col // rim == src
    col_y = (col // size) * rim + col % rim == src
    tx = toeplitz(taps[0:1], rim).astype(bf16)
    ty = toeplitz(taps[1:2] * 0.5, rim).astype(bf16)
    wide_x = jnp.dot(tx, col_x.astype(f32).astype(bf16), preferred_element_type=f32).astype(bf16)
    wide_y = jnp.dot(ty, col_y.astype(f32).astype(bf16), preferred_element_type=f32).astype(bf16)
    full_x = jnp.dot(row_hi.astype(f32).astype(bf16), wide_x, preferred_element_type=f32)
    full_y = jnp.dot(row_lo.astype(f32).astype(bf16), wide_y, preferred_element_type=f32)
    r, c = iota((size, 3 * size), 0), iota((size, 3 * size), 1)
    dd = jnp.where(r % rim == c % rim, full_x, 0.0)
    ee = jnp.where(r // rim == (c // rim) % rim, full_y, 0.0)
    return dd.astype(bf16), ee.astype(bf16)


def cells_kernel(
    rim, bumps, taps, centre, width, colour, opacity, brick_tf, view_order, density,
    coarse, g0, g1, g2, total, dd, ee, optical_s, e0, e1, e2, padded
):
    by, bx = pl.program_id(0), pl.program_id(1)
    bricks = brick_tf.shape[2]
    rows_x, rows_y, rows_z = density.shape
    depth = rows_z // bricks
    f32, bf16 = jnp.float32, jnp.bfloat16

    @pl.when(jnp.logical_and(by == 0, bx == 0))
    def _():
        padded[...] = jnp.zeros(padded.shape, f32)
        padded[0:2, 0:taps.shape[1]] = taps[...].astype(f32)
        dd_v, ee_v = blur_matrices(rim, padded[...])
        dd[...] = dd_v
        ee[...] = ee_v

    emitted = (e0, e1, e2)
    coarse[...] = density[...].astype(bf16)
    for bz in range(bricks):
        zs = slice(bz * depth, (bz + 1) * depth)
        k = brick_tf[bx, by, bz]
        cen, neg, opa, col = [], [], [], []
        for j in range(bumps):
            cen.append(centre[j, k])
            wide = jnp.full((8, depth), width[j, k], f32)
            neg.append((-LOG2E / (wide * wide))[None])
            opa.append(opacity[j, k] * (-LOG2E))
            col.append([colour[c, j, k] * 0.5 for c in range(3)])
        for x in range(rows_x):
            d = density[x, :, zs].reshape(rows_y // 8, 8, depth)
            opt, em = None, [None] * 3
            for j in range(bumps):
                w = d - cen[j]
                b = jnp.exp2((w * w) * neg[j])
                opt = opa[j] * b if opt is None else opt + opa[j] * b
                for c in range(3):
                    em[c] = col[j][c] * b if em[c] is None else em[c] + col[j][c] * b
            rows = slice(x * rows_y, (x + 1) * rows_y)
            optical_s[rows, zs] = opt.reshape(rows_y, depth)
            for c in range(3):
                emitted[c][rows, zs] = em[c].reshape(rows_y, depth)
    order = view_order[bx, by]
    zr, zc = iota((rows_z, rows_z), 0), iota((rows_z, rows_z), 1)
    sign = 1 - 2 * order
    tri = jnp.where((zc - zr) * sign > 0, 1.0, 0.0).astype(bf16)
    opt = optical_s[...]
    hi = opt.astype(bf16)
    lo = (opt - hi.astype(f32)).astype(bf16)
    ahead = jnp.dot(hi, tri, preferred_element_type=f32) + jnp.dot(lo, tri, preferred_element_type=f32)
    weight = jnp.exp2(ahead) * (1.0 - jnp.exp2(opt))
    for c, out in enumerate((g0, g1, g2)):
        out[...] = (weight * emitted[c][...]).reshape(rows_x, rows_y, rows_z)
    folded = opt[:, :depth]
    for bz in range(1, bricks):
        folded = folded + opt[:, bz * depth:(bz + 1) * depth]
    summed = jnp.sum(folded.reshape(rows_x, rows_y, depth), axis=2, keepdims=True)
    lane = iota((rows_y, 128), 1)
    acc = jnp.zeros((rows_y, 128), f32)
    for x in range(rows_x):
        acc = jnp.where(lane == bx * rows_x + x, summed[x], acc)

    @pl.when(bx == 0)
    def _():
        total[...] = acc

    @pl.when(bx > 0)
    def _():
        total[...] += acc


def image_kernel(
    rim, depth_count, x_rounds, y_rounds, x_parity, y_parity, depth_index, *refs
):
    refs = list(refs)
    coarse, g0, g1, g2, total, dd, ee = refs[:7]
    refs = refs[7:]
    xr = refs[:x_rounds]
    refs = refs[x_rounds:]
    strips = refs[:2 * y_rounds]
    refs = refs[2 * y_rounds:]
    corners = refs[:x_rounds * y_rounds]
    refs = refs[x_rounds * y_rounds:]
    outs = refs[:depth_count]
    cx, ac, img, sems = refs[depth_count:]
    f32, bf16 = jnp.float32, jnp.bfloat16
    px, py, me = x_parity(), y_parity(), depth_index()
    rows_x, rows_y, rows_z = coarse.shape
    half = rows_x // rim
    groups = rows_y // rim

    def y_cols(r):
        return slice(rows_y + r * rim, rows_y + (r + 1) * rim)

    copies = [(coarse, cx.at[rim:rim + rows_x, 0:rows_y])]
    for n in range(x_rounds):
        at = (rows_x + rim) * ((1 - px) if n == 0 else px)
        copies.append((xr[n], cx.at[pl.ds(at, rim), 0:rows_y]))
    for r in range(y_rounds):
        for n in range(2):
            at = rim + rim * ((1 - px) if n == 0 else px)
            copies.append((strips[2 * r + n], cx.at[pl.ds(at, rim), y_cols(r)]))
        for n in range(x_rounds):
            at = (rows_x + rim) * ((1 - px) if n == 0 else px)
            copies.append((corners[r * x_rounds + n], cx.at[pl.ds(at, rim), y_cols(r)]))
    started = []
    for i, (src, dst) in enumerate(copies):
        copy = pltpu.make_async_copy(src, dst, sems.at[i])
        copy.start()
        started.append(copy)
    if x_rounds < 2:
        for n in range(x_rounds, 2):
            at = (rows_x + rim) * ((1 - px) if n == 0 else px)
            cx[pl.ds(at, rim)] = jnp.zeros((rim,) + cx.shape[1:], bf16)
    for r in range(y_rounds, 2):
        slot = (groups + 1) * ((1 - py) if r == 0 else py)
        ac[pl.ds(slot, 1)] = jnp.zeros((1,) + ac.shape[1:], bf16)
    for copy in started:
        copy.wait()
    for g in range(groups + y_rounds):
        if g < groups:
            slot = g + 1
        else:
            slot = (groups + 1) * ((1 - py) if g == groups else py)
        for h in range(half):
            rhs = cx[h * rim:(h + 3) * rim, g * rim:(g + 1) * rim, :].reshape(3 * rim * rim, rows_z)
            across = jnp.dot(dd[...], rhs, preferred_element_type=f32).astype(bf16)
            ac[slot, h * rim:(h + 1) * rim] = across.reshape(rim, rim, rows_z)
    lane = iota((rim, 128), 1)
    for g in range(groups):
        accs = [jnp.zeros((rim, 128), f32) for c in range(3)]
        for h in range(half):
            rhs = ac[g:g + 3, h * rim:(h + 1) * rim].reshape(3 * rim * rim, rows_z)
            occ = jnp.dot(ee[...], rhs, preferred_element_type=f32)
            shade = (1.0 - jnp.tanh(occ)).reshape(rim, rim, rows_z)
            for c, gref in enumerate((g0, g1, g2)):
                v = shade * gref[h * rim:(h + 1) * rim, g * rim:(g + 1) * rim, :]
                folded = v[:, :, :128]
                for z in range(128, rows_z, 128):
                    folded = folded + v[:, :, z:z + 128]
                summed = jnp.sum(folded, axis=2, keepdims=True)
                for x in range(rim):
                    accs[c] = jnp.where(lane == h * rim + x, summed[x], accs[c])
        for c in range(3):
            img[c, g * rim:(g + 1) * rim, :] = accs[c]
    img[3] = jnp.exp2(total[...])
    for c in range(4):
        img[4 + c, 0:rows_x, 0:rows_y] = img[c].T[:rows_x, :]
    block = rows_x // depth_count
    for k in range(depth_count):
        at = pl.multiple_of((me ^ k) * block, block)
        outs[k][...] = img[4:8, pl.ds(at, block), 0:rows_y]


def picture_kernel(rim, depth_count, block, depth_index, view_order, *refs):
    parts = [ref[...] for ref in refs[:depth_count]]
    out = refs[depth_count]
    me = depth_index()
    shape = parts[0].shape[1:]
    brick = (me * block) // rim
    order = jnp.zeros(shape, jnp.int32)
    for y in range(view_order.shape[1]):
        order = jnp.where(iota(shape, 1) // rim == y, view_order[brick, y], order)
    bit = 0
    while len(parts) > 1:
        mine = (me >> bit & 1) == order
        merged = []
        for a, b in zip(parts[::2], parts[1::2]):
            front = jnp.where(mine[None], a, b)
            back = jnp.where(mine[None], b, a)
            merged.append(
                jnp.concatenate([front[:3] + front[3:] * back[:3], front[3:] * back[3:]])
            )
        parts = merged
        bit += 1
    final = jnp.concatenate([parts[0][:3], 1.0 - parts[0][3:]])
    out[...] = final.reshape(out.shape)


def per_device(
    density, kernel_taps, tf_centre, tf_width, tf_color, tf_opacity, brick_tf, view_order
):
    f32, bf16 = jnp.float32, jnp.bfloat16
    rows_x, rows_y, rows_z = density.shape
    rim = (kernel_taps.shape[1] - 1) // 2
    bumps = tf_centre.shape[1]
    bricks = brick_tf.shape
    depth_count = lax.axis_size("depth")
    x_swaps = swap_rounds(lax.axis_size("sx"))
    y_swaps = swap_rounds(lax.axis_size("sy"))
    x_parity = lambda: lax.rem(lax.axis_index("sx"), 2)
    y_parity = lambda: lax.rem(lax.axis_index("sy"), 2)
    depth_index = lambda: lax.axis_index("depth")
    params = pltpu.CompilerParams(vmem_limit_bytes=VMEM_LIMIT)
    struct = jax.ShapeDtypeStruct

    sends = pl.pallas_call(
        functools.partial(strips_kernel, rim, len(y_swaps), x_parity, y_parity),
        out_shape=[struct((rim, rows_y, rows_z), bf16)] * 2
        + [struct((rim, rim, rows_z), bf16)] * (2 * len(y_swaps)),
        in_specs=[VMEM],
        out_specs=[VMEM] * (2 + 2 * len(y_swaps)),
        compiler_params=params,
        name="strips",
    )(density)
    strips = [
        lax.ppermute(piece, "sy", y_swaps[i // 2]) for i, piece in enumerate(sends[2:])
    ]
    x_halos = [lax.ppermute(piece, "sx", swaps) for piece, swaps in zip(sends[:2], x_swaps)]
    size = rim * rim
    cell_block = pl.BlockSpec((rows_x // bricks[0], rows_y // bricks[1], rows_z), lambda y, x: (x, y, 0))
    whole = lambda shape: pl.BlockSpec(shape, lambda y, x: (0,) * len(shape))
    group_rows = (rows_x // bricks[0]) * (rows_y // bricks[1])
    coarse, g0, g1, g2, total, dd, ee = pl.pallas_call(
        functools.partial(cells_kernel, rim, bumps),
        grid=(bricks[1], bricks[0]),
        out_shape=[struct(density.shape, bf16)]
        + [struct(density.shape, f32)] * 3
        + [struct((rows_y, 128), f32)]
        + [struct((size, 3 * size), bf16)] * 2,
        in_specs=[whole(kernel_taps.shape)] + [SMEM] * 6 + [cell_block],
        out_specs=[cell_block] * 4
        + [pl.BlockSpec((rows_y // bricks[1], 128), lambda y, x: (y, 0))]
        + [whole((size, 3 * size))] * 2,
        scratch_shapes=[pltpu.VMEM((group_rows, rows_z), f32)] * 4 + [pltpu.VMEM((8, 128), f32)],
        compiler_params=params,
        cost_estimate=pl.CostEstimate(flops=density.size * 60, bytes_accessed=density.size * 20, transcendentals=density.size * 6),
        name="cells",
    )(kernel_taps, tf_centre.T, tf_width.T, tf_color.T, tf_opacity.T, brick_tf, view_order, density)

    strips, dd = lax.optimization_barrier((strips, dd))
    corners = [
        lax.ppermute(strips[2 * r + n], "sx", swaps)
        for r in range(len(y_swaps))
        for n, swaps in enumerate(x_swaps)
    ]

    block = rows_x // depth_count
    n_copies = 1 + len(x_swaps) + 2 * len(y_swaps) + len(corners)
    parts = pl.pallas_call(
        functools.partial(
            image_kernel, rim, depth_count, len(x_swaps), len(y_swaps), x_parity, y_parity, depth_index
        ),
        out_shape=[struct((4, block, rows_y), f32)] * depth_count,
        in_specs=[ANY] + [VMEM] * 6 + [ANY] * (n_copies - 1),
        out_specs=[VMEM] * depth_count,
        scratch_shapes=[
            pltpu.VMEM((rows_x + 2 * rim, rows_y + rim * len(y_swaps), rows_z), bf16),
            pltpu.VMEM((rows_y // rim + 2, rows_x, rim, rows_z), bf16),
            pltpu.VMEM((8, rows_y, 128), f32),
            pltpu.SemaphoreType.DMA((n_copies,)),
        ],
        compiler_params=params,
        name="image",
    )(coarse, g0, g1, g2, total, dd, ee, *x_halos, *strips, *corners)
    pieces = [parts[0]] + [
        lax.ppermute(parts[k], "depth", [(i, i ^ k) for i in range(depth_count)])
        for k in range(1, depth_count)
    ]
    return pl.pallas_call(
        functools.partial(picture_kernel, rim, depth_count, block, depth_index),
        out_shape=struct((4, 1, 1, block, rows_y), f32),
        in_specs=[SMEM] + [VMEM] * depth_count,
        out_specs=VMEM,
        compiler_params=pltpu.CompilerParams(vmem_limit_bytes=2 * 1024 * 1024),
        name="picture",
    )(view_order, *pieces)


def solution(mesh):
    return jax.shard_map(
        per_device,
        mesh=mesh,
        in_specs=(
            P("sx", "sy", "depth"),
            P(),
            P(),
            P(),
            P(),
            P(),
            P("sx", "sy", "depth"),
            P("sx", "sy"),
        ),
        out_specs=P(None, "sx", "depth", None, "sy"),
        check_vma=False,
    )
```

```python
import functools
import math
import jax
import jax.numpy as jnp
from jax import lax
from jax.experimental import pallas as pl
from jax.experimental.pallas import tpu as pltpu
from jax.sharding import PartitionSpec as P

LOG2E = math.log2(math.e)
VMEM = pl.BlockSpec(memory_space=pltpu.VMEM)
HBM = pl.BlockSpec(memory_space=pltpu.HBM)
MIB = 1024 * 1024
F32, BF16 = jnp.float32, jnp.bfloat16


def iota(shape, dim):
    return lax.broadcasted_iota(jnp.int32, shape, dim)


def line_swaps(count, shift):
    pairs = [(i, i + 1) for i in range(shift, count - 1, 2)]
    return pairs + [(b, a) for a, b in pairs]


class Place:
    def __init__(self):
        self.depth = lax.axis_index("depth")
        x_parity = lax.rem(lax.axis_index("sx") + self.depth, 2)
        y_parity = lax.rem(lax.axis_index("sy"), 2)
        self.half = (1 - x_parity, x_parity)
        self.group = (1 - y_parity, y_parity)


def group_rows(place, rim, g):
    return pl.ds(pl.multiple_of(place.group[g] * rim, rim), rim)


def half_rows(place, rim, h):
    return pl.ds(place.half[h] * rim, rim)


def first_kernel(rim, density, coarse, held, sems):
    place = Place()
    pieces = 4
    size = rim // pieces
    copies = []
    for i in range(pieces):
        copy = pltpu.make_async_copy(
            density.at[pl.ds(place.half[0] * rim + i * size, size)],
            held.at[i * size:(i + 1) * size],
            sems.at[i],
        )
        copy.start()
        copies.append(copy)
    for i, copy in enumerate(copies):
        copy.wait()
        rows = slice(i * size, (i + 1) * size)
        for g in range(2):
            coarse[g, rows] = held[rows, group_rows(place, rim, g), :].astype(BF16)


def toeplitz(taps, rim):
    return pltpu.roll(jnp.broadcast_to(taps, (rim, 128)), 0, 1, stride=1, stride_axis=0)


def blur_matrices(rim, place, taps):
    size = rim * rim
    wide = 3 * size
    shift = rim.bit_length() - 1
    pick = lambda mask: jnp.where(mask, 1.0, 0.0).astype(BF16)
    row_hi = pick(iota((size, rim), 0) >> shift == iota((size, rim), 1))
    row_lo = pick(iota((size, rim), 0) & (rim - 1) == iota((size, rim), 1))
    col = iota((128, wide), 1)
    src = iota((128, wide), 0)
    k, j, b = col >> 2 * shift, col >> shift & (rim - 1), col & (rim - 1)
    k_x = jnp.where(place.half[0] == 1, k, 2 - k)
    k_y = jnp.where(place.group[0] == 1, k, 2 - k)
    tx = toeplitz(taps[0:1], rim).astype(BF16)
    ty = toeplitz(taps[1:2] * 0.5, rim).astype(BF16)
    dot = functools.partial(jnp.dot, preferred_element_type=F32)
    full_x = dot(row_hi, dot(tx, pick(k_x * rim + j == src)).astype(BF16))
    full_y = dot(row_lo, dot(ty, pick(k_y * rim + b == src)).astype(BF16))
    r, c = iota((size, wide), 0), iota((size, wide), 1)
    mx = jnp.where(r & (rim - 1) == c & (rim - 1), full_x, 0.0)
    my = jnp.where(r >> shift == c >> shift & (rim - 1), full_y, 0.0)
    return mx.astype(BF16), my.astype(BF16)


def matrices_kernel(rim, taps, mx, my, padded):
    padded[...] = jnp.zeros(padded.shape, F32)
    padded[0:2, 0:taps.shape[1]] = taps[...].astype(F32)
    mx[...], my[...] = blur_matrices(rim, Place(), padded[...])


def cells_kernel(rim, bumps, h, *refs):
    tables, (density, *refs) = refs[:6], refs[6:]
    coarse = None
    if h == 1:
        coarse, *refs = refs
    shaded, total, order_map, optical_s, emitted_s, *refs = refs
    held, (*locals_, sems) = refs[0] if h == 1 else density, refs[h:]
    place = Place()
    copies = [
        pltpu.make_async_copy(src, dst, sems.at[i])
        for i, (src, dst) in enumerate(zip(tables, locals_))
    ]
    parts = []
    if h == 1:
        for g in range(2):
            at = group_rows(place, rim, g)
            parts.append(
                pltpu.make_async_copy(
                    density.at[half_rows(place, rim, h), at, :], held.at[:, at, :], sems.at[6 + g]
                )
            )
    for copy in copies + parts:
        copy.start()
    for copy in copies:
        copy.wait()
    centre, width, colour, opacity, brick_tf, view_order = locals_
    bricks = brick_tf.shape[2]
    rows_z = held.shape[2]
    depth = rows_z // bricks
    lane = iota((rim, 128), 1)
    for g in range(2):
        bx, by = place.half[h], place.group[g]
        cells = held.at[:, group_rows(place, rim, g), :]
        if h == 1:
            parts[g].wait()
            coarse[g] = cells[...].astype(BF16)
        for bz in range(bricks):
            zs = slice(bz * depth, (bz + 1) * depth)
            k = brick_tf[bx, by, bz]
            cen, neg, opa, col = [], [], [], []
            for j in range(bumps):
                cen.append(centre[j, k])
                wide = jnp.full((8, depth), width[j, k], F32)
                neg.append((-LOG2E / (wide * wide))[None])
                opa.append(opacity[j, k] * (-LOG2E))
                col.append([colour[c, j, k] * 0.5 for c in range(3)])
            for x in range(rim):
                d = cells[x, :, zs].reshape(rim // 8, 8, depth)
                opt, em = None, [None] * 3
                for j in range(bumps):
                    w = d - cen[j]
                    b = jnp.exp2((w * w) * neg[j])
                    opt = opa[j] * b if opt is None else opt + opa[j] * b
                    for c in range(3):
                        em[c] = col[j][c] * b if em[c] is None else em[c] + col[j][c] * b
                rows = slice(x * rim, (x + 1) * rim)
                optical_s[g, rows, zs] = opt.reshape(rim, depth)
                for c in range(3):
                    emitted_s[c, g, rows, zs] = em[c].reshape(rim, depth)
        order = view_order[bx, by]
        behind = iota((rows_z, rows_z), 1) - iota((rows_z, rows_z), 0)
        tri = jnp.where(behind * (1 - 2 * order) > 0, 1.0, 0.0).astype(BF16)
        opt = optical_s[g]
        hi = opt.astype(BF16)
        lo = (opt - hi.astype(F32)).astype(BF16)
        ahead = jnp.dot(hi, tri, preferred_element_type=F32)
        ahead = ahead + jnp.dot(lo, tri, preferred_element_type=F32)
        weight = jnp.exp2(ahead) * (1.0 - jnp.exp2(opt))
        for c in range(3):
            shaded[c, g] = (weight * emitted_s[c, g]).reshape(rim, rim, rows_z)
        total[g] = rays(opt.reshape(rim, rim, rows_z), bx * rim, lane)
    shape = order_map.shape
    block = shape[0]
    order = jnp.zeros(shape, jnp.int32)
    for y in range(2):
        order = jnp.where(
            iota(shape, 1) // rim == y, view_order[place.depth * block // rim, y], order
        )
    order_map[...] = order


def rays(cells, first_lane, lane):
    folded = cells[:, :, :128]
    for z in range(128, cells.shape[2], 128):
        folded = folded + cells[:, :, z:z + 128]
    summed = jnp.sum(folded, axis=2, keepdims=True)
    acc = jnp.zeros(lane.shape, F32)
    for x in range(cells.shape[0]):
        acc = jnp.where(lane == first_lane + x, summed[x], acc)
    return acc


def across_kernel(rim, mx, first, second, third, *outs):
    rows_z = first.shape[3]
    flat = (rim * rim, rows_z)
    for g, out in enumerate(outs):
        cells = jnp.concatenate([r[g].reshape(flat) for r in (first, second, third)], axis=0)
        blurred = jnp.dot(mx[...], cells, preferred_element_type=F32)
        out[...] = blurred.astype(BF16).reshape(out.shape)


def lit(rim, my_blocks, pieces, shaded, g, first_lane, lane):
    rows_z = pieces[0].shape[2]
    cells = jnp.concatenate([p.reshape(rim * rim, rows_z) for p in pieces], axis=0)
    occlusion = jnp.dot(my_blocks, cells, preferred_element_type=F32)
    shade = (1.0 - jnp.tanh(occlusion)).reshape(rim, rim, rows_z)
    return [rays(shade * shaded[c, g], first_lane, lane) for c in range(3)]


def early_kernel(rim, my, s0, e0, s1, e1, shaded0, shaded1, out):
    place = Place()
    size = rim * rim
    lane = iota((rim, 128), 1)
    acc = None
    for h, (s, e, shaded) in enumerate(((s0, e0, shaded0), (s1, e1, shaded1))):
        part = lit(rim, my[:, size:], (e[...], s[...]), shaded, 1, place.half[h] * rim, lane)
        acc = part if acc is None else [a + b for a, b in zip(acc, part)]
    for c in range(3):
        out[c] = acc[c]


def late_kernel(rim, h, reverse, my, s, e, halo, shaded, before, out):
    place = Place()
    lane = iota((rim, 128), 1)
    pieces = (halo[...], e[...], s[...]) if reverse else (e[...], s[...], halo[...])
    part = lit(rim, my[...], pieces, shaded, int(reverse), place.half[h] * rim, lane)
    for c in range(3):
        out[c] = part[c] if before is None else part[c] + before[c]


def blocks_kernel(rim, depth_count, late_s, late_e, total0, total1, *refs):
    outs, (img,) = refs[:depth_count], refs[depth_count:]
    place = Place()
    rows = 2 * rim
    for g, colours in enumerate((late_s, late_e)):
        at = group_rows(place, rim, g)
        for c in range(3):
            img[c, at, :] = colours[c]
        img[3, at, :] = jnp.exp2(total0[g] + total1[g])
    for c in range(4):
        img[4 + c, :, 0:rows] = img[c].T[:rows, :]
    block = rows // depth_count
    for k in range(depth_count):
        at = pl.multiple_of((place.depth ^ k) * block, block)
        outs[k][...] = img[4:8, pl.ds(at, block), 0:rows]


def picture_kernel(depth_count, order_map, *refs):
    parts = [ref[...] for ref in refs[:depth_count]]
    out = refs[depth_count]
    me = lax.axis_index("depth")
    bit = 0
    while len(parts) > 1:
        mine = (me >> bit & 1) == order_map[...]
        merged = []
        for a, b in zip(parts[::2], parts[1::2]):
            front = jnp.where(mine[None], a, b)
            back = jnp.where(mine[None], b, a)
            merged.append(
                jnp.concatenate([front[:3] + front[3:] * back[:3], front[3:] * back[3:]])
            )
        parts = merged
        bit += 1
    final = jnp.concatenate([parts[0][:3], 1.0 - parts[0][3:]])
    out[...] = final.reshape(out.shape)


def call(kernel, name, ins, outs, scratch=(), limit=16 * MIB, **more):
    return pl.pallas_call(
        kernel,
        out_shape=outs,
        in_specs=ins,
        out_specs=jax.tree.map(lambda _: VMEM, outs),
        scratch_shapes=list(scratch),
        compiler_params=pltpu.CompilerParams(vmem_limit_bytes=limit),
        name=name,
        **more,
    )


def per_device(
    density, kernel_taps, tf_centre, tf_width, tf_color, tf_opacity, brick_tf, view_order
):
    rows_x, rows_y, rows_z = density.shape
    rim = (kernel_taps.shape[1] - 1) // 2
    bumps = tf_centre.shape[1]
    size = rim * rim
    depth_count = lax.axis_size("depth")
    count_x, count_y = lax.axis_size("sx"), lax.axis_size("sy")
    struct = jax.ShapeDtypeStruct
    block = rows_x // depth_count

    def swap_x(piece, first):
        pairs = []
        for d in range(depth_count):
            pairs += [
                (d * count_x + a, d * count_x + b) for a, b in line_swaps(count_x, (first + d) % 2)
            ]
        return lax.ppermute(piece, ("depth", "sx"), pairs)

    def swap_y(piece, shift):
        pairs = line_swaps(count_y, shift)
        return lax.ppermute(piece, "sy", pairs) if pairs else None

    coarse = [None, None]
    coarse[0], held = call(
        functools.partial(first_kernel, rim),
        "first",
        [HBM],
        [struct((2, rim, rim, rows_z), BF16), struct((rim, rows_y, rows_z), F32)],
        [pltpu.SemaphoreType.DMA((4,))],
    )(density)
    halo_x = [swap_x(coarse[0], 0), None]
    shaded, total, order_map = [None, None], [None, None], None
    tables = (tf_centre.T, tf_width.T, tf_color.T, tf_opacity.T, brick_tf, view_order)
    for h in (1, 0):
        outs = [struct((2, rim, rim, rows_z), BF16)] if h == 1 else []
        outs += [struct((3, 2, rim, rim, rows_z), F32), struct((2, rim, 128), F32)]
        outs += [struct((block, rows_y), jnp.int32)]
        results = call(
            functools.partial(cells_kernel, rim, bumps, h),
            f"cells{h}",
            [HBM] * 6 + [HBM if h == 1 else VMEM],
            outs,
            [pltpu.VMEM((2, size, rows_z), F32), pltpu.VMEM((3, 2, size, rows_z), F32)]
            + ([pltpu.VMEM((rim, rows_y, rows_z), F32)] if h == 1 else [])
            + [pltpu.SMEM(t.shape, t.dtype) for t in tables]
            + [pltpu.SemaphoreType.DMA((8,))],
            cost_estimate=pl.CostEstimate(
                flops=density.size * 30, bytes_accessed=density.size * 10, transcendentals=density.size * 3
            ),
        )(*tables, density if h == 1 else held)
        if h == 1:
            coarse[1] = results[0]
            halo_x[1] = swap_x(coarse[1], 1)
        shaded[h], total[h], order_map = results[-3:]
    mx, my = call(
        functools.partial(matrices_kernel, rim),
        "matrices",
        [VMEM],
        [struct((size, 3 * size), BF16)] * 2,
        [pltpu.VMEM((8, 128), F32)],
    )(kernel_taps)

    strips, halo_y = [None, None], [None, None]
    for h in range(2):
        first, second, third = (
            (coarse[1], coarse[0], halo_x[0]) if h == 0 else (halo_x[1], coarse[1], coarse[0])
        )
        strips[h] = call(
            functools.partial(across_kernel, rim),
            f"across{h}",
            [VMEM] * 4,
            [struct((rim, rim, rows_z), BF16)] * 2,
        )(mx, first, second, third)
        halo_y[h] = [swap_y(strips[h][g], g) for g in range(2)]

    def late(h, g, before):
        halo = halo_y[h][g]
        if halo is None:
            halo = jnp.zeros_like(strips[h][g])
        args = [my, *strips[h], halo, shaded[h]] + ([] if before is None else [before])
        kernel = functools.partial(late_kernel, rim, h, g == 1)
        if before is None:
            kernel = lambda *refs: late_kernel(rim, h, g == 1, *refs[:5], None, *refs[5:])
        return call(
            kernel, f"late{h}{g}", [VMEM] * len(args), struct((3, rim, 128), F32)
        )(*args)

    if halo_y[0][1] is None:
        group1 = call(
            functools.partial(early_kernel, rim), "early", [VMEM] * 7, struct((3, rim, 128), F32)
        )(my, *strips[0], *strips[1], *shaded)
    else:
        group1 = late(1, 1, late(0, 1, None))
    group0 = late(1, 0, late(0, 0, None))

    parts = call(
        functools.partial(blocks_kernel, rim, depth_count),
        "blocks",
        [VMEM] * 4,
        [struct((4, block, rows_y), F32)] * depth_count,
        [pltpu.VMEM((8, rows_y, 128), F32)],
    )(group0, group1, *total)
    pieces = [parts[0]] + [
        lax.ppermute(parts[k], "depth", [(i, i ^ k) for i in range(depth_count)])
        for k in range(1, depth_count)
    ]
    return call(
        functools.partial(picture_kernel, depth_count),
        "picture",
        [VMEM] * (1 + depth_count),
        struct((4, 1, 1, block, rows_y), F32),
        limit=2 * MIB,
    )(order_map, *pieces)


def solution(mesh):
    return jax.shard_map(
        per_device,
        mesh=mesh,
        in_specs=(
            P("sx", "sy", "depth"),
            P(),
            P(),
            P(),
            P(),
            P(),
            P("sx", "sy", "depth"),
            P("sx", "sy"),
        ),
        out_specs=P(None, "sx", "depth", None, "sy"),
        check_vma=False,
    )
```

```python
import functools
import math
import jax
import jax.numpy as jnp
from jax import lax
from jax.experimental import pallas as pl
from jax.experimental.pallas import tpu as pltpu
from jax.sharding import PartitionSpec as P

LOG2E = math.log2(math.e)
VMEM = pl.BlockSpec(memory_space=pltpu.VMEM)
HBM = pl.BlockSpec(memory_space=pltpu.HBM)
MIB = 1024 * 1024
F32, BF16 = jnp.float32, jnp.bfloat16


def iota(shape, dim):
    return lax.broadcasted_iota(jnp.int32, shape, dim)


def both_ways(pairs):
    return pairs + [(b, a) for a, b in pairs]


def line_pairs(count, shift):
    return [(i, i + 1) for i in range(shift, count - 1, 2)]


def plane_swaps(depth_count, count, first):
    pairs, left = [], {}
    for d in range(depth_count):
        used = set()
        for a, b in line_pairs(count, (first + d) % 2):
            pairs.append((d * count + a, d * count + b))
            used |= {a, b}
        for a in range(count):
            if a not in used:
                left.setdefault(a, []).append(d * count + a)
    for over in left.values():
        pairs += list(zip(over[::2], over[1::2]))
    return both_ways(pairs)


class Place:
    def __init__(self):
        self.depth = lax.axis_index("depth")
        x_parity = lax.rem(lax.axis_index("sx") + self.depth, 2)
        y_parity = lax.rem(lax.axis_index("sy"), 2)
        self.half = (1 - x_parity, x_parity)
        at, last = lax.axis_index("sx"), lax.axis_size("sx") - 1
        self.has_halo = [
            jnp.logical_or(jnp.logical_and(h == 1, at < last), jnp.logical_and(h == 0, at > 0))
            for h in self.half
        ]
        self.group = (1 - y_parity, y_parity)


def group_rows(place, rim, g):
    return pl.ds(pl.multiple_of(place.group[g] * rim, rim), rim)


def half_rows(place, rim, h):
    return pl.ds(place.half[h] * rim, rim)


def first_kernel(rim, density, coarse, held, sems):
    place = Place()
    pieces = 4
    size = rim // pieces
    copies = []
    for i in range(pieces):
        copy = pltpu.make_async_copy(
            density.at[pl.ds(place.half[0] * rim + i * size, size)],
            held.at[i * size:(i + 1) * size],
            sems.at[i],
        )
        copy.start()
        copies.append(copy)
    for i, copy in enumerate(copies):
        copy.wait()
        rows = slice(i * size, (i + 1) * size)
        for g in range(2):
            coarse[g, rows] = held[rows, group_rows(place, rim, g), :].astype(BF16)


def toeplitz(taps, rim):
    return pltpu.roll(jnp.broadcast_to(taps, (rim, 128)), 0, 1, stride=1, stride_axis=0)


def blur_matrices(rim, place, taps):
    size = rim * rim
    wide = 3 * size
    shift = rim.bit_length() - 1
    pick = lambda mask: jnp.where(mask, 1.0, 0.0).astype(BF16)
    row_hi = pick(iota((size, rim), 0) >> shift == iota((size, rim), 1))
    row_lo = pick(iota((size, rim), 0) & (rim - 1) == iota((size, rim), 1))
    col = iota((128, wide), 1)
    src = iota((128, wide), 0)
    k, j, b = col >> 2 * shift, col >> shift & (rim - 1), col & (rim - 1)
    k_x = jnp.where(place.half[0] == 1, k, 2 - k)
    k_y = jnp.where(place.group[0] == 1, k, 2 - k)
    tx = toeplitz(taps[0:1], rim).astype(BF16)
    ty = toeplitz(taps[1:2] * 0.5, rim).astype(BF16)
    dot = functools.partial(jnp.dot, preferred_element_type=F32)
    full_x = dot(row_hi, dot(tx, pick(k_x * rim + j == src)).astype(BF16))
    full_y = dot(row_lo, dot(ty, pick(k_y * rim + b == src)).astype(BF16))
    r, c = iota((size, wide), 0), iota((size, wide), 1)
    mx = jnp.where(r & (rim - 1) == c & (rim - 1), full_x, 0.0)
    my = jnp.where(r >> shift == c >> shift & (rim - 1), full_y, 0.0)
    return mx.astype(BF16), my.astype(BF16)


def matrices_kernel(rim, taps, mx, my, padded):
    padded[...] = jnp.zeros(padded.shape, F32)
    padded[0:2, 0:taps.shape[1]] = taps[...].astype(F32)
    mx[...], my[...] = blur_matrices(rim, Place(), padded[...])


def cells_kernel(rim, bumps, h, *refs):
    tables, (density, *refs) = refs[:6], refs[6:]
    coarse = None
    if h == 1:
        coarse, *refs = refs
    shaded, total, order_map, optical_s, emitted_s, *refs = refs
    held, (*locals_, sems) = refs[0] if h == 1 else density, refs[h:]
    place = Place()
    copies = [
        pltpu.make_async_copy(src, dst, sems.at[i])
        for i, (src, dst) in enumerate(zip(tables, locals_))
    ]
    parts = []
    if h == 1:
        for g in range(2):
            at = group_rows(place, rim, g)
            parts.append(
                pltpu.make_async_copy(
                    density.at[half_rows(place, rim, h), at, :], held.at[:, at, :], sems.at[6 + g]
                )
            )
    for copy in copies + parts:
        copy.start()
    for copy in copies:
        copy.wait()
    centre, width, colour, opacity, brick_tf, view_order = locals_
    bricks = brick_tf.shape[2]
    rows_z = held.shape[2]
    depth = rows_z // bricks
    lane = iota((rim, 128), 1)
    for g in range(2):
        bx, by = place.half[h], place.group[g]
        cells = held.at[:, group_rows(place, rim, g), :]
        if h == 1:
            parts[g].wait()
            coarse[g] = cells[...].astype(BF16)
        for bz in range(bricks):
            zs = slice(bz * depth, (bz + 1) * depth)
            k = brick_tf[bx, by, bz]
            cen, neg, opa, col = [], [], [], []
            for j in range(bumps):
                cen.append(centre[j, k])
                wide = jnp.full((8, depth), width[j, k], F32)
                neg.append((-LOG2E / (wide * wide))[None])
                opa.append(opacity[j, k] * (-LOG2E))
                col.append([colour[c, j, k] * 0.5 for c in range(3)])
            for x in range(rim):
                d = cells[x, :, zs].reshape(rim // 8, 8, depth)
                opt, em = None, [None] * 3
                for j in range(bumps):
                    w = d - cen[j]
                    b = jnp.exp2((w * w) * neg[j])
                    opt = opa[j] * b if opt is None else opt + opa[j] * b
                    for c in range(3):
                        em[c] = col[j][c] * b if em[c] is None else em[c] + col[j][c] * b
                rows = slice(x * rim, (x + 1) * rim)
                optical_s[g, rows, zs] = opt.reshape(rim, depth)
                for c in range(3):
                    emitted_s[c, g, rows, zs] = em[c].reshape(rim, depth)
        order = view_order[bx, by]
        behind = iota((rows_z, rows_z), 1) - iota((rows_z, rows_z), 0)
        tri = jnp.where(behind * (1 - 2 * order) > 0, 1.0, 0.0).astype(BF16)
        opt = optical_s[g]
        hi = opt.astype(BF16)
        lo = (opt - hi.astype(F32)).astype(BF16)
        ahead = jnp.dot(hi, tri, preferred_element_type=F32)
        ahead = ahead + jnp.dot(lo, tri, preferred_element_type=F32)
        weight = jnp.exp2(ahead) * (1.0 - jnp.exp2(opt))
        for c in range(3):
            shaded[c, g] = (weight * emitted_s[c, g]).reshape(rim, rim, rows_z)
        total[g] = rays(opt.reshape(rim, rim, rows_z), bx * rim, lane)
    for n in range(order_map.shape[0]):
        shape = order_map.shape[1:]
        order = jnp.zeros(shape, jnp.int32)
        for y in range(2):
            order = jnp.where(
                iota(shape, 1) // rim == y, view_order[n * shape[0] // rim, y], order
            )
        order_map[n] = order


def rays(cells, first_lane, lane):
    folded = cells[:, :, :128]
    for z in range(128, cells.shape[2], 128):
        folded = folded + cells[:, :, z:z + 128]
    summed = jnp.sum(folded, axis=2, keepdims=True)
    acc = jnp.zeros(lane.shape, F32)
    for x in range(cells.shape[0]):
        acc = jnp.where(lane == first_lane + x, summed[x], acc)
    return acc


def across_kernel(rim, h, mx, first, second, third, *outs):
    place = Place()
    rows_z = first.shape[3]
    flat = (rim * rim, rows_z)
    for g, out in enumerate(outs):
        blocks = [r[g].reshape(flat) for r in (first, second, third)]
        halo = 0 if h == 1 else 2
        blocks[halo] = jnp.where(place.has_halo[h], blocks[halo], jnp.zeros_like(blocks[halo]))
        cells = jnp.concatenate(blocks, axis=0)
        blurred = jnp.dot(mx[...], cells, preferred_element_type=F32)
        out[...] = blurred.astype(BF16).reshape(out.shape)


def lit(rim, my_blocks, pieces, shaded, g, first_lane, lane):
    rows_z = pieces[0].shape[2]
    cells = jnp.concatenate([p.reshape(rim * rim, rows_z) for p in pieces], axis=0)
    occlusion = jnp.dot(my_blocks, cells, preferred_element_type=F32)
    shade = (1.0 - jnp.tanh(occlusion)).reshape(rim, rim, rows_z)
    return [rays(shade * shaded[c, g], first_lane, lane) for c in range(3)]


def early_kernel(rim, my, s0, e0, s1, e1, shaded0, shaded1, out):
    place = Place()
    size = rim * rim
    lane = iota((rim, 128), 1)
    acc = None
    for h, (s, e, shaded) in enumerate(((s0, e0, shaded0), (s1, e1, shaded1))):
        part = lit(rim, my[:, size:], (e[...], s[...]), shaded, 1, place.half[h] * rim, lane)
        acc = part if acc is None else [a + b for a, b in zip(acc, part)]
    for c in range(3):
        out[c] = acc[c]


def late_kernel(rim, h, reverse, my, s, e, halo, shaded, before, out):
    place = Place()
    lane = iota((rim, 128), 1)
    pieces = (halo[...], e[...], s[...]) if reverse else (e[...], s[...], halo[...])
    part = lit(rim, my[...], pieces, shaded, int(reverse), place.half[h] * rim, lane)
    for c in range(3):
        out[c] = part[c] if before is None else part[c] + before[c]


def blocks_kernel(rim, depth_count, late_s, late_e, total0, total1, *refs):
    outs, (img,) = refs[:2], refs[2:]
    place = Place()
    rows = 2 * rim
    for g, colours in enumerate((late_s, late_e)):
        at = group_rows(place, rim, g)
        for c in range(3):
            img[c, at, :] = colours[c]
        img[3, at, :] = jnp.exp2(total0[g] + total1[g])
    for c in range(4):
        img[4 + c, :, 0:rows] = img[c].T[:rows, :]
    block = rows // depth_count
    bit = place.depth & 1
    for n in range(depth_count // 2):
        for out, b in ((outs[0], bit), (outs[1], 1 - bit)):
            out[n] = img[4:8, pl.ds(pl.multiple_of((2 * n + b) * block, block), block), 0:rows]


def merge_kernel(level, order_map, kept, theirs, *outs):
    me = lax.axis_index("depth")
    bit = me >> level & 1
    low = me & (2 << level) - 1
    merged = []
    for n in range(kept.shape[0]):
        mine = (bit == order_map[(n << level + 1) + low])[None]
        front = jnp.where(mine, kept[n], theirs[n])
        back = jnp.where(mine, theirs[n], kept[n])
        merged.append((front[:3] + front[3:] * back[:3], front[3:] * back[3:]))
    if len(merged) == 1:
        colour, through = merged[0]
        outs[0][...] = jnp.concatenate([colour, 1.0 - through]).reshape(outs[0].shape)
        return
    up = me >> level + 1 & 1
    for n in range(len(merged) // 2):
        even, odd = (jnp.concatenate(merged[2 * n + i]) for i in range(2))
        outs[0][n] = jnp.where(up == 1, odd, even)
        outs[1][n] = jnp.where(up == 1, even, odd)


def call(kernel, name, ins, outs, scratch=(), limit=16 * MIB, **more):
    return pl.pallas_call(
        kernel,
        out_shape=outs,
        in_specs=ins,
        out_specs=jax.tree.map(lambda _: VMEM, outs),
        scratch_shapes=list(scratch),
        compiler_params=pltpu.CompilerParams(vmem_limit_bytes=limit),
        name=name,
        **more,
    )


def per_device(
    density, kernel_taps, tf_centre, tf_width, tf_color, tf_opacity, brick_tf, view_order
):
    rows_x, rows_y, rows_z = density.shape
    rim = (kernel_taps.shape[1] - 1) // 2
    bumps = tf_centre.shape[1]
    size = rim * rim
    depth_count = lax.axis_size("depth")
    count_x, count_y = lax.axis_size("sx"), lax.axis_size("sy")
    struct = jax.ShapeDtypeStruct
    block = rows_x // depth_count

    def swap_x(piece, first):
        return lax.ppermute(piece, ("depth", "sx"), plane_swaps(depth_count, count_x, first))

    def swap_y(piece, shift):
        pairs = both_ways(line_pairs(count_y, shift))
        return lax.ppermute(piece, "sy", pairs) if pairs else None

    in_hbm = lambda array: pltpu.with_memory_space_constraint(array, pltpu.HBM)
    density = in_hbm(density)
    coarse = [None, None]
    coarse[0], held = call(
        functools.partial(first_kernel, rim),
        "first",
        [HBM],
        [struct((2, rim, rim, rows_z), BF16), struct((rim, rows_y, rows_z), F32)],
        [pltpu.SemaphoreType.DMA((4,))],
    )(density)
    halo_x = [swap_x(coarse[0], 0), None]
    shaded, total, order_map = [None, None], [None, None], None
    tables = (tf_centre.T, tf_width.T, tf_color.T, tf_opacity.T, brick_tf, view_order)
    tables = [in_hbm(table) for table in tables]
    for h in (1, 0):
        outs = [struct((2, rim, rim, rows_z), BF16)] if h == 1 else []
        outs += [struct((3, 2, rim, rim, rows_z), F32), struct((2, rim, 128), F32)]
        outs += [struct((depth_count, block, rows_y), jnp.int32)]
        results = call(
            functools.partial(cells_kernel, rim, bumps, h),
            f"cells{h}",
            [HBM] * 6 + [HBM if h == 1 else VMEM],
            outs,
            [pltpu.VMEM((2, size, rows_z), F32), pltpu.VMEM((3, 2, size, rows_z), F32)]
            + ([pltpu.VMEM((rim, rows_y, rows_z), F32)] if h == 1 else [])
            + [pltpu.SMEM(t.shape, t.dtype) for t in tables]
            + [pltpu.SemaphoreType.DMA((8,))],
            cost_estimate=pl.CostEstimate(
                flops=density.size * 30, bytes_accessed=density.size * 10, transcendentals=density.size * 3
            ),
        )(*tables, density if h == 1 else held)
        if h == 1:
            coarse[1] = results[0]
            halo_x[1] = swap_x(coarse[1], 1)
        shaded[h], total[h], order_map = results[-3:]
    mx, my = call(
        functools.partial(matrices_kernel, rim),
        "matrices",
        [VMEM],
        [struct((size, 3 * size), BF16)] * 2,
        [pltpu.VMEM((8, 128), F32)],
    )(kernel_taps)

    strips, halo_y = [None, None], [None, None]
    for h in range(2):
        first, second, third = (
            (coarse[1], coarse[0], halo_x[0]) if h == 0 else (halo_x[1], coarse[1], coarse[0])
        )
        strips[h] = call(
            functools.partial(across_kernel, rim, h),
            f"across{h}",
            [VMEM] * 4,
            [struct((rim, rim, rows_z), BF16)] * 2,
        )(mx, first, second, third)
        halo_y[h] = [swap_y(strips[h][g], g) for g in range(2)]

    def late(h, g, before):
        halo = halo_y[h][g]
        if halo is None:
            halo = jnp.zeros_like(strips[h][g])
        args = [my, *strips[h], halo, shaded[h]] + ([] if before is None else [before])
        kernel = functools.partial(late_kernel, rim, h, g == 1)
        if before is None:
            kernel = lambda *refs: late_kernel(rim, h, g == 1, *refs[:5], None, *refs[5:])
        return call(
            kernel, f"late{h}{g}", [VMEM] * len(args), struct((3, rim, 128), F32)
        )(*args)

    if halo_y[0][1] is None:
        group1 = call(
            functools.partial(early_kernel, rim), "early", [VMEM] * 7, struct((3, rim, 128), F32)
        )(my, *strips[0], *strips[1], *shaded)
    else:
        group1 = late(1, 1, late(0, 1, None))
    group0 = late(1, 0, late(0, 0, None))

    kept, given = call(
        functools.partial(blocks_kernel, rim, depth_count),
        "blocks",
        [VMEM] * 4,
        [struct((depth_count // 2, 4, block, rows_y), F32)] * 2,
        [pltpu.VMEM((8, rows_y, 128), F32)],
    )(group0, group1, *total)
    level = 0
    while True:
        theirs = lax.ppermute(given, "depth", [(i, i ^ 1 << level) for i in range(depth_count)])
        left = kept.shape[0] // 2
        outs = [struct((left, 4, block, rows_y), F32)] * 2
        merged = call(
            functools.partial(merge_kernel, level),
            f"merge{level}",
            [VMEM] * 3,
            outs if left else struct((4, 1, 1, block, rows_y), F32),
            limit=2 * MIB,
        )(order_map, kept, theirs)
        if not left:
            return merged
        kept, given = merged
        level += 1


def solution(mesh):
    return jax.shard_map(
        per_device,
        mesh=mesh,
        in_specs=(
            P("sx", "sy", "depth"),
            P(),
            P(),
            P(),
            P(),
            P(),
            P("sx", "sy", "depth"),
            P("sx", "sy"),
        ),
        out_specs=P(None, "sx", "depth", None, "sy"),
        check_vma=False,
    )
```

```python
import functools
import math
import jax
import jax.numpy as jnp
from jax import lax
from jax.experimental import pallas as pl
from jax.experimental.pallas import tpu as pltpu
from jax.sharding import PartitionSpec as P

LOG2E = math.log2(math.e)
VMEM = pl.BlockSpec(memory_space=pltpu.VMEM)
HBM = pl.BlockSpec(memory_space=pltpu.HBM)
MIB = 1024 * 1024
F32, BF16 = jnp.float32, jnp.bfloat16


def iota(shape, dim):
    return lax.broadcasted_iota(jnp.int32, shape, dim)


def both_ways(pairs):
    return pairs + [(b, a) for a, b in pairs]


def line_pairs(count, shift):
    return [(i, i + 1) for i in range(shift, count - 1, 2)]


def plane_swaps(depth_count, count, first):
    pairs, left = [], {}
    for d in range(depth_count):
        used = set()
        for a, b in line_pairs(count, (first + d) % 2):
            pairs.append((d * count + a, d * count + b))
            used |= {a, b}
        for a in range(count):
            if a not in used:
                left.setdefault(a, []).append(d * count + a)
    for over in left.values():
        pairs += list(zip(over[::2], over[1::2]))
    return both_ways(pairs)


class Place:
    def __init__(self):
        self.depth = lax.axis_index("depth")
        x_parity = lax.rem(lax.axis_index("sx") + self.depth, 2)
        y_parity = lax.rem(lax.axis_index("sy"), 2)
        self.half = (1 - x_parity, x_parity)
        at, last = lax.axis_index("sx"), lax.axis_size("sx") - 1
        self.has_halo = [
            jnp.logical_or(jnp.logical_and(h == 1, at < last), jnp.logical_and(h == 0, at > 0))
            for h in self.half
        ]
        self.group = (1 - y_parity, y_parity)


def group_rows(place, rim, g):
    return pl.ds(pl.multiple_of(place.group[g] * rim, rim), rim)


def half_rows(place, rim, h):
    return pl.ds(place.half[h] * rim, rim)


def first_kernel(rim, density, held, coarse0, coarse1, sems):
    place = Place()
    copies = [
        pltpu.make_async_copy(
            density.at[half_rows(place, rim, h), group_rows(place, rim, 0), :], held.at[h], sems.at[h]
        )
        for h in range(2)
    ]
    for copy in copies:
        copy.start()
    for h, coarse in enumerate((coarse0, coarse1)):
        copies[h].wait()
        coarse[...] = held[h].astype(BF16)


def toeplitz(taps, rim):
    return pltpu.roll(jnp.broadcast_to(taps, (rim, 128)), 0, 1, stride=1, stride_axis=0)


def blur_matrices(rim, place, taps):
    size = rim * rim
    wide = 3 * size
    shift = rim.bit_length() - 1
    pick = lambda mask: jnp.where(mask, 1.0, 0.0).astype(BF16)
    row_hi = pick(iota((size, rim), 0) >> shift == iota((size, rim), 1))
    row_lo = pick(iota((size, rim), 0) & (rim - 1) == iota((size, rim), 1))
    col = iota((128, wide), 1)
    src = iota((128, wide), 0)
    k, j, b = col >> 2 * shift, col >> shift & (rim - 1), col & (rim - 1)
    k_x = jnp.where(place.half[0] == 1, k, 2 - k)
    k_y = jnp.where(place.group[0] == 1, k, 2 - k)
    tx = toeplitz(taps[0:1], rim).astype(BF16)
    ty = toeplitz(taps[1:2] * 0.5, rim).astype(BF16)
    dot = functools.partial(jnp.dot, preferred_element_type=F32)
    full_x = dot(row_hi, dot(tx, pick(k_x * rim + j == src)).astype(BF16))
    full_y = dot(row_lo, dot(ty, pick(k_y * rim + b == src)).astype(BF16))
    r, c = iota((size, wide), 0), iota((size, wide), 1)
    mx = jnp.where(r & (rim - 1) == c & (rim - 1), full_x, 0.0)
    my = jnp.where(r >> shift == c >> shift & (rim - 1), full_y, 0.0)
    return mx.astype(BF16), my.astype(BF16)


def matrices_kernel(rim, taps, mx, my, padded):
    padded[...] = jnp.zeros(padded.shape, F32)
    padded[0:2, 0:taps.shape[1]] = taps[...].astype(F32)
    mx[...], my[...] = blur_matrices(rim, Place(), padded[...])


def cells_kernel(rim, bumps, g, *refs):
    tables, (density, *refs) = refs[:6], refs[6:]
    coarse, held = None, density
    if g == 1:
        *coarse, = refs[:2]
        refs = refs[2:]
    shaded, total, order_map, optical_s, emitted_s, *refs = refs
    if g == 1:
        held, *refs = refs
    *locals_, sems = refs
    place = Place()
    copies = [
        pltpu.make_async_copy(src, dst, sems.at[i])
        for i, (src, dst) in enumerate(zip(tables, locals_))
    ]
    parts = []
    if g == 1:
        for h in range(2):
            rows = density.at[half_rows(place, rim, h), group_rows(place, rim, g), :]
            parts.append(pltpu.make_async_copy(rows, held.at[h], sems.at[6 + h]))
    for copy in parts + copies:
        copy.start()
    for copy in copies:
        copy.wait()
    centre, width, colour, opacity, brick_tf, view_order = locals_
    bricks = brick_tf.shape[2]
    rows_z = held.shape[3]
    depth = rows_z // bricks
    lane = iota((rim, 128), 1)
    for h in range(2):
        bx, by = place.half[h], place.group[g]
        cells = held.at[h]
        if g == 1:
            parts[h].wait()
            coarse[h][...] = cells[...].astype(BF16)
        for bz in range(bricks):
            zs = slice(bz * depth, (bz + 1) * depth)
            k = brick_tf[bx, by, bz]
            cen, neg, opa, col = [], [], [], []
            for j in range(bumps):
                cen.append(centre[j, k])
                wide = jnp.full((8, depth), width[j, k], F32)
                neg.append((-LOG2E / (wide * wide))[None])
                opa.append(opacity[j, k] * (-LOG2E))
                col.append([colour[c, j, k] * 0.5 for c in range(3)])
            for x in range(rim):
                d = cells[x, :, zs].reshape(rim // 8, 8, depth)
                opt, em = None, [None] * 3
                for j in range(bumps):
                    w = d - cen[j]
                    b = jnp.exp2((w * w) * neg[j])
                    opt = opa[j] * b if opt is None else opt + opa[j] * b
                    for c in range(3):
                        em[c] = col[j][c] * b if em[c] is None else em[c] + col[j][c] * b
                rows = slice(x * rim, (x + 1) * rim)
                optical_s[h, rows, zs] = opt.reshape(rim, depth)
                for c in range(3):
                    emitted_s[c, h, rows, zs] = em[c].reshape(rim, depth)
        order = view_order[bx, by]
        behind = iota((rows_z, rows_z), 1) - iota((rows_z, rows_z), 0)
        tri = jnp.where(behind * (1 - 2 * order) > 0, 1.0, 0.0).astype(BF16)
        opt = optical_s[h]
        hi = opt.astype(BF16)
        lo = (opt - hi.astype(F32)).astype(BF16)
        ahead = jnp.dot(hi, tri, preferred_element_type=F32)
        ahead = ahead + jnp.dot(lo, tri, preferred_element_type=F32)
        weight = jnp.exp2(ahead) * (1.0 - jnp.exp2(opt))
        for c in range(3):
            shaded[c, h] = (weight * emitted_s[c, h]).reshape(rim, rim, rows_z)
        part = rays(opt.reshape(rim, rim, rows_z), bx * rim, lane)
        total[...] = part if h == 0 else total[...] + part
    for n in range(order_map.shape[0]):
        shape = order_map.shape[1:]
        order = jnp.zeros(shape, jnp.int32)
        for y in range(2):
            order = jnp.where(
                iota(shape, 1) // rim == y, view_order[n * shape[0] // rim, y], order
            )
        order_map[n] = order


def rays(cells, first_lane, lane):
    folded = cells[:, :, :128]
    for z in range(128, cells.shape[2], 128):
        folded = folded + cells[:, :, z:z + 128]
    summed = jnp.sum(folded, axis=2, keepdims=True)
    acc = jnp.zeros(lane.shape, F32)
    for x in range(cells.shape[0]):
        acc = jnp.where(lane == first_lane + x, summed[x], acc)
    return acc


def across_kernel(rim, mx, coarse0, coarse1, halo0, halo1, *outs):
    place = Place()
    rows_z = coarse0.shape[2]
    flat = lambda r: r[...].reshape(rim * rim, rows_z)
    halos = []
    for h, halo in enumerate((halo0, halo1)):
        cells = flat(halo)
        halos.append(jnp.where(place.has_halo[h], cells, jnp.zeros_like(cells)))
    blocks = [halos[1], flat(coarse1), flat(coarse0), halos[0]]
    for h, out in enumerate(outs):
        cells = jnp.concatenate(blocks[1 - h:4 - h], axis=0)
        blurred = jnp.dot(mx[...], cells, preferred_element_type=F32)
        out[...] = blurred.astype(BF16).reshape(out.shape)


def lit(rim, my_blocks, pieces, shaded, h, first_lane, lane):
    rows_z = pieces[0].shape[2]
    cells = jnp.concatenate([p.reshape(rim * rim, rows_z) for p in pieces], axis=0)
    occlusion = jnp.dot(my_blocks, cells, preferred_element_type=F32)
    shade = (1.0 - jnp.tanh(occlusion)).reshape(rim, rim, rows_z)
    return [rays(shade * shaded[c, h], first_lane, lane) for c in range(3)]


def early_kernel(rim, my, s0, s1, e0, e1, shaded, out):
    place = Place()
    lane = iota((rim, 128), 1)
    acc = None
    for h, (s, e) in enumerate(((s0, e0), (s1, e1))):
        pieces = (e[...], s[...])
        part = lit(rim, my[:, rim * rim:], pieces, shaded, h, place.half[h] * rim, lane)
        acc = part if acc is None else [a + b for a, b in zip(acc, part)]
    for c in range(3):
        out[c] = acc[c]


def late_kernel(rim, h, reverse, my, s, e, halo, shaded, before, out):
    place = Place()
    lane = iota((rim, 128), 1)
    pieces = (halo[...], e[...], s[...]) if reverse else (e[...], s[...], halo[...])
    part = lit(rim, my[...], pieces, shaded, h, place.half[h] * rim, lane)
    for c in range(3):
        out[c] = part[c] if before is None else part[c] + before[c]


def blocks_kernel(rim, depth_count, late_s, late_e, total0, total1, *refs):
    outs, (img,) = refs[:2], refs[2:]
    place = Place()
    rows = 2 * rim
    for g, colours in enumerate((late_s, late_e)):
        at = group_rows(place, rim, g)
        for c in range(3):
            img[c, at, :] = colours[c]
        img[3, at, :] = jnp.exp2((total0, total1)[g][...])
    for c in range(4):
        img[4 + c, :, 0:rows] = img[c].T[:rows, :]
    block = rows // depth_count
    bit = place.depth & 1
    for n in range(depth_count // 2):
        for out, b in ((outs[0], bit), (outs[1], 1 - bit)):
            out[n] = img[4:8, pl.ds(pl.multiple_of((2 * n + b) * block, block), block), 0:rows]


def merge_kernel(level, order_map, kept, theirs, *outs):
    me = lax.axis_index("depth")
    bit = me >> level & 1
    low = me & (2 << level) - 1
    merged = []
    for n in range(kept.shape[0]):
        mine = (bit == order_map[(n << level + 1) + low])[None]
        front = jnp.where(mine, kept[n], theirs[n])
        back = jnp.where(mine, theirs[n], kept[n])
        merged.append((front[:3] + front[3:] * back[:3], front[3:] * back[3:]))
    if len(merged) == 1:
        colour, through = merged[0]
        outs[0][...] = jnp.concatenate([colour, 1.0 - through]).reshape(outs[0].shape)
        return
    up = me >> level + 1 & 1
    for n in range(len(merged) // 2):
        even, odd = (jnp.concatenate(merged[2 * n + i]) for i in range(2))
        outs[0][n] = jnp.where(up == 1, odd, even)
        outs[1][n] = jnp.where(up == 1, even, odd)


def call(kernel, name, ins, outs, scratch=(), limit=16 * MIB, **more):
    return pl.pallas_call(
        kernel,
        out_shape=outs,
        in_specs=ins,
        out_specs=jax.tree.map(lambda _: VMEM, outs),
        scratch_shapes=list(scratch),
        compiler_params=pltpu.CompilerParams(vmem_limit_bytes=limit),
        name=name,
        **more,
    )


def per_device(
    density, kernel_taps, tf_centre, tf_width, tf_color, tf_opacity, brick_tf, view_order
):
    rows_x, rows_y, rows_z = density.shape
    rim = (kernel_taps.shape[1] - 1) // 2
    bumps = tf_centre.shape[1]
    size = rim * rim
    depth_count = lax.axis_size("depth")
    count_x, count_y = lax.axis_size("sx"), lax.axis_size("sy")
    struct = jax.ShapeDtypeStruct
    block = rows_x // depth_count

    def swap_x(piece, first):
        return lax.ppermute(piece, ("depth", "sx"), plane_swaps(depth_count, count_x, first))

    def swap_y(piece, shift):
        pairs = both_ways(line_pairs(count_y, shift))
        return lax.ppermute(piece, "sy", pairs) if pairs else None

    in_hbm = lambda array: pltpu.with_memory_space_constraint(array, pltpu.HBM)
    density = in_hbm(density)
    piece = struct((rim, rim, rows_z), BF16)
    coarse, halo_x = [None, None], [None, None]
    held, *coarse[0] = call(
        functools.partial(first_kernel, rim),
        "first",
        [HBM],
        [struct((2, rim, rim, rows_z), F32), piece, piece],
        [pltpu.SemaphoreType.DMA((2,))],
    )(density)
    halo_x[0] = [swap_x(coarse[0][h], h) for h in range(2)]
    shaded, total, order_map = [None, None], [None, None], None
    tables = (tf_centre.T, tf_width.T, tf_color.T, tf_opacity.T, brick_tf, view_order)
    tables = [in_hbm(table) for table in tables]
    for g in (1, 0):
        outs = [piece, piece] if g == 1 else []
        outs += [struct((3, 2, rim, rim, rows_z), F32), struct((rim, 128), F32)]
        outs += [struct((depth_count, block, rows_y), jnp.int32)]
        results = call(
            functools.partial(cells_kernel, rim, bumps, g),
            f"cells{g}",
            [HBM] * 6 + [HBM if g == 1 else VMEM],
            outs,
            [pltpu.VMEM((2, size, rows_z), F32), pltpu.VMEM((3, 2, size, rows_z), F32)]
            + ([pltpu.VMEM((2, rim, rim, rows_z), F32)] if g == 1 else [])
            + [pltpu.SMEM(t.shape, t.dtype) for t in tables]
            + [pltpu.SemaphoreType.DMA((8,))],
            cost_estimate=pl.CostEstimate(
                flops=density.size * 30, bytes_accessed=density.size * 10, transcendentals=density.size * 3
            ),
        )(*tables, density if g == 1 else held)
        if g == 1:
            coarse[1] = results[:2]
            halo_x[1] = [swap_x(coarse[1][h], h) for h in range(2)]
        shaded[g], total[g], order_map = results[-3:]
    mx, my = call(
        functools.partial(matrices_kernel, rim),
        "matrices",
        [VMEM],
        [struct((size, 3 * size), BF16)] * 2,
        [pltpu.VMEM((8, 128), F32)],
    )(kernel_taps)

    strips, halo_y = [None, None], [None, None]
    for g in range(2):
        strips[g] = call(
            functools.partial(across_kernel, rim), f"across{g}", [VMEM] * 5, [piece, piece]
        )(mx, *coarse[g], *halo_x[g])
        halo_y[g] = [swap_y(strips[g][h], g) for h in range(2)]

    def late(h, g, before):
        halo = halo_y[g][h]
        args = [my, strips[0][h], strips[1][h], halo, shaded[g]]
        args += [] if before is None else [before]
        kernel = functools.partial(late_kernel, rim, h, g == 1)
        if before is None:
            kernel = lambda *refs: late_kernel(rim, h, g == 1, *refs[:5], None, *refs[5:])
        return call(
            kernel, f"late{h}{g}", [VMEM] * len(args), struct((3, rim, 128), F32)
        )(*args)

    if halo_y[1][0] is None:
        group1 = call(
            functools.partial(early_kernel, rim), "early", [VMEM] * 6, struct((3, rim, 128), F32)
        )(my, *strips[0], *strips[1], shaded[1])
    else:
        group1 = late(1, 1, late(0, 1, None))
    group0 = late(1, 0, late(0, 0, None))

    kept, given = call(
        functools.partial(blocks_kernel, rim, depth_count),
        "blocks",
        [VMEM] * 4,
        [struct((depth_count // 2, 4, block, rows_y), F32)] * 2,
        [pltpu.VMEM((8, rows_y, 128), F32)],
    )(group0, group1, *total)
    level = 0
    while True:
        theirs = lax.ppermute(given, "depth", [(i, i ^ 1 << level) for i in range(depth_count)])
        left = kept.shape[0] // 2
        outs = [struct((left, 4, block, rows_y), F32)] * 2
        merged = call(
            functools.partial(merge_kernel, level),
            f"merge{level}",
            [VMEM] * 3,
            outs if left else struct((4, 1, 1, block, rows_y), F32),
            limit=2 * MIB,
        )(order_map, kept, theirs)
        if not left:
            return merged
        kept, given = merged
        level += 1


def solution(mesh):
    return jax.shard_map(
        per_device,
        mesh=mesh,
        in_specs=(
            P("sx", "sy", "depth"),
            P(),
            P(),
            P(),
            P(),
            P(),
            P("sx", "sy", "depth"),
            P("sx", "sy"),
        ),
        out_specs=P(None, "sx", "depth", None, "sy"),
        check_vma=False,
    )
```

```python
import functools
import math
import jax
import jax.numpy as jnp
from jax import lax
from jax.experimental import pallas as pl
from jax.experimental.pallas import tpu as pltpu
from jax.sharding import PartitionSpec as P

LOG2E = math.log2(math.e)
VMEM = pl.BlockSpec(memory_space=pltpu.VMEM)
HBM = pl.BlockSpec(memory_space=pltpu.HBM)
MIB = 1024 * 1024
F32, BF16 = jnp.float32, jnp.bfloat16
dot = functools.partial(jnp.dot, preferred_element_type=F32)


def iota(shape, dim):
    return lax.broadcasted_iota(jnp.int32, shape, dim)


def line_pairs(count, shift):
    return [(i, i + 1) for i in range(shift, count - 1, 2)]


def swaps(counts, x_round, y_round):
    depth_count, count_x, count_y = counts
    index = lambda d, x, y: (d * count_x + x) * count_y + y
    stay = lambda count: [(i, i) for i in range(count)]
    pairs_x = stay(count_x) if x_round is None else line_pairs(count_x, x_round)
    pairs_y = stay(count_y) if y_round is None else line_pairs(count_y, y_round)
    ends = {((a, c), (b, e)) for a, b in pairs_x for c, e in pairs_y}
    if x_round is not None and y_round is not None:
        ends |= {((a, e), (b, c)) for a, b in pairs_x for c, e in pairs_y}
    used = {end for pair in ends for end in pair}
    pairs = []
    for d in range(depth_count):
        pairs += [(index(d, *a), index(d, *b)) for a, b in sorted(ends)]
    for x in range(count_x):
        for y in range(count_y):
            if (x, y) not in used:
                pairs += [
                    (index(d, x, y), index(d + 1, x, y)) for d in range(0, depth_count - 1, 2)
                ]
    return pairs + [(b, a) for a, b in pairs]


class Place:
    def __init__(self):
        self.depth = lax.axis_index("depth")
        self.half, self.has_x = self.sides("sx")
        self.group, self.has_y = self.sides("sy")

    def sides(self, axis):
        at, last = lax.axis_index(axis), lax.axis_size(axis) - 1
        parity = lax.rem(at, 2)
        upper, lower = at < last, at > 0
        order = (1 - parity, parity)
        either = lambda side: jnp.where(side == 1, upper.astype(jnp.int32), lower.astype(jnp.int32))
        return order, [either(side) == 1 for side in order]


def group_rows(place, rim, g):
    return pl.ds(pl.multiple_of(place.group[g] * rim, rim), rim)


def half_rows(place, rim, h):
    return pl.ds(place.half[h] * rim, rim)


def first_kernel(rim, rounds, density, *refs):
    place = Place()
    n_tables = (len(refs) - 4 - 2 * rounds) // 2
    tables, refs = refs[:n_tables], refs[n_tables:]
    held, xs, refs = refs[0], refs[1:3], refs[3:]
    strips, refs = refs[:2 * rounds], refs[2 * rounds:]
    tables_out, sems = refs[:n_tables], refs[n_tables]
    copies = []
    for g in range(2):
        for h in range(2):
            rows = density.at[half_rows(place, rim, h), group_rows(place, rim, g), :]
            copies.append(pltpu.make_async_copy(rows, held.at[g, h], sems.at[2 * g + h]))
    for i, (src, dst) in enumerate(zip(tables, tables_out)):
        copies.append(pltpu.make_async_copy(src, dst, sems.at[4 + i]))
    for copy in copies:
        copy.start()
    for g in range(2):
        for h in range(2):
            copies[2 * g + h].wait()
            coarse = held[g, h].astype(BF16)
            xs[h][g] = coarse
            if g < rounds:
                strips[2 * g + h][...] = coarse
    for copy in copies[4:]:
        copy.wait()


def toeplitz(taps, rim):
    return pltpu.roll(jnp.broadcast_to(taps, (rim, 128)), 0, 1, stride=1, stride_axis=0)


def blur_matrices(rim, place, taps):
    size = rim * rim
    wide = 3 * size
    shift = rim.bit_length() - 1
    pick = lambda mask: jnp.where(mask, 1.0, 0.0).astype(BF16)
    row_hi = pick(iota((size, rim), 0) >> shift == iota((size, rim), 1))
    row_lo = pick(iota((size, rim), 0) & (rim - 1) == iota((size, rim), 1))
    col = iota((128, wide), 1)
    src = iota((128, wide), 0)
    k, j, b = col >> 2 * shift, col >> shift & (rim - 1), col & (rim - 1)
    k_x = jnp.where(place.half[0] == 1, k, 2 - k)
    k_y = jnp.where(place.group[0] == 1, k, 2 - k)
    tx = toeplitz(taps[0:1], rim).astype(BF16)
    ty = toeplitz(taps[1:2] * 0.5, rim).astype(BF16)
    full_x = dot(row_hi, dot(tx, pick(k_x * rim + j == src)).astype(BF16))
    full_y = dot(row_lo, dot(ty, pick(k_y * rim + b == src)).astype(BF16))
    r, c = iota((size, size), 0), iota((size, size), 1)
    same_x = r & (rim - 1) == c & (rim - 1)
    same_y = r >> shift == c >> shift
    parts = []
    for full, same in ((full_x, same_x), (full_y, same_y)):
        blocks = [
            jnp.where(same, full[:, n * size:(n + 1) * size], 0.0).astype(BF16) for n in range(3)
        ]
        parts.append(jnp.concatenate(blocks, axis=1))
    return parts


def prepare_kernel(
    rim, taps, centre, width, colour, opacity, brick_tf, view_order,
    mx, my, table, signs, order_map, padded
):
    place = Place()
    padded[...] = jnp.zeros(padded.shape, F32)
    padded[0:2, 0:taps.shape[1]] = taps[...].astype(F32)
    mx[...], my[...] = blur_matrices(rim, place, padded[...])
    wide = width[...]
    rows = [centre[...], (-LOG2E) / (wide * wide), opacity[...] * (-LOG2E)]
    rows += [colour[c] * 0.5 for c in range(3)]
    rows = jnp.concatenate(rows, axis=0)
    which = iota(rows.shape, 1)
    n = 0
    for g in range(2):
        for h in range(2):
            bricks = brick_tf[place.half[h]]
            bricks = jnp.where(place.group[g] == 0, bricks[0:1], bricks[1:2])
            for bz in range(bricks.shape[1]):
                mine = jnp.where(which == bricks[:, bz:bz + 1], rows, 0.0)
                mine = jnp.sum(mine, axis=1, keepdims=True)
                table[n] = jnp.broadcast_to(mine, table.shape[1:])
                n += 1
            orders = view_order[...]
            orders = jnp.where(place.half[h] == 0, orders[0:1], orders[1:2])
            order = jnp.where(place.group[g] == 0, orders[:, 0:1], orders[:, 1:2])
            signs[g, h] = jnp.broadcast_to(1 - 2 * order, signs.shape[2:])
    block, shape = order_map.shape[1], order_map.shape[1:]
    for n in range(order_map.shape[0]):
        brick = n * block // rim
        orders = view_order[brick:brick + 1]
        order_map[n] = jnp.where(
            iota(shape, 1) < rim,
            jnp.broadcast_to(orders[:, 0:1], shape),
            jnp.broadcast_to(orders[:, 1:2], shape),
        )


def cells_kernel(rim, bumps, g, held, table, signs, shaded, total, optical_s, emitted_s):
    place = Place()
    rows_z = held.shape[4]
    depth = 128
    bricks = rows_z // depth
    lane = iota((rim, 128), 1)
    for h in range(2):
        cells = held.at[g, h]
        for bz in range(bricks):
            zs = slice(bz * depth, (bz + 1) * depth)
            at = (2 * g + h) * bricks + bz
            row = lambda i: jnp.broadcast_to(table[at, i:i + 1, :], (8, depth))[None]
            cen = [row(j) for j in range(bumps)]
            neg = [row(bumps + j) for j in range(bumps)]
            opa = [row(2 * bumps + j) for j in range(bumps)]
            col = [[row((3 + c) * bumps + j) for c in range(3)] for j in range(bumps)]
            for x in range(rim):
                d = cells[x, :, zs].reshape(rim // 8, 8, depth)
                opt, em = None, [None] * 3
                for j in range(bumps):
                    w = d - cen[j]
                    b = jnp.exp2((w * w) * neg[j])
                    opt = opa[j] * b if opt is None else opt + opa[j] * b
                    for c in range(3):
                        em[c] = col[j][c] * b if em[c] is None else em[c] + col[j][c] * b
                rows = slice(x * rim, (x + 1) * rim)
                optical_s[h, rows, zs] = opt.reshape(rim, depth)
                for c in range(3):
                    emitted_s[c, h, rows, zs] = em[c].reshape(rim, depth)
        behind = iota((rows_z, rows_z), 1) - iota((rows_z, rows_z), 0)
        sign = jnp.broadcast_to(signs[g, h][0:1, 0:1], (rows_z, rows_z))
        tri = jnp.where(behind * sign > 0, 1.0, 0.0).astype(BF16)
        opt = optical_s[h]
        hi = opt.astype(BF16)
        lo = (opt - hi.astype(F32)).astype(BF16)
        ahead = dot(hi, tri) + dot(lo, tri)
        weight = jnp.exp2(ahead) * (1.0 - jnp.exp2(opt))
        for c in range(3):
            shaded[c, h] = (weight * emitted_s[c, h]).reshape(rim, rim, rows_z)
        part = rays(opt.reshape(rim, rim, rows_z), place.half[h] * rim, lane)
        total[...] = part if h == 0 else total[...] + part


def rays(cells, first_lane, lane):
    folded = cells[:, :, :128]
    for z in range(128, cells.shape[2], 128):
        folded = folded + cells[:, :, z:z + 128]
    summed = jnp.sum(folded, axis=2, keepdims=True)
    acc = jnp.zeros(lane.shape, F32)
    for x in range(cells.shape[0]):
        acc = jnp.where(lane == first_lane + x, summed[x], acc)
    return acc


def blur_x(place, rim, mx, near, halos):
    flat = lambda cells: cells.reshape(rim * rim, cells.shape[-1])
    edges = []
    for h, halo in enumerate(halos):
        cells = flat(halo)
        edges.append(jnp.where(place.has_x[h], cells, jnp.zeros_like(cells)))
    blocks = [edges[1], flat(near[1]), flat(near[0]), edges[0]]
    return [
        dot(mx[...], jnp.concatenate(blocks[1 - h:4 - h], axis=0)).astype(BF16) for h in range(2)
    ]


def lit(place, rim, occlusion, shaded, h):
    rows_z = occlusion.shape[1]
    lane = iota((rim, 128), 1)
    shade = (1.0 - jnp.tanh(occlusion)).reshape(rim, rim, rows_z)
    return [rays(shade * shaded[c, h], place.half[h] * rim, lane) for c in range(3)]


def own_kernel(rim, early, mx, my, xs0, xs1, halo0, halo1, *refs):
    place = Place()
    size = rim * rim
    across = [
        blur_x(place, rim, mx, [xs0[g], xs1[g]], [halo0[g], halo1[g]]) for g in range(2)
    ]
    if early:
        shaded, out, partial = refs
    else:
        partial, = refs
    for h in range(2):
        s, e = across[0][h], across[1][h]
        partial[0, h] = dot(my[:, :2 * size], jnp.concatenate([e, s], axis=0))
        other = dot(my[:, size:], jnp.concatenate([e, s], axis=0))
        if not early:
            partial[1, h] = other
            continue
        part = lit(place, rim, other, shaded, h)
        for c in range(3):
            out[c] = part[c] if h == 0 else out[c] + part[c]


def late_kernel(rim, g, mx, my, near0, near1, halo0, halo1, partial, shaded, out):
    place = Place()
    size = rim * rim
    across = blur_x(place, rim, mx, [near0[...], near1[...]], [halo0[...], halo1[...]])
    block = my[:, 2 * size:] if g == 0 else my[:, :size]
    for h in range(2):
        cells = jnp.where(place.has_y[g], across[h], jnp.zeros_like(across[h]))
        part = lit(place, rim, partial[g, h] + dot(block, cells), shaded, h)
        for c in range(3):
            out[c] = part[c] if h == 0 else out[c] + part[c]


def blocks_kernel(rim, depth_count, late_s, late_e, total0, total1, *refs):
    outs, (img,) = refs[:2], refs[2:]
    place = Place()
    rows = 2 * rim
    for g, (colours, total) in enumerate(((late_s, total0), (late_e, total1))):
        at = group_rows(place, rim, g)
        for c in range(3):
            img[c, at, :] = colours[c]
        img[3, at, :] = jnp.exp2(total[...])
    for c in range(4):
        img[4 + c, :, 0:rows] = img[c].T[:rows, :]
    block = rows // depth_count
    bit = place.depth & 1
    for n in range(depth_count // 2):
        for out, b in ((outs[0], bit), (outs[1], 1 - bit)):
            out[n] = img[4:8, pl.ds(pl.multiple_of((2 * n + b) * block, block), block), 0:rows]


def merge_kernel(level, order_map, kept, theirs, *outs):
    me = lax.axis_index("depth")
    bit = me >> level & 1
    low = me & (2 << level) - 1
    merged = []
    for n in range(kept.shape[0]):
        mine = (bit == order_map[(n << level + 1) + low])[None]
        front = jnp.where(mine, kept[n], theirs[n])
        back = jnp.where(mine, theirs[n], kept[n])
        merged.append((front[:3] + front[3:] * back[:3], front[3:] * back[3:]))
    if len(merged) == 1:
        colour, through = merged[0]
        outs[0][...] = jnp.concatenate([colour, 1.0 - through]).reshape(outs[0].shape)
        return
    up = me >> level + 1 & 1
    for n in range(len(merged) // 2):
        even, odd = (jnp.concatenate(merged[2 * n + i]) for i in range(2))
        outs[0][n] = jnp.where(up == 1, odd, even)
        outs[1][n] = jnp.where(up == 1, even, odd)


def call(kernel, name, ins, outs, scratch=(), limit=16 * MIB, **more):
    return pl.pallas_call(
        kernel,
        out_shape=outs,
        in_specs=ins,
        out_specs=jax.tree.map(lambda _: VMEM, outs),
        scratch_shapes=list(scratch),
        compiler_params=pltpu.CompilerParams(vmem_limit_bytes=limit),
        name=name,
        **more,
    )


def per_device(
    density, kernel_taps, tf_centre, tf_width, tf_color, tf_opacity, brick_tf, view_order
):
    rows_x, rows_y, rows_z = density.shape
    rim = (kernel_taps.shape[1] - 1) // 2
    bumps = tf_centre.shape[1]
    size = rim * rim
    axes = ("depth", "sx", "sy")
    counts = tuple(lax.axis_size(axis) for axis in axes)
    depth_count, count_y = counts[0], counts[2]
    struct = jax.ShapeDtypeStruct
    block = rows_x // depth_count
    rounds = sum(1 for shift in range(2) if line_pairs(count_y, shift))

    def swap(piece, x_round, y_round):
        return lax.ppermute(piece, axes, swaps(counts, x_round, y_round))

    in_hbm = lambda array: pltpu.with_memory_space_constraint(array, pltpu.HBM)
    tables = (
        kernel_taps, tf_centre.T, tf_width.T, tf_color.T, tf_opacity.T, brick_tf, view_order
    )
    piece = struct((rim, rim, rows_z), BF16)
    both = struct((2, rim, rim, rows_z), BF16)
    held, xs0, xs1, *refs = call(
        functools.partial(first_kernel, rim, rounds),
        "first",
        [HBM] * (1 + len(tables)),
        [struct((2, 2, rim, rim, rows_z), F32), both, both]
        + [piece] * (2 * rounds)
        + [struct(t.shape, t.dtype) for t in tables],
        [pltpu.SemaphoreType.DMA((4 + len(tables),))],
    )(in_hbm(density), *[in_hbm(t) for t in tables])
    strips, tables = refs[:2 * rounds], refs[2 * rounds:]
    near, corner = [], []
    for r in range(rounds):
        near.append([swap(strips[2 * r + h], None, r) for h in range(2)])
    halo_x = [swap(cells, h, None) for h, cells in enumerate((xs0, xs1))]
    bricks = rows_z // 128
    mx, my, table, signs, order_map = call(
        functools.partial(prepare_kernel, rim),
        "prepare",
        [VMEM] * len(tables),
        [struct((size, 3 * size), BF16)] * 2
        + [struct((4 * bricks, 6 * bumps, 128), F32), struct((2, 2, 8, 128), jnp.int32)]
        + [struct((depth_count, block, rows_y), jnp.int32)],
        [pltpu.VMEM((8, 128), F32)],
    )(*tables)
    shaded, total = [None, None], [None, None]
    for g in (1, 0):
        shaded[g], total[g] = call(
            functools.partial(cells_kernel, rim, bumps, g),
            f"cells{g}",
            [VMEM] * 3,
            [struct((3, 2, rim, rim, rows_z), F32), struct((rim, 128), F32)],
            [pltpu.VMEM((2, size, rows_z), F32), pltpu.VMEM((3, 2, size, rows_z), F32)],
            cost_estimate=pl.CostEstimate(
                flops=density.size * 30, bytes_accessed=density.size * 10, transcendentals=density.size * 3
            ),
        )(held, table, signs)

    for r in range(rounds):
        first, total[1] = lax.optimization_barrier((near[r][0], total[1]))
        corner.append([swap(first, 0, None), swap(strips[2 * r + 1], 1, r)])

    early = rounds < 2
    colours = struct((3, rim, 128), F32)
    partial = struct((2, 2, size, rows_z), F32)
    own = call(
        functools.partial(own_kernel, rim, early),
        "own",
        [VMEM] * (7 if early else 6),
        [colours, partial] if early else [partial],
    )(mx, my, xs0, xs1, *halo_x, *([shaded[1]] if early else []))
    partial = own[-1]
    lights = [None, own[0]]
    for r in range(rounds):
        lights[r] = call(
            functools.partial(late_kernel, rim, r), f"late{r}", [VMEM] * 8, colours
        )(mx, my, *near[r], *corner[r], partial, shaded[r])

    kept, given = call(
        functools.partial(blocks_kernel, rim, depth_count),
        "blocks",
        [VMEM] * 4,
        [struct((depth_count // 2, 4, block, rows_y), F32)] * 2,
        [pltpu.VMEM((8, rows_y, 128), F32)],
    )(*lights, *total)
    level = 0
    while True:
        theirs = lax.ppermute(given, "depth", [(i, i ^ 1 << level) for i in range(depth_count)])
        left = kept.shape[0] // 2
        outs = [struct((left, 4, block, rows_y), F32)] * 2
        merged = call(
            functools.partial(merge_kernel, level),
            f"merge{level}",
            [VMEM] * 3,
            outs if left else struct((4, 1, 1, block, rows_y), F32),
            limit=2 * MIB,
        )(order_map, kept, theirs)
        if not left:
            return merged
        kept, given = merged
        level += 1


def solution(mesh):
    return jax.shard_map(
        per_device,
        mesh=mesh,
        in_specs=(
            P("sx", "sy", "depth"),
            P(),
            P(),
            P(),
            P(),
            P(),
            P("sx", "sy", "depth"),
            P("sx", "sy"),
        ),
        out_specs=P(None, "sx", "depth", None, "sy"),
        check_vma=False,
    )
```

```python
import functools
import math
import jax
import jax.numpy as jnp
from jax import lax
from jax.experimental import pallas as pl
from jax.experimental.pallas import tpu as pltpu
from jax.sharding import PartitionSpec as P

LOG2E = math.log2(math.e)
VMEM = pl.BlockSpec(memory_space=pltpu.VMEM)
HBM = pl.BlockSpec(memory_space=pltpu.HBM)
MIB = 1024 * 1024
F32, BF16 = jnp.float32, jnp.bfloat16
dot = functools.partial(jnp.dot, preferred_element_type=F32)


def iota(shape, dim):
    return lax.broadcasted_iota(jnp.int32, shape, dim)


def line_pairs(count, shift):
    return [(i, i + 1) for i in range(shift, count - 1, 2)]


def swaps(counts, x_round, y_round):
    depth_count, count_x, count_y = counts
    index = lambda d, x, y: (d * count_x + x) * count_y + y
    stay = lambda count: [(i, i) for i in range(count)]
    pairs_x = stay(count_x) if x_round is None else line_pairs(count_x, x_round)
    pairs_y = stay(count_y) if y_round is None else line_pairs(count_y, y_round)
    ends = {((a, c), (b, e)) for a, b in pairs_x for c, e in pairs_y}
    if x_round is not None and y_round is not None:
        ends |= {((a, e), (b, c)) for a, b in pairs_x for c, e in pairs_y}
    used = {end for pair in ends for end in pair}
    pairs = []
    for d in range(depth_count):
        pairs += [(index(d, *a), index(d, *b)) for a, b in sorted(ends)]
    for x in range(count_x):
        for y in range(count_y):
            if (x, y) not in used:
                pairs += [
                    (index(d, x, y), index(d + 1, x, y)) for d in range(0, depth_count - 1, 2)
                ]
    return pairs + [(b, a) for a, b in pairs]


class Place:
    def __init__(self):
        self.depth = lax.axis_index("depth")
        self.half, self.has_x = self.sides("sx")
        self.group, self.has_y = self.sides("sy")

    def sides(self, axis):
        at, last = lax.axis_index(axis), lax.axis_size(axis) - 1
        parity = lax.rem(at, 2)
        upper, lower = at < last, at > 0
        order = (1 - parity, parity)
        either = lambda side: jnp.where(side == 1, upper.astype(jnp.int32), lower.astype(jnp.int32))
        return order, [either(side) == 1 for side in order]


def group_rows(place, rim, g):
    return pl.ds(pl.multiple_of(place.group[g] * rim, rim), rim)


def half_rows(place, rim, h):
    return pl.ds(place.half[h] * rim, rim)


def first_kernel(rim, rounds, density, *refs):
    place = Place()
    n_tables = (len(refs) - 4 - 2 * rounds) // 2
    tables, refs = refs[:n_tables], refs[n_tables:]
    held, xs, refs = refs[0], refs[1:3], refs[3:]
    strips, refs = refs[:2 * rounds], refs[2 * rounds:]
    tables_out, sems = refs[:n_tables], refs[n_tables]
    copies = []
    for g in range(2):
        for h in range(2):
            rows = density.at[half_rows(place, rim, h), group_rows(place, rim, g), :]
            copies.append(pltpu.make_async_copy(rows, held.at[g, h], sems.at[2 * g + h]))
    for i, (src, dst) in enumerate(zip(tables, tables_out)):
        copies.append(pltpu.make_async_copy(src, dst, sems.at[4 + i]))
    for copy in copies:
        copy.start()
    for g in range(2):
        for h in range(2):
            copies[2 * g + h].wait()
            coarse = held[g, h].astype(BF16)
            xs[h][g] = coarse
            if g < rounds:
                strips[2 * g + h][...] = coarse
    for copy in copies[4:]:
        copy.wait()


def toeplitz(taps, rim):
    return pltpu.roll(jnp.broadcast_to(taps, (rim, 128)), 0, 1, stride=1, stride_axis=0)


def blur_matrices(rim, place, taps):
    size = rim * rim
    wide = 3 * size
    shift = rim.bit_length() - 1
    pick = lambda mask: jnp.where(mask, 1.0, 0.0).astype(BF16)
    row_hi = pick(iota((size, rim), 0) >> shift == iota((size, rim), 1))
    row_lo = pick(iota((size, rim), 0) & (rim - 1) == iota((size, rim), 1))
    col = iota((128, wide), 1)
    src = iota((128, wide), 0)
    k, j, b = col >> 2 * shift, col >> shift & (rim - 1), col & (rim - 1)
    k_x = jnp.where(place.half[0] == 1, k, 2 - k)
    k_y = jnp.where(place.group[0] == 1, k, 2 - k)
    tx = toeplitz(taps[0:1], rim).astype(BF16)
    ty = toeplitz(taps[1:2] * 0.5, rim).astype(BF16)
    full_x = dot(row_hi, dot(tx, pick(k_x * rim + j == src)).astype(BF16))
    full_y = dot(row_lo, dot(ty, pick(k_y * rim + b == src)).astype(BF16))
    r, c = iota((size, size), 0), iota((size, size), 1)
    same_x = r & (rim - 1) == c & (rim - 1)
    same_y = r >> shift == c >> shift
    parts = []
    for full, same in ((full_x, same_x), (full_y, same_y)):
        blocks = [
            jnp.where(same, full[:, n * size:(n + 1) * size], 0.0).astype(BF16) for n in range(3)
        ]
        parts.append(jnp.concatenate(blocks, axis=1))
    return parts


def prepare_kernel(
    rim, taps, centre, width, colour, opacity, brick_tf, view_order,
    mx, my, table, signs, order_map, padded
):
    place = Place()
    padded[...] = jnp.zeros(padded.shape, F32)
    padded[0:2, 0:taps.shape[1]] = taps[...].astype(F32)
    mx[...], my[...] = blur_matrices(rim, place, padded[...])
    wide = width[...]
    rows = [centre[...], (-LOG2E) / (wide * wide), opacity[...] * (-LOG2E)]
    rows += [colour[c] * 0.5 for c in range(3)]
    rows = jnp.concatenate(rows, axis=0)
    which = iota(rows.shape, 1)
    n = 0
    for g in range(2):
        for h in range(2):
            bricks = brick_tf[place.half[h]]
            bricks = jnp.where(place.group[g] == 0, bricks[0:1], bricks[1:2])
            for bz in range(bricks.shape[1]):
                mine = jnp.where(which == bricks[:, bz:bz + 1], rows, 0.0)
                mine = jnp.sum(mine, axis=1, keepdims=True)
                table[n] = jnp.broadcast_to(mine, table.shape[1:])
                n += 1
            orders = view_order[...]
            orders = jnp.where(place.half[h] == 0, orders[0:1], orders[1:2])
            order = jnp.where(place.group[g] == 0, orders[:, 0:1], orders[:, 1:2])
            signs[g, h] = jnp.broadcast_to(1 - 2 * order, signs.shape[2:])
    block, shape = order_map.shape[1], order_map.shape[1:]
    for n in range(order_map.shape[0]):
        brick = n * block // rim
        orders = view_order[brick:brick + 1]
        order_map[n] = jnp.where(
            iota(shape, 1) < rim,
            jnp.broadcast_to(orders[:, 0:1], shape),
            jnp.broadcast_to(orders[:, 1:2], shape),
        )


def cells_kernel(rim, bumps, g, held, table, signs, shaded, total, optical_s, emitted_s):
    place = Place()
    rows_z = held.shape[4]
    depth = 128
    bricks = rows_z // depth
    lane = iota((rim, 128), 1)
    for h in range(2):
        cells = held.at[g, h]
        for bz in range(bricks):
            zs = slice(bz * depth, (bz + 1) * depth)
            at = (2 * g + h) * bricks + bz
            row = lambda i: jnp.broadcast_to(table[at, i:i + 1, :], (8, depth))[None]
            cen = [row(j) for j in range(bumps)]
            neg = [row(bumps + j) for j in range(bumps)]
            opa = [row(2 * bumps + j) for j in range(bumps)]
            col = [[row((3 + c) * bumps + j) for c in range(3)] for j in range(bumps)]
            for x in range(rim):
                d = cells[x, :, zs].reshape(rim // 8, 8, depth)
                opt, em = None, [None] * 3
                for j in range(bumps):
                    w = d - cen[j]
                    b = jnp.exp2((w * w) * neg[j])
                    opt = opa[j] * b if opt is None else opt + opa[j] * b
                    for c in range(3):
                        em[c] = col[j][c] * b if em[c] is None else em[c] + col[j][c] * b
                rows = slice(x * rim, (x + 1) * rim)
                optical_s[h, rows, zs] = opt.reshape(rim, depth)
                for c in range(3):
                    emitted_s[c, h, rows, zs] = em[c].reshape(rim, depth)
        behind = iota((rows_z, rows_z), 1) - iota((rows_z, rows_z), 0)
        sign = jnp.broadcast_to(signs[g, h][0:1, 0:1], (rows_z, rows_z))
        tri = jnp.where(behind * sign > 0, 1.0, 0.0).astype(BF16)
        opt = optical_s[h]
        hi = opt.astype(BF16)
        lo = (opt - hi.astype(F32)).astype(BF16)
        ahead = dot(hi, tri) + dot(lo, tri)
        weight = jnp.exp2(ahead) * (1.0 - jnp.exp2(opt))
        for c in range(3):
            shaded[c, h] = (weight * emitted_s[c, h]).reshape(rim, rim, rows_z)
        part = rays(opt.reshape(rim, rim, rows_z), place.half[h] * rim, lane)
        total[...] = part if h == 0 else total[...] + part


def rays(cells, first_lane, lane):
    folded = cells[:, :, :128]
    for z in range(128, cells.shape[2], 128):
        folded = folded + cells[:, :, z:z + 128]
    summed = jnp.sum(folded, axis=2, keepdims=True)
    acc = jnp.zeros(lane.shape, F32)
    for x in range(cells.shape[0]):
        acc = jnp.where(lane == first_lane + x, summed[x], acc)
    return acc


def blur_x(place, rim, mx, near, halos):
    flat = lambda cells: cells.reshape(rim * rim, cells.shape[-1])
    edges = []
    for h, halo in enumerate(halos):
        cells = flat(halo)
        edges.append(jnp.where(place.has_x[h], cells, jnp.zeros_like(cells)))
    blocks = [edges[1], flat(near[1]), flat(near[0]), edges[0]]
    return [
        dot(mx[...], jnp.concatenate(blocks[1 - h:4 - h], axis=0)).astype(BF16) for h in range(2)
    ]


def lit(place, rim, occlusion, shaded, h):
    rows_z = occlusion.shape[1]
    lane = iota((rim, 128), 1)
    shade = (1.0 - jnp.tanh(occlusion)).reshape(rim, rim, rows_z)
    return [rays(shade * shaded[c, h], place.half[h] * rim, lane) for c in range(3)]


def own_kernel(rim, early, mx, my, xs0, xs1, halo0, halo1, *refs):
    place = Place()
    size = rim * rim
    across = [
        blur_x(place, rim, mx, [xs0[g], xs1[g]], [halo0[g], halo1[g]]) for g in range(2)
    ]
    if early:
        shaded, out, partial = refs
    else:
        partial, = refs
    for h in range(2):
        s, e = across[0][h], across[1][h]
        partial[0, h] = dot(my[:, :2 * size], jnp.concatenate([e, s], axis=0))
        other = dot(my[:, size:], jnp.concatenate([e, s], axis=0))
        if not early:
            partial[1, h] = other
            continue
        part = lit(place, rim, other, shaded, h)
        for c in range(3):
            out[c] = part[c] if h == 0 else out[c] + part[c]


def late_kernel(rim, g, mx, my, near0, near1, halo0, halo1, partial, shaded, out):
    place = Place()
    size = rim * rim
    across = blur_x(place, rim, mx, [near0[...], near1[...]], [halo0[...], halo1[...]])
    block = my[:, 2 * size:] if g == 0 else my[:, :size]
    for h in range(2):
        cells = jnp.where(place.has_y[g], across[h], jnp.zeros_like(across[h]))
        part = lit(place, rim, partial[g, h] + dot(block, cells), shaded, h)
        for c in range(3):
            out[c] = part[c] if h == 0 else out[c] + part[c]


def blocks_kernel(rim, depth_count, late_s, late_e, total0, total1, *refs):
    outs, (img,) = refs[:2], refs[2:]
    place = Place()
    rows = 2 * rim
    for g, (colours, total) in enumerate(((late_s, total0), (late_e, total1))):
        at = group_rows(place, rim, g)
        for c in range(3):
            img[c, at, :] = colours[c]
        img[3, at, :] = jnp.exp2(total[...])
    for c in range(4):
        img[4 + c, :, 0:rows] = img[c].T[:rows, :]
    block = rows // depth_count
    bit = place.depth & 1
    for n in range(depth_count // 2):
        for out, b in ((outs[0], bit), (outs[1], 1 - bit)):
            out[n] = img[4:8, pl.ds(pl.multiple_of((2 * n + b) * block, block), block), 0:rows]


def merge_kernel(level, order_map, kept, theirs, *outs):
    me = lax.axis_index("depth")
    bit = me >> level & 1
    low = me & (2 << level) - 1
    merged = []
    for n in range(kept.shape[0]):
        mine = (bit == order_map[(n << level + 1) + low])[None]
        front = jnp.where(mine, kept[n], theirs[n])
        back = jnp.where(mine, theirs[n], kept[n])
        merged.append((front[:3] + front[3:] * back[:3], front[3:] * back[3:]))
    if len(merged) == 1:
        colour, through = merged[0]
        outs[0][...] = jnp.concatenate([colour, 1.0 - through]).reshape(outs[0].shape)
        return
    up = me >> level + 1 & 1
    for n in range(len(merged) // 2):
        even, odd = (jnp.concatenate(merged[2 * n + i]) for i in range(2))
        outs[0][n] = jnp.where(up == 1, odd, even)
        outs[1][n] = jnp.where(up == 1, even, odd)


def call(kernel, name, ins, outs, scratch=(), limit=16 * MIB, **more):
    return pl.pallas_call(
        kernel,
        out_shape=outs,
        in_specs=ins,
        out_specs=jax.tree.map(lambda _: VMEM, outs),
        scratch_shapes=list(scratch),
        compiler_params=pltpu.CompilerParams(vmem_limit_bytes=limit),
        name=name,
        **more,
    )


def per_device(
    density, kernel_taps, tf_centre, tf_width, tf_color, tf_opacity, brick_tf, view_order
):
    rows_x, rows_y, rows_z = density.shape
    rim = (kernel_taps.shape[1] - 1) // 2
    bumps = tf_centre.shape[1]
    size = rim * rim
    axes = ("depth", "sx", "sy")
    counts = tuple(lax.axis_size(axis) for axis in axes)
    depth_count, count_y = counts[0], counts[2]
    struct = jax.ShapeDtypeStruct
    block = rows_x // depth_count
    rounds = sum(1 for shift in range(2) if line_pairs(count_y, shift))

    def swap(piece, x_round, y_round):
        return lax.ppermute(piece, axes, swaps(counts, x_round, y_round))

    in_hbm = lambda array: pltpu.with_memory_space_constraint(array, pltpu.HBM)
    tables = (
        kernel_taps, tf_centre.T, tf_width.T, tf_color.T, tf_opacity.T, brick_tf, view_order
    )
    piece = struct((rim, rim, rows_z), BF16)
    both = struct((2, rim, rim, rows_z), BF16)
    held, xs0, xs1, *refs = call(
        functools.partial(first_kernel, rim, rounds),
        "first",
        [HBM] * (1 + len(tables)),
        [struct((2, 2, rim, rim, rows_z), F32), both, both]
        + [piece] * (2 * rounds)
        + [struct(t.shape, t.dtype) for t in tables],
        [pltpu.SemaphoreType.DMA((4 + len(tables),))],
    )(in_hbm(density), *[in_hbm(t) for t in tables])
    strips, tables = refs[:2 * rounds], refs[2 * rounds:]
    near = [[swap(strips[2 * r], None, r), None] for r in range(rounds)]
    halo_x = [swap(cells, h, None) for h, cells in enumerate((xs0, xs1))]

    bricks = rows_z // 128
    mx, my, table, signs, order_map = call(
        functools.partial(prepare_kernel, rim),
        "prepare",
        [VMEM] * len(tables),
        [struct((size, 3 * size), BF16)] * 2
        + [struct((4 * bricks, 6 * bumps, 128), F32), struct((2, 2, 8, 128), jnp.int32)]
        + [struct((depth_count, block, rows_y), jnp.int32)],
        [pltpu.VMEM((8, 128), F32)],
    )(*tables)
    corner = [[None, None] for r in range(rounds)]
    for r in range(rounds):
        strip, table = lax.optimization_barrier((strips[2 * r + 1], table))
        corner[r][1] = swap(strip, 1, r)
        near[r][1] = swap(strip, None, r)
    shaded, total = [None, None], [None, None]
    for g in (1, 0):
        shaded[g], total[g] = call(
            functools.partial(cells_kernel, rim, bumps, g),
            f"cells{g}",
            [VMEM] * 3,
            [struct((3, 2, rim, rim, rows_z), F32), struct((rim, 128), F32)],
            [pltpu.VMEM((2, size, rows_z), F32), pltpu.VMEM((3, 2, size, rows_z), F32)],
            cost_estimate=pl.CostEstimate(
                flops=density.size * 30, bytes_accessed=density.size * 10, transcendentals=density.size * 3
            ),
        )(held, table, signs)

    for r in range(rounds):
        strip, total[1] = lax.optimization_barrier((near[r][0], total[1]))
        corner[r][0] = swap(strip, 0, None)

    early = rounds < 2
    colours = struct((3, rim, 128), F32)
    partial = struct((2, 2, size, rows_z), F32)
    own = call(
        functools.partial(own_kernel, rim, early),
        "own",
        [VMEM] * (7 if early else 6),
        [colours, partial] if early else [partial],
    )(mx, my, xs0, xs1, *halo_x, *([shaded[1]] if early else []))
    partial = own[-1]
    lights = [None, own[0]]
    for r in range(rounds):
        lights[r] = call(
            functools.partial(late_kernel, rim, r), f"late{r}", [VMEM] * 8, colours
        )(mx, my, *near[r], *corner[r], partial, shaded[r])

    kept, given = call(
        functools.partial(blocks_kernel, rim, depth_count),
        "blocks",
        [VMEM] * 4,
        [struct((depth_count // 2, 4, block, rows_y), F32)] * 2,
        [pltpu.VMEM((8, rows_y, 128), F32)],
    )(*lights, *total)
    level = 0
    while True:
        theirs = lax.ppermute(given, "depth", [(i, i ^ 1 << level) for i in range(depth_count)])
        left = kept.shape[0] // 2
        outs = [struct((left, 4, block, rows_y), F32)] * 2
        merged = call(
            functools.partial(merge_kernel, level),
            f"merge{level}",
            [VMEM] * 3,
            outs if left else struct((4, 1, 1, block, rows_y), F32),
            limit=2 * MIB,
        )(order_map, kept, theirs)
        if not left:
            return merged
        kept, given = merged
        level += 1


def solution(mesh):
    return jax.shard_map(
        per_device,
        mesh=mesh,
        in_specs=(
            P("sx", "sy", "depth"),
            P(),
            P(),
            P(),
            P(),
            P(),
            P("sx", "sy", "depth"),
            P("sx", "sy"),
        ),
        out_specs=P(None, "sx", "depth", None, "sy"),
        check_vma=False,
    )
```

```python
import functools
import math
import jax
import jax.numpy as jnp
from jax import lax
from jax.experimental import pallas as pl
from jax.experimental.pallas import tpu as pltpu
from jax.sharding import PartitionSpec as P

LOG2E = math.log2(math.e)
VMEM = pl.BlockSpec(memory_space=pltpu.VMEM)
HBM = pl.BlockSpec(memory_space=pltpu.HBM)
MIB = 1024 * 1024
F32, BF16 = jnp.float32, jnp.bfloat16
dot = functools.partial(jnp.dot, preferred_element_type=F32)


def iota(shape, dim):
    return lax.broadcasted_iota(jnp.int32, shape, dim)


def line_pairs(count, shift):
    return [(i, i + 1) for i in range(shift, count - 1, 2)]


def swaps(counts, x_round, y_round):
    depth_count, count_x, count_y = counts
    index = lambda d, x, y: (d * count_x + x) * count_y + y
    stay = lambda count: [(i, i) for i in range(count)]
    pairs_x = stay(count_x) if x_round is None else line_pairs(count_x, x_round)
    pairs_y = stay(count_y) if y_round is None else line_pairs(count_y, y_round)
    ends = {((a, c), (b, e)) for a, b in pairs_x for c, e in pairs_y}
    if x_round is not None and y_round is not None:
        ends |= {((a, e), (b, c)) for a, b in pairs_x for c, e in pairs_y}
    used = {end for pair in ends for end in pair}
    pairs = []
    for d in range(depth_count):
        pairs += [(index(d, *a), index(d, *b)) for a, b in sorted(ends)]
    for x in range(count_x):
        for y in range(count_y):
            if (x, y) not in used:
                pairs += [
                    (index(d, x, y), index(d + 1, x, y)) for d in range(0, depth_count - 1, 2)
                ]
    return pairs + [(b, a) for a, b in pairs]


class Place:
    def __init__(self):
        self.depth = lax.axis_index("depth")
        self.half, self.has_x = self.sides("sx")
        self.group, self.has_y = self.sides("sy")

    def sides(self, axis):
        at, last = lax.axis_index(axis), lax.axis_size(axis) - 1
        parity = lax.rem(at, 2)
        upper, lower = at < last, at > 0
        order = (1 - parity, parity)
        either = lambda side: jnp.where(side == 1, upper.astype(jnp.int32), lower.astype(jnp.int32))
        return order, [either(side) == 1 for side in order]


def group_rows(place, rim, g):
    return pl.ds(pl.multiple_of(place.group[g] * rim, rim), rim)


def half_rows(place, rim, h):
    return pl.ds(place.half[h] * rim, rim)


def first_kernel(rim, rounds, density, *refs):
    place = Place()
    n_tables = (len(refs) - 4 - 2 * rounds) // 2
    tables, refs = refs[:n_tables], refs[n_tables:]
    held, xs, refs = refs[0], refs[1:3], refs[3:]
    strips, refs = refs[:2 * rounds], refs[2 * rounds:]
    tables_out, sems = refs[:n_tables], refs[n_tables]
    copies = []
    for g in range(2):
        for h in range(2):
            rows = density.at[half_rows(place, rim, h), group_rows(place, rim, g), :]
            copies.append(pltpu.make_async_copy(rows, held.at[g, h], sems.at[2 * g + h]))
    for i, (src, dst) in enumerate(zip(tables, tables_out)):
        copies.append(pltpu.make_async_copy(src, dst, sems.at[4 + i]))
    for copy in copies:
        copy.start()
    for g in range(2):
        for h in range(2):
            copies[2 * g + h].wait()
            coarse = held[g, h].astype(BF16)
            xs[h][g] = coarse
            if g < rounds:
                strips[2 * g + h][...] = coarse
    for copy in copies[4:]:
        copy.wait()


def toeplitz(taps, rim):
    return pltpu.roll(jnp.broadcast_to(taps, (rim, 128)), 0, 1, stride=1, stride_axis=0)


def blur_matrices(rim, place, taps):
    size = rim * rim
    wide = 3 * size
    shift = rim.bit_length() - 1
    pick = lambda mask: jnp.where(mask, 1.0, 0.0).astype(BF16)
    row_hi = pick(iota((size, rim), 0) >> shift == iota((size, rim), 1))
    row_lo = pick(iota((size, rim), 0) & (rim - 1) == iota((size, rim), 1))
    col = iota((128, wide), 1)
    src = iota((128, wide), 0)
    k, j, b = col >> 2 * shift, col >> shift & (rim - 1), col & (rim - 1)
    k_x = jnp.where(place.half[0] == 1, k, 2 - k)
    k_y = jnp.where(place.group[0] == 1, k, 2 - k)
    tx = toeplitz(taps[0:1], rim).astype(BF16)
    ty = toeplitz(taps[1:2] * 0.5, rim).astype(BF16)
    full_x = dot(row_hi, dot(tx, pick(k_x * rim + j == src)).astype(BF16))
    full_y = dot(row_lo, dot(ty, pick(k_y * rim + b == src)).astype(BF16))
    r, c = iota((size, size), 0), iota((size, size), 1)
    same_x = r & (rim - 1) == c & (rim - 1)
    same_y = r >> shift == c >> shift
    parts = []
    for full, same in ((full_x, same_x), (full_y, same_y)):
        blocks = [
            jnp.where(same, full[:, n * size:(n + 1) * size], 0.0).astype(BF16) for n in range(3)
        ]
        parts.append(jnp.concatenate(blocks, axis=1))
    return parts


def prepare_kernel(
    rim, taps, centre, width, colour, opacity, brick_tf, view_order,
    mx, my, table, signs, order_map, padded
):
    place = Place()
    padded[...] = jnp.zeros(padded.shape, F32)
    padded[0:2, 0:taps.shape[1]] = taps[...].astype(F32)
    mx[...], my[...] = blur_matrices(rim, place, padded[...])
    wide = width[...]
    rows = [centre[...], (-LOG2E) / (wide * wide), opacity[...] * (-LOG2E)]
    rows += [colour[c] * 0.5 for c in range(3)]
    rows = jnp.concatenate(rows, axis=0)
    which = iota(rows.shape, 1)
    n = 0
    for g in range(2):
        for h in range(2):
            bricks = brick_tf[place.half[h]]
            bricks = jnp.where(place.group[g] == 0, bricks[0:1], bricks[1:2])
            for bz in range(bricks.shape[1]):
                mine = jnp.where(which == bricks[:, bz:bz + 1], rows, 0.0)
                mine = jnp.sum(mine, axis=1, keepdims=True)
                table[n] = jnp.broadcast_to(mine, table.shape[1:])
                n += 1
            orders = view_order[...]
            orders = jnp.where(place.half[h] == 0, orders[0:1], orders[1:2])
            order = jnp.where(place.group[g] == 0, orders[:, 0:1], orders[:, 1:2])
            signs[g, h] = jnp.broadcast_to(1 - 2 * order, signs.shape[2:])
    block, shape = order_map.shape[1], order_map.shape[1:]
    for n in range(order_map.shape[0]):
        brick = n * block // rim
        orders = view_order[brick:brick + 1]
        order_map[n] = jnp.where(
            iota(shape, 1) < rim,
            jnp.broadcast_to(orders[:, 0:1], shape),
            jnp.broadcast_to(orders[:, 1:2], shape),
        )


def cells_kernel(rim, bumps, g, held, table, signs, shaded, total, optical_s, emitted_s):
    place = Place()
    rows_z = held.shape[4]
    depth = 128
    bricks = rows_z // depth
    lane = iota((rim, 128), 1)
    for h in range(2):
        cells = held.at[g, h]
        for bz in range(bricks):
            zs = slice(bz * depth, (bz + 1) * depth)
            at = (2 * g + h) * bricks + bz
            row = lambda i: jnp.broadcast_to(table[at, i:i + 1, :], (8, depth))[None]
            cen = [row(j) for j in range(bumps)]
            neg = [row(bumps + j) for j in range(bumps)]
            opa = [row(2 * bumps + j) for j in range(bumps)]
            col = [[row((3 + c) * bumps + j) for c in range(3)] for j in range(bumps)]
            for x in range(rim):
                d = cells[x, :, zs].reshape(rim // 8, 8, depth)
                opt, em = None, [None] * 3
                for j in range(bumps):
                    w = d - cen[j]
                    b = jnp.exp2((w * w) * neg[j])
                    opt = opa[j] * b if opt is None else opt + opa[j] * b
                    for c in range(3):
                        em[c] = col[j][c] * b if em[c] is None else em[c] + col[j][c] * b
                rows = slice(x * rim, (x + 1) * rim)
                optical_s[h, rows, zs] = opt.reshape(rim, depth)
                for c in range(3):
                    emitted_s[c, h, rows, zs] = em[c].reshape(rim, depth)
        behind = iota((rows_z, rows_z), 1) - iota((rows_z, rows_z), 0)
        sign = jnp.broadcast_to(signs[g, h][0:1, 0:1], (rows_z, rows_z))
        tri = jnp.where(behind * sign > 0, 1.0, 0.0).astype(BF16)
        opt = optical_s[h]
        hi = opt.astype(BF16)
        lo = (opt - hi.astype(F32)).astype(BF16)
        ahead = dot(hi, tri) + dot(lo, tri)
        weight = jnp.exp2(ahead) * (1.0 - jnp.exp2(opt))
        for c in range(3):
            shaded[c, h] = (weight * emitted_s[c, h]).reshape(rim, rim, rows_z)
        part = rays(opt.reshape(rim, rim, rows_z), place.half[h] * rim, lane)
        total[...] = part if h == 0 else total[...] + part


def rays(cells, first_lane, lane):
    folded = cells[:, :, :128]
    for z in range(128, cells.shape[2], 128):
        folded = folded + cells[:, :, z:z + 128]
    summed = jnp.sum(folded, axis=2, keepdims=True)
    acc = jnp.zeros(lane.shape, F32)
    for x in range(cells.shape[0]):
        acc = jnp.where(lane == first_lane + x, summed[x], acc)
    return acc


def blur_x(place, rim, mx, near, halos):
    flat = lambda cells: cells.reshape(rim * rim, cells.shape[-1])
    edges = []
    for h, halo in enumerate(halos):
        cells = flat(halo)
        edges.append(jnp.where(place.has_x[h], cells, jnp.zeros_like(cells)))
    blocks = [edges[1], flat(near[1]), flat(near[0]), edges[0]]
    return [
        dot(mx[...], jnp.concatenate(blocks[1 - h:4 - h], axis=0)).astype(BF16) for h in range(2)
    ]


def lit(place, rim, occlusion, shaded, h):
    rows_z = occlusion.shape[1]
    lane = iota((rim, 128), 1)
    shade = (1.0 - jnp.tanh(occlusion)).reshape(rim, rim, rows_z)
    return [rays(shade * shaded[c, h], place.half[h] * rim, lane) for c in range(3)]


def own_kernel(rim, early, mx, my, xs0, xs1, halo0, halo1, *refs):
    place = Place()
    size = rim * rim
    across = [
        blur_x(place, rim, mx, [xs0[g], xs1[g]], [halo0[g], halo1[g]]) for g in range(2)
    ]
    if early:
        shaded, out, partial = refs
    else:
        partial, = refs
    for h in range(2):
        s, e = across[0][h], across[1][h]
        partial[0, h] = dot(my[:, :2 * size], jnp.concatenate([e, s], axis=0))
        other = dot(my[:, size:], jnp.concatenate([e, s], axis=0))
        if not early:
            partial[1, h] = other
            continue
        part = lit(place, rim, other, shaded, h)
        for c in range(3):
            out[c] = part[c] if h == 0 else out[c] + part[c]


def late_kernel(rim, g, mx, my, near0, near1, halo0, halo1, partial, shaded, out):
    place = Place()
    size = rim * rim
    across = blur_x(place, rim, mx, [near0[...], near1[...]], [halo0[...], halo1[...]])
    block = my[:, 2 * size:] if g == 0 else my[:, :size]
    for h in range(2):
        cells = jnp.where(place.has_y[g], across[h], jnp.zeros_like(across[h]))
        part = lit(place, rim, partial[g, h] + dot(block, cells), shaded, h)
        for c in range(3):
            out[c] = part[c] if h == 0 else out[c] + part[c]


def blocks_kernel(rim, depth_count, late_s, late_e, total0, total1, *refs):
    outs, (img,) = refs[:2], refs[2:]
    place = Place()
    rows = 2 * rim
    for g, (colours, total) in enumerate(((late_s, total0), (late_e, total1))):
        at = group_rows(place, rim, g)
        for c in range(3):
            img[c, at, :] = colours[c]
        img[3, at, :] = jnp.exp2(total[...])
    for c in range(4):
        img[4 + c, :, 0:rows] = img[c].T[:rows, :]
    block = rows // depth_count
    bit = place.depth & 1
    for n in range(depth_count // 2):
        for out, b in ((outs[0], bit), (outs[1], 1 - bit)):
            out[n] = img[4:8, pl.ds(pl.multiple_of((2 * n + b) * block, block), block), 0:rows]


def merge_kernel(level, order_map, kept, theirs, *outs):
    me = lax.axis_index("depth")
    bit = me >> level & 1
    low = me & (2 << level) - 1
    merged = []
    for n in range(kept.shape[0]):
        mine = (bit == order_map[(n << level + 1) + low])[None]
        front = jnp.where(mine, kept[n], theirs[n])
        back = jnp.where(mine, theirs[n], kept[n])
        merged.append((front[:3] + front[3:] * back[:3], front[3:] * back[3:]))
    if len(merged) == 1:
        colour, through = merged[0]
        outs[0][...] = jnp.concatenate([colour, 1.0 - through]).reshape(outs[0].shape)
        return
    up = me >> level + 1 & 1
    for n in range(len(merged) // 2):
        even, odd = (jnp.concatenate(merged[2 * n + i]) for i in range(2))
        outs[0][n] = jnp.where(up == 1, odd, even)
        outs[1][n] = jnp.where(up == 1, even, odd)


def call(kernel, name, ins, outs, scratch=(), limit=16 * MIB, **more):
    return pl.pallas_call(
        kernel,
        out_shape=outs,
        in_specs=ins,
        out_specs=jax.tree.map(lambda _: VMEM, outs),
        scratch_shapes=list(scratch),
        compiler_params=pltpu.CompilerParams(vmem_limit_bytes=limit),
        name=name,
        **more,
    )


def per_device(
    density, kernel_taps, tf_centre, tf_width, tf_color, tf_opacity, brick_tf, view_order
):
    rows_x, rows_y, rows_z = density.shape
    rim = (kernel_taps.shape[1] - 1) // 2
    bumps = tf_centre.shape[1]
    size = rim * rim
    axes = ("depth", "sx", "sy")
    counts = tuple(lax.axis_size(axis) for axis in axes)
    depth_count, count_y = counts[0], counts[2]
    struct = jax.ShapeDtypeStruct
    block = rows_x // depth_count
    rounds = sum(1 for shift in range(2) if line_pairs(count_y, shift))

    def swap(piece, x_round, y_round):
        return lax.ppermute(piece, axes, swaps(counts, x_round, y_round))

    in_hbm = lambda array: pltpu.with_memory_space_constraint(array, pltpu.HBM)
    tables = (
        kernel_taps, tf_centre.T, tf_width.T, tf_color.T, tf_opacity.T, brick_tf, view_order
    )
    piece = struct((rim, rim, rows_z), BF16)
    both = struct((2, rim, rim, rows_z), BF16)
    held, xs0, xs1, *refs = call(
        functools.partial(first_kernel, rim, rounds),
        "first",
        [HBM] * (1 + len(tables)),
        [struct((2, 2, rim, rim, rows_z), F32), both, both]
        + [piece] * (2 * rounds)
        + [struct(t.shape, t.dtype) for t in tables],
        [pltpu.SemaphoreType.DMA((4 + len(tables),))],
    )(in_hbm(density), *[in_hbm(t) for t in tables])
    strips, tables = refs[:2 * rounds], refs[2 * rounds:]
    near = [[swap(strips[2 * r], None, r), None] for r in range(rounds)]
    halo_x = [swap(xs0, 0, None), None]

    bricks = rows_z // 128
    mx, my, table, signs, order_map = call(
        functools.partial(prepare_kernel, rim),
        "prepare",
        [VMEM] * len(tables),
        [struct((size, 3 * size), BF16)] * 2
        + [struct((4 * bricks, 6 * bumps, 128), F32), struct((2, 2, 8, 128), jnp.int32)]
        + [struct((depth_count, block, rows_y), jnp.int32)],
        [pltpu.VMEM((8, 128), F32)],
    )(*tables)
    cells, table = lax.optimization_barrier((xs1, table))
    halo_x[1] = swap(cells, 1, None)
    shaded, total = [None, None], [None, None]
    for g in (1, 0):
        shaded[g], total[g] = call(
            functools.partial(cells_kernel, rim, bumps, g),
            f"cells{g}",
            [VMEM] * 3,
            [struct((3, 2, rim, rim, rows_z), F32), struct((rim, 128), F32)],
            [pltpu.VMEM((2, size, rows_z), F32), pltpu.VMEM((3, 2, size, rows_z), F32)],
            cost_estimate=pl.CostEstimate(
                flops=density.size * 30, bytes_accessed=density.size * 10, transcendentals=density.size * 3
            ),
        )(held, table, signs)

    corner = [[None, None] for r in range(rounds)]
    for r in range(rounds):
        strip, total[1] = lax.optimization_barrier((strips[2 * r + 1], total[1]))
        arrived, total[1] = lax.optimization_barrier((near[r][0], total[1]))
        corner[r] = [swap(arrived, 0, None), swap(strip, 1, r)]
        near[r][1] = swap(strip, None, r)

    early = rounds < 2
    colours = struct((3, rim, 128), F32)
    partial = struct((2, 2, size, rows_z), F32)
    own = call(
        functools.partial(own_kernel, rim, early),
        "own",
        [VMEM] * (7 if early else 6),
        [colours, partial] if early else [partial],
    )(mx, my, xs0, xs1, *halo_x, *([shaded[1]] if early else []))
    partial = own[-1]
    lights = [None, own[0]]
    for r in range(rounds):
        lights[r] = call(
            functools.partial(late_kernel, rim, r), f"late{r}", [VMEM] * 8, colours
        )(mx, my, *near[r], *corner[r], partial, shaded[r])

    kept, given = call(
        functools.partial(blocks_kernel, rim, depth_count),
        "blocks",
        [VMEM] * 4,
        [struct((depth_count // 2, 4, block, rows_y), F32)] * 2,
        [pltpu.VMEM((8, rows_y, 128), F32)],
    )(*lights, *total)
    level = 0
    while True:
        theirs = lax.ppermute(given, "depth", [(i, i ^ 1 << level) for i in range(depth_count)])
        left = kept.shape[0] // 2
        outs = [struct((left, 4, block, rows_y), F32)] * 2
        merged = call(
            functools.partial(merge_kernel, level),
            f"merge{level}",
            [VMEM] * 3,
            outs if left else struct((4, 1, 1, block, rows_y), F32),
            limit=2 * MIB,
        )(order_map, kept, theirs)
        if not left:
            return merged
        kept, given = merged
        level += 1


def solution(mesh):
    return jax.shard_map(
        per_device,
        mesh=mesh,
        in_specs=(
            P("sx", "sy", "depth"),
            P(),
            P(),
            P(),
            P(),
            P(),
            P("sx", "sy", "depth"),
            P("sx", "sy"),
        ),
        out_specs=P(None, "sx", "depth", None, "sy"),
        check_vma=False,
    )
```

```python
import functools
import math
import jax
import jax.numpy as jnp
from jax import lax
from jax.experimental import pallas as pl
from jax.experimental.pallas import tpu as pltpu
from jax.sharding import PartitionSpec as P

LOG2E = math.log2(math.e)
VMEM = pl.BlockSpec(memory_space=pltpu.VMEM)
HBM = pl.BlockSpec(memory_space=pltpu.HBM)
MIB = 1024 * 1024
F32, BF16 = jnp.float32, jnp.bfloat16
dot = functools.partial(jnp.dot, preferred_element_type=F32)


def iota(shape, dim):
    return lax.broadcasted_iota(jnp.int32, shape, dim)


def line_pairs(count, shift):
    return [(i, i + 1) for i in range(shift, count - 1, 2)]


def swaps(counts, x_round, y_round):
    depth_count, count_x, count_y = counts
    index = lambda d, x, y: (d * count_x + x) * count_y + y
    stay = lambda count: [(i, i) for i in range(count)]
    pairs_x = stay(count_x) if x_round is None else line_pairs(count_x, x_round)
    pairs_y = stay(count_y) if y_round is None else line_pairs(count_y, y_round)
    ends = {((a, c), (b, e)) for a, b in pairs_x for c, e in pairs_y}
    if x_round is not None and y_round is not None:
        ends |= {((a, e), (b, c)) for a, b in pairs_x for c, e in pairs_y}
    used = {end for pair in ends for end in pair}
    pairs = []
    for d in range(depth_count):
        pairs += [(index(d, *a), index(d, *b)) for a, b in sorted(ends)]
    for x in range(count_x):
        for y in range(count_y):
            if (x, y) not in used:
                pairs += [
                    (index(d, x, y), index(d + 1, x, y)) for d in range(0, depth_count - 1, 2)
                ]
    return pairs + [(b, a) for a, b in pairs]


class Place:
    def __init__(self):
        self.depth = lax.axis_index("depth")
        self.half, self.has_x = self.sides("sx")
        self.group, self.has_y = self.sides("sy")

    def sides(self, axis):
        at, last = lax.axis_index(axis), lax.axis_size(axis) - 1
        parity = lax.rem(at, 2)
        upper, lower = at < last, at > 0
        order = (1 - parity, parity)
        either = lambda side: jnp.where(side == 1, upper.astype(jnp.int32), lower.astype(jnp.int32))
        return order, [either(side) == 1 for side in order]


def group_rows(place, rim, g):
    return pl.ds(pl.multiple_of(place.group[g] * rim, rim), rim)


def half_rows(place, rim, h):
    return pl.ds(place.half[h] * rim, rim)


def first_kernel(rim, rounds, density, *refs):
    place = Place()
    n_tables = (len(refs) - 4 - 2 * rounds) // 2
    tables, refs = refs[:n_tables], refs[n_tables:]
    held, xs, refs = refs[0], refs[1:3], refs[3:]
    strips, refs = refs[:2 * rounds], refs[2 * rounds:]
    tables_out, sems = refs[:n_tables], refs[n_tables]
    copies = []
    for g in range(2):
        for h in range(2):
            rows = density.at[half_rows(place, rim, h), group_rows(place, rim, g), :]
            copies.append(pltpu.make_async_copy(rows, held.at[g, h], sems.at[2 * g + h]))
    for i, (src, dst) in enumerate(zip(tables, tables_out)):
        copies.append(pltpu.make_async_copy(src, dst, sems.at[4 + i]))
    for copy in copies:
        copy.start()
    for g in range(2):
        for h in range(2):
            copies[2 * g + h].wait()
            coarse = held[g, h].astype(BF16)
            xs[h][g] = coarse
            if g < rounds:
                strips[2 * g + h][...] = coarse
    for copy in copies[4:]:
        copy.wait()


def toeplitz(taps, rim):
    return pltpu.roll(jnp.broadcast_to(taps, (rim, 128)), 0, 1, stride=1, stride_axis=0)


def blur_matrices(rim, place, taps):
    size = rim * rim
    wide = 3 * size
    shift = rim.bit_length() - 1
    pick = lambda mask: jnp.where(mask, 1.0, 0.0).astype(BF16)
    row_hi = pick(iota((size, rim), 0) >> shift == iota((size, rim), 1))
    row_lo = pick(iota((size, rim), 0) & (rim - 1) == iota((size, rim), 1))
    col = iota((128, wide), 1)
    src = iota((128, wide), 0)
    k, j, b = col >> 2 * shift, col >> shift & (rim - 1), col & (rim - 1)
    k_x = jnp.where(place.half[0] == 1, k, 2 - k)
    k_y = jnp.where(place.group[0] == 1, k, 2 - k)
    tx = toeplitz(taps[0:1], rim).astype(BF16)
    ty = toeplitz(taps[1:2] * 0.5, rim).astype(BF16)
    full_x = dot(row_hi, dot(tx, pick(k_x * rim + j == src)).astype(BF16))
    full_y = dot(row_lo, dot(ty, pick(k_y * rim + b == src)).astype(BF16))
    r, c = iota((size, size), 0), iota((size, size), 1)
    same_x = r & (rim - 1) == c & (rim - 1)
    same_y = r >> shift == c >> shift
    parts = []
    for full, same in ((full_x, same_x), (full_y, same_y)):
        blocks = [
            jnp.where(same, full[:, n * size:(n + 1) * size], 0.0).astype(BF16) for n in range(3)
        ]
        parts.append(jnp.concatenate(blocks, axis=1))
    return parts


def prepare_kernel(
    rim, taps, centre, width, colour, opacity, brick_tf, view_order,
    mx, my, table, signs, order_map, padded
):
    place = Place()
    padded[...] = jnp.zeros(padded.shape, F32)
    padded[0:2, 0:taps.shape[1]] = taps[...].astype(F32)
    mx[...], my[...] = blur_matrices(rim, place, padded[...])
    wide = width[...]
    rows = [centre[...], (-LOG2E) / (wide * wide), opacity[...] * (-LOG2E)]
    rows += [colour[c] * 0.5 for c in range(3)]
    rows = jnp.concatenate(rows, axis=0)
    which = iota(rows.shape, 1)
    n = 0
    for g in range(2):
        for h in range(2):
            bricks = brick_tf[place.half[h]]
            bricks = jnp.where(place.group[g] == 0, bricks[0:1], bricks[1:2])
            for bz in range(bricks.shape[1]):
                mine = jnp.where(which == bricks[:, bz:bz + 1], rows, 0.0)
                mine = jnp.sum(mine, axis=1, keepdims=True)
                table[n] = jnp.broadcast_to(mine, table.shape[1:])
                n += 1
            orders = view_order[...]
            orders = jnp.where(place.half[h] == 0, orders[0:1], orders[1:2])
            order = jnp.where(place.group[g] == 0, orders[:, 0:1], orders[:, 1:2])
            signs[g, h] = jnp.broadcast_to(1 - 2 * order, signs.shape[2:])
    block, shape = order_map.shape[1], order_map.shape[1:]
    for n in range(order_map.shape[0]):
        brick = n * block // rim
        orders = view_order[brick:brick + 1]
        order_map[n] = jnp.where(
            iota(shape, 1) < rim,
            jnp.broadcast_to(orders[:, 0:1], shape),
            jnp.broadcast_to(orders[:, 1:2], shape),
        )


def cells_kernel(rim, bumps, g, held, table, signs, shaded, total, optical_s, emitted_s):
    place = Place()
    rows_z = held.shape[4]
    depth = 128
    bricks = rows_z // depth
    lane = iota((rim, 128), 1)
    for h in range(2):
        cells = held.at[g, h]
        for bz in range(bricks):
            zs = slice(bz * depth, (bz + 1) * depth)
            at = (2 * g + h) * bricks + bz
            row = lambda i: jnp.broadcast_to(table[at, i:i + 1, :], (8, depth))[None]
            cen = [row(j) for j in range(bumps)]
            neg = [row(bumps + j) for j in range(bumps)]
            opa = [row(2 * bumps + j) for j in range(bumps)]
            col = [[row((3 + c) * bumps + j) for c in range(3)] for j in range(bumps)]
            for x in range(rim):
                d = cells[x, :, zs].reshape(rim // 8, 8, depth)
                opt, em = None, [None] * 3
                for j in range(bumps):
                    w = d - cen[j]
                    b = jnp.exp2((w * w) * neg[j])
                    opt = opa[j] * b if opt is None else opt + opa[j] * b
                    for c in range(3):
                        em[c] = col[j][c] * b if em[c] is None else em[c] + col[j][c] * b
                rows = slice(x * rim, (x + 1) * rim)
                optical_s[h, rows, zs] = opt.reshape(rim, depth)
                for c in range(3):
                    emitted_s[c, h, rows, zs] = em[c].reshape(rim, depth)
        behind = iota((rows_z, rows_z), 1) - iota((rows_z, rows_z), 0)
        sign = jnp.broadcast_to(signs[g, h][0:1, 0:1], (rows_z, rows_z))
        tri = jnp.where(behind * sign > 0, 1.0, 0.0).astype(BF16)
        opt = optical_s[h]
        hi = opt.astype(BF16)
        lo = (opt - hi.astype(F32)).astype(BF16)
        ahead = dot(hi, tri) + dot(lo, tri)
        weight = jnp.exp2(ahead) * (1.0 - jnp.exp2(opt))
        for c in range(3):
            shaded[c, h] = (weight * emitted_s[c, h]).reshape(rim, rim, rows_z)
        part = rays(opt.reshape(rim, rim, rows_z), place.half[h] * rim, lane)
        total[...] = part if h == 0 else total[...] + part


def rays(cells, first_lane, lane):
    folded = cells[:, :, :128]
    for z in range(128, cells.shape[2], 128):
        folded = folded + cells[:, :, z:z + 128]
    summed = jnp.sum(folded, axis=2, keepdims=True)
    acc = jnp.zeros(lane.shape, F32)
    for x in range(cells.shape[0]):
        acc = jnp.where(lane == first_lane + x, summed[x], acc)
    return acc


def blur_x(place, rim, mx, near, halos):
    flat = lambda cells: cells.reshape(rim * rim, cells.shape[-1])
    edges = []
    for h, halo in enumerate(halos):
        cells = flat(halo)
        edges.append(jnp.where(place.has_x[h], cells, jnp.zeros_like(cells)))
    blocks = [edges[1], flat(near[1]), flat(near[0]), edges[0]]
    return [
        dot(mx[...], jnp.concatenate(blocks[1 - h:4 - h], axis=0)).astype(BF16) for h in range(2)
    ]


def lit(place, rim, occlusion, shaded, h):
    rows_z = occlusion.shape[1]
    lane = iota((rim, 128), 1)
    shade = (1.0 - jnp.tanh(occlusion)).reshape(rim, rim, rows_z)
    return [rays(shade * shaded[c, h], place.half[h] * rim, lane) for c in range(3)]


def own_kernel(rim, early, mx, my, xs0, xs1, halo0, halo1, *refs):
    place = Place()
    size = rim * rim
    across = [
        blur_x(place, rim, mx, [xs0[g], xs1[g]], [halo0[g], halo1[g]]) for g in range(2)
    ]
    if early:
        shaded, out, partial = refs
    else:
        partial, = refs
    for h in range(2):
        s, e = across[0][h], across[1][h]
        partial[0, h] = dot(my[:, :2 * size], jnp.concatenate([e, s], axis=0))
        other = dot(my[:, size:], jnp.concatenate([e, s], axis=0))
        if not early:
            partial[1, h] = other
            continue
        part = lit(place, rim, other, shaded, h)
        for c in range(3):
            out[c] = part[c] if h == 0 else out[c] + part[c]


def late_kernel(rim, g, mx, my, near0, near1, halo0, halo1, partial, shaded, out):
    place = Place()
    size = rim * rim
    across = blur_x(place, rim, mx, [near0[...], near1[...]], [halo0[...], halo1[...]])
    block = my[:, 2 * size:] if g == 0 else my[:, :size]
    for h in range(2):
        cells = jnp.where(place.has_y[g], across[h], jnp.zeros_like(across[h]))
        part = lit(place, rim, partial[g, h] + dot(block, cells), shaded, h)
        for c in range(3):
            out[c] = part[c] if h == 0 else out[c] + part[c]


def blocks_kernel(rim, depth_count, late_s, late_e, total0, total1, *refs):
    outs, (img,) = refs[:2], refs[2:]
    place = Place()
    rows = 2 * rim
    for g, (colours, total) in enumerate(((late_s, total0), (late_e, total1))):
        at = group_rows(place, rim, g)
        for c in range(3):
            img[c, at, :] = colours[c]
        img[3, at, :] = jnp.exp2(total[...])
    for c in range(4):
        img[4 + c, :, 0:rows] = img[c].T[:rows, :]
    block = rows // depth_count
    bit = place.depth & 1
    for n in range(depth_count // 2):
        for out, b in ((outs[0], bit), (outs[1], 1 - bit)):
            out[n] = img[4:8, pl.ds(pl.multiple_of((2 * n + b) * block, block), block), 0:rows]


def merge_kernel(level, order_map, kept, theirs, *outs):
    me = lax.axis_index("depth")
    bit = me >> level & 1
    low = me & (2 << level) - 1
    merged = []
    for n in range(kept.shape[0]):
        mine = (bit == order_map[(n << level + 1) + low])[None]
        front = jnp.where(mine, kept[n], theirs[n])
        back = jnp.where(mine, theirs[n], kept[n])
        merged.append((front[:3] + front[3:] * back[:3], front[3:] * back[3:]))
    if len(merged) == 1:
        colour, through = merged[0]
        outs[0][...] = jnp.concatenate([colour, 1.0 - through]).reshape(outs[0].shape)
        return
    up = me >> level + 1 & 1
    for n in range(len(merged) // 2):
        even, odd = (jnp.concatenate(merged[2 * n + i]) for i in range(2))
        outs[0][n] = jnp.where(up == 1, odd, even)
        outs[1][n] = jnp.where(up == 1, even, odd)


def call(kernel, name, ins, outs, scratch=(), limit=16 * MIB, **more):
    return pl.pallas_call(
        kernel,
        out_shape=outs,
        in_specs=ins,
        out_specs=jax.tree.map(lambda _: VMEM, outs),
        scratch_shapes=list(scratch),
        compiler_params=pltpu.CompilerParams(vmem_limit_bytes=limit),
        name=name,
        **more,
    )


def per_device(
    density, kernel_taps, tf_centre, tf_width, tf_color, tf_opacity, brick_tf, view_order
):
    rows_x, rows_y, rows_z = density.shape
    rim = (kernel_taps.shape[1] - 1) // 2
    bumps = tf_centre.shape[1]
    size = rim * rim
    axes = ("depth", "sx", "sy")
    counts = tuple(lax.axis_size(axis) for axis in axes)
    depth_count, count_y = counts[0], counts[2]
    struct = jax.ShapeDtypeStruct
    block = rows_x // depth_count
    rounds = sum(1 for shift in range(2) if line_pairs(count_y, shift))

    def swap(piece, x_round, y_round):
        return lax.ppermute(piece, axes, swaps(counts, x_round, y_round))

    in_hbm = lambda array: pltpu.with_memory_space_constraint(array, pltpu.HBM)
    tables = (
        kernel_taps, tf_centre.T, tf_width.T, tf_color.T, tf_opacity.T, brick_tf, view_order
    )
    piece = struct((rim, rim, rows_z), BF16)
    both = struct((2, rim, rim, rows_z), BF16)
    held, xs0, xs1, *refs = call(
        functools.partial(first_kernel, rim, rounds),
        "first",
        [HBM] * (1 + len(tables)),
        [struct((2, 2, rim, rim, rows_z), F32), both, both]
        + [piece] * (2 * rounds)
        + [struct(t.shape, t.dtype) for t in tables],
        [pltpu.SemaphoreType.DMA((4 + len(tables),))],
    )(in_hbm(density), *[in_hbm(t) for t in tables])
    strips, tables = refs[:2 * rounds], refs[2 * rounds:]
    near = [[swap(strips[2 * r], None, r), None] for r in range(rounds)]
    halo_x = [swap(xs0, 0, None), None]

    bricks = rows_z // 128
    mx, my, table, signs, order_map = call(
        functools.partial(prepare_kernel, rim),
        "prepare",
        [VMEM] * len(tables),
        [struct((size, 3 * size), BF16)] * 2
        + [struct((4 * bricks, 6 * bumps, 128), F32), struct((2, 2, 8, 128), jnp.int32)]
        + [struct((depth_count, block, rows_y), jnp.int32)],
        [pltpu.VMEM((8, 128), F32)],
    )(*tables)
    cells, table = lax.optimization_barrier((xs1, table))
    halo_x[1] = swap(cells, 1, None)
    shaded, total = [None, None], [None, None]
    for g in (1, 0):
        shaded[g], total[g] = call(
            functools.partial(cells_kernel, rim, bumps, g),
            f"cells{g}",
            [VMEM] * 3,
            [struct((3, 2, rim, rim, rows_z), F32), struct((rim, 128), F32)],
            [pltpu.VMEM((2, size, rows_z), F32), pltpu.VMEM((3, 2, size, rows_z), F32)],
            cost_estimate=pl.CostEstimate(
                flops=density.size * 30, bytes_accessed=density.size * 10, transcendentals=density.size * 3
            ),
        )(held, table, signs)

    corner = [[None, None] for r in range(rounds)]
    for r in range(rounds):
        strip, arrived, total[1] = lax.optimization_barrier(
            (strips[2 * r + 1], near[r][0], total[1])
        )
        corner[r] = [swap(arrived, 0, None), swap(strip, 1, r)]
        near[r][1] = swap(strip, None, r)

    early = rounds < 2
    colours = struct((3, rim, 128), F32)
    partial = struct((2, 2, size, rows_z), F32)
    own = call(
        functools.partial(own_kernel, rim, early),
        "own",
        [VMEM] * (7 if early else 6),
        [colours, partial] if early else [partial],
    )(mx, my, xs0, xs1, *halo_x, *([shaded[1]] if early else []))
    partial = own[-1]
    lights = [None, own[0]]
    for r in range(rounds):
        lights[r] = call(
            functools.partial(late_kernel, rim, r), f"late{r}", [VMEM] * 8, colours
        )(mx, my, *near[r], *corner[r], partial, shaded[r])

    kept, given = call(
        functools.partial(blocks_kernel, rim, depth_count),
        "blocks",
        [VMEM] * 4,
        [struct((depth_count // 2, 4, block, rows_y), F32)] * 2,
        [pltpu.VMEM((8, rows_y, 128), F32)],
    )(*lights, *total)
    level = 0
    while True:
        theirs = lax.ppermute(given, "depth", [(i, i ^ 1 << level) for i in range(depth_count)])
        left = kept.shape[0] // 2
        outs = [struct((left, 4, block, rows_y), F32)] * 2
        merged = call(
            functools.partial(merge_kernel, level),
            f"merge{level}",
            [VMEM] * 3,
            outs if left else struct((4, 1, 1, block, rows_y), F32),
            limit=2 * MIB,
        )(order_map, kept, theirs)
        if not left:
            return merged
        kept, given = merged
        level += 1


def solution(mesh):
    return jax.shard_map(
        per_device,
        mesh=mesh,
        in_specs=(
            P("sx", "sy", "depth"),
            P(),
            P(),
            P(),
            P(),
            P(),
            P("sx", "sy", "depth"),
            P("sx", "sy"),
        ),
        out_specs=P(None, "sx", "depth", None, "sy"),
        check_vma=False,
    )
```

```python
import functools
import math
import jax
import jax.numpy as jnp
from jax import lax
from jax.experimental import pallas as pl
from jax.experimental.pallas import tpu as pltpu
from jax.sharding import PartitionSpec as P

LOG2E = math.log2(math.e)
VMEM = pl.BlockSpec(memory_space=pltpu.VMEM)
HBM = pl.BlockSpec(memory_space=pltpu.HBM)
MIB = 1024 * 1024
F32, BF16 = jnp.float32, jnp.bfloat16
dot = functools.partial(jnp.dot, preferred_element_type=F32)


def iota(shape, dim):
    return lax.broadcasted_iota(jnp.int32, shape, dim)


def line_pairs(count, shift):
    return [(i, i + 1) for i in range(shift, count - 1, 2)]


def swaps(counts, x_round, y_round):
    depth_count, count_x, count_y = counts
    index = lambda d, x, y: (d * count_x + x) * count_y + y
    stay = lambda count: [(i, i) for i in range(count)]
    pairs_x = stay(count_x) if x_round is None else line_pairs(count_x, x_round)
    pairs_y = stay(count_y) if y_round is None else line_pairs(count_y, y_round)
    ends = {((a, c), (b, e)) for a, b in pairs_x for c, e in pairs_y}
    if x_round is not None and y_round is not None:
        ends |= {((a, e), (b, c)) for a, b in pairs_x for c, e in pairs_y}
    used = {end for pair in ends for end in pair}
    pairs = []
    for d in range(depth_count):
        pairs += [(index(d, *a), index(d, *b)) for a, b in sorted(ends)]
    for x in range(count_x):
        for y in range(count_y):
            if (x, y) not in used:
                pairs += [
                    (index(d, x, y), index(d + 1, x, y)) for d in range(0, depth_count - 1, 2)
                ]
    return pairs + [(b, a) for a, b in pairs]


class Place:
    def __init__(self):
        self.depth = lax.axis_index("depth")
        self.half, self.has_x = self.sides("sx")
        self.group, self.has_y = self.sides("sy")

    def sides(self, axis):
        at, last = lax.axis_index(axis), lax.axis_size(axis) - 1
        parity = lax.rem(at, 2)
        upper, lower = at < last, at > 0
        order = (1 - parity, parity)
        either = lambda side: jnp.where(side == 1, upper.astype(jnp.int32), lower.astype(jnp.int32))
        return order, [either(side) == 1 for side in order]


def group_rows(place, rim, g):
    return pl.ds(pl.multiple_of(place.group[g] * rim, rim), rim)


def half_rows(place, rim, h):
    return pl.ds(place.half[h] * rim, rim)


def first_kernel(rim, rounds, density, *refs):
    place = Place()
    n_tables = (len(refs) - 4 - 2 * rounds) // 2
    tables, refs = refs[:n_tables], refs[n_tables:]
    held, xs, refs = refs[0], refs[1:3], refs[3:]
    strips, refs = refs[:2 * rounds], refs[2 * rounds:]
    tables_out, sems = refs[:n_tables], refs[n_tables]
    copies = []
    for g in range(2):
        for h in range(2):
            rows = density.at[half_rows(place, rim, h), group_rows(place, rim, g), :]
            copies.append(pltpu.make_async_copy(rows, held.at[g, h], sems.at[2 * g + h]))
    for i, (src, dst) in enumerate(zip(tables, tables_out)):
        copies.append(pltpu.make_async_copy(src, dst, sems.at[4 + i]))
    for copy in copies:
        copy.start()
    for g in range(2):
        for h in range(2):
            copies[2 * g + h].wait()
            coarse = held[g, h].astype(BF16)
            xs[h][g] = coarse
            if g < rounds:
                strips[2 * g + h][...] = coarse
    for copy in copies[4:]:
        copy.wait()


def toeplitz(taps, rim):
    return pltpu.roll(jnp.broadcast_to(taps, (rim, 128)), 0, 1, stride=1, stride_axis=0)


def blur_matrices(rim, place, taps):
    size = rim * rim
    wide = 3 * size
    shift = rim.bit_length() - 1
    pick = lambda mask: jnp.where(mask, 1.0, 0.0).astype(BF16)
    row_hi = pick(iota((size, rim), 0) >> shift == iota((size, rim), 1))
    row_lo = pick(iota((size, rim), 0) & (rim - 1) == iota((size, rim), 1))
    col = iota((128, wide), 1)
    src = iota((128, wide), 0)
    k, j, b = col >> 2 * shift, col >> shift & (rim - 1), col & (rim - 1)
    k_x = jnp.where(place.half[0] == 1, k, 2 - k)
    k_y = jnp.where(place.group[0] == 1, k, 2 - k)
    tx = toeplitz(taps[0:1], rim).astype(BF16)
    ty = toeplitz(taps[1:2] * 0.5, rim).astype(BF16)
    full_x = dot(row_hi, dot(tx, pick(k_x * rim + j == src)).astype(BF16))
    full_y = dot(row_lo, dot(ty, pick(k_y * rim + b == src)).astype(BF16))
    r, c = iota((size, size), 0), iota((size, size), 1)
    same_x = r & (rim - 1) == c & (rim - 1)
    same_y = r >> shift == c >> shift
    parts = []
    for full, same in ((full_x, same_x), (full_y, same_y)):
        blocks = [
            jnp.where(same, full[:, n * size:(n + 1) * size], 0.0).astype(BF16) for n in range(3)
        ]
        parts.append(jnp.concatenate(blocks, axis=1))
    return parts


def matrices_kernel(rim, taps, mx, my, padded):
    padded[...] = jnp.zeros(padded.shape, F32)
    padded[0:2, 0:taps.shape[1]] = taps[...].astype(F32)
    mx[...], my[...] = blur_matrices(rim, Place(), padded[...])


def prepare_kernel(
    rim, centre, width, colour, opacity, brick_tf, view_order, table, signs, order_map
):
    place = Place()
    wide = width[...]
    rows = [centre[...], (-LOG2E) / (wide * wide), opacity[...] * (-LOG2E)]
    rows += [colour[c] * 0.5 for c in range(3)]
    rows = jnp.concatenate(rows, axis=0)
    which = iota(rows.shape, 1)
    n = 0
    for g in range(2):
        for h in range(2):
            bricks = brick_tf[place.half[h]]
            bricks = jnp.where(place.group[g] == 0, bricks[0:1], bricks[1:2])
            for bz in range(bricks.shape[1]):
                mine = jnp.where(which == bricks[:, bz:bz + 1], rows, 0.0)
                mine = jnp.sum(mine, axis=1, keepdims=True)
                table[n] = jnp.broadcast_to(mine, table.shape[1:])
                n += 1
            orders = view_order[...]
            orders = jnp.where(place.half[h] == 0, orders[0:1], orders[1:2])
            order = jnp.where(place.group[g] == 0, orders[:, 0:1], orders[:, 1:2])
            signs[g, h] = jnp.broadcast_to(1 - 2 * order, signs.shape[2:])
    block, shape = order_map.shape[1], order_map.shape[1:]
    for n in range(order_map.shape[0]):
        brick = n * block // rim
        orders = view_order[brick:brick + 1]
        order_map[n] = jnp.where(
            iota(shape, 1) < rim,
            jnp.broadcast_to(orders[:, 0:1], shape),
            jnp.broadcast_to(orders[:, 1:2], shape),
        )


def cells_kernel(rim, bumps, g, held, table, signs, shaded, total, optical_s, emitted_s):
    place = Place()
    rows_z = held.shape[4]
    depth = 128
    bricks = rows_z // depth
    lane = iota((rim, 128), 1)
    for h in range(2):
        cells = held.at[g, h]
        for bz in range(bricks):
            zs = slice(bz * depth, (bz + 1) * depth)
            at = (2 * g + h) * bricks + bz
            row = lambda i: jnp.broadcast_to(table[at, i:i + 1, :], (8, depth))[None]
            cen = [row(j) for j in range(bumps)]
            neg = [row(bumps + j) for j in range(bumps)]
            opa = [row(2 * bumps + j) for j in range(bumps)]
            col = [[row((3 + c) * bumps + j) for c in range(3)] for j in range(bumps)]
            for x in range(rim):
                d = cells[x, :, zs].reshape(rim // 8, 8, depth)
                opt, em = None, [None] * 3
                for j in range(bumps):
                    w = d - cen[j]
                    b = jnp.exp2((w * w) * neg[j])
                    opt = opa[j] * b if opt is None else opt + opa[j] * b
                    for c in range(3):
                        em[c] = col[j][c] * b if em[c] is None else em[c] + col[j][c] * b
                rows = slice(x * rim, (x + 1) * rim)
                optical_s[h, rows, zs] = opt.reshape(rim, depth)
                for c in range(3):
                    emitted_s[c, h, rows, zs] = em[c].reshape(rim, depth)
        behind = iota((rows_z, rows_z), 1) - iota((rows_z, rows_z), 0)
        sign = jnp.broadcast_to(signs[g, h][0:1, 0:1], (rows_z, rows_z))
        tri = jnp.where(behind * sign > 0, 1.0, 0.0).astype(BF16)
        opt = optical_s[h]
        hi = opt.astype(BF16)
        lo = (opt - hi.astype(F32)).astype(BF16)
        ahead = dot(hi, tri) + dot(lo, tri)
        weight = jnp.exp2(ahead) * (1.0 - jnp.exp2(opt))
        for c in range(3):
            shaded[c, h] = (weight * emitted_s[c, h]).reshape(rim, rim, rows_z)
        part = rays(opt.reshape(rim, rim, rows_z), place.half[h] * rim, lane)
        total[...] = part if h == 0 else total[...] + part


def rays(cells, first_lane, lane):
    folded = cells[:, :, :128]
    for z in range(128, cells.shape[2], 128):
        folded = folded + cells[:, :, z:z + 128]
    summed = jnp.sum(folded, axis=2, keepdims=True)
    acc = jnp.zeros(lane.shape, F32)
    for x in range(cells.shape[0]):
        acc = jnp.where(lane == first_lane + x, summed[x], acc)
    return acc


def blur_x(place, rim, mx, h, near, halo):
    flat = lambda cells: cells.reshape(rim * rim, cells.shape[-1])
    edge = flat(halo)
    edge = jnp.where(place.has_x[h], edge, jnp.zeros_like(edge))
    own = [flat(near[1]), flat(near[0])]
    blocks = own + [edge] if h == 0 else [edge] + own
    return dot(mx[...], jnp.concatenate(blocks, axis=0)).astype(BF16)


def lit(place, rim, occlusion, shaded, h):
    rows_z = occlusion.shape[1]
    lane = iota((rim, 128), 1)
    shade = (1.0 - jnp.tanh(occlusion)).reshape(rim, rim, rows_z)
    return [rays(shade * shaded[c, h], place.half[h] * rim, lane) for c in range(3)]


def own_kernel(rim, h, early, mx, my, xs0, xs1, halo, *refs):
    place = Place()
    size = rim * rim
    s, e = (blur_x(place, rim, mx, h, [xs0[g], xs1[g]], halo[g]) for g in range(2))
    cells = jnp.concatenate([e, s], axis=0)
    partial = refs[-1]
    partial[0] = dot(my[:, :2 * size], cells)
    other = dot(my[:, size:], cells)
    if not early:
        partial[1] = other
        return
    shaded, out, partial = refs
    for c, part in enumerate(lit(place, rim, other, shaded, h)):
        out[c] = part


def late(rim, g, h, mx, my, near0, near1, halo, partial, shaded):
    place = Place()
    size = rim * rim
    across = blur_x(place, rim, mx, h, [near0[...], near1[...]], halo[...])
    across = jnp.where(place.has_y[g], across, jnp.zeros_like(across))
    block = my[:, 2 * size:] if g == 0 else my[:, :size]
    return lit(place, rim, partial[g] + dot(block, across), shaded, h)


def late_kernel(rim, g, h, *refs):
    *refs, out = refs
    for c, part in enumerate(late(rim, g, h, *refs)):
        out[c] = part


def last_kernel(rim, depth_count, *refs):
    (light_s, light_e0, light_e1, total0, total1), refs = refs[:5], refs[5:]
    refs, (kept, given, img) = refs[:7], refs[7:]
    place = Place()
    rows = 2 * rim
    at_s, at_e = group_rows(place, rim, 0), group_rows(place, rim, 1)
    for c, part in enumerate(late(rim, 0, 1, *refs)):
        img[c, at_s, :] = light_s[c] + part
        img[c, at_e, :] = light_e0[c] + light_e1[c]
    img[3, at_s, :] = jnp.exp2(total0[...])
    img[3, at_e, :] = jnp.exp2(total1[...])
    for c in range(4):
        img[4 + c, :, 0:rows] = img[c].T[:rows, :]
    block = rows // depth_count
    bit = place.depth & 1
    for n in range(depth_count // 2):
        for out, b in ((kept, bit), (given, 1 - bit)):
            out[n] = img[4:8, pl.ds(pl.multiple_of((2 * n + b) * block, block), block), 0:rows]


def merge_kernel(level, order_map, kept, theirs, *outs):
    me = lax.axis_index("depth")
    bit = me >> level & 1
    low = me & (2 << level) - 1
    merged = []
    for n in range(kept.shape[0]):
        mine = (bit == order_map[(n << level + 1) + low])[None]
        front = jnp.where(mine, kept[n], theirs[n])
        back = jnp.where(mine, theirs[n], kept[n])
        merged.append((front[:3] + front[3:] * back[:3], front[3:] * back[3:]))
    if len(merged) == 1:
        colour, through = merged[0]
        outs[0][...] = jnp.concatenate([colour, 1.0 - through]).reshape(outs[0].shape)
        return
    up = me >> level + 1 & 1
    for n in range(len(merged) // 2):
        even, odd = (jnp.concatenate(merged[2 * n + i]) for i in range(2))
        outs[0][n] = jnp.where(up == 1, odd, even)
        outs[1][n] = jnp.where(up == 1, even, odd)


def call(kernel, name, ins, outs, scratch=(), limit=16 * MIB, **more):
    return pl.pallas_call(
        kernel,
        out_shape=outs,
        in_specs=ins,
        out_specs=jax.tree.map(lambda _: VMEM, outs),
        scratch_shapes=list(scratch),
        compiler_params=pltpu.CompilerParams(vmem_limit_bytes=limit),
        name=name,
        **more,
    )


def per_device(
    density, kernel_taps, tf_centre, tf_width, tf_color, tf_opacity, brick_tf, view_order
):
    rows_x, rows_y, rows_z = density.shape
    rim = (kernel_taps.shape[1] - 1) // 2
    bumps = tf_centre.shape[1]
    size = rim * rim
    axes = ("depth", "sx", "sy")
    counts = tuple(lax.axis_size(axis) for axis in axes)
    depth_count, count_y = counts[0], counts[2]
    struct = jax.ShapeDtypeStruct
    block = rows_x // depth_count
    rounds = sum(1 for shift in range(2) if line_pairs(count_y, shift))

    def swap(piece, x_round, y_round):
        return lax.ppermute(piece, axes, swaps(counts, x_round, y_round))

    in_hbm = lambda array: pltpu.with_memory_space_constraint(array, pltpu.HBM)
    tables = (
        kernel_taps, tf_centre.T, tf_width.T, tf_color.T, tf_opacity.T, brick_tf, view_order
    )
    piece = struct((rim, rim, rows_z), BF16)
    both = struct((2, rim, rim, rows_z), BF16)
    held, xs0, xs1, *refs = call(
        functools.partial(first_kernel, rim, rounds),
        "first",
        [HBM] * (1 + len(tables)),
        [struct((2, 2, rim, rim, rows_z), F32), both, both]
        + [piece] * (2 * rounds)
        + [struct(t.shape, t.dtype) for t in tables],
        [pltpu.SemaphoreType.DMA((4 + len(tables),))],
    )(in_hbm(density), *[in_hbm(t) for t in tables])
    strips, tables = refs[:2 * rounds], refs[2 * rounds:]
    near = [[swap(strips[2 * r], None, r), None] for r in range(rounds)]

    bricks = rows_z // 128
    table, signs, order_map = call(
        functools.partial(prepare_kernel, rim),
        "prepare",
        [VMEM] * (len(tables) - 1),
        [struct((4 * bricks, 6 * bumps, 128), F32), struct((2, 2, 8, 128), jnp.int32)]
        + [struct((depth_count, block, rows_y), jnp.int32)],
    )(*tables[1:])
    halo_x = [swap(cells, h, None) for h, cells in enumerate((xs0, xs1))]
    mx, my = call(
        functools.partial(matrices_kernel, rim),
        "matrices",
        [VMEM],
        [struct((size, 3 * size), BF16)] * 2,
        [pltpu.VMEM((8, 128), F32)],
    )(tables[0])
    shaded, total = [None, None], [None, None]
    for g in (1, 0):
        shaded[g], total[g] = call(
            functools.partial(cells_kernel, rim, bumps, g),
            f"cells{g}",
            [VMEM] * 3,
            [struct((3, 2, rim, rim, rows_z), F32), struct((rim, 128), F32)],
            [pltpu.VMEM((2, size, rows_z), F32), pltpu.VMEM((3, 2, size, rows_z), F32)],
            cost_estimate=pl.CostEstimate(
                flops=density.size * (100000 if g == 0 else 1),
                bytes_accessed=density.size * (10000 if g == 0 else 1),
                transcendentals=density.size * 3,
            ),
        )(held, table, signs)

    corner = [[None, None] for r in range(rounds)]
    for r in range(rounds):
        strip, arrived, total[1] = lax.optimization_barrier(
            (strips[2 * r + 1], near[r][0], total[1])
        )
        corner[r] = [swap(arrived, 0, None), swap(strip, 1, r)]
        near[r][1] = swap(strip, None, r)

    early = rounds < 2
    colours = struct((3, rim, 128), F32)
    partial, lights = [None, None], [[None, None], [None, None]]
    for h in range(2):
        unlit = struct((2 - early, size, rows_z), F32)
        results = call(
            functools.partial(own_kernel, rim, h, early),
            f"own{h}",
            [VMEM] * (6 if early else 5),
            [colours, unlit] if early else [unlit],
        )(mx, my, xs0, xs1, halo_x[h], *([shaded[1]] if early else []))
        partial[h] = results[-1]
        if early:
            lights[1][h] = results[0]
    for g in range(rounds):
        for h in range(2 if g == 1 else 1):
            lights[g][h] = call(
                functools.partial(late_kernel, rim, g, h), f"late{g}{h}", [VMEM] * 7, colours
            )(mx, my, *near[g], corner[g][h], partial[h], shaded[g])
    kept, given = call(
        functools.partial(last_kernel, rim, depth_count),
        "last",
        [VMEM] * 12,
        [struct((depth_count // 2, 4, block, rows_y), F32)] * 2,
        [pltpu.VMEM((8, rows_y, 128), F32)],
    )(lights[0][0], *lights[1], *total, mx, my, *near[0], corner[0][1], partial[1], shaded[0])
    level = 0
    while True:
        theirs = lax.ppermute(given, "depth", [(i, i ^ 1 << level) for i in range(depth_count)])
        left = kept.shape[0] // 2
        outs = [struct((left, 4, block, rows_y), F32)] * 2
        merged = call(
            functools.partial(merge_kernel, level),
            f"merge{level}",
            [VMEM] * 3,
            outs if left else struct((4, 1, 1, block, rows_y), F32),
            limit=2 * MIB,
        )(order_map, kept, theirs)
        if not left:
            return merged
        kept, given = merged
        level += 1


def solution(mesh):
    return jax.shard_map(
        per_device,
        mesh=mesh,
        in_specs=(
            P("sx", "sy", "depth"),
            P(),
            P(),
            P(),
            P(),
            P(),
            P("sx", "sy", "depth"),
            P("sx", "sy"),
        ),
        out_specs=P(None, "sx", "depth", None, "sy"),
        check_vma=False,
    )
```

```python
import functools
import math
import jax
import jax.numpy as jnp
from jax import lax
from jax.experimental import pallas as pl
from jax.experimental.pallas import tpu as pltpu
from jax.sharding import PartitionSpec as P

LOG2E = math.log2(math.e)
VMEM = pl.BlockSpec(memory_space=pltpu.VMEM)
HBM = pl.BlockSpec(memory_space=pltpu.HBM)
MIB = 1024 * 1024
F32, BF16 = jnp.float32, jnp.bfloat16
dot = functools.partial(jnp.dot, preferred_element_type=F32)


def iota(shape, dim):
    return lax.broadcasted_iota(jnp.int32, shape, dim)


def line_pairs(count, shift):
    return [(i, i + 1) for i in range(shift, count - 1, 2)]


def swaps(counts, x_round, y_round):
    depth_count, count_x, count_y = counts
    index = lambda d, x, y: (d * count_x + x) * count_y + y
    stay = lambda count: [(i, i) for i in range(count)]
    pairs_x = stay(count_x) if x_round is None else line_pairs(count_x, x_round)
    pairs_y = stay(count_y) if y_round is None else line_pairs(count_y, y_round)
    ends = {((a, c), (b, e)) for a, b in pairs_x for c, e in pairs_y}
    if x_round is not None and y_round is not None:
        ends |= {((a, e), (b, c)) for a, b in pairs_x for c, e in pairs_y}
    used = {end for pair in ends for end in pair}
    pairs = []
    for d in range(depth_count):
        pairs += [(index(d, *a), index(d, *b)) for a, b in sorted(ends)]
    for x in range(count_x):
        for y in range(count_y):
            if (x, y) not in used:
                pairs += [
                    (index(d, x, y), index(d + 1, x, y)) for d in range(0, depth_count - 1, 2)
                ]
    return pairs + [(b, a) for a, b in pairs]


class Place:
    def __init__(self):
        self.depth = lax.axis_index("depth")
        self.half, self.has_x = self.sides("sx")
        self.group, self.has_y = self.sides("sy")

    def sides(self, axis):
        at, last = lax.axis_index(axis), lax.axis_size(axis) - 1
        parity = lax.rem(at, 2)
        upper, lower = at < last, at > 0
        order = (1 - parity, parity)
        either = lambda side: jnp.where(side == 1, upper.astype(jnp.int32), lower.astype(jnp.int32))
        return order, [either(side) == 1 for side in order]


def group_rows(place, rim, g):
    return pl.ds(pl.multiple_of(place.group[g] * rim, rim), rim)


def half_rows(place, rim, h):
    return pl.ds(place.half[h] * rim, rim)


def first_kernel(rim, rounds, density, *refs):
    place = Place()
    n_tables = (len(refs) - 4 - 2 * rounds) // 2
    tables, refs = refs[:n_tables], refs[n_tables:]
    held, xs, refs = refs[0], refs[1:3], refs[3:]
    strips, refs = refs[:2 * rounds], refs[2 * rounds:]
    tables_out, sems = refs[:n_tables], refs[n_tables]
    copies = []
    for g in range(2):
        for h in range(2):
            rows = density.at[half_rows(place, rim, h), group_rows(place, rim, g), :]
            copies.append(pltpu.make_async_copy(rows, held.at[g, h], sems.at[2 * g + h]))
    for i, (src, dst) in enumerate(zip(tables, tables_out)):
        copies.append(pltpu.make_async_copy(src, dst, sems.at[4 + i]))
    for copy in copies:
        copy.start()
    for g in range(2):
        for h in range(2):
            copies[2 * g + h].wait()
            coarse = held[g, h].astype(BF16)
            xs[h][g] = coarse
            if g < rounds:
                strips[2 * g + h][...] = coarse
    for copy in copies[4:]:
        copy.wait()


def toeplitz(taps, rim):
    return pltpu.roll(jnp.broadcast_to(taps, (rim, 128)), 0, 1, stride=1, stride_axis=0)


def blur_matrices(rim, place, taps):
    size = rim * rim
    wide = 3 * size
    shift = rim.bit_length() - 1
    pick = lambda mask: jnp.where(mask, 1.0, 0.0).astype(BF16)
    row_hi = pick(iota((size, rim), 0) >> shift == iota((size, rim), 1))
    row_lo = pick(iota((size, rim), 0) & (rim - 1) == iota((size, rim), 1))
    col = iota((128, wide), 1)
    src = iota((128, wide), 0)
    k, j, b = col >> 2 * shift, col >> shift & (rim - 1), col & (rim - 1)
    k_x = jnp.where(place.half[0] == 1, k, 2 - k)
    k_y = jnp.where(place.group[0] == 1, k, 2 - k)
    tx = toeplitz(taps[0:1], rim).astype(BF16)
    ty = toeplitz(taps[1:2] * 0.5, rim).astype(BF16)
    full_x = dot(row_hi, dot(tx, pick(k_x * rim + j == src)).astype(BF16))
    full_y = dot(row_lo, dot(ty, pick(k_y * rim + b == src)).astype(BF16))
    r, c = iota((size, size), 0), iota((size, size), 1)
    same_x = r & (rim - 1) == c & (rim - 1)
    same_y = r >> shift == c >> shift
    parts = []
    for full, same in ((full_x, same_x), (full_y, same_y)):
        blocks = [
            jnp.where(same, full[:, n * size:(n + 1) * size], 0.0).astype(BF16) for n in range(3)
        ]
        parts.append(jnp.concatenate(blocks, axis=1))
    return parts


def matrices_kernel(rim, taps, mx, my, padded):
    padded[...] = jnp.zeros(padded.shape, F32)
    padded[0:2, 0:taps.shape[1]] = taps[...].astype(F32)
    mx[...], my[...] = blur_matrices(rim, Place(), padded[...])


def prepare_kernel(
    rim, centre, width, colour, opacity, brick_tf, view_order, table, signs, order_map
):
    place = Place()
    wide = width[...]
    rows = [centre[...], (-LOG2E) / (wide * wide), opacity[...] * (-LOG2E)]
    rows += [colour[c] * 0.5 for c in range(3)]
    rows = jnp.concatenate(rows, axis=0)
    which = iota(rows.shape, 1)
    n = 0
    for g in range(2):
        for h in range(2):
            bricks = brick_tf[place.half[h]]
            bricks = jnp.where(place.group[g] == 0, bricks[0:1], bricks[1:2])
            for bz in range(bricks.shape[1]):
                mine = jnp.where(which == bricks[:, bz:bz + 1], rows, 0.0)
                mine = jnp.sum(mine, axis=1, keepdims=True)
                table[n] = jnp.broadcast_to(mine, table.shape[1:])
                n += 1
            orders = view_order[...]
            orders = jnp.where(place.half[h] == 0, orders[0:1], orders[1:2])
            order = jnp.where(place.group[g] == 0, orders[:, 0:1], orders[:, 1:2])
            signs[g, h] = jnp.broadcast_to(1 - 2 * order, signs.shape[2:])
    block, shape = order_map.shape[1], order_map.shape[1:]
    for n in range(order_map.shape[0]):
        brick = n * block // rim
        orders = view_order[brick:brick + 1]
        order_map[n] = jnp.where(
            iota(shape, 1) < rim,
            jnp.broadcast_to(orders[:, 0:1], shape),
            jnp.broadcast_to(orders[:, 1:2], shape),
        )


def cells_kernel(rim, bumps, g, held, table, signs, shaded, total, optical_s, emitted_s):
    place = Place()
    rows_z = held.shape[4]
    depth = 128
    bricks = rows_z // depth
    lane = iota((rim, 128), 1)
    for h in range(2):
        cells = held.at[g, h]
        for bz in range(bricks):
            zs = slice(bz * depth, (bz + 1) * depth)
            at = (2 * g + h) * bricks + bz
            row = lambda i: jnp.broadcast_to(table[at, i:i + 1, :], (8, depth))[None]
            cen = [row(j) for j in range(bumps)]
            neg = [row(bumps + j) for j in range(bumps)]
            opa = [row(2 * bumps + j) for j in range(bumps)]
            col = [[row((3 + c) * bumps + j) for c in range(3)] for j in range(bumps)]
            for x in range(rim):
                d = cells[x, :, zs].reshape(rim // 8, 8, depth)
                opt, em = None, [None] * 3
                for j in range(bumps):
                    w = d - cen[j]
                    b = jnp.exp2((w * w) * neg[j])
                    opt = opa[j] * b if opt is None else opt + opa[j] * b
                    for c in range(3):
                        em[c] = col[j][c] * b if em[c] is None else em[c] + col[j][c] * b
                rows = slice(x * rim, (x + 1) * rim)
                optical_s[h, rows, zs] = opt.reshape(rim, depth)
                for c in range(3):
                    emitted_s[c, h, rows, zs] = em[c].reshape(rim, depth)
        behind = iota((rows_z, rows_z), 1) - iota((rows_z, rows_z), 0)
        sign = jnp.broadcast_to(signs[g, h][0:1, 0:1], (rows_z, rows_z))
        tri = jnp.where(behind * sign > 0, 1.0, 0.0).astype(BF16)
        opt = optical_s[h]
        hi = opt.astype(BF16)
        lo = (opt - hi.astype(F32)).astype(BF16)
        ahead = dot(hi, tri) + dot(lo, tri)
        weight = jnp.exp2(ahead) * (1.0 - jnp.exp2(opt))
        for c in range(3):
            shaded[c, h] = (weight * emitted_s[c, h]).reshape(rim, rim, rows_z)
        part = rays(opt.reshape(rim, rim, rows_z), place.half[h] * rim, lane)
        total[...] = part if h == 0 else total[...] + part


def rays(cells, first_lane, lane):
    folded = cells[:, :, :128]
    for z in range(128, cells.shape[2], 128):
        folded = folded + cells[:, :, z:z + 128]
    summed = jnp.sum(folded, axis=2, keepdims=True)
    acc = jnp.zeros(lane.shape, F32)
    for x in range(cells.shape[0]):
        acc = jnp.where(lane == first_lane + x, summed[x], acc)
    return acc


def blur_x(place, rim, mx, h, near, halo):
    flat = lambda cells: cells.reshape(rim * rim, cells.shape[-1])
    edge = flat(halo)
    edge = jnp.where(place.has_x[h], edge, jnp.zeros_like(edge))
    own = [flat(near[1]), flat(near[0])]
    blocks = own + [edge] if h == 0 else [edge] + own
    return dot(mx[...], jnp.concatenate(blocks, axis=0)).astype(BF16)


def lit(place, rim, occlusion, shaded, h):
    rows_z = occlusion.shape[1]
    lane = iota((rim, 128), 1)
    shade = (1.0 - jnp.tanh(occlusion)).reshape(rim, rim, rows_z)
    return [rays(shade * shaded[c, h], place.half[h] * rim, lane) for c in range(3)]


def own_kernel(rim, early, mx, my, xs0, xs1, halo0, halo1, *refs):
    place = Place()
    size = rim * rim
    if early:
        shaded, out, partial = refs
    else:
        partial, = refs
    for h, halo in enumerate((halo0, halo1)):
        s, e = (blur_x(place, rim, mx, h, [xs0[g], xs1[g]], halo[g]) for g in range(2))
        cells = jnp.concatenate([e, s], axis=0)
        partial[0, h] = dot(my[:, :2 * size], cells)
        other = dot(my[:, size:], cells)
        if not early:
            partial[1, h] = other
            continue
        for c, part in enumerate(lit(place, rim, other, shaded, h)):
            out[c] = part if h == 0 else out[c] + part


def late(rim, g, mx, my, near0, partial, near1, halo0, halo1, shaded):
    place = Place()
    size = rim * rim
    block = my[:, 2 * size:] if g == 0 else my[:, :size]
    acc = None
    for h, halo in enumerate((halo0, halo1)):
        across = blur_x(place, rim, mx, h, [near0[...], near1[...]], halo[...])
        across = jnp.where(place.has_y[g], across, jnp.zeros_like(across))
        part = lit(place, rim, partial[g, h] + dot(block, across), shaded, h)
        acc = part if h == 0 else [a + b for a, b in zip(acc, part)]
    return acc


def late_kernel(rim, g, *refs):
    *refs, out = refs
    for c, part in enumerate(late(rim, g, *refs)):
        out[c] = part


def last_kernel(rim, depth_count, *refs):
    refs, (light_e, total0, total1, kept, given, img) = refs[:8], refs[8:]
    place = Place()
    rows = 2 * rim
    at_s, at_e = group_rows(place, rim, 0), group_rows(place, rim, 1)
    for c, part in enumerate(late(rim, 0, *refs)):
        img[c, at_s, :] = part
        img[c, at_e, :] = light_e[c]
    img[3, at_s, :] = jnp.exp2(total0[...])
    img[3, at_e, :] = jnp.exp2(total1[...])
    for c in range(4):
        img[4 + c, :, 0:rows] = img[c].T[:rows, :]
    block = rows // depth_count
    bit = place.depth & 1
    for n in range(depth_count // 2):
        for out, b in ((kept, bit), (given, 1 - bit)):
            out[n] = img[4:8, pl.ds(pl.multiple_of((2 * n + b) * block, block), block), 0:rows]


def merge_kernel(level, order_map, kept, theirs, *outs):
    me = lax.axis_index("depth")
    bit = me >> level & 1
    low = me & (2 << level) - 1
    merged = []
    for n in range(kept.shape[0]):
        mine = (bit == order_map[(n << level + 1) + low])[None]
        front = jnp.where(mine, kept[n], theirs[n])
        back = jnp.where(mine, theirs[n], kept[n])
        merged.append((front[:3] + front[3:] * back[:3], front[3:] * back[3:]))
    if len(merged) == 1:
        colour, through = merged[0]
        outs[0][...] = jnp.concatenate([colour, 1.0 - through]).reshape(outs[0].shape)
        return
    up = me >> level + 1 & 1
    for n in range(len(merged) // 2):
        even, odd = (jnp.concatenate(merged[2 * n + i]) for i in range(2))
        outs[0][n] = jnp.where(up == 1, odd, even)
        outs[1][n] = jnp.where(up == 1, even, odd)


def call(kernel, name, ins, outs, scratch=(), limit=16 * MIB, **more):
    return pl.pallas_call(
        kernel,
        out_shape=outs,
        in_specs=ins,
        out_specs=jax.tree.map(lambda _: VMEM, outs),
        scratch_shapes=list(scratch),
        compiler_params=pltpu.CompilerParams(vmem_limit_bytes=limit),
        name=name,
        **more,
    )


def per_device(
    density, kernel_taps, tf_centre, tf_width, tf_color, tf_opacity, brick_tf, view_order
):
    rows_x, rows_y, rows_z = density.shape
    rim = (kernel_taps.shape[1] - 1) // 2
    bumps = tf_centre.shape[1]
    size = rim * rim
    axes = ("depth", "sx", "sy")
    counts = tuple(lax.axis_size(axis) for axis in axes)
    depth_count, count_y = counts[0], counts[2]
    struct = jax.ShapeDtypeStruct
    block = rows_x // depth_count
    rounds = sum(1 for shift in range(2) if line_pairs(count_y, shift))

    def swap(piece, x_round, y_round):
        return lax.ppermute(piece, axes, swaps(counts, x_round, y_round))

    in_hbm = lambda array: pltpu.with_memory_space_constraint(array, pltpu.HBM)
    tables = (
        kernel_taps, tf_centre.T, tf_width.T, tf_color.T, tf_opacity.T, brick_tf, view_order
    )
    piece = struct((rim, rim, rows_z), BF16)
    both = struct((2, rim, rim, rows_z), BF16)
    held, xs0, xs1, *refs = call(
        functools.partial(first_kernel, rim, rounds),
        "first",
        [HBM] * (1 + len(tables)),
        [struct((2, 2, rim, rim, rows_z), F32), both, both]
        + [piece] * (2 * rounds)
        + [struct(t.shape, t.dtype) for t in tables],
        [pltpu.SemaphoreType.DMA((4 + len(tables),))],
    )(in_hbm(density), *[in_hbm(t) for t in tables])
    strips, tables = refs[:2 * rounds], refs[2 * rounds:]
    near = [[swap(strips[2 * r], None, r), None] for r in range(rounds)]

    bricks = rows_z // 128
    table, signs, order_map = call(
        functools.partial(prepare_kernel, rim),
        "prepare",
        [VMEM] * (len(tables) - 1),
        [struct((4 * bricks, 6 * bumps, 128), F32), struct((2, 2, 8, 128), jnp.int32)]
        + [struct((depth_count, block, rows_y), jnp.int32)],
    )(*tables[1:])
    halo_x = [swap(cells, h, None) for h, cells in enumerate((xs0, xs1))]
    mx, my = call(
        functools.partial(matrices_kernel, rim),
        "matrices",
        [VMEM],
        [struct((size, 3 * size), BF16)] * 2,
        [pltpu.VMEM((8, 128), F32)],
    )(tables[0])
    shaded, total = [None, None], [None, None]
    for g in (1, 0):
        shaded[g], total[g] = call(
            functools.partial(cells_kernel, rim, bumps, g),
            f"cells{g}",
            [VMEM] * 3,
            [struct((3, 2, rim, rim, rows_z), F32), struct((rim, 128), F32)],
            [pltpu.VMEM((2, size, rows_z), F32), pltpu.VMEM((3, 2, size, rows_z), F32)],
            cost_estimate=pl.CostEstimate(
                flops=density.size * (100000 if g == 0 else 1),
                bytes_accessed=density.size * (10000 if g == 0 else 1),
                transcendentals=density.size * 3,
            ),
        )(held, table, signs)

    corner = [[None, None] for r in range(rounds)]
    for r in range(rounds):
        near[r][1] = swap(strips[2 * r + 1], None, r)
        strip, arrived, total[1] = lax.optimization_barrier(
            (strips[2 * r + 1], near[r][0], total[1])
        )
        corner[r] = [swap(arrived, 0, None), swap(strip, 1, r)]

    early = rounds < 2
    colours = struct((3, rim, 128), F32)
    unlit = struct((2 - early, 2, size, rows_z), F32)
    results = call(
        functools.partial(own_kernel, rim, early),
        "own",
        [VMEM] * (7 if early else 6),
        [colours, unlit] if early else [unlit],
    )(mx, my, xs0, xs1, *halo_x, *([shaded[1]] if early else []))
    partial = results[-1]
    if early:
        light = results[0]
    else:
        light = call(functools.partial(late_kernel, rim, 1), "late", [VMEM] * 8, colours)(
            mx, my, near[1][0], partial, near[1][1], *corner[1], shaded[1]
        )
    kept, given = call(
        functools.partial(last_kernel, rim, depth_count),
        "last",
        [VMEM] * 11,
        [struct((depth_count // 2, 4, block, rows_y), F32)] * 2,
        [pltpu.VMEM((8, rows_y, 128), F32)],
    )(mx, my, near[0][0], partial, near[0][1], *corner[0], shaded[0], light, *total)
    level = 0
    while True:
        theirs = lax.ppermute(given, "depth", [(i, i ^ 1 << level) for i in range(depth_count)])
        left = kept.shape[0] // 2
        outs = [struct((left, 4, block, rows_y), F32)] * 2
        merged = call(
            functools.partial(merge_kernel, level),
            f"merge{level}",
            [VMEM] * 3,
            outs if left else struct((4, 1, 1, block, rows_y), F32),
            limit=2 * MIB,
        )(order_map, kept, theirs)
        if not left:
            return merged
        kept, given = merged
        level += 1


def solution(mesh):
    return jax.shard_map(
        per_device,
        mesh=mesh,
        in_specs=(
            P("sx", "sy", "depth"),
            P(),
            P(),
            P(),
            P(),
            P(),
            P("sx", "sy", "depth"),
            P("sx", "sy"),
        ),
        out_specs=P(None, "sx", "depth", None, "sy"),
        check_vma=False,
    )
```

```python
import functools
import math
import jax
import jax.numpy as jnp
from jax import lax
from jax.experimental import pallas as pl
from jax.experimental.pallas import tpu as pltpu
from jax.sharding import PartitionSpec as P

LOG2E = math.log2(math.e)
VMEM = pl.BlockSpec(memory_space=pltpu.VMEM)
HBM = pl.BlockSpec(memory_space=pltpu.HBM)
MIB = 1024 * 1024
F32, BF16 = jnp.float32, jnp.bfloat16
dot = functools.partial(jnp.dot, preferred_element_type=F32)


def iota(shape, dim):
    return lax.broadcasted_iota(jnp.int32, shape, dim)


def line_pairs(count, shift):
    return [(i, i + 1) for i in range(shift, count - 1, 2)]


def swaps(counts, x_round, y_round):
    depth_count, count_x, count_y = counts
    index = lambda d, x, y: (d * count_x + x) * count_y + y
    stay = lambda count: [(i, i) for i in range(count)]
    pairs_x = stay(count_x) if x_round is None else line_pairs(count_x, x_round)
    pairs_y = stay(count_y) if y_round is None else line_pairs(count_y, y_round)
    ends = {((a, c), (b, e)) for a, b in pairs_x for c, e in pairs_y}
    if x_round is not None and y_round is not None:
        ends |= {((a, e), (b, c)) for a, b in pairs_x for c, e in pairs_y}
    used = {end for pair in ends for end in pair}
    pairs = []
    for d in range(depth_count):
        pairs += [(index(d, *a), index(d, *b)) for a, b in sorted(ends)]
    for x in range(count_x):
        for y in range(count_y):
            if (x, y) not in used:
                pairs += [
                    (index(d, x, y), index(d + 1, x, y)) for d in range(0, depth_count - 1, 2)
                ]
    return pairs + [(b, a) for a, b in pairs]


class Place:
    def __init__(self):
        self.depth = lax.axis_index("depth")
        self.half, self.has_x = self.sides("sx")
        self.group, self.has_y = self.sides("sy")

    def sides(self, axis):
        at, last = lax.axis_index(axis), lax.axis_size(axis) - 1
        parity = lax.rem(at, 2)
        upper, lower = at < last, at > 0
        order = (1 - parity, parity)
        either = lambda side: jnp.where(side == 1, upper.astype(jnp.int32), lower.astype(jnp.int32))
        return order, [either(side) == 1 for side in order]


def group_rows(place, rim, g):
    return pl.ds(pl.multiple_of(place.group[g] * rim, rim), rim)


def half_rows(place, rim, h):
    return pl.ds(place.half[h] * rim, rim)


def first_kernel(rim, rounds, density, *refs):
    place = Place()
    n_tables = (len(refs) - 4 - 2 * rounds) // 2
    tables, refs = refs[:n_tables], refs[n_tables:]
    held, xs, refs = refs[0], refs[1:3], refs[3:]
    strips, refs = refs[:2 * rounds], refs[2 * rounds:]
    tables_out, sems = refs[:n_tables], refs[n_tables]
    copies = []
    for g in range(2):
        for h in range(2):
            rows = density.at[half_rows(place, rim, h), group_rows(place, rim, g), :]
            copies.append(pltpu.make_async_copy(rows, held.at[g, h], sems.at[2 * g + h]))
    for i, (src, dst) in enumerate(zip(tables, tables_out)):
        copies.append(pltpu.make_async_copy(src, dst, sems.at[4 + i]))
    for copy in copies:
        copy.start()
    for g in range(2):
        for h in range(2):
            copies[2 * g + h].wait()
            coarse = held[g, h].astype(BF16)
            xs[h][g] = coarse
            if g < rounds:
                strips[2 * g + h][...] = coarse
    for copy in copies[4:]:
        copy.wait()


def toeplitz(taps, rim):
    return pltpu.roll(jnp.broadcast_to(taps, (rim, 128)), 0, 1, stride=1, stride_axis=0)


def blur_matrices(rim, place, taps):
    size = rim * rim
    wide = 3 * size
    shift = rim.bit_length() - 1
    pick = lambda mask: jnp.where(mask, 1.0, 0.0).astype(BF16)
    row_hi = pick(iota((size, rim), 0) >> shift == iota((size, rim), 1))
    row_lo = pick(iota((size, rim), 0) & (rim - 1) == iota((size, rim), 1))
    col = iota((128, wide), 1)
    src = iota((128, wide), 0)
    k, j, b = col >> 2 * shift, col >> shift & (rim - 1), col & (rim - 1)
    k_x = jnp.where(place.half[0] == 1, k, 2 - k)
    k_y = jnp.where(place.group[0] == 1, k, 2 - k)
    tx = toeplitz(taps[0:1], rim).astype(BF16)
    ty = toeplitz(taps[1:2] * 0.5, rim).astype(BF16)
    full_x = dot(row_hi, dot(tx, pick(k_x * rim + j == src)).astype(BF16))
    full_y = dot(row_lo, dot(ty, pick(k_y * rim + b == src)).astype(BF16))
    r, c = iota((size, size), 0), iota((size, size), 1)
    same_x = r & (rim - 1) == c & (rim - 1)
    same_y = r >> shift == c >> shift
    parts = []
    for full, same in ((full_x, same_x), (full_y, same_y)):
        blocks = [
            jnp.where(same, full[:, n * size:(n + 1) * size], 0.0).astype(BF16) for n in range(3)
        ]
        parts.append(jnp.concatenate(blocks, axis=1))
    return parts


def matrices_kernel(rim, taps, mx, my, padded):
    padded[...] = jnp.zeros(padded.shape, F32)
    padded[0:2, 0:taps.shape[1]] = taps[...].astype(F32)
    mx[...], my[...] = blur_matrices(rim, Place(), padded[...])


def prepare_kernel(
    rim, centre, width, colour, opacity, brick_tf, view_order, table, signs, order_map
):
    place = Place()
    wide = width[...]
    rows = [centre[...], (-LOG2E) / (wide * wide), opacity[...] * (-LOG2E)]
    rows += [colour[c] * 0.5 for c in range(3)]
    rows = jnp.concatenate(rows, axis=0)
    which = iota(rows.shape, 1)
    n = 0
    for g in range(2):
        for h in range(2):
            bricks = brick_tf[place.half[h]]
            bricks = jnp.where(place.group[g] == 0, bricks[0:1], bricks[1:2])
            for bz in range(bricks.shape[1]):
                mine = jnp.where(which == bricks[:, bz:bz + 1], rows, 0.0)
                mine = jnp.sum(mine, axis=1, keepdims=True)
                table[n] = jnp.broadcast_to(mine, table.shape[1:])
                n += 1
            orders = view_order[...]
            orders = jnp.where(place.half[h] == 0, orders[0:1], orders[1:2])
            order = jnp.where(place.group[g] == 0, orders[:, 0:1], orders[:, 1:2])
            signs[g, h] = jnp.broadcast_to(1 - 2 * order, signs.shape[2:])
    block, shape = order_map.shape[1], order_map.shape[1:]
    for n in range(order_map.shape[0]):
        brick = n * block // rim
        orders = view_order[brick:brick + 1]
        order_map[n] = jnp.where(
            iota(shape, 1) < rim,
            jnp.broadcast_to(orders[:, 0:1], shape),
            jnp.broadcast_to(orders[:, 1:2], shape),
        )


def cells_kernel(rim, bumps, g, held, table, signs, shaded, total, optical_s, emitted_s):
    place = Place()
    rows_z = held.shape[4]
    depth = 128
    bricks = rows_z // depth
    lane = iota((rim, 128), 1)
    for h in range(2):
        cells = held.at[g, h]
        for bz in range(bricks):
            zs = slice(bz * depth, (bz + 1) * depth)
            at = (2 * g + h) * bricks + bz
            row = lambda i: jnp.broadcast_to(table[at, i:i + 1, :], (8, depth))[None]
            cen = [row(j) for j in range(bumps)]
            neg = [row(bumps + j) for j in range(bumps)]
            opa = [row(2 * bumps + j) for j in range(bumps)]
            col = [[row((3 + c) * bumps + j) for c in range(3)] for j in range(bumps)]
            for x in range(rim):
                d = cells[x, :, zs].reshape(rim // 8, 8, depth)
                opt, em = None, [None] * 3
                for j in range(bumps):
                    w = d - cen[j]
                    b = jnp.exp2((w * w) * neg[j])
                    opt = opa[j] * b if opt is None else opt + opa[j] * b
                    for c in range(3):
                        em[c] = col[j][c] * b if em[c] is None else em[c] + col[j][c] * b
                rows = slice(x * rim, (x + 1) * rim)
                optical_s[h, rows, zs] = opt.reshape(rim, depth)
                for c in range(3):
                    emitted_s[c, h, rows, zs] = em[c].reshape(rim, depth)
        behind = iota((rows_z, rows_z), 1) - iota((rows_z, rows_z), 0)
        sign = jnp.broadcast_to(signs[g, h][0:1, 0:1], (rows_z, rows_z))
        tri = jnp.where(behind * sign > 0, 1.0, 0.0).astype(BF16)
        opt = optical_s[h]
        hi = opt.astype(BF16)
        lo = (opt - hi.astype(F32)).astype(BF16)
        ahead = dot(hi, tri) + dot(lo, tri)
        weight = jnp.exp2(ahead) * (1.0 - jnp.exp2(opt))
        for c in range(3):
            shaded[c, h] = (weight * emitted_s[c, h]).reshape(rim, rim, rows_z)
        part = rays(opt.reshape(rim, rim, rows_z), place.half[h] * rim, lane)
        total[...] = part if h == 0 else total[...] + part


def rays(cells, first_lane, lane):
    folded = cells[:, :, :128]
    for z in range(128, cells.shape[2], 128):
        folded = folded + cells[:, :, z:z + 128]
    summed = jnp.sum(folded, axis=2, keepdims=True)
    acc = jnp.zeros(lane.shape, F32)
    for x in range(cells.shape[0]):
        acc = jnp.where(lane == first_lane + x, summed[x], acc)
    return acc


def blur_x(place, rim, mx, h, near, halo):
    flat = lambda cells: cells.reshape(rim * rim, cells.shape[-1])
    edge = flat(halo)
    edge = jnp.where(place.has_x[h], edge, jnp.zeros_like(edge))
    own = [flat(near[1]), flat(near[0])]
    blocks = own + [edge] if h == 0 else [edge] + own
    return dot(mx[...], jnp.concatenate(blocks, axis=0)).astype(BF16)


def lit(place, rim, occlusion, shaded, h):
    rows_z = occlusion.shape[1]
    lane = iota((rim, 128), 1)
    shade = (1.0 - jnp.tanh(occlusion)).reshape(rim, rim, rows_z)
    return [rays(shade * shaded[c, h], place.half[h] * rim, lane) for c in range(3)]


def own_kernel(rim, early, mx, my, xs0, xs1, halo0, halo1, *refs):
    place = Place()
    size = rim * rim
    if early:
        shaded, out, partial = refs
    else:
        partial, = refs
    for h, halo in enumerate((halo0, halo1)):
        s, e = (blur_x(place, rim, mx, h, [xs0[g], xs1[g]], halo[g]) for g in range(2))
        cells = jnp.concatenate([e, s], axis=0)
        partial[0, h] = dot(my[:, :2 * size], cells)
        other = dot(my[:, size:], cells)
        if not early:
            partial[1, h] = other
            continue
        for c, part in enumerate(lit(place, rim, other, shaded, h)):
            out[c] = part if h == 0 else out[c] + part


def late(rim, g, mx, my, near0, partial, near1, halo0, halo1, shaded):
    place = Place()
    size = rim * rim
    block = my[:, 2 * size:] if g == 0 else my[:, :size]
    acc = None
    for h, halo in enumerate((halo0, halo1)):
        across = blur_x(place, rim, mx, h, [near0[...], near1[...]], halo[...])
        across = jnp.where(place.has_y[g], across, jnp.zeros_like(across))
        part = lit(place, rim, partial[g, h] + dot(block, across), shaded, h)
        acc = part if h == 0 else [a + b for a, b in zip(acc, part)]
    return acc


def late_kernel(rim, g, *refs):
    *refs, out = refs
    for c, part in enumerate(late(rim, g, *refs)):
        out[c] = part


def last_kernel(rim, depth_count, *refs):
    refs, (light_e, total0, total1, kept, given, img) = refs[:8], refs[8:]
    place = Place()
    rows = 2 * rim
    at_s, at_e = group_rows(place, rim, 0), group_rows(place, rim, 1)
    for c, part in enumerate(late(rim, 0, *refs)):
        img[c, at_s, :] = part
        img[c, at_e, :] = light_e[c]
    img[3, at_s, :] = jnp.exp2(total0[...])
    img[3, at_e, :] = jnp.exp2(total1[...])
    for c in range(4):
        img[4 + c, :, 0:rows] = img[c].T[:rows, :]
    block = rows // depth_count
    bit = place.depth & 1
    for n in range(depth_count // 2):
        for out, b in ((kept, bit), (given, 1 - bit)):
            out[n] = img[4:8, pl.ds(pl.multiple_of((2 * n + b) * block, block), block), 0:rows]


def merge_kernel(level, order_map, kept, theirs, *outs):
    me = lax.axis_index("depth")
    bit = me >> level & 1
    low = me & (2 << level) - 1
    merged = []
    for n in range(kept.shape[0]):
        mine = (bit == order_map[(n << level + 1) + low])[None]
        front = jnp.where(mine, kept[n], theirs[n])
        back = jnp.where(mine, theirs[n], kept[n])
        merged.append((front[:3] + front[3:] * back[:3], front[3:] * back[3:]))
    if len(merged) == 1:
        colour, through = merged[0]
        outs[0][...] = jnp.concatenate([colour, 1.0 - through]).reshape(outs[0].shape)
        return
    up = me >> level + 1 & 1
    for n in range(len(merged) // 2):
        even, odd = (jnp.concatenate(merged[2 * n + i]) for i in range(2))
        outs[0][n] = jnp.where(up == 1, odd, even)
        outs[1][n] = jnp.where(up == 1, even, odd)


def call(kernel, name, ins, outs, scratch=(), limit=16 * MIB, **more):
    return pl.pallas_call(
        kernel,
        out_shape=outs,
        in_specs=ins,
        out_specs=jax.tree.map(lambda _: VMEM, outs),
        scratch_shapes=list(scratch),
        compiler_params=pltpu.CompilerParams(vmem_limit_bytes=limit),
        name=name,
        **more,
    )


def per_device(
    density, kernel_taps, tf_centre, tf_width, tf_color, tf_opacity, brick_tf, view_order
):
    rows_x, rows_y, rows_z = density.shape
    rim = (kernel_taps.shape[1] - 1) // 2
    bumps = tf_centre.shape[1]
    size = rim * rim
    axes = ("depth", "sx", "sy")
    counts = tuple(lax.axis_size(axis) for axis in axes)
    depth_count, count_y = counts[0], counts[2]
    struct = jax.ShapeDtypeStruct
    block = rows_x // depth_count
    rounds = sum(1 for shift in range(2) if line_pairs(count_y, shift))

    def swap(piece, x_round, y_round):
        return lax.ppermute(piece, axes, swaps(counts, x_round, y_round))

    in_hbm = lambda array: pltpu.with_memory_space_constraint(array, pltpu.HBM)
    tables = (
        kernel_taps, tf_centre.T, tf_width.T, tf_color.T, tf_opacity.T, brick_tf, view_order
    )
    piece = struct((rim, rim, rows_z), BF16)
    both = struct((2, rim, rim, rows_z), BF16)
    held, xs0, xs1, *refs = call(
        functools.partial(first_kernel, rim, rounds),
        "first",
        [HBM] * (1 + len(tables)),
        [struct((2, 2, rim, rim, rows_z), F32), both, both]
        + [piece] * (2 * rounds)
        + [struct(t.shape, t.dtype) for t in tables],
        [pltpu.SemaphoreType.DMA((4 + len(tables),))],
    )(in_hbm(density), *[in_hbm(t) for t in tables])
    strips, tables = refs[:2 * rounds], refs[2 * rounds:]
    near = [[swap(strips[2 * r], None, r), None] for r in range(rounds)]

    bricks = rows_z // 128
    table, signs, order_map = call(
        functools.partial(prepare_kernel, rim),
        "prepare",
        [VMEM] * (len(tables) - 1),
        [struct((4 * bricks, 6 * bumps, 128), F32), struct((2, 2, 8, 128), jnp.int32)]
        + [struct((depth_count, block, rows_y), jnp.int32)],
    )(*tables[1:])
    halo_x = [swap(cells, h, None) for h, cells in enumerate((xs0, xs1))]
    shaded, total = [None, None], [None, None]
    for g in (1, 0):
        shaded[g], total[g] = call(
            functools.partial(cells_kernel, rim, bumps, g),
            f"cells{g}",
            [VMEM] * 3,
            [struct((3, 2, rim, rim, rows_z), F32), struct((rim, 128), F32)],
            [pltpu.VMEM((2, size, rows_z), F32), pltpu.VMEM((3, 2, size, rows_z), F32)],
            cost_estimate=pl.CostEstimate(
                flops=density.size,
                bytes_accessed=density.size,
                transcendentals=density.size * 3,
            ),
        )(held, table, signs)

    corner = [[None, None] for r in range(rounds)]
    for r in range(rounds):
        near[r][1] = swap(strips[2 * r + 1], None, r)
        strip, table = lax.optimization_barrier((strips[2 * r + 1], table))
        corner[r][1] = swap(strip, 1, r)
        arrived, total[0] = lax.optimization_barrier((near[r][0], total[0]))
        corner[r][0] = swap(arrived, 0, None)
    taps, total[0] = lax.optimization_barrier((tables[0], total[0]))
    mx, my = call(
        functools.partial(matrices_kernel, rim),
        "matrices",
        [VMEM],
        [struct((size, 3 * size), BF16)] * 2,
        [pltpu.VMEM((8, 128), F32)],
        cost_estimate=pl.CostEstimate(
            flops=density.size * 100000, bytes_accessed=density.size * 10000, transcendentals=0
        ),
    )(taps)

    early = rounds < 2
    colours = struct((3, rim, 128), F32)
    unlit = struct((2 - early, 2, size, rows_z), F32)
    results = call(
        functools.partial(own_kernel, rim, early),
        "own",
        [VMEM] * (7 if early else 6),
        [colours, unlit] if early else [unlit],
    )(mx, my, xs0, xs1, *halo_x, *([shaded[1]] if early else []))
    partial = results[-1]
    if early:
        light = results[0]
    else:
        light = call(functools.partial(late_kernel, rim, 1), "late", [VMEM] * 8, colours)(
            mx, my, near[1][0], partial, near[1][1], *corner[1], shaded[1]
        )
    kept, given = call(
        functools.partial(last_kernel, rim, depth_count),
        "last",
        [VMEM] * 11,
        [struct((depth_count // 2, 4, block, rows_y), F32)] * 2,
        [pltpu.VMEM((8, rows_y, 128), F32)],
    )(mx, my, near[0][0], partial, near[0][1], *corner[0], shaded[0], light, *total)
    level = 0
    while True:
        theirs = lax.ppermute(given, "depth", [(i, i ^ 1 << level) for i in range(depth_count)])
        left = kept.shape[0] // 2
        outs = [struct((left, 4, block, rows_y), F32)] * 2
        merged = call(
            functools.partial(merge_kernel, level),
            f"merge{level}",
            [VMEM] * 3,
            outs if left else struct((4, 1, 1, block, rows_y), F32),
            limit=2 * MIB,
        )(order_map, kept, theirs)
        if not left:
            return merged
        kept, given = merged
        level += 1


def solution(mesh):
    return jax.shard_map(
        per_device,
        mesh=mesh,
        in_specs=(
            P("sx", "sy", "depth"),
            P(),
            P(),
            P(),
            P(),
            P(),
            P("sx", "sy", "depth"),
            P("sx", "sy"),
        ),
        out_specs=P(None, "sx", "depth", None, "sy"),
        check_vma=False,
    )
```

```python
import functools
import math
import jax
import jax.numpy as jnp
from jax import lax
from jax.experimental import pallas as pl
from jax.experimental.pallas import tpu as pltpu
from jax.sharding import PartitionSpec as P

LOG2E = math.log2(math.e)
VMEM = pl.BlockSpec(memory_space=pltpu.VMEM)
HBM = pl.BlockSpec(memory_space=pltpu.HBM)
MIB = 1024 * 1024
F32, BF16 = jnp.float32, jnp.bfloat16
dot = functools.partial(jnp.dot, preferred_element_type=F32)


def iota(shape, dim):
    return lax.broadcasted_iota(jnp.int32, shape, dim)


def line_pairs(count, shift):
    return [(i, i + 1) for i in range(shift, count - 1, 2)]


def swaps(counts, x_round, y_round):
    depth_count, count_x, count_y = counts
    index = lambda d, x, y: (d * count_x + x) * count_y + y
    stay = lambda count: [(i, i) for i in range(count)]
    pairs_x = stay(count_x) if x_round is None else line_pairs(count_x, x_round)
    pairs_y = stay(count_y) if y_round is None else line_pairs(count_y, y_round)
    ends = {((a, c), (b, e)) for a, b in pairs_x for c, e in pairs_y}
    if x_round is not None and y_round is not None:
        ends |= {((a, e), (b, c)) for a, b in pairs_x for c, e in pairs_y}
    used = {end for pair in ends for end in pair}
    pairs = []
    for d in range(depth_count):
        pairs += [(index(d, *a), index(d, *b)) for a, b in sorted(ends)]
    for x in range(count_x):
        for y in range(count_y):
            if (x, y) not in used:
                pairs += [
                    (index(d, x, y), index(d + 1, x, y)) for d in range(0, depth_count - 1, 2)
                ]
    return pairs + [(b, a) for a, b in pairs]


class Place:
    def __init__(self):
        self.depth = lax.axis_index("depth")
        self.half, self.has_x = self.sides("sx")
        self.group, self.has_y = self.sides("sy")

    def sides(self, axis):
        at, last = lax.axis_index(axis), lax.axis_size(axis) - 1
        parity = lax.rem(at, 2)
        upper, lower = at < last, at > 0
        order = (1 - parity, parity)
        either = lambda side: jnp.where(side == 1, upper.astype(jnp.int32), lower.astype(jnp.int32))
        return order, [either(side) == 1 for side in order]


def group_rows(place, rim, g):
    return pl.ds(pl.multiple_of(place.group[g] * rim, rim), rim)


def half_rows(place, rim, h):
    return pl.ds(place.half[h] * rim, rim)


def first_kernel(rim, rounds, density, *refs):
    place = Place()
    tables, refs = refs[:7], refs[7:]
    held, xs, refs = refs[0], refs[1:3], refs[3:]
    strips, refs = refs[:2 * rounds], refs[2 * rounds:]
    mx, my, table, signs, order_map, *local_tables, padded, sems = refs
    copies = []
    for i, (src, dst) in enumerate(zip(tables, local_tables)):
        copies.append(pltpu.make_async_copy(src, dst, sems.at[4 + i]))
    parts = []
    for g in range(2):
        for h in range(2):
            rows = density.at[half_rows(place, rim, h), group_rows(place, rim, g), :]
            parts.append(pltpu.make_async_copy(rows, held.at[g, h], sems.at[2 * g + h]))
    for copy in copies + parts:
        copy.start()
    for copy in copies:
        copy.wait()
    taps, *local_tables = local_tables
    padded[...] = jnp.zeros(padded.shape, F32)
    padded[0:2, 0:taps.shape[1]] = taps[...].astype(F32)
    mx[...], my[...] = blur_matrices(rim, place, padded[...])
    look_up(rim, place, *local_tables, table, signs, order_map)
    for g in range(2):
        for h in range(2):
            parts[2 * g + h].wait()
            coarse = held[g, h].astype(BF16)
            xs[h][g] = coarse
            if g < rounds:
                strips[2 * g + h][...] = coarse


def toeplitz(taps, rim):
    return pltpu.roll(jnp.broadcast_to(taps, (rim, 128)), 0, 1, stride=1, stride_axis=0)


def blur_matrices(rim, place, taps):
    size = rim * rim
    wide = 3 * size
    shift = rim.bit_length() - 1
    pick = lambda mask: jnp.where(mask, 1.0, 0.0).astype(BF16)
    row_hi = pick(iota((size, rim), 0) >> shift == iota((size, rim), 1))
    row_lo = pick(iota((size, rim), 0) & (rim - 1) == iota((size, rim), 1))
    col = iota((128, wide), 1)
    src = iota((128, wide), 0)
    k, j, b = col >> 2 * shift, col >> shift & (rim - 1), col & (rim - 1)
    k_x = jnp.where(place.half[0] == 1, k, 2 - k)
    k_y = jnp.where(place.group[0] == 1, k, 2 - k)
    tx = toeplitz(taps[0:1], rim).astype(BF16)
    ty = toeplitz(taps[1:2] * 0.5, rim).astype(BF16)
    full_x = dot(row_hi, dot(tx, pick(k_x * rim + j == src)).astype(BF16))
    full_y = dot(row_lo, dot(ty, pick(k_y * rim + b == src)).astype(BF16))
    r, c = iota((size, size), 0), iota((size, size), 1)
    same_x = r & (rim - 1) == c & (rim - 1)
    same_y = r >> shift == c >> shift
    parts = []
    for full, same in ((full_x, same_x), (full_y, same_y)):
        blocks = [
            jnp.where(same, full[:, n * size:(n + 1) * size], 0.0).astype(BF16) for n in range(3)
        ]
        parts.append(jnp.concatenate(blocks, axis=1))
    return parts


def look_up(
    rim, place, centre, width, colour, opacity, brick_tf, view_order, table, signs, order_map
):
    wide = width[...]
    rows = [centre[...], (-LOG2E) / (wide * wide), opacity[...] * (-LOG2E)]
    rows += [colour[c] * 0.5 for c in range(3)]
    rows = jnp.concatenate(rows, axis=0)
    which = iota(rows.shape, 1)
    n = 0
    for g in range(2):
        for h in range(2):
            bricks = brick_tf[place.half[h]]
            bricks = jnp.where(place.group[g] == 0, bricks[0:1], bricks[1:2])
            for bz in range(bricks.shape[1]):
                mine = jnp.where(which == bricks[:, bz:bz + 1], rows, 0.0)
                mine = jnp.sum(mine, axis=1, keepdims=True)
                table[n] = jnp.broadcast_to(mine, table.shape[1:])
                n += 1
            orders = view_order[...]
            orders = jnp.where(place.half[h] == 0, orders[0:1], orders[1:2])
            order = jnp.where(place.group[g] == 0, orders[:, 0:1], orders[:, 1:2])
            signs[g, h] = jnp.broadcast_to(1 - 2 * order, signs.shape[2:])
    block, shape = order_map.shape[1], order_map.shape[1:]
    for n in range(order_map.shape[0]):
        brick = n * block // rim
        orders = view_order[brick:brick + 1]
        order_map[n] = jnp.where(
            iota(shape, 1) < rim,
            jnp.broadcast_to(orders[:, 0:1], shape),
            jnp.broadcast_to(orders[:, 1:2], shape),
        )


def cells_kernel(rim, bumps, g, held, table, signs, shaded, total, optical_s, emitted_s):
    place = Place()
    rows_z = held.shape[4]
    depth = 128
    bricks = rows_z // depth
    lane = iota((rim, 128), 1)
    for h in range(2):
        cells = held.at[g, h]
        for bz in range(bricks):
            zs = slice(bz * depth, (bz + 1) * depth)
            at = (2 * g + h) * bricks + bz
            row = lambda i: jnp.broadcast_to(table[at, i:i + 1, :], (8, depth))[None]
            cen = [row(j) for j in range(bumps)]
            neg = [row(bumps + j) for j in range(bumps)]
            opa = [row(2 * bumps + j) for j in range(bumps)]
            col = [[row((3 + c) * bumps + j) for c in range(3)] for j in range(bumps)]
            for x in range(rim):
                d = cells[x, :, zs].reshape(rim // 8, 8, depth)
                opt, em = None, [None] * 3
                for j in range(bumps):
                    w = d - cen[j]
                    b = jnp.exp2((w * w) * neg[j])
                    opt = opa[j] * b if opt is None else opt + opa[j] * b
                    for c in range(3):
                        em[c] = col[j][c] * b if em[c] is None else em[c] + col[j][c] * b
                rows = slice(x * rim, (x + 1) * rim)
                optical_s[h, rows, zs] = opt.reshape(rim, depth)
                for c in range(3):
                    emitted_s[c, h, rows, zs] = em[c].reshape(rim, depth)
        behind = iota((rows_z, rows_z), 1) - iota((rows_z, rows_z), 0)
        sign = jnp.broadcast_to(signs[g, h][0:1, 0:1], (rows_z, rows_z))
        tri = jnp.where(behind * sign > 0, 1.0, 0.0).astype(BF16)
        opt = optical_s[h]
        hi = opt.astype(BF16)
        lo = (opt - hi.astype(F32)).astype(BF16)
        ahead = dot(hi, tri) + dot(lo, tri)
        weight = jnp.exp2(ahead) * (1.0 - jnp.exp2(opt))
        for c in range(3):
            shaded[c, h] = (weight * emitted_s[c, h]).reshape(rim, rim, rows_z)
        part = rays(opt.reshape(rim, rim, rows_z), place.half[h] * rim, lane)
        total[...] = part if h == 0 else total[...] + part


def rays(cells, first_lane, lane):
    folded = cells[:, :, :128]
    for z in range(128, cells.shape[2], 128):
        folded = folded + cells[:, :, z:z + 128]
    summed = jnp.sum(folded, axis=2, keepdims=True)
    acc = jnp.zeros(lane.shape, F32)
    for x in range(cells.shape[0]):
        acc = jnp.where(lane == first_lane + x, summed[x], acc)
    return acc


def blur_x(place, rim, mx, h, near, halo):
    flat = lambda cells: cells.reshape(rim * rim, cells.shape[-1])
    edge = flat(halo)
    edge = jnp.where(place.has_x[h], edge, jnp.zeros_like(edge))
    own = [flat(near[1]), flat(near[0])]
    blocks = own + [edge] if h == 0 else [edge] + own
    return dot(mx[...], jnp.concatenate(blocks, axis=0)).astype(BF16)


def lit(place, rim, occlusion, shaded, h):
    rows_z = occlusion.shape[1]
    lane = iota((rim, 128), 1)
    shade = (1.0 - jnp.tanh(occlusion)).reshape(rim, rim, rows_z)
    return [rays(shade * shaded[c, h], place.half[h] * rim, lane) for c in range(3)]


def own_kernel(rim, early, mx, my, xs0, xs1, halo0, halo1, *refs):
    place = Place()
    size = rim * rim
    if early:
        shaded, out, partial = refs
    else:
        partial, = refs
    halos = (halo0, halo1)
    across = [
        [blur_x(place, rim, mx, h, [xs0[g], xs1[g]], halos[h][g]) for h in range(2)]
        for g in range(2)
    ]
    for h in range(2):
        cells = jnp.concatenate([across[1][h], across[0][h]], axis=0)
        partial[0, h] = dot(my[:, :2 * size], cells)
        other = dot(my[:, size:], cells)
        if not early:
            partial[1, h] = other
            continue
        for c, part in enumerate(lit(place, rim, other, shaded, h)):
            out[c] = part if h == 0 else out[c] + part


def late(rim, g, mx, my, near0, partial, near1, halo0, halo1, shaded):
    place = Place()
    size = rim * rim
    block = my[:, 2 * size:] if g == 0 else my[:, :size]
    across = [
        blur_x(place, rim, mx, h, [near0[...], near1[...]], halo[...])
        for h, halo in enumerate((halo0, halo1))
    ]
    across = [jnp.where(place.has_y[g], cells, jnp.zeros_like(cells)) for cells in across]
    occlusion = [partial[g, h] + dot(block, across[h]) for h in range(2)]
    lights = [lit(place, rim, occlusion[h], shaded, h) for h in range(2)]
    return [a + b for a, b in zip(*lights)]


def late_kernel(rim, g, *refs):
    *refs, out = refs
    for c, part in enumerate(late(rim, g, *refs)):
        out[c] = part


def last_kernel(rim, depth_count, *refs):
    refs, (light_e, total0, total1, kept, given, img) = refs[:8], refs[8:]
    place = Place()
    rows = 2 * rim
    at_s, at_e = group_rows(place, rim, 0), group_rows(place, rim, 1)
    for c, part in enumerate(late(rim, 0, *refs)):
        img[c, at_s, :] = part
        img[c, at_e, :] = light_e[c]
    img[3, at_s, :] = jnp.exp2(total0[...])
    img[3, at_e, :] = jnp.exp2(total1[...])
    for c in range(4):
        img[4 + c, :, 0:rows] = img[c].T[:rows, :]
    block = rows // depth_count
    bit = place.depth & 1
    for n in range(depth_count // 2):
        for out, b in ((kept, bit), (given, 1 - bit)):
            out[n] = img[4:8, pl.ds(pl.multiple_of((2 * n + b) * block, block), block), 0:rows]


def merge_kernel(level, order_map, kept, theirs, *outs):
    me = lax.axis_index("depth")
    bit = me >> level & 1
    low = me & (2 << level) - 1
    merged = []
    for n in range(kept.shape[0]):
        mine = (bit == order_map[(n << level + 1) + low])[None]
        front = jnp.where(mine, kept[n], theirs[n])
        back = jnp.where(mine, theirs[n], kept[n])
        merged.append((front[:3] + front[3:] * back[:3], front[3:] * back[3:]))
    if len(merged) == 1:
        colour, through = merged[0]
        outs[0][...] = jnp.concatenate([colour, 1.0 - through]).reshape(outs[0].shape)
        return
    up = me >> level + 1 & 1
    for n in range(len(merged) // 2):
        even, odd = (jnp.concatenate(merged[2 * n + i]) for i in range(2))
        outs[0][n] = jnp.where(up == 1, odd, even)
        outs[1][n] = jnp.where(up == 1, even, odd)


def call(kernel, name, ins, outs, scratch=(), limit=16 * MIB, **more):
    return pl.pallas_call(
        kernel,
        out_shape=outs,
        in_specs=ins,
        out_specs=jax.tree.map(lambda _: VMEM, outs),
        scratch_shapes=list(scratch),
        compiler_params=pltpu.CompilerParams(vmem_limit_bytes=limit),
        name=name,
        **more,
    )


def per_device(
    density, kernel_taps, tf_centre, tf_width, tf_color, tf_opacity, brick_tf, view_order
):
    rows_x, rows_y, rows_z = density.shape
    rim = (kernel_taps.shape[1] - 1) // 2
    bumps = tf_centre.shape[1]
    size = rim * rim
    axes = ("depth", "sx", "sy")
    counts = tuple(lax.axis_size(axis) for axis in axes)
    depth_count, count_y = counts[0], counts[2]
    struct = jax.ShapeDtypeStruct
    block = rows_x // depth_count
    rounds = sum(1 for shift in range(2) if line_pairs(count_y, shift))

    def swap(piece, x_round, y_round):
        return lax.ppermute(piece, axes, swaps(counts, x_round, y_round))

    in_hbm = lambda array: pltpu.with_memory_space_constraint(array, pltpu.HBM)
    tables = (
        kernel_taps, tf_centre.T, tf_width.T, tf_color.T, tf_opacity.T, brick_tf, view_order
    )
    piece = struct((rim, rim, rows_z), BF16)
    both = struct((2, rim, rim, rows_z), BF16)
    bricks = rows_z // 128
    held, xs0, xs1, *refs = call(
        functools.partial(first_kernel, rim, rounds),
        "first",
        [HBM] * (1 + len(tables)),
        [struct((2, 2, rim, rim, rows_z), F32), both, both]
        + [piece] * (2 * rounds)
        + [struct((size, 3 * size), BF16)] * 2
        + [struct((4 * bricks, 6 * bumps, 128), F32), struct((2, 2, 8, 128), jnp.int32)]
        + [struct((depth_count, block, rows_y), jnp.int32)],
        [pltpu.VMEM(t.shape, t.dtype) for t in tables]
        + [pltpu.VMEM((8, 128), F32), pltpu.SemaphoreType.DMA((4 + len(tables),))],
    )(in_hbm(density), *[in_hbm(t) for t in tables])
    strips, (mx, my, table, signs, order_map) = refs[:2 * rounds], refs[2 * rounds:]
    near = [[swap(strips[2 * r], None, r), None] for r in range(rounds)]

    halo_x = [swap(cells, h, None) for h, cells in enumerate((xs0, xs1))]
    shaded, total = [None, None], [None, None]
    for g in (1, 0):
        shaded[g], total[g] = call(
            functools.partial(cells_kernel, rim, bumps, g),
            f"cells{g}",
            [VMEM] * 3,
            [struct((3, 2, rim, rim, rows_z), F32), struct((rim, 128), F32)],
            [pltpu.VMEM((2, size, rows_z), F32), pltpu.VMEM((3, 2, size, rows_z), F32)],
            cost_estimate=pl.CostEstimate(
                flops=density.size * (100000 if g == 0 else 1),
                bytes_accessed=density.size,
                transcendentals=density.size * 3,
            ),
        )(held, table, signs)

    corner = [[None, None] for r in range(rounds)]
    for r in range(rounds):
        near[r][1] = swap(strips[2 * r + 1], None, r)
        strip, arrived, total[1] = lax.optimization_barrier(
            (strips[2 * r + 1], near[r][0], total[1])
        )
        corner[r] = [swap(arrived, 0, None), swap(strip, 1, r)]

    early = rounds < 2
    colours = struct((3, rim, 128), F32)
    unlit = struct((2 - early, 2, size, rows_z), F32)
    results = call(
        functools.partial(own_kernel, rim, early),
        "own",
        [VMEM] * (7 if early else 6),
        [colours, unlit] if early else [unlit],
    )(mx, my, xs0, xs1, *halo_x, *([shaded[1]] if early else []))
    partial = results[-1]
    if early:
        light = results[0]
    else:
        light = call(functools.partial(late_kernel, rim, 1), "late", [VMEM] * 8, colours)(
            mx, my, near[1][0], partial, near[1][1], *corner[1], shaded[1]
        )
    kept, given = call(
        functools.partial(last_kernel, rim, depth_count),
        "last",
        [VMEM] * 11,
        [struct((depth_count // 2, 4, block, rows_y), F32)] * 2,
        [pltpu.VMEM((8, rows_y, 128), F32)],
    )(mx, my, near[0][0], partial, near[0][1], *corner[0], shaded[0], light, *total)
    level = 0
    while True:
        theirs = lax.ppermute(given, "depth", [(i, i ^ 1 << level) for i in range(depth_count)])
        left = kept.shape[0] // 2
        outs = [struct((left, 4, block, rows_y), F32)] * 2
        merged = call(
            functools.partial(merge_kernel, level),
            f"merge{level}",
            [VMEM] * 3,
            outs if left else struct((4, 1, 1, block, rows_y), F32),
            limit=2 * MIB,
        )(order_map, kept, theirs)
        if not left:
            return merged
        kept, given = merged
        level += 1


def solution(mesh):
    return jax.shard_map(
        per_device,
        mesh=mesh,
        in_specs=(
            P("sx", "sy", "depth"),
            P(),
            P(),
            P(),
            P(),
            P(),
            P("sx", "sy", "depth"),
            P("sx", "sy"),
        ),
        out_specs=P(None, "sx", "depth", None, "sy"),
        check_vma=False,
    )
```

```python
import functools
import math
import jax
import jax.numpy as jnp
from jax import lax
from jax.experimental import pallas as pl
from jax.experimental.pallas import tpu as pltpu
from jax.sharding import PartitionSpec as P

LOG2E = math.log2(math.e)
VMEM = pl.BlockSpec(memory_space=pltpu.VMEM)
HBM = pl.BlockSpec(memory_space=pltpu.HBM)
MIB = 1024 * 1024
F32, BF16 = jnp.float32, jnp.bfloat16
dot = functools.partial(jnp.dot, preferred_element_type=F32)


def iota(shape, dim):
    return lax.broadcasted_iota(jnp.int32, shape, dim)


def line_pairs(count, shift):
    return [(i, i + 1) for i in range(shift, count - 1, 2)]


def swaps(counts, x_round, y_round):
    depth_count, count_x, count_y = counts
    index = lambda d, x, y: (d * count_x + x) * count_y + y
    stay = lambda count: [(i, i) for i in range(count)]
    pairs_x = stay(count_x) if x_round is None else line_pairs(count_x, x_round)
    pairs_y = stay(count_y) if y_round is None else line_pairs(count_y, y_round)
    ends = {((a, c), (b, e)) for a, b in pairs_x for c, e in pairs_y}
    if x_round is not None and y_round is not None:
        ends |= {((a, e), (b, c)) for a, b in pairs_x for c, e in pairs_y}
    used = {end for pair in ends for end in pair}
    pairs = []
    for d in range(depth_count):
        pairs += [(index(d, *a), index(d, *b)) for a, b in sorted(ends)]
    for x in range(count_x):
        for y in range(count_y):
            if (x, y) not in used:
                pairs += [
                    (index(d, x, y), index(d + 1, x, y)) for d in range(0, depth_count - 1, 2)
                ]
    return pairs + [(b, a) for a, b in pairs]


class Place:
    def __init__(self):
        self.depth = lax.axis_index("depth")
        self.half, self.has_x = self.sides("sx")
        self.group, self.has_y = self.sides("sy")

    def sides(self, axis):
        at, last = lax.axis_index(axis), lax.axis_size(axis) - 1
        parity = lax.rem(at, 2)
        upper, lower = at < last, at > 0
        order = (1 - parity, parity)
        either = lambda side: jnp.where(side == 1, upper.astype(jnp.int32), lower.astype(jnp.int32))
        return order, [either(side) == 1 for side in order]


def group_rows(place, rim, g):
    return pl.ds(pl.multiple_of(place.group[g] * rim, rim), rim)


def half_rows(place, rim, h):
    return pl.ds(place.half[h] * rim, rim)


def first_kernel(rim, rounds, density, *refs):
    place = Place()
    n_tables = (len(refs) - 4 - 2 * rounds) // 2
    tables, refs = refs[:n_tables], refs[n_tables:]
    held, xs, refs = refs[0], refs[1:3], refs[3:]
    strips, refs = refs[:2 * rounds], refs[2 * rounds:]
    tables_out, sems = refs[:n_tables], refs[n_tables]
    copies = []
    for g in range(2):
        for h in range(2):
            rows = density.at[half_rows(place, rim, h), group_rows(place, rim, g), :]
            copies.append(pltpu.make_async_copy(rows, held.at[g, h], sems.at[2 * g + h]))
    for i, (src, dst) in enumerate(zip(tables, tables_out)):
        copies.append(pltpu.make_async_copy(src, dst, sems.at[4 + i]))
    for copy in copies:
        copy.start()
    for g in range(2):
        for h in range(2):
            copies[2 * g + h].wait()
            coarse = held[g, h].astype(BF16)
            xs[h][g] = coarse
            if g < rounds:
                strips[2 * g + h][...] = coarse
    for copy in copies[4:]:
        copy.wait()


def toeplitz(taps, rim):
    return pltpu.roll(jnp.broadcast_to(taps, (rim, 128)), 0, 1, stride=1, stride_axis=0)


def blur_matrices(rim, place, taps):
    size = rim * rim
    wide = 3 * size
    shift = rim.bit_length() - 1
    pick = lambda mask: jnp.where(mask, 1.0, 0.0).astype(BF16)
    row_hi = pick(iota((size, rim), 0) >> shift == iota((size, rim), 1))
    row_lo = pick(iota((size, rim), 0) & (rim - 1) == iota((size, rim), 1))
    col = iota((128, wide), 1)
    src = iota((128, wide), 0)
    k, j, b = col >> 2 * shift, col >> shift & (rim - 1), col & (rim - 1)
    k_x = jnp.where(place.half[0] == 1, k, 2 - k)
    k_y = jnp.where(place.group[0] == 1, k, 2 - k)
    tx = toeplitz(taps[0:1], rim).astype(BF16)
    ty = toeplitz(taps[1:2] * 0.5, rim).astype(BF16)
    full_x = dot(row_hi, dot(tx, pick(k_x * rim + j == src)).astype(BF16))
    full_y = dot(row_lo, dot(ty, pick(k_y * rim + b == src)).astype(BF16))
    r, c = iota((size, size), 0), iota((size, size), 1)
    same_x = r & (rim - 1) == c & (rim - 1)
    same_y = r >> shift == c >> shift
    parts = []
    for full, same in ((full_x, same_x), (full_y, same_y)):
        blocks = [
            jnp.where(same, full[:, n * size:(n + 1) * size], 0.0).astype(BF16) for n in range(3)
        ]
        parts.append(jnp.concatenate(blocks, axis=1))
    return parts


def matrices_kernel(rim, taps, mx, my, padded):
    padded[...] = jnp.zeros(padded.shape, F32)
    padded[0:2, 0:taps.shape[1]] = taps[...].astype(F32)
    mx[...], my[...] = blur_matrices(rim, Place(), padded[...])


def prepare_kernel(
    rim, centre, width, colour, opacity, brick_tf, view_order, table, signs, order_map
):
    place = Place()
    wide = width[...]
    rows = [centre[...], (-LOG2E) / (wide * wide), opacity[...] * (-LOG2E)]
    rows += [colour[c] * 0.5 for c in range(3)]
    rows = jnp.concatenate(rows, axis=0)
    which = iota(rows.shape, 1)
    n = 0
    for g in range(2):
        for h in range(2):
            bricks = brick_tf[place.half[h]]
            bricks = jnp.where(place.group[g] == 0, bricks[0:1], bricks[1:2])
            for bz in range(bricks.shape[1]):
                mine = jnp.where(which == bricks[:, bz:bz + 1], rows, 0.0)
                mine = jnp.sum(mine, axis=1, keepdims=True)
                table[n] = jnp.broadcast_to(mine, table.shape[1:])
                n += 1
            orders = view_order[...]
            orders = jnp.where(place.half[h] == 0, orders[0:1], orders[1:2])
            order = jnp.where(place.group[g] == 0, orders[:, 0:1], orders[:, 1:2])
            signs[g, h] = jnp.broadcast_to(1 - 2 * order, signs.shape[2:])
    block, shape = order_map.shape[1], order_map.shape[1:]
    for n in range(order_map.shape[0]):
        brick = n * block // rim
        orders = view_order[brick:brick + 1]
        order_map[n] = jnp.where(
            iota(shape, 1) < rim,
            jnp.broadcast_to(orders[:, 0:1], shape),
            jnp.broadcast_to(orders[:, 1:2], shape),
        )


def cells_kernel(rim, bumps, g, held, table, signs, shaded, total, optical_s, emitted_s):
    place = Place()
    rows_z = held.shape[4]
    depth = 128
    bricks = rows_z // depth
    lane = iota((rim, 128), 1)
    for h in range(2):
        cells = held.at[g, h]
        for bz in range(bricks):
            zs = slice(bz * depth, (bz + 1) * depth)
            at = (2 * g + h) * bricks + bz
            row = lambda i: jnp.broadcast_to(table[at, i:i + 1, :], (8, depth))[None]
            cen = [row(j) for j in range(bumps)]
            neg = [row(bumps + j) for j in range(bumps)]
            opa = [row(2 * bumps + j) for j in range(bumps)]
            col = [[row((3 + c) * bumps + j) for c in range(3)] for j in range(bumps)]
            for x in range(rim):
                d = cells[x, :, zs].reshape(rim // 8, 8, depth)
                opt, em = None, [None] * 3
                for j in range(bumps):
                    w = d - cen[j]
                    b = jnp.exp2((w * w) * neg[j])
                    opt = opa[j] * b if opt is None else opt + opa[j] * b
                    for c in range(3):
                        em[c] = col[j][c] * b if em[c] is None else em[c] + col[j][c] * b
                rows = slice(x * rim, (x + 1) * rim)
                optical_s[h, rows, zs] = opt.reshape(rim, depth)
                for c in range(3):
                    emitted_s[c, h, rows, zs] = em[c].reshape(rim, depth)
        behind = iota((rows_z, rows_z), 1) - iota((rows_z, rows_z), 0)
        sign = jnp.broadcast_to(signs[g, h][0:1, 0:1], (rows_z, rows_z))
        tri = jnp.where(behind * sign > 0, 1.0, 0.0).astype(BF16)
        opt = optical_s[h]
        hi = opt.astype(BF16)
        lo = (opt - hi.astype(F32)).astype(BF16)
        ahead = dot(hi, tri) + dot(lo, tri)
        weight = jnp.exp2(ahead) * (1.0 - jnp.exp2(opt))
        for c in range(3):
            shaded[c, h] = (weight * emitted_s[c, h]).reshape(rim, rim, rows_z)
        part = rays(opt.reshape(rim, rim, rows_z), place.half[h] * rim, lane)
        total[...] = part if h == 0 else total[...] + part


def rays(cells, first_lane, lane):
    folded = cells[:, :, :128]
    for z in range(128, cells.shape[2], 128):
        folded = folded + cells[:, :, z:z + 128]
    summed = jnp.sum(folded, axis=2, keepdims=True)
    acc = jnp.zeros(lane.shape, F32)
    for x in range(cells.shape[0]):
        acc = jnp.where(lane == first_lane + x, summed[x], acc)
    return acc


def blur_x(place, rim, mx, h, near, halo):
    flat = lambda cells: cells.reshape(rim * rim, cells.shape[-1])
    edge = flat(halo)
    edge = jnp.where(place.has_x[h], edge, jnp.zeros_like(edge))
    own = [flat(near[1]), flat(near[0])]
    blocks = own + [edge] if h == 0 else [edge] + own
    return dot(mx[...], jnp.concatenate(blocks, axis=0)).astype(BF16)


def lit(place, rim, occlusion, shaded, h):
    rows_z = occlusion.shape[1]
    lane = iota((rim, 128), 1)
    shade = (1.0 - jnp.tanh(occlusion)).reshape(rim, rim, rows_z)
    return [rays(shade * shaded[c, h], place.half[h] * rim, lane) for c in range(3)]


def own_kernel(rim, early, mx, my, xs0, xs1, halo0, halo1, *refs):
    place = Place()
    size = rim * rim
    if early:
        shaded, out, partial = refs
    else:
        partial, = refs
    halos = (halo0, halo1)
    across = [
        [blur_x(place, rim, mx, h, [xs0[g], xs1[g]], halos[h][g]) for h in range(2)]
        for g in range(2)
    ]
    for h in range(2):
        cells = jnp.concatenate([across[1][h], across[0][h]], axis=0)
        partial[0, h] = dot(my[:, :2 * size], cells)
        other = dot(my[:, size:], cells)
        if not early:
            partial[1, h] = other
            continue
        for c, part in enumerate(lit(place, rim, other, shaded, h)):
            out[c] = part if h == 0 else out[c] + part


def late(rim, g, mx, my, near0, partial, near1, halo0, halo1, shaded):
    place = Place()
    size = rim * rim
    block = my[:, 2 * size:] if g == 0 else my[:, :size]
    across = [
        blur_x(place, rim, mx, h, [near0[...], near1[...]], halo[...])
        for h, halo in enumerate((halo0, halo1))
    ]
    across = [jnp.where(place.has_y[g], cells, jnp.zeros_like(cells)) for cells in across]
    occlusion = [partial[g, h] + dot(block, across[h]) for h in range(2)]
    lights = [lit(place, rim, occlusion[h], shaded, h) for h in range(2)]
    return [a + b for a, b in zip(*lights)]


def late_kernel(rim, g, *refs):
    *refs, out = refs
    for c, part in enumerate(late(rim, g, *refs)):
        out[c] = part


def last_kernel(rim, depth_count, *refs):
    refs, (light_e, total0, total1, kept, given, img) = refs[:8], refs[8:]
    place = Place()
    rows = 2 * rim
    at_s, at_e = group_rows(place, rim, 0), group_rows(place, rim, 1)
    for c, part in enumerate(late(rim, 0, *refs)):
        img[c, at_s, :] = part
        img[c, at_e, :] = light_e[c]
    img[3, at_s, :] = jnp.exp2(total0[...])
    img[3, at_e, :] = jnp.exp2(total1[...])
    for c in range(4):
        img[4 + c, :, 0:rows] = img[c].T[:rows, :]
    block = rows // depth_count
    bit = place.depth & 1
    for n in range(depth_count // 2):
        for out, b in ((kept, bit), (given, 1 - bit)):
            out[n] = img[4:8, pl.ds(pl.multiple_of((2 * n + b) * block, block), block), 0:rows]


def merge_kernel(level, order_map, kept, theirs, *outs):
    me = lax.axis_index("depth")
    bit = me >> level & 1
    low = me & (2 << level) - 1
    merged = []
    for n in range(kept.shape[0]):
        mine = (bit == order_map[(n << level + 1) + low])[None]
        front = jnp.where(mine, kept[n], theirs[n])
        back = jnp.where(mine, theirs[n], kept[n])
        merged.append((front[:3] + front[3:] * back[:3], front[3:] * back[3:]))
    if len(merged) == 1:
        colour, through = merged[0]
        outs[0][...] = jnp.concatenate([colour, 1.0 - through]).reshape(outs[0].shape)
        return
    up = me >> level + 1 & 1
    for n in range(len(merged) // 2):
        even, odd = (jnp.concatenate(merged[2 * n + i]) for i in range(2))
        outs[0][n] = jnp.where(up == 1, odd, even)
        outs[1][n] = jnp.where(up == 1, even, odd)


def call(kernel, name, ins, outs, scratch=(), limit=16 * MIB, **more):
    return pl.pallas_call(
        kernel,
        out_shape=outs,
        in_specs=ins,
        out_specs=jax.tree.map(lambda _: VMEM, outs),
        scratch_shapes=list(scratch),
        compiler_params=pltpu.CompilerParams(vmem_limit_bytes=limit),
        name=name,
        **more,
    )


def per_device(
    density, kernel_taps, tf_centre, tf_width, tf_color, tf_opacity, brick_tf, view_order
):
    rows_x, rows_y, rows_z = density.shape
    rim = (kernel_taps.shape[1] - 1) // 2
    bumps = tf_centre.shape[1]
    size = rim * rim
    axes = ("depth", "sx", "sy")
    counts = tuple(lax.axis_size(axis) for axis in axes)
    depth_count, count_y = counts[0], counts[2]
    struct = jax.ShapeDtypeStruct
    block = rows_x // depth_count
    rounds = sum(1 for shift in range(2) if line_pairs(count_y, shift))

    def swap(piece, x_round, y_round):
        return lax.ppermute(piece, axes, swaps(counts, x_round, y_round))

    in_hbm = lambda array: pltpu.with_memory_space_constraint(array, pltpu.HBM)
    tables = (
        kernel_taps, tf_centre.T, tf_width.T, tf_color.T, tf_opacity.T, brick_tf, view_order
    )
    piece = struct((rim, rim, rows_z), BF16)
    both = struct((2, rim, rim, rows_z), BF16)
    held, xs0, xs1, *refs = call(
        functools.partial(first_kernel, rim, rounds),
        "first",
        [HBM] * (1 + len(tables)),
        [struct((2, 2, rim, rim, rows_z), F32), both, both]
        + [piece] * (2 * rounds)
        + [struct(t.shape, t.dtype) for t in tables],
        [pltpu.SemaphoreType.DMA((4 + len(tables),))],
    )(in_hbm(density), *[in_hbm(t) for t in tables])
    strips, tables = refs[:2 * rounds], refs[2 * rounds:]
    near = [[swap(strips[2 * r], None, r), None] for r in range(rounds)]

    bricks = rows_z // 128
    table, signs, order_map = call(
        functools.partial(prepare_kernel, rim),
        "prepare",
        [VMEM] * (len(tables) - 1),
        [struct((4 * bricks, 6 * bumps, 128), F32), struct((2, 2, 8, 128), jnp.int32)]
        + [struct((depth_count, block, rows_y), jnp.int32)],
    )(*tables[1:])
    halo_x = [swap(cells, h, None) for h, cells in enumerate((xs0, xs1))]
    mx, my = call(
        functools.partial(matrices_kernel, rim),
        "matrices",
        [VMEM],
        [struct((size, 3 * size), BF16)] * 2,
        [pltpu.VMEM((8, 128), F32)],
    )(tables[0])
    shaded, total = [None, None], [None, None]
    for g in (1, 0):
        shaded[g], total[g] = call(
            functools.partial(cells_kernel, rim, bumps, g),
            f"cells{g}",
            [VMEM] * 3,
            [struct((3, 2, rim, rim, rows_z), F32), struct((rim, 128), F32)],
            [pltpu.VMEM((2, size, rows_z), F32), pltpu.VMEM((3, 2, size, rows_z), F32)],
            cost_estimate=pl.CostEstimate(
                flops=density.size * (100000 if g == 0 else 1),
                bytes_accessed=density.size * (10000 if g == 0 else 1),
                transcendentals=density.size * 3,
            ),
        )(held, table, signs)

    corner = [[None, None] for r in range(rounds)]
    for r in range(rounds):
        near[r][1] = swap(strips[2 * r + 1], None, r)
        strip, arrived, total[1] = lax.optimization_barrier(
            (strips[2 * r + 1], near[r][0], total[1])
        )
        corner[r] = [swap(arrived, 0, None), swap(strip, 1, r)]

    early = rounds < 2
    colours = struct((3, rim, 128), F32)
    unlit = struct((2 - early, 2, size, rows_z), F32)
    results = call(
        functools.partial(own_kernel, rim, early),
        "own",
        [VMEM] * (7 if early else 6),
        [colours, unlit] if early else [unlit],
    )(mx, my, xs0, xs1, *halo_x, *([shaded[1]] if early else []))
    partial = results[-1]
    if early:
        light = results[0]
    else:
        light = call(functools.partial(late_kernel, rim, 1), "late", [VMEM] * 8, colours)(
            mx, my, near[1][0], partial, near[1][1], *corner[1], shaded[1]
        )
    kept, given = call(
        functools.partial(last_kernel, rim, depth_count),
        "last",
        [VMEM] * 11,
        [struct((depth_count // 2, 4, block, rows_y), F32)] * 2,
        [pltpu.VMEM((8, rows_y, 128), F32)],
    )(mx, my, near[0][0], partial, near[0][1], *corner[0], shaded[0], light, *total)
    level = 0
    while True:
        theirs = lax.ppermute(given, "depth", [(i, i ^ 1 << level) for i in range(depth_count)])
        left = kept.shape[0] // 2
        outs = [struct((left, 4, block, rows_y), F32)] * 2
        merged = call(
            functools.partial(merge_kernel, level),
            f"merge{level}",
            [VMEM] * 3,
            outs if left else struct((4, 1, 1, block, rows_y), F32),
            limit=2 * MIB,
        )(order_map, kept, theirs)
        if not left:
            return merged
        kept, given = merged
        level += 1


def solution(mesh):
    return jax.shard_map(
        per_device,
        mesh=mesh,
        in_specs=(
            P("sx", "sy", "depth"),
            P(),
            P(),
            P(),
            P(),
            P(),
            P("sx", "sy", "depth"),
            P("sx", "sy"),
        ),
        out_specs=P(None, "sx", "depth", None, "sy"),
        check_vma=False,
    )
```

```python
import functools
import math
import jax
import jax.numpy as jnp
from jax import lax
from jax.experimental import pallas as pl
from jax.experimental.pallas import tpu as pltpu
from jax.sharding import PartitionSpec as P

LOG2E = math.log2(math.e)
VMEM = pl.BlockSpec(memory_space=pltpu.VMEM)
HBM = pl.BlockSpec(memory_space=pltpu.HBM)
MIB = 1024 * 1024
F32, BF16 = jnp.float32, jnp.bfloat16
dot = functools.partial(jnp.dot, preferred_element_type=F32)


def iota(shape, dim):
    return lax.broadcasted_iota(jnp.int32, shape, dim)


def line_pairs(count, shift):
    return [(i, i + 1) for i in range(shift, count - 1, 2)]


def swaps(counts, axis, shift):
    depth_count, count_x, count_y = counts
    index = lambda d, x, y: (d * count_x + x) * count_y + y
    pairs = []
    for x in range(count_x):
        for y in range(count_y):
            ends = [p for p in line_pairs(counts[axis], shift) if (x, y)[axis - 1] in p]
            if not ends:
                pairs += [
                    (index(d, x, y), index(d + 1, x, y)) for d in range(0, depth_count - 1, 2)
                ]
            elif (x, y)[axis - 1] == ends[0][0]:
                other = (ends[0][1], y) if axis == 1 else (x, ends[0][1])
                pairs += [(index(d, x, y), index(d, *other)) for d in range(depth_count)]
    return pairs + [(b, a) for a, b in pairs]


class Place:
    def __init__(self):
        self.depth = lax.axis_index("depth")
        self.half, self.has_x = self.sides("sx")
        self.group, self.has_y = self.sides("sy")

    def sides(self, axis):
        at, last = lax.axis_index(axis), lax.axis_size(axis) - 1
        parity = lax.rem(at, 2)
        upper, lower = at < last, at > 0
        order = (1 - parity, parity)
        either = lambda side: jnp.where(side == 1, upper.astype(jnp.int32), lower.astype(jnp.int32))
        return order, [either(side) == 1 for side in order]


def group_rows(place, rim, g):
    return pl.ds(pl.multiple_of(place.group[g] * rim, rim), rim)


def half_rows(place, rim, h):
    return pl.ds(place.half[h] * rim, rim)


def first_kernel(rim, density, *refs):
    place = Place()
    n_tables = (len(refs) - 6) // 2
    tables, held, coarse = refs[:n_tables], refs[n_tables], refs[n_tables + 1:n_tables + 5]
    tables_out, sems = refs[n_tables + 5:-1], refs[-1]
    copies = []
    for g in range(2):
        for h in range(2):
            rows = density.at[half_rows(place, rim, h), group_rows(place, rim, g), :]
            copies.append(pltpu.make_async_copy(rows, held.at[g, h], sems.at[2 * g + h]))
    for i, (src, dst) in enumerate(zip(tables, tables_out)):
        copies.append(pltpu.make_async_copy(src, dst, sems.at[4 + i]))
    for copy in copies:
        copy.start()
    for g in range(2):
        for h in range(2):
            copies[2 * g + h].wait()
            coarse[2 * g + h][...] = held[g, h].astype(BF16)
    for copy in copies[4:]:
        copy.wait()


def toeplitz(taps, rim):
    return pltpu.roll(jnp.broadcast_to(taps, (rim, 128)), 0, 1, stride=1, stride_axis=0)


def blur_matrices(rim, place, taps):
    size = rim * rim
    wide = 3 * size
    shift = rim.bit_length() - 1
    pick = lambda mask: jnp.where(mask, 1.0, 0.0).astype(BF16)
    row_hi = pick(iota((size, rim), 0) >> shift == iota((size, rim), 1))
    row_lo = pick(iota((size, rim), 0) & (rim - 1) == iota((size, rim), 1))
    col = iota((128, wide), 1)
    src = iota((128, wide), 0)
    k, j, b = col >> 2 * shift, col >> shift & (rim - 1), col & (rim - 1)
    k_x = jnp.where(place.half[0] == 1, k, 2 - k)
    k_y = jnp.where(place.group[0] == 1, k, 2 - k)
    tx = toeplitz(taps[0:1], rim).astype(BF16)
    ty = toeplitz(taps[1:2] * 0.5, rim).astype(BF16)
    full_x = dot(row_hi, dot(tx, pick(k_x * rim + j == src)).astype(BF16))
    full_y = dot(row_lo, dot(ty, pick(k_y * rim + b == src)).astype(BF16))
    r, c = iota((size, size), 0), iota((size, size), 1)
    same_x = r & (rim - 1) == c & (rim - 1)
    same_y = r >> shift == c >> shift
    parts = []
    for full, same in ((full_x, same_x), (full_y, same_y)):
        blocks = [
            jnp.where(same, full[:, n * size:(n + 1) * size], 0.0).astype(BF16) for n in range(3)
        ]
        parts.append(jnp.concatenate(blocks, axis=1))
    return parts


def matrices_kernel(rim, taps, mx, my, padded):
    padded[...] = jnp.zeros(padded.shape, F32)
    padded[0:2, 0:taps.shape[1]] = taps[...].astype(F32)
    mx[...], my[...] = blur_matrices(rim, Place(), padded[...])


def prepare_kernel(
    rim, centre, width, colour, opacity, brick_tf, view_order, table, signs, order_map
):
    place = Place()
    wide = width[...]
    rows = [centre[...], (-LOG2E) / (wide * wide), opacity[...] * (-LOG2E)]
    rows += [colour[c] * 0.5 for c in range(3)]
    rows = jnp.concatenate(rows, axis=0)
    which = iota(rows.shape, 1)
    n = 0
    for g in range(2):
        for h in range(2):
            bricks = brick_tf[place.half[h]]
            bricks = jnp.where(place.group[g] == 0, bricks[0:1], bricks[1:2])
            for bz in range(bricks.shape[1]):
                mine = jnp.where(which == bricks[:, bz:bz + 1], rows, 0.0)
                mine = jnp.sum(mine, axis=1, keepdims=True)
                table[n] = jnp.broadcast_to(mine, table.shape[1:])
                n += 1
            orders = view_order[...]
            orders = jnp.where(place.half[h] == 0, orders[0:1], orders[1:2])
            order = jnp.where(place.group[g] == 0, orders[:, 0:1], orders[:, 1:2])
            signs[g, h] = jnp.broadcast_to(1 - 2 * order, signs.shape[2:])
    block, shape = order_map.shape[1], order_map.shape[1:]
    for n in range(order_map.shape[0]):
        brick = n * block // rim
        orders = view_order[brick:brick + 1]
        order_map[n] = jnp.where(
            iota(shape, 1) < rim,
            jnp.broadcast_to(orders[:, 0:1], shape),
            jnp.broadcast_to(orders[:, 1:2], shape),
        )


def cells_kernel(rim, bumps, g, held, table, signs, shaded, total, optical_s, emitted_s):
    place = Place()
    rows_z = held.shape[4]
    depth = 128
    bricks = rows_z // depth
    lane = iota((rim, 128), 1)
    for h in range(2):
        cells = held.at[g, h]
        for bz in range(bricks):
            zs = slice(bz * depth, (bz + 1) * depth)
            at = (2 * g + h) * bricks + bz
            row = lambda i: jnp.broadcast_to(table[at, i:i + 1, :], (8, depth))[None]
            cen = [row(j) for j in range(bumps)]
            neg = [row(bumps + j) for j in range(bumps)]
            opa = [row(2 * bumps + j) for j in range(bumps)]
            col = [[row((3 + c) * bumps + j) for c in range(3)] for j in range(bumps)]
            for x in range(rim):
                d = cells[x, :, zs].reshape(rim // 8, 8, depth)
                opt, em = None, [None] * 3
                for j in range(bumps):
                    w = d - cen[j]
                    b = jnp.exp2((w * w) * neg[j])
                    opt = opa[j] * b if opt is None else opt + opa[j] * b
                    for c in range(3):
                        em[c] = col[j][c] * b if em[c] is None else em[c] + col[j][c] * b
                rows = slice(x * rim, (x + 1) * rim)
                optical_s[h, rows, zs] = opt.reshape(rim, depth)
                for c in range(3):
                    emitted_s[c, h, rows, zs] = em[c].reshape(rim, depth)
        behind = iota((rows_z, rows_z), 1) - iota((rows_z, rows_z), 0)
        sign = jnp.broadcast_to(signs[g, h][0:1, 0:1], (rows_z, rows_z))
        tri = jnp.where(behind * sign > 0, 1.0, 0.0).astype(BF16)
        opt = optical_s[h]
        hi = opt.astype(BF16)
        lo = (opt - hi.astype(F32)).astype(BF16)
        ahead = dot(hi, tri) + dot(lo, tri)
        weight = jnp.exp2(ahead) * (1.0 - jnp.exp2(opt))
        for c in range(3):
            shaded[c, h] = (weight * emitted_s[c, h]).reshape(rim, rim, rows_z)
        part = rays(opt.reshape(rim, rim, rows_z), place.half[h] * rim, lane)
        total[...] = part if h == 0 else total[...] + part


def rays(cells, first_lane, lane):
    folded = cells[:, :, :128]
    for z in range(128, cells.shape[2], 128):
        folded = folded + cells[:, :, z:z + 128]
    summed = jnp.sum(folded, axis=2, keepdims=True)
    acc = jnp.zeros(lane.shape, F32)
    for x in range(cells.shape[0]):
        acc = jnp.where(lane == first_lane + x, summed[x], acc)
    return acc


def blur_x(place, rim, mx, h, near, halo):
    flat = lambda cells: cells.reshape(rim * rim, cells.shape[-1])
    edge = flat(halo)
    edge = jnp.where(place.has_x[h], edge, jnp.zeros_like(edge))
    own = [flat(near[1]), flat(near[0])]
    blocks = own + [edge] if h == 0 else [edge] + own
    return dot(mx[...], jnp.concatenate(blocks, axis=0)).astype(BF16)


def lit(place, rim, occlusion, shaded, h):
    rows_z = occlusion.shape[1]
    lane = iota((rim, 128), 1)
    shade = (1.0 - jnp.tanh(occlusion)).reshape(rim, rim, rows_z)
    return [rays(shade * shaded[c, h], place.half[h] * rim, lane) for c in range(3)]


def strip_kernel(rim, h, mx, near0, near1, halo, out):
    across = blur_x(Place(), rim, mx, h, [near0[...], near1[...]], halo[...])
    out[...] = across.reshape(out.shape)


def own_kernel(rim, early, mx, my, near0, near1, halo0, halo1, strip0, strip1, *refs):
    place = Place()
    size = rim * rim
    across = [
        blur_x(place, rim, mx, h, [near0[...], near1[...]], halo[...])
        for h, halo in enumerate((halo0, halo1))
    ]
    if early:
        shaded, out, partial = refs
    else:
        partial, *others = refs
    for h, strip in enumerate((strip0, strip1)):
        cells = jnp.concatenate([across[h], strip[...].reshape(size, strip.shape[2])], axis=0)
        partial[0, h] = dot(my[:, :2 * size], cells)
        other = dot(my[:, size:], cells)
        if not early:
            others[h][...] = across[h].reshape(strip.shape)
            partial[1, h] = other
            continue
        for c, part in enumerate(lit(place, rim, other, shaded, h)):
            out[c] = part if h == 0 else out[c] + part


def late(rim, g, my, partial, halo0, halo1, shaded):
    place = Place()
    size = rim * rim
    block = my[:, 2 * size:] if g == 0 else my[:, :size]
    occlusion = []
    for h, halo in enumerate((halo0, halo1)):
        cells = halo[...].reshape(size, halo.shape[2])
        cells = jnp.where(place.has_y[g], cells, jnp.zeros_like(cells))
        occlusion.append(partial[g, h] + dot(block, cells))
    lights = [lit(place, rim, occlusion[h], shaded, h) for h in range(2)]
    return [a + b for a, b in zip(*lights)]


def late_kernel(rim, g, *refs):
    *refs, out = refs
    for c, part in enumerate(late(rim, g, *refs)):
        out[c] = part


def last_kernel(rim, depth_count, *refs):
    refs, (light_e, total0, total1, kept, given, img) = refs[:5], refs[5:]
    place = Place()
    rows = 2 * rim
    at_s, at_e = group_rows(place, rim, 0), group_rows(place, rim, 1)
    for c, part in enumerate(late(rim, 0, *refs)):
        img[c, at_s, :] = part
        img[c, at_e, :] = light_e[c]
    img[3, at_s, :] = jnp.exp2(total0[...])
    img[3, at_e, :] = jnp.exp2(total1[...])
    for c in range(4):
        img[4 + c, :, 0:rows] = img[c].T[:rows, :]
    block = rows // depth_count
    bit = place.depth & 1
    for n in range(depth_count // 2):
        for out, b in ((kept, bit), (given, 1 - bit)):
            out[n] = img[4:8, pl.ds(pl.multiple_of((2 * n + b) * block, block), block), 0:rows]


def merge_kernel(level, order_map, kept, theirs, *outs):
    me = lax.axis_index("depth")
    bit = me >> level & 1
    low = me & (2 << level) - 1
    merged = []
    for n in range(kept.shape[0]):
        mine = (bit == order_map[(n << level + 1) + low])[None]
        front = jnp.where(mine, kept[n], theirs[n])
        back = jnp.where(mine, theirs[n], kept[n])
        merged.append((front[:3] + front[3:] * back[:3], front[3:] * back[3:]))
    if len(merged) == 1:
        colour, through = merged[0]
        outs[0][...] = jnp.concatenate([colour, 1.0 - through]).reshape(outs[0].shape)
        return
    up = me >> level + 1 & 1
    for n in range(len(merged) // 2):
        even, odd = (jnp.concatenate(merged[2 * n + i]) for i in range(2))
        outs[0][n] = jnp.where(up == 1, odd, even)
        outs[1][n] = jnp.where(up == 1, even, odd)


def call(kernel, name, ins, outs, scratch=(), limit=16 * MIB, **more):
    return pl.pallas_call(
        kernel,
        out_shape=outs,
        in_specs=ins,
        out_specs=jax.tree.map(lambda _: VMEM, outs),
        scratch_shapes=list(scratch),
        compiler_params=pltpu.CompilerParams(vmem_limit_bytes=limit),
        name=name,
        **more,
    )


def per_device(
    density, kernel_taps, tf_centre, tf_width, tf_color, tf_opacity, brick_tf, view_order
):
    rows_x, rows_y, rows_z = density.shape
    rim = (kernel_taps.shape[1] - 1) // 2
    bumps = tf_centre.shape[1]
    size = rim * rim
    axes = ("depth", "sx", "sy")
    counts = tuple(lax.axis_size(axis) for axis in axes)
    depth_count, count_y = counts[0], counts[2]
    struct = jax.ShapeDtypeStruct
    block = rows_x // depth_count
    rounds = sum(1 for shift in range(2) if line_pairs(count_y, shift))

    def swap(piece, axis, shift):
        return lax.ppermute(piece, axes, swaps(counts, axis, shift))

    in_hbm = lambda array: pltpu.with_memory_space_constraint(array, pltpu.HBM)
    tables = (
        kernel_taps, tf_centre.T, tf_width.T, tf_color.T, tf_opacity.T, brick_tf, view_order
    )
    piece = struct((rim, rim, rows_z), BF16)
    held, *refs = call(
        functools.partial(first_kernel, rim),
        "first",
        [HBM] * (1 + len(tables)),
        [struct((2, 2, rim, rim, rows_z), F32)]
        + [piece] * 4
        + [struct(t.shape, t.dtype) for t in tables],
        [pltpu.SemaphoreType.DMA((4 + len(tables),))],
    )(in_hbm(density), *[in_hbm(t) for t in tables])
    coarse, tables = [refs[0:2], refs[2:4]], refs[4:]
    bricks = rows_z // 128
    table, signs, order_map = call(
        functools.partial(prepare_kernel, rim),
        "prepare",
        [VMEM] * (len(tables) - 1),
        [struct((4 * bricks, 6 * bumps, 128), F32), struct((2, 2, 8, 128), jnp.int32)]
        + [struct((depth_count, block, rows_y), jnp.int32)],
    )(*tables[1:])
    halo_x = [[swap(coarse[0][h], 1, h) for h in range(2)], None]
    mx, my = call(
        functools.partial(matrices_kernel, rim),
        "matrices",
        [VMEM],
        [struct((size, 3 * size), BF16)] * 2,
        [pltpu.VMEM((8, 128), F32)],
    )(tables[0])
    shaded, total = [None, None], [None, None]
    for g in (1, 0):
        shaded[g], total[g] = call(
            functools.partial(cells_kernel, rim, bumps, g),
            f"cells{g}",
            [VMEM] * 3,
            [struct((3, 2, rim, rim, rows_z), F32), struct((rim, 128), F32)],
            [pltpu.VMEM((2, size, rows_z), F32), pltpu.VMEM((3, 2, size, rows_z), F32)],
            cost_estimate=pl.CostEstimate(
                flops=density.size * (100000 if g == 0 else 1),
                bytes_accessed=density.size,
                transcendentals=density.size * 3,
            ),
        )(held, table, signs)

    strips, halo_y = [], []
    for h in range(2):
        if h == 0:
            mx, total[1] = lax.optimization_barrier((mx, total[1]))
        strip = call(functools.partial(strip_kernel, rim, h), f"strip{h}", [VMEM] * 4, piece)(
            mx, *coarse[0], halo_x[0][h]
        )
        strips.append(strip)
        halo_y.append(swap(strip, 2, 0))
        if h == 0:
            pieces = lax.optimization_barrier((*coarse[1], strip))
            halo_x[1] = [swap(pieces[n], 1, n) for n in range(2)]
    early = rounds < 2
    colours = struct((3, rim, 128), F32)
    unlit = struct((2 - early, 2, size, rows_z), F32)
    results = call(
        functools.partial(own_kernel, rim, early),
        "own",
        [VMEM] * (9 if early else 8),
        [colours, unlit] if early else [unlit, piece, piece],
    )(mx, my, *coarse[1], *halo_x[1], *strips, *([shaded[1]] if early else []))
    if early:
        light, partial = results
    else:
        partial, *others = results
        light = call(functools.partial(late_kernel, rim, 1), "late", [VMEM] * 5, colours)(
            my, partial, *[swap(strip, 2, 1) for strip in others], shaded[1]
        )
    kept, given = call(
        functools.partial(last_kernel, rim, depth_count),
        "last",
        [VMEM] * 8,
        [struct((depth_count // 2, 4, block, rows_y), F32)] * 2,
        [pltpu.VMEM((8, rows_y, 128), F32)],
    )(my, partial, *halo_y, shaded[0], light, *total)
    level = 0
    while True:
        theirs = lax.ppermute(given, "depth", [(i, i ^ 1 << level) for i in range(depth_count)])
        left = kept.shape[0] // 2
        outs = [struct((left, 4, block, rows_y), F32)] * 2
        merged = call(
            functools.partial(merge_kernel, level),
            f"merge{level}",
            [VMEM] * 3,
            outs if left else struct((4, 1, 1, block, rows_y), F32),
            limit=2 * MIB,
        )(order_map, kept, theirs)
        if not left:
            return merged
        kept, given = merged
        level += 1


def solution(mesh):
    return jax.shard_map(
        per_device,
        mesh=mesh,
        in_specs=(
            P("sx", "sy", "depth"),
            P(),
            P(),
            P(),
            P(),
            P(),
            P("sx", "sy", "depth"),
            P("sx", "sy"),
        ),
        out_specs=P(None, "sx", "depth", None, "sy"),
        check_vma=False,
    )
```

```python
import functools
import math
import jax
import jax.numpy as jnp
from jax import lax
from jax.experimental import pallas as pl
from jax.experimental.pallas import tpu as pltpu
from jax.sharding import PartitionSpec as P

LOG2E = math.log2(math.e)
VMEM = pl.BlockSpec(memory_space=pltpu.VMEM)
HBM = pl.BlockSpec(memory_space=pltpu.HBM)
MIB = 1024 * 1024
F32, BF16 = jnp.float32, jnp.bfloat16
dot = functools.partial(jnp.dot, preferred_element_type=F32)


def iota(shape, dim):
    return lax.broadcasted_iota(jnp.int32, shape, dim)


def line_pairs(count, shift):
    return [(i, i + 1) for i in range(shift, count - 1, 2)]


def swaps(counts, axis, shift):
    depth_count, count_x, count_y = counts
    index = lambda d, x, y: (d * count_x + x) * count_y + y
    pairs = []
    for x in range(count_x):
        for y in range(count_y):
            ends = [p for p in line_pairs(counts[axis], shift) if (x, y)[axis - 1] in p]
            if not ends:
                pairs += [
                    (index(d, x, y), index(d + 1, x, y)) for d in range(0, depth_count - 1, 2)
                ]
            elif (x, y)[axis - 1] == ends[0][0]:
                other = (ends[0][1], y) if axis == 1 else (x, ends[0][1])
                pairs += [(index(d, x, y), index(d, *other)) for d in range(depth_count)]
    return pairs + [(b, a) for a, b in pairs]


class Place:
    def __init__(self):
        self.depth = lax.axis_index("depth")
        self.half, self.has_x = self.sides("sx")
        self.group, self.has_y = self.sides("sy")

    def sides(self, axis):
        at, last = lax.axis_index(axis), lax.axis_size(axis) - 1
        parity = lax.rem(at, 2)
        upper, lower = at < last, at > 0
        order = (1 - parity, parity)
        either = lambda side: jnp.where(side == 1, upper.astype(jnp.int32), lower.astype(jnp.int32))
        return order, [either(side) == 1 for side in order]


def group_rows(place, rim, g):
    return pl.ds(pl.multiple_of(place.group[g] * rim, rim), rim)


def half_rows(place, rim, h):
    return pl.ds(place.half[h] * rim, rim)


def first_kernel(rim, density, *refs):
    place = Place()
    n_tables = (len(refs) - 6) // 2
    tables, held, coarse = refs[:n_tables], refs[n_tables], refs[n_tables + 1:n_tables + 5]
    tables_out, sems = refs[n_tables + 5:-1], refs[-1]
    copies = []
    for g in range(2):
        for h in range(2):
            rows = density.at[half_rows(place, rim, h), group_rows(place, rim, g), :]
            copies.append(pltpu.make_async_copy(rows, held.at[g, h], sems.at[2 * g + h]))
    for i, (src, dst) in enumerate(zip(tables, tables_out)):
        copies.append(pltpu.make_async_copy(src, dst, sems.at[4 + i]))
    for copy in copies:
        copy.start()
    for g in range(2):
        for h in range(2):
            copies[2 * g + h].wait()
            coarse[2 * g + h][...] = held[g, h].astype(BF16)
    for copy in copies[4:]:
        copy.wait()


def toeplitz(taps, rim):
    return pltpu.roll(jnp.broadcast_to(taps, (rim, 128)), 0, 1, stride=1, stride_axis=0)


def blur_matrices(rim, place, taps):
    size = rim * rim
    wide = 3 * size
    shift = rim.bit_length() - 1
    pick = lambda mask: jnp.where(mask, 1.0, 0.0).astype(BF16)
    row_hi = pick(iota((size, rim), 0) >> shift == iota((size, rim), 1))
    row_lo = pick(iota((size, rim), 0) & (rim - 1) == iota((size, rim), 1))
    col = iota((128, wide), 1)
    src = iota((128, wide), 0)
    k, j, b = col >> 2 * shift, col >> shift & (rim - 1), col & (rim - 1)
    k_x = jnp.where(place.half[0] == 1, k, 2 - k)
    k_y = jnp.where(place.group[0] == 1, k, 2 - k)
    tx = toeplitz(taps[0:1], rim).astype(BF16)
    ty = toeplitz(taps[1:2] * 0.5, rim).astype(BF16)
    full_x = dot(row_hi, dot(tx, pick(k_x * rim + j == src)).astype(BF16))
    full_y = dot(row_lo, dot(ty, pick(k_y * rim + b == src)).astype(BF16))
    r, c = iota((size, size), 0), iota((size, size), 1)
    same_x = r & (rim - 1) == c & (rim - 1)
    same_y = r >> shift == c >> shift
    parts = []
    for full, same in ((full_x, same_x), (full_y, same_y)):
        blocks = [
            jnp.where(same, full[:, n * size:(n + 1) * size], 0.0).astype(BF16) for n in range(3)
        ]
        parts.append(jnp.concatenate(blocks, axis=1))
    return parts


def matrices_kernel(rim, taps, mx, my, padded):
    padded[...] = jnp.zeros(padded.shape, F32)
    padded[0:2, 0:taps.shape[1]] = taps[...].astype(F32)
    mx[...], my[...] = blur_matrices(rim, Place(), padded[...])


def prepare_kernel(
    rim, centre, width, colour, opacity, brick_tf, view_order, table, signs, order_map
):
    place = Place()
    wide = width[...]
    rows = [centre[...], (-LOG2E) / (wide * wide), opacity[...] * (-LOG2E)]
    rows += [colour[c] * 0.5 for c in range(3)]
    rows = jnp.concatenate(rows, axis=0)
    which = iota(rows.shape, 1)
    n = 0
    for g in range(2):
        for h in range(2):
            bricks = brick_tf[place.half[h]]
            bricks = jnp.where(place.group[g] == 0, bricks[0:1], bricks[1:2])
            for bz in range(bricks.shape[1]):
                mine = jnp.where(which == bricks[:, bz:bz + 1], rows, 0.0)
                mine = jnp.sum(mine, axis=1, keepdims=True)
                table[n] = jnp.broadcast_to(mine, table.shape[1:])
                n += 1
            orders = view_order[...]
            orders = jnp.where(place.half[h] == 0, orders[0:1], orders[1:2])
            order = jnp.where(place.group[g] == 0, orders[:, 0:1], orders[:, 1:2])
            signs[g, h] = jnp.broadcast_to(1 - 2 * order, signs.shape[2:])
    block, shape = order_map.shape[1], order_map.shape[1:]
    for n in range(order_map.shape[0]):
        brick = n * block // rim
        orders = view_order[brick:brick + 1]
        order_map[n] = jnp.where(
            iota(shape, 1) < rim,
            jnp.broadcast_to(orders[:, 0:1], shape),
            jnp.broadcast_to(orders[:, 1:2], shape),
        )


def cells_kernel(rim, bumps, g, held, table, signs, shaded, total, optical_s, emitted_s):
    place = Place()
    rows_z = held.shape[4]
    depth = 128
    bricks = rows_z // depth
    lane = iota((rim, 128), 1)
    for h in range(2):
        cells = held.at[g, h]
        for bz in range(bricks):
            zs = slice(bz * depth, (bz + 1) * depth)
            at = (2 * g + h) * bricks + bz
            row = lambda i: jnp.broadcast_to(table[at, i:i + 1, :], (8, depth))[None]
            cen = [row(j) for j in range(bumps)]
            neg = [row(bumps + j) for j in range(bumps)]
            opa = [row(2 * bumps + j) for j in range(bumps)]
            col = [[row((3 + c) * bumps + j) for c in range(3)] for j in range(bumps)]
            for x in range(rim):
                d = cells[x, :, zs].reshape(rim // 8, 8, depth)
                opt, em = None, [None] * 3
                for j in range(bumps):
                    w = d - cen[j]
                    b = jnp.exp2((w * w) * neg[j])
                    opt = opa[j] * b if opt is None else opt + opa[j] * b
                    for c in range(3):
                        em[c] = col[j][c] * b if em[c] is None else em[c] + col[j][c] * b
                rows = slice(x * rim, (x + 1) * rim)
                optical_s[h, rows, zs] = opt.reshape(rim, depth)
                for c in range(3):
                    emitted_s[c, h, rows, zs] = em[c].reshape(rim, depth)
        behind = iota((rows_z, rows_z), 1) - iota((rows_z, rows_z), 0)
        sign = jnp.broadcast_to(signs[g, h][0:1, 0:1], (rows_z, rows_z))
        tri = jnp.where(behind * sign > 0, 1.0, 0.0).astype(BF16)
        opt = optical_s[h]
        hi = opt.astype(BF16)
        lo = (opt - hi.astype(F32)).astype(BF16)
        ahead = dot(hi, tri) + dot(lo, tri)
        weight = jnp.exp2(ahead) * (1.0 - jnp.exp2(opt))
        for c in range(3):
            shaded[c, h] = (weight * emitted_s[c, h]).reshape(rim, rim, rows_z)
        part = rays(opt.reshape(rim, rim, rows_z), place.half[h] * rim, lane)
        total[...] = part if h == 0 else total[...] + part


def rays(cells, first_lane, lane):
    folded = cells[:, :, :128]
    for z in range(128, cells.shape[2], 128):
        folded = folded + cells[:, :, z:z + 128]
    summed = jnp.sum(folded, axis=2, keepdims=True)
    acc = jnp.zeros(lane.shape, F32)
    for x in range(cells.shape[0]):
        acc = jnp.where(lane == first_lane + x, summed[x], acc)
    return acc


def blur_x(place, rim, mx, h, near, halo):
    flat = lambda cells: cells.reshape(rim * rim, cells.shape[-1])
    edge = flat(halo)
    edge = jnp.where(place.has_x[h], edge, jnp.zeros_like(edge))
    own = [flat(near[1]), flat(near[0])]
    blocks = own + [edge] if h == 0 else [edge] + own
    return dot(mx[...], jnp.concatenate(blocks, axis=0)).astype(BF16)


def lit(place, rim, occlusion, shaded, h):
    rows_z = occlusion.shape[1]
    lane = iota((rim, 128), 1)
    shade = (1.0 - jnp.tanh(occlusion)).reshape(rim, rim, rows_z)
    return [rays(shade * shaded[c, h], place.half[h] * rim, lane) for c in range(3)]


def strip_kernel(rim, h, mx, near0, near1, halo, out):
    across = blur_x(Place(), rim, mx, h, [near0[...], near1[...]], halo[...])
    out[...] = across.reshape(out.shape)


def own_kernel(rim, early, strip0, strip1, mx, my, near0, near1, halo0, halo1, *refs):
    place = Place()
    size = rim * rim
    across = [
        blur_x(place, rim, mx, h, [near0[...], near1[...]], halo[...])
        for h, halo in enumerate((halo0, halo1))
    ]
    if early:
        shaded, out, partial = refs
    else:
        partial, *others = refs
    for h, strip in enumerate((strip0, strip1)):
        cells = jnp.concatenate([across[h], strip[...].reshape(size, strip.shape[2])], axis=0)
        partial[0, h] = dot(my[:, :2 * size], cells)
        other = dot(my[:, size:], cells)
        if not early:
            others[h][...] = across[h].reshape(strip.shape)
            partial[1, h] = other
            continue
        for c, part in enumerate(lit(place, rim, other, shaded, h)):
            out[c] = part if h == 0 else out[c] + part


def late(rim, g, my, partial, halo0, halo1, shaded):
    place = Place()
    size = rim * rim
    block = my[:, 2 * size:] if g == 0 else my[:, :size]
    occlusion = []
    for h, halo in enumerate((halo0, halo1)):
        cells = halo[...].reshape(size, halo.shape[2])
        cells = jnp.where(place.has_y[g], cells, jnp.zeros_like(cells))
        occlusion.append(partial[g, h] + dot(block, cells))
    lights = [lit(place, rim, occlusion[h], shaded, h) for h in range(2)]
    return [a + b for a, b in zip(*lights)]


def late_kernel(rim, g, *refs):
    *refs, out = refs
    for c, part in enumerate(late(rim, g, *refs)):
        out[c] = part


def last_kernel(rim, depth_count, *refs):
    refs, (light_e, total0, total1, kept, given, img) = refs[:5], refs[5:]
    place = Place()
    rows = 2 * rim
    at_s, at_e = group_rows(place, rim, 0), group_rows(place, rim, 1)
    for c, part in enumerate(late(rim, 0, *refs)):
        img[c, at_s, :] = part
        img[c, at_e, :] = light_e[c]
    img[3, at_s, :] = jnp.exp2(total0[...])
    img[3, at_e, :] = jnp.exp2(total1[...])
    for c in range(4):
        img[4 + c, :, 0:rows] = img[c].T[:rows, :]
    block = rows // depth_count
    bit = place.depth & 1
    for n in range(depth_count // 2):
        for out, b in ((kept, bit), (given, 1 - bit)):
            out[n] = img[4:8, pl.ds(pl.multiple_of((2 * n + b) * block, block), block), 0:rows]


def merge_kernel(level, order_map, kept, theirs, *outs):
    me = lax.axis_index("depth")
    bit = me >> level & 1
    low = me & (2 << level) - 1
    merged = []
    for n in range(kept.shape[0]):
        mine = (bit == order_map[(n << level + 1) + low])[None]
        front = jnp.where(mine, kept[n], theirs[n])
        back = jnp.where(mine, theirs[n], kept[n])
        merged.append((front[:3] + front[3:] * back[:3], front[3:] * back[3:]))
    if len(merged) == 1:
        colour, through = merged[0]
        outs[0][...] = jnp.concatenate([colour, 1.0 - through]).reshape(outs[0].shape)
        return
    up = me >> level + 1 & 1
    for n in range(len(merged) // 2):
        even, odd = (jnp.concatenate(merged[2 * n + i]) for i in range(2))
        outs[0][n] = jnp.where(up == 1, odd, even)
        outs[1][n] = jnp.where(up == 1, even, odd)


def call(kernel, name, ins, outs, scratch=(), limit=16 * MIB, **more):
    return pl.pallas_call(
        kernel,
        out_shape=outs,
        in_specs=ins,
        out_specs=jax.tree.map(lambda _: VMEM, outs),
        scratch_shapes=list(scratch),
        compiler_params=pltpu.CompilerParams(vmem_limit_bytes=limit),
        name=name,
        **more,
    )


def per_device(
    density, kernel_taps, tf_centre, tf_width, tf_color, tf_opacity, brick_tf, view_order
):
    rows_x, rows_y, rows_z = density.shape
    rim = (kernel_taps.shape[1] - 1) // 2
    bumps = tf_centre.shape[1]
    size = rim * rim
    axes = ("depth", "sx", "sy")
    counts = tuple(lax.axis_size(axis) for axis in axes)
    depth_count, count_y = counts[0], counts[2]
    struct = jax.ShapeDtypeStruct
    block = rows_x // depth_count
    rounds = sum(1 for shift in range(2) if line_pairs(count_y, shift))

    def swap(piece, axis, shift):
        return lax.ppermute(piece, axes, swaps(counts, axis, shift))

    in_hbm = lambda array: pltpu.with_memory_space_constraint(array, pltpu.HBM)
    tables = (
        kernel_taps, tf_centre.T, tf_width.T, tf_color.T, tf_opacity.T, brick_tf, view_order
    )
    piece = struct((rim, rim, rows_z), BF16)
    held, *refs = call(
        functools.partial(first_kernel, rim),
        "first",
        [HBM] * (1 + len(tables)),
        [struct((2, 2, rim, rim, rows_z), F32)]
        + [piece] * 4
        + [struct(t.shape, t.dtype) for t in tables],
        [pltpu.SemaphoreType.DMA((4 + len(tables),))],
    )(in_hbm(density), *[in_hbm(t) for t in tables])
    coarse, tables = [refs[0:2], refs[2:4]], refs[4:]
    bricks = rows_z // 128
    table, signs, order_map = call(
        functools.partial(prepare_kernel, rim),
        "prepare",
        [VMEM] * (len(tables) - 1),
        [struct((4 * bricks, 6 * bumps, 128), F32), struct((2, 2, 8, 128), jnp.int32)]
        + [struct((depth_count, block, rows_y), jnp.int32)],
    )(*tables[1:])
    halo_x = [[swap(coarse[g][h], 1, h) for h in range(2)] for g in range(2)]
    mx, my = call(
        functools.partial(matrices_kernel, rim),
        "matrices",
        [VMEM],
        [struct((size, 3 * size), BF16)] * 2,
        [pltpu.VMEM((8, 128), F32)],
    )(tables[0])
    shaded, total = [None, None], [None, None]
    for g in (1, 0):
        shaded[g], total[g] = call(
            functools.partial(cells_kernel, rim, bumps, g),
            f"cells{g}",
            [VMEM] * 3,
            [struct((3, 2, rim, rim, rows_z), F32), struct((rim, 128), F32)],
            [pltpu.VMEM((2, size, rows_z), F32), pltpu.VMEM((3, 2, size, rows_z), F32)],
            cost_estimate=pl.CostEstimate(
                flops=density.size * (100000 if g == 0 else 1),
                bytes_accessed=density.size,
                transcendentals=density.size * 3,
            ),
        )(held, table, signs)

    strips, halo_y = [], []
    for h in range(2):
        if h == 0:
            mx, total[1] = lax.optimization_barrier((mx, total[1]))
        strip = call(functools.partial(strip_kernel, rim, h), f"strip{h}", [VMEM] * 4, piece)(
            mx, *coarse[0], halo_x[0][h]
        )
        strips.append(strip)
        halo_y.append(swap(strip, 2, 0))
    early = rounds < 2
    colours = struct((3, rim, 128), F32)
    unlit = struct((2 - early, 2, size, rows_z), F32)
    results = call(
        functools.partial(own_kernel, rim, early),
        "own",
        [VMEM] * (9 if early else 8),
        [colours, unlit] if early else [unlit, piece, piece],
    )(*strips, mx, my, *coarse[1], *halo_x[1], *([shaded[1]] if early else []))
    if early:
        light, partial = results
    else:
        partial, *others = results
        light = call(functools.partial(late_kernel, rim, 1), "late", [VMEM] * 5, colours)(
            my, partial, *[swap(strip, 2, 1) for strip in others], shaded[1]
        )
    kept, given = call(
        functools.partial(last_kernel, rim, depth_count),
        "last",
        [VMEM] * 8,
        [struct((depth_count // 2, 4, block, rows_y), F32)] * 2,
        [pltpu.VMEM((8, rows_y, 128), F32)],
    )(my, partial, *halo_y, shaded[0], light, *total)
    level = 0
    while True:
        theirs = lax.ppermute(given, "depth", [(i, i ^ 1 << level) for i in range(depth_count)])
        left = kept.shape[0] // 2
        outs = [struct((left, 4, block, rows_y), F32)] * 2
        merged = call(
            functools.partial(merge_kernel, level),
            f"merge{level}",
            [VMEM] * 3,
            outs if left else struct((4, 1, 1, block, rows_y), F32),
            limit=2 * MIB,
        )(order_map, kept, theirs)
        if not left:
            return merged
        kept, given = merged
        level += 1


def solution(mesh):
    return jax.shard_map(
        per_device,
        mesh=mesh,
        in_specs=(
            P("sx", "sy", "depth"),
            P(),
            P(),
            P(),
            P(),
            P(),
            P("sx", "sy", "depth"),
            P("sx", "sy"),
        ),
        out_specs=P(None, "sx", "depth", None, "sy"),
        check_vma=False,
    )
```

```python
import functools
import math
import jax
import jax.numpy as jnp
from jax import lax
from jax.experimental import pallas as pl
from jax.experimental.pallas import tpu as pltpu
from jax.sharding import PartitionSpec as P

LOG2E = math.log2(math.e)
VMEM = pl.BlockSpec(memory_space=pltpu.VMEM)
HBM = pl.BlockSpec(memory_space=pltpu.HBM)
MIB = 1024 * 1024
F32, BF16 = jnp.float32, jnp.bfloat16
dot = functools.partial(jnp.dot, preferred_element_type=F32)


def iota(shape, dim):
    return lax.broadcasted_iota(jnp.int32, shape, dim)


def line_pairs(count, shift):
    return [(i, i + 1) for i in range(shift, count - 1, 2)]


def swaps(counts, axis, shift):
    depth_count, count_x, count_y = counts
    index = lambda d, x, y: (d * count_x + x) * count_y + y
    pairs = []
    for x in range(count_x):
        for y in range(count_y):
            ends = [p for p in line_pairs(counts[axis], shift) if (x, y)[axis - 1] in p]
            if not ends:
                pairs += [
                    (index(d, x, y), index(d + 1, x, y)) for d in range(0, depth_count - 1, 2)
                ]
            elif (x, y)[axis - 1] == ends[0][0]:
                other = (ends[0][1], y) if axis == 1 else (x, ends[0][1])
                pairs += [(index(d, x, y), index(d, *other)) for d in range(depth_count)]
    return pairs + [(b, a) for a, b in pairs]


class Place:
    def __init__(self):
        self.depth = lax.axis_index("depth")
        self.half, self.has_x = self.sides("sx")
        self.group, self.has_y = self.sides("sy")

    def sides(self, axis):
        at, last = lax.axis_index(axis), lax.axis_size(axis) - 1
        parity = lax.rem(at, 2)
        upper, lower = at < last, at > 0
        order = (1 - parity, parity)
        either = lambda side: jnp.where(side == 1, upper.astype(jnp.int32), lower.astype(jnp.int32))
        return order, [either(side) == 1 for side in order]


def group_rows(place, rim, g):
    return pl.ds(pl.multiple_of(place.group[g] * rim, rim), rim)


def half_rows(place, rim, h):
    return pl.ds(place.half[h] * rim, rim)


def first_kernel(rim, density, *refs):
    place = Place()
    n_tables = (len(refs) - 6) // 2
    tables, held, coarse = refs[:n_tables], refs[n_tables], refs[n_tables + 1:n_tables + 5]
    tables_out, sems = refs[n_tables + 5:-1], refs[-1]
    copies = []
    for g in range(2):
        for h in range(2):
            rows = density.at[half_rows(place, rim, h), group_rows(place, rim, g), :]
            copies.append(pltpu.make_async_copy(rows, held.at[g, h], sems.at[2 * g + h]))
    for i, (src, dst) in enumerate(zip(tables, tables_out)):
        copies.append(pltpu.make_async_copy(src, dst, sems.at[4 + i]))
    for copy in copies:
        copy.start()
    for g in range(2):
        for h in range(2):
            copies[2 * g + h].wait()
            coarse[2 * g + h][...] = held[g, h].astype(BF16)
    for copy in copies[4:]:
        copy.wait()


def toeplitz(taps, rim):
    return pltpu.roll(jnp.broadcast_to(taps, (rim, 128)), 0, 1, stride=1, stride_axis=0)


def blur_matrices(rim, place, taps):
    size = rim * rim
    wide = 3 * size
    shift = rim.bit_length() - 1
    pick = lambda mask: jnp.where(mask, 1.0, 0.0).astype(BF16)
    row_hi = pick(iota((size, rim), 0) >> shift == iota((size, rim), 1))
    row_lo = pick(iota((size, rim), 0) & (rim - 1) == iota((size, rim), 1))
    col = iota((128, wide), 1)
    src = iota((128, wide), 0)
    k, j, b = col >> 2 * shift, col >> shift & (rim - 1), col & (rim - 1)
    k_x = jnp.where(place.half[0] == 1, k, 2 - k)
    k_y = jnp.where(place.group[0] == 1, k, 2 - k)
    tx = toeplitz(taps[0:1], rim).astype(BF16)
    ty = toeplitz(taps[1:2] * 0.5, rim).astype(BF16)
    full_x = dot(row_hi, dot(tx, pick(k_x * rim + j == src)).astype(BF16))
    full_y = dot(row_lo, dot(ty, pick(k_y * rim + b == src)).astype(BF16))
    r, c = iota((size, size), 0), iota((size, size), 1)
    same_x = r & (rim - 1) == c & (rim - 1)
    same_y = r >> shift == c >> shift
    parts = []
    for full, same in ((full_x, same_x), (full_y, same_y)):
        blocks = [
            jnp.where(same, full[:, n * size:(n + 1) * size], 0.0).astype(BF16) for n in range(3)
        ]
        parts.append(jnp.concatenate(blocks, axis=1))
    return parts


def matrices_kernel(rim, taps, mx, my, padded):
    padded[...] = jnp.zeros(padded.shape, F32)
    padded[0:2, 0:taps.shape[1]] = taps[...].astype(F32)
    mx[...], my[...] = blur_matrices(rim, Place(), padded[...])


def prepare_kernel(
    rim, centre, width, colour, opacity, brick_tf, view_order, table, signs, order_map
):
    place = Place()
    wide = width[...]
    rows = [centre[...], (-LOG2E) / (wide * wide), opacity[...] * (-LOG2E)]
    rows += [colour[c] * 0.5 for c in range(3)]
    rows = jnp.concatenate(rows, axis=0)
    which = iota(rows.shape, 1)
    n = 0
    for g in range(2):
        for h in range(2):
            bricks = brick_tf[place.half[h]]
            bricks = jnp.where(place.group[g] == 0, bricks[0:1], bricks[1:2])
            for bz in range(bricks.shape[1]):
                mine = jnp.where(which == bricks[:, bz:bz + 1], rows, 0.0)
                mine = jnp.sum(mine, axis=1, keepdims=True)
                table[n] = jnp.broadcast_to(mine, table.shape[1:])
                n += 1
            orders = view_order[...]
            orders = jnp.where(place.half[h] == 0, orders[0:1], orders[1:2])
            order = jnp.where(place.group[g] == 0, orders[:, 0:1], orders[:, 1:2])
            signs[g, h] = jnp.broadcast_to(1 - 2 * order, signs.shape[2:])
    block, shape = order_map.shape[1], order_map.shape[1:]
    for n in range(order_map.shape[0]):
        brick = n * block // rim
        orders = view_order[brick:brick + 1]
        order_map[n] = jnp.where(
            iota(shape, 1) < rim,
            jnp.broadcast_to(orders[:, 0:1], shape),
            jnp.broadcast_to(orders[:, 1:2], shape),
        )


def cells_kernel(rim, bumps, g, held, table, signs, shaded, total, optical_s, emitted_s):
    place = Place()
    rows_z = held.shape[4]
    depth = 128
    bricks = rows_z // depth
    lane = iota((rim, 128), 1)
    for h in range(2):
        cells = held.at[g, h]
        for bz in range(bricks):
            zs = slice(bz * depth, (bz + 1) * depth)
            at = (2 * g + h) * bricks + bz
            row = lambda i: jnp.broadcast_to(table[at, i:i + 1, :], (8, depth))[None]
            cen = [row(j) for j in range(bumps)]
            neg = [row(bumps + j) for j in range(bumps)]
            opa = [row(2 * bumps + j) for j in range(bumps)]
            col = [[row((3 + c) * bumps + j) for c in range(3)] for j in range(bumps)]
            for x in range(rim):
                d = cells[x, :, zs].reshape(rim // 8, 8, depth)
                opt, em = None, [None] * 3
                for j in range(bumps):
                    w = d - cen[j]
                    b = jnp.exp2((w * w) * neg[j])
                    opt = opa[j] * b if opt is None else opt + opa[j] * b
                    for c in range(3):
                        em[c] = col[j][c] * b if em[c] is None else em[c] + col[j][c] * b
                rows = slice(x * rim, (x + 1) * rim)
                optical_s[h, rows, zs] = opt.reshape(rim, depth)
                for c in range(3):
                    emitted_s[c, h, rows, zs] = em[c].reshape(rim, depth)
        behind = iota((rows_z, rows_z), 1) - iota((rows_z, rows_z), 0)
        sign = jnp.broadcast_to(signs[g, h][0:1, 0:1], (rows_z, rows_z))
        tri = jnp.where(behind * sign > 0, 1.0, 0.0).astype(BF16)
        opt = optical_s[h]
        hi = opt.astype(BF16)
        lo = (opt - hi.astype(F32)).astype(BF16)
        ahead = dot(hi, tri) + dot(lo, tri)
        weight = jnp.exp2(ahead) * (1.0 - jnp.exp2(opt))
        for c in range(3):
            shaded[c, h] = (weight * emitted_s[c, h]).reshape(rim, rim, rows_z)
        part = rays(opt.reshape(rim, rim, rows_z), place.half[h] * rim, lane)
        total[...] = part if h == 0 else total[...] + part


def rays(cells, first_lane, lane):
    folded = cells[:, :, :128]
    for z in range(128, cells.shape[2], 128):
        folded = folded + cells[:, :, z:z + 128]
    summed = jnp.sum(folded, axis=2, keepdims=True)
    acc = jnp.zeros(lane.shape, F32)
    for x in range(cells.shape[0]):
        acc = jnp.where(lane == first_lane + x, summed[x], acc)
    return acc


def blur_x(place, rim, mx, h, near, halo):
    flat = lambda cells: cells.reshape(rim * rim, cells.shape[-1])
    edge = flat(halo)
    edge = jnp.where(place.has_x[h], edge, jnp.zeros_like(edge))
    own = [flat(near[1]), flat(near[0])]
    blocks = own + [edge] if h == 0 else [edge] + own
    return dot(mx[...], jnp.concatenate(blocks, axis=0)).astype(BF16)


def lit(place, rim, occlusion, shaded, h):
    rows_z = occlusion.shape[1]
    lane = iota((rim, 128), 1)
    shade = (1.0 - jnp.tanh(occlusion)).reshape(rim, rim, rows_z)
    return [rays(shade * shaded[c, h], place.half[h] * rim, lane) for c in range(3)]


def strip_kernel(rim, h, mx, near0, near1, halo, out):
    across = blur_x(Place(), rim, mx, h, [near0[...], near1[...]], halo[...])
    out[...] = across.reshape(out.shape)


def own_kernel(rim, early, strip0, halo0, strip1, halo1, mx, my, near0, near1, *refs):
    place = Place()
    size = rim * rim
    across = [
        blur_x(place, rim, mx, h, [near0[...], near1[...]], halo[...])
        for h, halo in enumerate((halo0, halo1))
    ]
    if early:
        shaded, out, partial = refs
    else:
        partial, *others = refs
    for h, strip in enumerate((strip0, strip1)):
        cells = jnp.concatenate([across[h], strip[...].reshape(size, strip.shape[2])], axis=0)
        partial[0, h] = dot(my[:, :2 * size], cells)
        other = dot(my[:, size:], cells)
        if not early:
            others[h][...] = across[h].reshape(strip.shape)
            partial[1, h] = other
            continue
        for c, part in enumerate(lit(place, rim, other, shaded, h)):
            out[c] = part if h == 0 else out[c] + part


def late(rim, g, my, partial, halo0, halo1, shaded):
    place = Place()
    size = rim * rim
    block = my[:, 2 * size:] if g == 0 else my[:, :size]
    occlusion = []
    for h, halo in enumerate((halo0, halo1)):
        cells = halo[...].reshape(size, halo.shape[2])
        cells = jnp.where(place.has_y[g], cells, jnp.zeros_like(cells))
        occlusion.append(partial[g, h] + dot(block, cells))
    lights = [lit(place, rim, occlusion[h], shaded, h) for h in range(2)]
    return [a + b for a, b in zip(*lights)]


def late_kernel(rim, g, *refs):
    *refs, out = refs
    for c, part in enumerate(late(rim, g, *refs)):
        out[c] = part


def last_kernel(rim, depth_count, *refs):
    refs, (light_e, total0, total1, kept, given, img) = refs[:5], refs[5:]
    place = Place()
    rows = 2 * rim
    at_s, at_e = group_rows(place, rim, 0), group_rows(place, rim, 1)
    for c, part in enumerate(late(rim, 0, *refs)):
        img[c, at_s, :] = part
        img[c, at_e, :] = light_e[c]
    img[3, at_s, :] = jnp.exp2(total0[...])
    img[3, at_e, :] = jnp.exp2(total1[...])
    for c in range(4):
        img[4 + c, :, 0:rows] = img[c].T[:rows, :]
    block = rows // depth_count
    bit = place.depth & 1
    for n in range(depth_count // 2):
        for out, b in ((kept, bit), (given, 1 - bit)):
            out[n] = img[4:8, pl.ds(pl.multiple_of((2 * n + b) * block, block), block), 0:rows]


def merge_kernel(level, order_map, kept, theirs, *outs):
    me = lax.axis_index("depth")
    bit = me >> level & 1
    low = me & (2 << level) - 1
    merged = []
    for n in range(kept.shape[0]):
        mine = (bit == order_map[(n << level + 1) + low])[None]
        front = jnp.where(mine, kept[n], theirs[n])
        back = jnp.where(mine, theirs[n], kept[n])
        merged.append((front[:3] + front[3:] * back[:3], front[3:] * back[3:]))
    if len(merged) == 1:
        colour, through = merged[0]
        outs[0][...] = jnp.concatenate([colour, 1.0 - through]).reshape(outs[0].shape)
        return
    up = me >> level + 1 & 1
    for n in range(len(merged) // 2):
        even, odd = (jnp.concatenate(merged[2 * n + i]) for i in range(2))
        outs[0][n] = jnp.where(up == 1, odd, even)
        outs[1][n] = jnp.where(up == 1, even, odd)


def call(kernel, name, ins, outs, scratch=(), limit=16 * MIB, **more):
    return pl.pallas_call(
        kernel,
        out_shape=outs,
        in_specs=ins,
        out_specs=jax.tree.map(lambda _: VMEM, outs),
        scratch_shapes=list(scratch),
        compiler_params=pltpu.CompilerParams(vmem_limit_bytes=limit),
        name=name,
        **more,
    )


def per_device(
    density, kernel_taps, tf_centre, tf_width, tf_color, tf_opacity, brick_tf, view_order
):
    rows_x, rows_y, rows_z = density.shape
    rim = (kernel_taps.shape[1] - 1) // 2
    bumps = tf_centre.shape[1]
    size = rim * rim
    axes = ("depth", "sx", "sy")
    counts = tuple(lax.axis_size(axis) for axis in axes)
    depth_count, count_y = counts[0], counts[2]
    struct = jax.ShapeDtypeStruct
    block = rows_x // depth_count
    rounds = sum(1 for shift in range(2) if line_pairs(count_y, shift))

    def swap(piece, axis, shift):
        return lax.ppermute(piece, axes, swaps(counts, axis, shift))

    in_hbm = lambda array: pltpu.with_memory_space_constraint(array, pltpu.HBM)
    tables = (
        kernel_taps, tf_centre.T, tf_width.T, tf_color.T, tf_opacity.T, brick_tf, view_order
    )
    piece = struct((rim, rim, rows_z), BF16)
    held, *refs = call(
        functools.partial(first_kernel, rim),
        "first",
        [HBM] * (1 + len(tables)),
        [struct((2, 2, rim, rim, rows_z), F32)]
        + [piece] * 4
        + [struct(t.shape, t.dtype) for t in tables],
        [pltpu.SemaphoreType.DMA((4 + len(tables),))],
    )(in_hbm(density), *[in_hbm(t) for t in tables])
    coarse, tables = [refs[0:2], refs[2:4]], refs[4:]
    bricks = rows_z // 128
    table, signs, order_map = call(
        functools.partial(prepare_kernel, rim),
        "prepare",
        [VMEM] * (len(tables) - 1),
        [struct((4 * bricks, 6 * bumps, 128), F32), struct((2, 2, 8, 128), jnp.int32)]
        + [struct((depth_count, block, rows_y), jnp.int32)],
    )(*tables[1:])
    halo_x = [[swap(coarse[g][h], 1, h) for h in range(2)] for g in range(2)]
    mx, my = call(
        functools.partial(matrices_kernel, rim),
        "matrices",
        [VMEM],
        [struct((size, 3 * size), BF16)] * 2,
        [pltpu.VMEM((8, 128), F32)],
    )(tables[0])
    strips, halo_y = [], []
    for h in range(2):
        if h == 1:
            mx, halo_x[1][0] = lax.optimization_barrier((mx, halo_x[1][0]))
        strip = call(functools.partial(strip_kernel, rim, h), f"strip{h}", [VMEM] * 4, piece)(
            mx, *coarse[0], halo_x[0][h]
        )
        strips.append(strip)
        halo_y.append(swap(strip, 2, 0))
    table, first = lax.optimization_barrier((table, strips[0]))
    strips[0] = first
    shaded, total = [None, None], [None, None]
    for g in (1, 0):
        shaded[g], total[g] = call(
            functools.partial(cells_kernel, rim, bumps, g),
            f"cells{g}",
            [VMEM] * 3,
            [struct((3, 2, rim, rim, rows_z), F32), struct((rim, 128), F32)],
            [pltpu.VMEM((2, size, rows_z), F32), pltpu.VMEM((3, 2, size, rows_z), F32)],
            cost_estimate=pl.CostEstimate(
                flops=density.size * (100000 if g == 0 else 1),
                bytes_accessed=density.size,
                transcendentals=density.size * 3,
            ),
        )(held, table, signs)

    early = rounds < 2
    colours = struct((3, rim, 128), F32)
    unlit = struct((2 - early, 2, size, rows_z), F32)
    results = call(
        functools.partial(own_kernel, rim, early),
        "own",
        [VMEM] * (9 if early else 8),
        [colours, unlit] if early else [unlit, piece, piece],
    )(
        strips[0], halo_x[1][0], strips[1], halo_x[1][1], mx, my, *coarse[1], *([shaded[1]] if early else [])
    )
    if early:
        light, partial = results
    else:
        partial, *others = results
        light = call(functools.partial(late_kernel, rim, 1), "late", [VMEM] * 5, colours)(
            my, partial, *[swap(strip, 2, 1) for strip in others], shaded[1]
        )
    kept, given = call(
        functools.partial(last_kernel, rim, depth_count),
        "last",
        [VMEM] * 8,
        [struct((depth_count // 2, 4, block, rows_y), F32)] * 2,
        [pltpu.VMEM((8, rows_y, 128), F32)],
    )(my, partial, *halo_y, shaded[0], light, *total)
    level = 0
    while True:
        theirs = lax.ppermute(given, "depth", [(i, i ^ 1 << level) for i in range(depth_count)])
        left = kept.shape[0] // 2
        outs = [struct((left, 4, block, rows_y), F32)] * 2
        merged = call(
            functools.partial(merge_kernel, level),
            f"merge{level}",
            [VMEM] * 3,
            outs if left else struct((4, 1, 1, block, rows_y), F32),
            limit=2 * MIB,
        )(order_map, kept, theirs)
        if not left:
            return merged
        kept, given = merged
        level += 1


def solution(mesh):
    return jax.shard_map(
        per_device,
        mesh=mesh,
        in_specs=(
            P("sx", "sy", "depth"),
            P(),
            P(),
            P(),
            P(),
            P(),
            P("sx", "sy", "depth"),
            P("sx", "sy"),
        ),
        out_specs=P(None, "sx", "depth", None, "sy"),
        check_vma=False,
    )
```

```python
import functools
import math
import jax
import jax.numpy as jnp
from jax import lax
from jax.experimental import pallas as pl
from jax.experimental.pallas import tpu as pltpu
from jax.sharding import PartitionSpec as P

LOG2E = math.log2(math.e)
VMEM = pl.BlockSpec(memory_space=pltpu.VMEM)
HBM = pl.BlockSpec(memory_space=pltpu.HBM)
MIB = 1024 * 1024
F32, BF16 = jnp.float32, jnp.bfloat16
dot = functools.partial(jnp.dot, preferred_element_type=F32)


def iota(shape, dim):
    return lax.broadcasted_iota(jnp.int32, shape, dim)


def line_pairs(count, shift):
    return [(i, i + 1) for i in range(shift, count - 1, 2)]


def swaps(counts, axis, shift):
    depth_count, count_x, count_y = counts
    index = lambda d, x, y: (d * count_x + x) * count_y + y
    pairs = []
    for x in range(count_x):
        for y in range(count_y):
            ends = [p for p in line_pairs(counts[axis], shift) if (x, y)[axis - 1] in p]
            if not ends:
                pairs += [
                    (index(d, x, y), index(d + 1, x, y)) for d in range(0, depth_count - 1, 2)
                ]
            elif (x, y)[axis - 1] == ends[0][0]:
                other = (ends[0][1], y) if axis == 1 else (x, ends[0][1])
                pairs += [(index(d, x, y), index(d, *other)) for d in range(depth_count)]
    return pairs + [(b, a) for a, b in pairs]


class Place:
    def __init__(self):
        self.depth = lax.axis_index("depth")
        self.half, self.has_x = self.sides("sx")
        self.group, self.has_y = self.sides("sy")

    def sides(self, axis):
        at, last = lax.axis_index(axis), lax.axis_size(axis) - 1
        parity = lax.rem(at, 2)
        upper, lower = at < last, at > 0
        order = (1 - parity, parity)
        either = lambda side: jnp.where(side == 1, upper.astype(jnp.int32), lower.astype(jnp.int32))
        return order, [either(side) == 1 for side in order]


def group_rows(place, rim, g):
    return pl.ds(pl.multiple_of(place.group[g] * rim, rim), rim)


def half_rows(place, rim, h):
    return pl.ds(place.half[h] * rim, rim)


def first_kernel(rim, density, *refs):
    place = Place()
    n_tables = (len(refs) - 6) // 2
    tables, held, coarse = refs[:n_tables], refs[n_tables], refs[n_tables + 1:n_tables + 5]
    tables_out, sems = refs[n_tables + 5:-1], refs[-1]
    copies = []
    for g in range(2):
        for h in range(2):
            rows = density.at[half_rows(place, rim, h), group_rows(place, rim, g), :]
            copies.append(pltpu.make_async_copy(rows, held.at[g, h], sems.at[2 * g + h]))
    for i, (src, dst) in enumerate(zip(tables, tables_out)):
        copies.append(pltpu.make_async_copy(src, dst, sems.at[4 + i]))
    for copy in copies:
        copy.start()
    for g in range(2):
        for h in range(2):
            copies[2 * g + h].wait()
            coarse[2 * g + h][...] = held[g, h].astype(BF16)
    for copy in copies[4:]:
        copy.wait()


def toeplitz(taps, rim):
    return pltpu.roll(jnp.broadcast_to(taps, (rim, 128)), 0, 1, stride=1, stride_axis=0)


def blur_matrices(rim, place, taps):
    size = rim * rim
    wide = 3 * size
    shift = rim.bit_length() - 1
    pick = lambda mask: jnp.where(mask, 1.0, 0.0).astype(BF16)
    row_hi = pick(iota((size, rim), 0) >> shift == iota((size, rim), 1))
    row_lo = pick(iota((size, rim), 0) & (rim - 1) == iota((size, rim), 1))
    col = iota((128, wide), 1)
    src = iota((128, wide), 0)
    k, j, b = col >> 2 * shift, col >> shift & (rim - 1), col & (rim - 1)
    k_x = jnp.where(place.half[0] == 1, k, 2 - k)
    k_y = jnp.where(place.group[0] == 1, k, 2 - k)
    tx = toeplitz(taps[0:1], rim).astype(BF16)
    ty = toeplitz(taps[1:2] * 0.5, rim).astype(BF16)
    full_x = dot(row_hi, dot(tx, pick(k_x * rim + j == src)).astype(BF16))
    full_y = dot(row_lo, dot(ty, pick(k_y * rim + b == src)).astype(BF16))
    r, c = iota((size, size), 0), iota((size, size), 1)
    same_x = r & (rim - 1) == c & (rim - 1)
    same_y = r >> shift == c >> shift
    parts = []
    for full, same in ((full_x, same_x), (full_y, same_y)):
        blocks = [
            jnp.where(same, full[:, n * size:(n + 1) * size], 0.0).astype(BF16) for n in range(3)
        ]
        parts.append(jnp.concatenate(blocks, axis=1))
    return parts


def matrices_kernel(rim, taps, mx, my, padded):
    padded[...] = jnp.zeros(padded.shape, F32)
    padded[0:2, 0:taps.shape[1]] = taps[...].astype(F32)
    mx[...], my[...] = blur_matrices(rim, Place(), padded[...])


def prepare_kernel(
    rim, centre, width, colour, opacity, brick_tf, view_order, table, signs, order_map
):
    place = Place()
    wide = width[...]
    rows = [centre[...], (-LOG2E) / (wide * wide), opacity[...] * (-LOG2E)]
    rows += [colour[c] * 0.5 for c in range(3)]
    rows = jnp.concatenate(rows, axis=0)
    which = iota(rows.shape, 1)
    n = 0
    for g in range(2):
        for h in range(2):
            bricks = brick_tf[place.half[h]]
            bricks = jnp.where(place.group[g] == 0, bricks[0:1], bricks[1:2])
            for bz in range(bricks.shape[1]):
                mine = jnp.where(which == bricks[:, bz:bz + 1], rows, 0.0)
                mine = jnp.sum(mine, axis=1, keepdims=True)
                table[n] = jnp.broadcast_to(mine, table.shape[1:])
                n += 1
            orders = view_order[...]
            orders = jnp.where(place.half[h] == 0, orders[0:1], orders[1:2])
            order = jnp.where(place.group[g] == 0, orders[:, 0:1], orders[:, 1:2])
            signs[g, h] = jnp.broadcast_to(1 - 2 * order, signs.shape[2:])
    block, shape = order_map.shape[1], order_map.shape[1:]
    for n in range(order_map.shape[0]):
        brick = n * block // rim
        orders = view_order[brick:brick + 1]
        order_map[n] = jnp.where(
            iota(shape, 1) < rim,
            jnp.broadcast_to(orders[:, 0:1], shape),
            jnp.broadcast_to(orders[:, 1:2], shape),
        )


def cells_kernel(rim, bumps, g, held, table, signs, shaded, total, optical_s, emitted_s):
    place = Place()
    rows_z = held.shape[4]
    depth = 128
    bricks = rows_z // depth
    lane = iota((rim, 128), 1)
    for h in range(2):
        cells = held.at[g, h]
        for bz in range(bricks):
            zs = slice(bz * depth, (bz + 1) * depth)
            at = (2 * g + h) * bricks + bz
            row = lambda i: jnp.broadcast_to(table[at, i:i + 1, :], (8, depth))[None]
            cen = [row(j) for j in range(bumps)]
            neg = [row(bumps + j) for j in range(bumps)]
            opa = [row(2 * bumps + j) for j in range(bumps)]
            col = [[row((3 + c) * bumps + j) for c in range(3)] for j in range(bumps)]
            for x in range(rim):
                d = cells[x, :, zs].reshape(rim // 8, 8, depth)
                opt, em = None, [None] * 3
                for j in range(bumps):
                    w = d - cen[j]
                    b = jnp.exp2((w * w) * neg[j])
                    opt = opa[j] * b if opt is None else opt + opa[j] * b
                    for c in range(3):
                        em[c] = col[j][c] * b if em[c] is None else em[c] + col[j][c] * b
                rows = slice(x * rim, (x + 1) * rim)
                optical_s[h, rows, zs] = opt.reshape(rim, depth)
                for c in range(3):
                    emitted_s[c, h, rows, zs] = em[c].reshape(rim, depth)
        behind = iota((rows_z, rows_z), 1) - iota((rows_z, rows_z), 0)
        sign = jnp.broadcast_to(signs[g, h][0:1, 0:1], (rows_z, rows_z))
        tri = jnp.where(behind * sign > 0, 1.0, 0.0).astype(BF16)
        opt = optical_s[h]
        hi = opt.astype(BF16)
        lo = (opt - hi.astype(F32)).astype(BF16)
        ahead = dot(hi, tri) + dot(lo, tri)
        weight = jnp.exp2(ahead) * (1.0 - jnp.exp2(opt))
        for c in range(3):
            shaded[c, h] = (weight * emitted_s[c, h]).reshape(rim, rim, rows_z)
        part = rays(opt.reshape(rim, rim, rows_z), place.half[h] * rim, lane)
        total[...] = part if h == 0 else total[...] + part


def rays(cells, first_lane, lane):
    folded = cells[:, :, :128]
    for z in range(128, cells.shape[2], 128):
        folded = folded + cells[:, :, z:z + 128]
    summed = jnp.sum(folded, axis=2, keepdims=True)
    acc = jnp.zeros(lane.shape, F32)
    for x in range(cells.shape[0]):
        acc = jnp.where(lane == first_lane + x, summed[x], acc)
    return acc


def blur_x(place, rim, mx, h, near, halo):
    flat = lambda cells: cells.reshape(rim * rim, cells.shape[-1])
    edge = flat(halo)
    edge = jnp.where(place.has_x[h], edge, jnp.zeros_like(edge))
    own = [flat(near[1]), flat(near[0])]
    blocks = own + [edge] if h == 0 else [edge] + own
    return dot(mx[...], jnp.concatenate(blocks, axis=0)).astype(BF16)


def lit(place, rim, occlusion, shaded, h):
    rows_z = occlusion.shape[1]
    lane = iota((rim, 128), 1)
    shade = (1.0 - jnp.tanh(occlusion)).reshape(rim, rim, rows_z)
    return [rays(shade * shaded[c, h], place.half[h] * rim, lane) for c in range(3)]


def strip_kernel(rim, h, mx, near0, near1, halo, out):
    across = blur_x(Place(), rim, mx, h, [near0[...], near1[...]], halo[...])
    out[...] = across.reshape(out.shape)


def own_kernel(rim, early, strip0, halo0, strip1, halo1, mx, my, near0, near1, *refs):
    place = Place()
    size = rim * rim
    across = [
        blur_x(place, rim, mx, h, [near0[...], near1[...]], halo[...])
        for h, halo in enumerate((halo0, halo1))
    ]
    if early:
        shaded, out, partial = refs
    else:
        partial, *others = refs
    for h, strip in enumerate((strip0, strip1)):
        cells = jnp.concatenate([across[h], strip[...].reshape(size, strip.shape[2])], axis=0)
        partial[0, h] = dot(my[:, :2 * size], cells)
        other = dot(my[:, size:], cells)
        if not early:
            others[h][...] = across[h].reshape(strip.shape)
            partial[1, h] = other
            continue
        for c, part in enumerate(lit(place, rim, other, shaded, h)):
            out[c] = part if h == 0 else out[c] + part


def late(rim, g, my, partial, halo0, halo1, shaded):
    place = Place()
    size = rim * rim
    block = my[:, 2 * size:] if g == 0 else my[:, :size]
    occlusion = []
    for h, halo in enumerate((halo0, halo1)):
        cells = halo[...].reshape(size, halo.shape[2])
        cells = jnp.where(place.has_y[g], cells, jnp.zeros_like(cells))
        occlusion.append(partial[g, h] + dot(block, cells))
    lights = [lit(place, rim, occlusion[h], shaded, h) for h in range(2)]
    return [a + b for a, b in zip(*lights)]


def late_kernel(rim, g, *refs):
    *refs, out = refs
    for c, part in enumerate(late(rim, g, *refs)):
        out[c] = part


def last_kernel(rim, depth_count, *refs):
    refs, (light_e, total0, total1, kept, given, img) = refs[:5], refs[5:]
    place = Place()
    rows = 2 * rim
    at_s, at_e = group_rows(place, rim, 0), group_rows(place, rim, 1)
    for c, part in enumerate(late(rim, 0, *refs)):
        img[c, at_s, :] = part
        img[c, at_e, :] = light_e[c]
    img[3, at_s, :] = jnp.exp2(total0[...])
    img[3, at_e, :] = jnp.exp2(total1[...])
    for c in range(4):
        img[4 + c, :, 0:rows] = img[c].T[:rows, :]
    block = rows // depth_count
    bit = place.depth & 1
    for n in range(depth_count // 2):
        for out, b in ((kept, bit), (given, 1 - bit)):
            out[n] = img[4:8, pl.ds(pl.multiple_of((2 * n + b) * block, block), block), 0:rows]


def merge_kernel(level, order_map, kept, theirs, *outs):
    me = lax.axis_index("depth")
    bit = me >> level & 1
    low = me & (2 << level) - 1
    merged = []
    for n in range(kept.shape[0]):
        mine = (bit == order_map[(n << level + 1) + low])[None]
        front = jnp.where(mine, kept[n], theirs[n])
        back = jnp.where(mine, theirs[n], kept[n])
        merged.append((front[:3] + front[3:] * back[:3], front[3:] * back[3:]))
    if len(merged) == 1:
        colour, through = merged[0]
        outs[0][...] = jnp.concatenate([colour, 1.0 - through]).reshape(outs[0].shape)
        return
    up = me >> level + 1 & 1
    for n in range(len(merged) // 2):
        even, odd = (jnp.concatenate(merged[2 * n + i]) for i in range(2))
        outs[0][n] = jnp.where(up == 1, odd, even)
        outs[1][n] = jnp.where(up == 1, even, odd)


def call(kernel, name, ins, outs, scratch=(), limit=16 * MIB, **more):
    return pl.pallas_call(
        kernel,
        out_shape=outs,
        in_specs=ins,
        out_specs=jax.tree.map(lambda _: VMEM, outs),
        scratch_shapes=list(scratch),
        compiler_params=pltpu.CompilerParams(vmem_limit_bytes=limit),
        name=name,
        **more,
    )


def per_device(
    density, kernel_taps, tf_centre, tf_width, tf_color, tf_opacity, brick_tf, view_order
):
    rows_x, rows_y, rows_z = density.shape
    rim = (kernel_taps.shape[1] - 1) // 2
    bumps = tf_centre.shape[1]
    size = rim * rim
    axes = ("depth", "sx", "sy")
    counts = tuple(lax.axis_size(axis) for axis in axes)
    depth_count, count_y = counts[0], counts[2]
    struct = jax.ShapeDtypeStruct
    block = rows_x // depth_count
    rounds = sum(1 for shift in range(2) if line_pairs(count_y, shift))

    def swap(piece, axis, shift):
        return lax.ppermute(piece, axes, swaps(counts, axis, shift))

    in_hbm = lambda array: pltpu.with_memory_space_constraint(array, pltpu.HBM)
    tables = (
        kernel_taps, tf_centre.T, tf_width.T, tf_color.T, tf_opacity.T, brick_tf, view_order
    )
    piece = struct((rim, rim, rows_z), BF16)
    held, *refs = call(
        functools.partial(first_kernel, rim),
        "first",
        [HBM] * (1 + len(tables)),
        [struct((2, 2, rim, rim, rows_z), F32)]
        + [piece] * 4
        + [struct(t.shape, t.dtype) for t in tables],
        [pltpu.SemaphoreType.DMA((4 + len(tables),))],
    )(in_hbm(density), *[in_hbm(t) for t in tables])
    coarse, tables = [refs[0:2], refs[2:4]], refs[4:]
    bricks = rows_z // 128
    table, signs, order_map = call(
        functools.partial(prepare_kernel, rim),
        "prepare",
        [VMEM] * (len(tables) - 1),
        [struct((4 * bricks, 6 * bumps, 128), F32), struct((2, 2, 8, 128), jnp.int32)]
        + [struct((depth_count, block, rows_y), jnp.int32)],
    )(*tables[1:])
    halo_x = [[swap(coarse[0][h], 1, h) for h in range(2)], None]
    mx, my = call(
        functools.partial(matrices_kernel, rim),
        "matrices",
        [VMEM],
        [struct((size, 3 * size), BF16)] * 2,
        [pltpu.VMEM((8, 128), F32)],
    )(tables[0])
    *others, table, mx = lax.optimization_barrier((*coarse[1], table, mx))
    halo_x[1] = [swap(others[h], 1, h) for h in range(2)]
    strips, halo_y = [], []
    for h in range(2):
        strip = call(functools.partial(strip_kernel, rim, h), f"strip{h}", [VMEM] * 4, piece)(
            mx, *coarse[0], halo_x[0][h]
        )
        strips.append(strip)
        halo_y.append(swap(strip, 2, 0))
    table, first = lax.optimization_barrier((table, strips[0]))
    strips[0] = first
    shaded, total = [None, None], [None, None]
    for g in (1, 0):
        shaded[g], total[g] = call(
            functools.partial(cells_kernel, rim, bumps, g),
            f"cells{g}",
            [VMEM] * 3,
            [struct((3, 2, rim, rim, rows_z), F32), struct((rim, 128), F32)],
            [pltpu.VMEM((2, size, rows_z), F32), pltpu.VMEM((3, 2, size, rows_z), F32)],
            cost_estimate=pl.CostEstimate(
                flops=density.size * (100000 if g == 0 else 1),
                bytes_accessed=density.size,
                transcendentals=density.size * 3,
            ),
        )(held, table, signs)

    early = rounds < 2
    colours = struct((3, rim, 128), F32)
    unlit = struct((2 - early, 2, size, rows_z), F32)
    results = call(
        functools.partial(own_kernel, rim, early),
        "own",
        [VMEM] * (9 if early else 8),
        [colours, unlit] if early else [unlit, piece, piece],
    )(
        strips[0], halo_x[1][0], strips[1], halo_x[1][1], mx, my, *coarse[1], *([shaded[1]] if early else [])
    )
    if early:
        light, partial = results
    else:
        partial, *others = results
        light = call(functools.partial(late_kernel, rim, 1), "late", [VMEM] * 5, colours)(
            my, partial, *[swap(strip, 2, 1) for strip in others], shaded[1]
        )
    kept, given = call(
        functools.partial(last_kernel, rim, depth_count),
        "last",
        [VMEM] * 8,
        [struct((depth_count // 2, 4, block, rows_y), F32)] * 2,
        [pltpu.VMEM((8, rows_y, 128), F32)],
    )(my, partial, *halo_y, shaded[0], light, *total)
    level = 0
    while True:
        theirs = lax.ppermute(given, "depth", [(i, i ^ 1 << level) for i in range(depth_count)])
        left = kept.shape[0] // 2
        outs = [struct((left, 4, block, rows_y), F32)] * 2
        merged = call(
            functools.partial(merge_kernel, level),
            f"merge{level}",
            [VMEM] * 3,
            outs if left else struct((4, 1, 1, block, rows_y), F32),
            limit=2 * MIB,
        )(order_map, kept, theirs)
        if not left:
            return merged
        kept, given = merged
        level += 1


def solution(mesh):
    return jax.shard_map(
        per_device,
        mesh=mesh,
        in_specs=(
            P("sx", "sy", "depth"),
            P(),
            P(),
            P(),
            P(),
            P(),
            P("sx", "sy", "depth"),
            P("sx", "sy"),
        ),
        out_specs=P(None, "sx", "depth", None, "sy"),
        check_vma=False,
    )
```

```python
import functools
import math
import jax
import jax.numpy as jnp
from jax import lax
from jax.experimental import pallas as pl
from jax.experimental.pallas import tpu as pltpu
from jax.sharding import PartitionSpec as P

LOG2E = math.log2(math.e)
VMEM = pl.BlockSpec(memory_space=pltpu.VMEM)
HBM = pl.BlockSpec(memory_space=pltpu.HBM)
MIB = 1024 * 1024
F32, BF16 = jnp.float32, jnp.bfloat16
dot = functools.partial(jnp.dot, preferred_element_type=F32)


def iota(shape, dim):
    return lax.broadcasted_iota(jnp.int32, shape, dim)


def line_pairs(count, shift):
    return [(i, i + 1) for i in range(shift, count - 1, 2)]


def swaps(counts, axis, shift):
    depth_count, count_x, count_y = counts
    index = lambda d, x, y: (d * count_x + x) * count_y + y
    pairs = []
    for x in range(count_x):
        for y in range(count_y):
            ends = [p for p in line_pairs(counts[axis], shift) if (x, y)[axis - 1] in p]
            if not ends:
                pairs += [
                    (index(d, x, y), index(d + 1, x, y)) for d in range(0, depth_count - 1, 2)
                ]
            elif (x, y)[axis - 1] == ends[0][0]:
                other = (ends[0][1], y) if axis == 1 else (x, ends[0][1])
                pairs += [(index(d, x, y), index(d, *other)) for d in range(depth_count)]
    return pairs + [(b, a) for a, b in pairs]


class Place:
    def __init__(self):
        self.depth = lax.axis_index("depth")
        self.half, self.has_x = self.sides("sx", 1)
        self.group, self.has_y = self.sides("sy", 0)

    def sides(self, axis, shift):
        at, last = lax.axis_index(axis), lax.axis_size(axis) - 1
        parity = lax.rem(at + shift, 2)
        upper, lower = at < last, at > 0
        order = (1 - parity, parity)
        either = lambda side: jnp.where(side == 1, upper.astype(jnp.int32), lower.astype(jnp.int32))
        return order, [either(side) == 1 for side in order]


def group_rows(place, rim, g):
    return pl.ds(pl.multiple_of(place.group[g] * rim, rim), rim)


def half_rows(place, rim, h):
    return pl.ds(place.half[h] * rim, rim)


def first_kernel(rim, density, *refs):
    place = Place()
    n_tables = (len(refs) - 6) // 2
    tables, held, coarse = refs[:n_tables], refs[n_tables], refs[n_tables + 1:n_tables + 5]
    tables_out, sems = refs[n_tables + 5:-1], refs[-1]
    copies = []
    for g in range(2):
        for h in range(2):
            rows = density.at[half_rows(place, rim, h), group_rows(place, rim, g), :]
            copies.append(pltpu.make_async_copy(rows, held.at[g, h], sems.at[2 * g + h]))
    for i, (src, dst) in enumerate(zip(tables, tables_out)):
        copies.append(pltpu.make_async_copy(src, dst, sems.at[4 + i]))
    for copy in copies:
        copy.start()
    for g in range(2):
        for h in range(2):
            copies[2 * g + h].wait()
            coarse[2 * g + h][...] = held[g, h].astype(BF16)
    for copy in copies[4:]:
        copy.wait()


def toeplitz(taps, rim):
    return pltpu.roll(jnp.broadcast_to(taps, (rim, 128)), 0, 1, stride=1, stride_axis=0)


def blur_matrices(rim, place, taps):
    size = rim * rim
    wide = 3 * size
    shift = rim.bit_length() - 1
    pick = lambda mask: jnp.where(mask, 1.0, 0.0).astype(BF16)
    row_hi = pick(iota((size, rim), 0) >> shift == iota((size, rim), 1))
    row_lo = pick(iota((size, rim), 0) & (rim - 1) == iota((size, rim), 1))
    col = iota((128, wide), 1)
    src = iota((128, wide), 0)
    k, j, b = col >> 2 * shift, col >> shift & (rim - 1), col & (rim - 1)
    k_x = jnp.where(place.half[0] == 1, k, 2 - k)
    k_y = jnp.where(place.group[0] == 1, k, 2 - k)
    tx = toeplitz(taps[0:1], rim).astype(BF16)
    ty = toeplitz(taps[1:2] * 0.5, rim).astype(BF16)
    full_x = dot(row_hi, dot(tx, pick(k_x * rim + j == src)).astype(BF16))
    full_y = dot(row_lo, dot(ty, pick(k_y * rim + b == src)).astype(BF16))
    r, c = iota((size, size), 0), iota((size, size), 1)
    same_x = r & (rim - 1) == c & (rim - 1)
    same_y = r >> shift == c >> shift
    parts = []
    for full, same in ((full_x, same_x), (full_y, same_y)):
        blocks = [
            jnp.where(same, full[:, n * size:(n + 1) * size], 0.0).astype(BF16) for n in range(3)
        ]
        parts.append(jnp.concatenate(blocks, axis=1))
    return parts


def matrices_kernel(rim, taps, mx, my, padded):
    padded[...] = jnp.zeros(padded.shape, F32)
    padded[0:2, 0:taps.shape[1]] = taps[...].astype(F32)
    mx[...], my[...] = blur_matrices(rim, Place(), padded[...])


def prepare_kernel(
    rim, centre, width, colour, opacity, brick_tf, view_order, table, signs, order_map
):
    place = Place()
    wide = width[...]
    rows = [centre[...], (-LOG2E) / (wide * wide), opacity[...] * (-LOG2E)]
    rows += [colour[c] * 0.5 for c in range(3)]
    rows = jnp.concatenate(rows, axis=0)
    which = iota(rows.shape, 1)
    n = 0
    for g in range(2):
        for h in range(2):
            bricks = brick_tf[place.half[h]]
            bricks = jnp.where(place.group[g] == 0, bricks[0:1], bricks[1:2])
            for bz in range(bricks.shape[1]):
                mine = jnp.where(which == bricks[:, bz:bz + 1], rows, 0.0)
                mine = jnp.sum(mine, axis=1, keepdims=True)
                table[n] = jnp.broadcast_to(mine, table.shape[1:])
                n += 1
            orders = view_order[...]
            orders = jnp.where(place.half[h] == 0, orders[0:1], orders[1:2])
            order = jnp.where(place.group[g] == 0, orders[:, 0:1], orders[:, 1:2])
            signs[g, h] = jnp.broadcast_to(1 - 2 * order, signs.shape[2:])
    block, shape = order_map.shape[1], order_map.shape[1:]
    for n in range(order_map.shape[0]):
        brick = n * block // rim
        orders = view_order[brick:brick + 1]
        order_map[n] = jnp.where(
            iota(shape, 1) < rim,
            jnp.broadcast_to(orders[:, 0:1], shape),
            jnp.broadcast_to(orders[:, 1:2], shape),
        )


def cells_kernel(rim, bumps, g, held, table, signs, shaded, total, optical_s, emitted_s):
    place = Place()
    rows_z = held.shape[4]
    depth = 128
    bricks = rows_z // depth
    lane = iota((rim, 128), 1)
    for h in range(2):
        cells = held.at[g, h]
        for bz in range(bricks):
            zs = slice(bz * depth, (bz + 1) * depth)
            at = (2 * g + h) * bricks + bz
            row = lambda i: jnp.broadcast_to(table[at, i:i + 1, :], (8, depth))[None]
            cen = [row(j) for j in range(bumps)]
            neg = [row(bumps + j) for j in range(bumps)]
            opa = [row(2 * bumps + j) for j in range(bumps)]
            col = [[row((3 + c) * bumps + j) for c in range(3)] for j in range(bumps)]
            for x in range(rim):
                d = cells[x, :, zs].reshape(rim // 8, 8, depth)
                opt, em = None, [None] * 3
                for j in range(bumps):
                    w = d - cen[j]
                    b = jnp.exp2((w * w) * neg[j])
                    opt = opa[j] * b if opt is None else opt + opa[j] * b
                    for c in range(3):
                        em[c] = col[j][c] * b if em[c] is None else em[c] + col[j][c] * b
                rows = slice(x * rim, (x + 1) * rim)
                optical_s[h, rows, zs] = opt.reshape(rim, depth)
                for c in range(3):
                    emitted_s[c, h, rows, zs] = em[c].reshape(rim, depth)
        behind = iota((rows_z, rows_z), 1) - iota((rows_z, rows_z), 0)
        sign = jnp.broadcast_to(signs[g, h][0:1, 0:1], (rows_z, rows_z))
        tri = jnp.where(behind * sign > 0, 1.0, 0.0).astype(BF16)
        opt = optical_s[h]
        hi = opt.astype(BF16)
        lo = (opt - hi.astype(F32)).astype(BF16)
        ahead = dot(hi, tri) + dot(lo, tri)
        weight = jnp.exp2(ahead) * (1.0 - jnp.exp2(opt))
        for c in range(3):
            shaded[c, h] = (weight * emitted_s[c, h]).reshape(rim, rim, rows_z)
        part = rays(opt.reshape(rim, rim, rows_z), place.half[h] * rim, lane)
        total[...] = part if h == 0 else total[...] + part


def rays(cells, first_lane, lane):
    folded = cells[:, :, :128]
    for z in range(128, cells.shape[2], 128):
        folded = folded + cells[:, :, z:z + 128]
    summed = jnp.sum(folded, axis=2, keepdims=True)
    acc = jnp.zeros(lane.shape, F32)
    for x in range(cells.shape[0]):
        acc = jnp.where(lane == first_lane + x, summed[x], acc)
    return acc


def blur_x(place, rim, mx, h, near, halo):
    flat = lambda cells: cells.reshape(rim * rim, cells.shape[-1])
    edge = flat(halo)
    edge = jnp.where(place.has_x[h], edge, jnp.zeros_like(edge))
    own = [flat(near[1]), flat(near[0])]
    blocks = own + [edge] if h == 0 else [edge] + own
    return dot(mx[...], jnp.concatenate(blocks, axis=0)).astype(BF16)


def lit(place, rim, occlusion, shaded, h):
    rows_z = occlusion.shape[1]
    lane = iota((rim, 128), 1)
    shade = (1.0 - jnp.tanh(occlusion)).reshape(rim, rim, rows_z)
    return [rays(shade * shaded[c, h], place.half[h] * rim, lane) for c in range(3)]


def strip_kernel(rim, h, mx, near0, near1, halo, out):
    across = blur_x(Place(), rim, mx, h, [near0[...], near1[...]], halo[...])
    out[...] = across.reshape(out.shape)


def own_kernel(rim, early, strip0, halo0, strip1, halo1, mx, my, near0, near1, *refs):
    place = Place()
    size = rim * rim
    across = [
        blur_x(place, rim, mx, h, [near0[...], near1[...]], halo[...])
        for h, halo in enumerate((halo0, halo1))
    ]
    if early:
        shaded, out, partial = refs
    else:
        partial, *others = refs
    for h, strip in enumerate((strip0, strip1)):
        cells = jnp.concatenate([across[h], strip[...].reshape(size, strip.shape[2])], axis=0)
        partial[0, h] = dot(my[:, :2 * size], cells)
        other = dot(my[:, size:], cells)
        if not early:
            others[h][...] = across[h].reshape(strip.shape)
            partial[1, h] = other
            continue
        for c, part in enumerate(lit(place, rim, other, shaded, h)):
            out[c] = part if h == 0 else out[c] + part


def late(rim, g, my, partial, halo0, halo1, shaded):
    place = Place()
    size = rim * rim
    block = my[:, 2 * size:] if g == 0 else my[:, :size]
    occlusion = []
    for h, halo in enumerate((halo0, halo1)):
        cells = halo[...].reshape(size, halo.shape[2])
        cells = jnp.where(place.has_y[g], cells, jnp.zeros_like(cells))
        occlusion.append(partial[g, h] + dot(block, cells))
    lights = [lit(place, rim, occlusion[h], shaded, h) for h in range(2)]
    return [a + b for a, b in zip(*lights)]


def late_kernel(rim, g, *refs):
    *refs, out = refs
    for c, part in enumerate(late(rim, g, *refs)):
        out[c] = part


def last_kernel(rim, depth_count, *refs):
    refs, (light_e, total0, total1, kept, given, img) = refs[:5], refs[5:]
    place = Place()
    rows = 2 * rim
    at_s, at_e = group_rows(place, rim, 0), group_rows(place, rim, 1)
    for c, part in enumerate(late(rim, 0, *refs)):
        img[c, at_s, :] = part
        img[c, at_e, :] = light_e[c]
    img[3, at_s, :] = jnp.exp2(total0[...])
    img[3, at_e, :] = jnp.exp2(total1[...])
    for c in range(4):
        img[4 + c, :, 0:rows] = img[c].T[:rows, :]
    block = rows // depth_count
    bit = place.depth & 1
    for n in range(depth_count // 2):
        for out, b in ((kept, bit), (given, 1 - bit)):
            out[n] = img[4:8, pl.ds(pl.multiple_of((2 * n + b) * block, block), block), 0:rows]


def merge_kernel(level, order_map, kept, theirs, *outs):
    me = lax.axis_index("depth")
    bit = me >> level & 1
    low = me & (2 << level) - 1
    merged = []
    for n in range(kept.shape[0]):
        mine = (bit == order_map[(n << level + 1) + low])[None]
        front = jnp.where(mine, kept[n], theirs[n])
        back = jnp.where(mine, theirs[n], kept[n])
        merged.append((front[:3] + front[3:] * back[:3], front[3:] * back[3:]))
    if len(merged) == 1:
        colour, through = merged[0]
        outs[0][...] = jnp.concatenate([colour, 1.0 - through]).reshape(outs[0].shape)
        return
    up = me >> level + 1 & 1
    for n in range(len(merged) // 2):
        even, odd = (jnp.concatenate(merged[2 * n + i]) for i in range(2))
        outs[0][n] = jnp.where(up == 1, odd, even)
        outs[1][n] = jnp.where(up == 1, even, odd)


def call(kernel, name, ins, outs, scratch=(), limit=16 * MIB, **more):
    return pl.pallas_call(
        kernel,
        out_shape=outs,
        in_specs=ins,
        out_specs=jax.tree.map(lambda _: VMEM, outs),
        scratch_shapes=list(scratch),
        compiler_params=pltpu.CompilerParams(vmem_limit_bytes=limit),
        name=name,
        **more,
    )


def per_device(
    density, kernel_taps, tf_centre, tf_width, tf_color, tf_opacity, brick_tf, view_order
):
    rows_x, rows_y, rows_z = density.shape
    rim = (kernel_taps.shape[1] - 1) // 2
    bumps = tf_centre.shape[1]
    size = rim * rim
    axes = ("depth", "sx", "sy")
    counts = tuple(lax.axis_size(axis) for axis in axes)
    depth_count, count_y = counts[0], counts[2]
    struct = jax.ShapeDtypeStruct
    block = rows_x // depth_count
    rounds = sum(1 for shift in range(2) if line_pairs(count_y, shift))

    def swap(piece, axis, shift):
        return lax.ppermute(piece, axes, swaps(counts, axis, shift))

    in_hbm = lambda array: pltpu.with_memory_space_constraint(array, pltpu.HBM)
    tables = (
        kernel_taps, tf_centre.T, tf_width.T, tf_color.T, tf_opacity.T, brick_tf, view_order
    )
    piece = struct((rim, rim, rows_z), BF16)
    held, *refs = call(
        functools.partial(first_kernel, rim),
        "first",
        [HBM] * (1 + len(tables)),
        [struct((2, 2, rim, rim, rows_z), F32)]
        + [piece] * 4
        + [struct(t.shape, t.dtype) for t in tables],
        [pltpu.SemaphoreType.DMA((4 + len(tables),))],
    )(in_hbm(density), *[in_hbm(t) for t in tables])
    coarse, tables = [refs[0:2], refs[2:4]], refs[4:]
    bricks = rows_z // 128
    table, signs, order_map = call(
        functools.partial(prepare_kernel, rim),
        "prepare",
        [VMEM] * (len(tables) - 1),
        [struct((4 * bricks, 6 * bumps, 128), F32), struct((2, 2, 8, 128), jnp.int32)]
        + [struct((depth_count, block, rows_y), jnp.int32)],
    )(*tables[1:])
    halo_x = [[swap(coarse[0][h], 1, 1 - h) for h in range(2)], None]
    mx, my = call(
        functools.partial(matrices_kernel, rim),
        "matrices",
        [VMEM],
        [struct((size, 3 * size), BF16)] * 2,
        [pltpu.VMEM((8, 128), F32)],
    )(tables[0])
    *others, table, mx = lax.optimization_barrier((*coarse[1], table, mx))
    halo_x[1] = [swap(others[h], 1, 1 - h) for h in range(2)]
    strips, halo_y = [], []
    for h in range(2):
        strip = call(functools.partial(strip_kernel, rim, h), f"strip{h}", [VMEM] * 4, piece)(
            mx, *coarse[0], halo_x[0][h]
        )
        strips.append(strip)
        halo_y.append(swap(strip, 2, 0))
    table, first = lax.optimization_barrier((table, strips[0]))
    strips[0] = first
    shaded, total = [None, None], [None, None]
    for g in (1, 0):
        shaded[g], total[g] = call(
            functools.partial(cells_kernel, rim, bumps, g),
            f"cells{g}",
            [VMEM] * 3,
            [struct((3, 2, rim, rim, rows_z), F32), struct((rim, 128), F32)],
            [pltpu.VMEM((2, size, rows_z), F32), pltpu.VMEM((3, 2, size, rows_z), F32)],
            cost_estimate=pl.CostEstimate(
                flops=density.size * (100000 if g == 0 else 1),
                bytes_accessed=density.size,
                transcendentals=density.size * 3,
            ),
        )(held, table, signs)

    early = rounds < 2
    colours = struct((3, rim, 128), F32)
    unlit = struct((2 - early, 2, size, rows_z), F32)
    results = call(
        functools.partial(own_kernel, rim, early),
        "own",
        [VMEM] * (9 if early else 8),
        [colours, unlit] if early else [unlit, piece, piece],
    )(
        strips[0], halo_x[1][0], strips[1], halo_x[1][1], mx, my, *coarse[1], *([shaded[1]] if early else [])
    )
    if early:
        light, partial = results
    else:
        partial, *others = results
        light = call(functools.partial(late_kernel, rim, 1), "late", [VMEM] * 5, colours)(
            my, partial, *[swap(strip, 2, 1) for strip in others], shaded[1]
        )
    kept, given = call(
        functools.partial(last_kernel, rim, depth_count),
        "last",
        [VMEM] * 8,
        [struct((depth_count // 2, 4, block, rows_y), F32)] * 2,
        [pltpu.VMEM((8, rows_y, 128), F32)],
    )(my, partial, *halo_y, shaded[0], light, *total)
    level = 0
    while True:
        theirs = lax.ppermute(given, "depth", [(i, i ^ 1 << level) for i in range(depth_count)])
        left = kept.shape[0] // 2
        outs = [struct((left, 4, block, rows_y), F32)] * 2
        merged = call(
            functools.partial(merge_kernel, level),
            f"merge{level}",
            [VMEM] * 3,
            outs if left else struct((4, 1, 1, block, rows_y), F32),
            limit=2 * MIB,
        )(order_map, kept, theirs)
        if not left:
            return merged
        kept, given = merged
        level += 1


def solution(mesh):
    return jax.shard_map(
        per_device,
        mesh=mesh,
        in_specs=(
            P("sx", "sy", "depth"),
            P(),
            P(),
            P(),
            P(),
            P(),
            P("sx", "sy", "depth"),
            P("sx", "sy"),
        ),
        out_specs=P(None, "sx", "depth", None, "sy"),
        check_vma=False,
    )
```

```python
import functools
import math
import jax
import jax.numpy as jnp
from jax import lax
from jax.experimental import pallas as pl
from jax.experimental.pallas import tpu as pltpu
from jax.sharding import PartitionSpec as P

LOG2E = math.log2(math.e)
VMEM = pl.BlockSpec(memory_space=pltpu.VMEM)
HBM = pl.BlockSpec(memory_space=pltpu.HBM)
MIB = 1024 * 1024
F32, BF16 = jnp.float32, jnp.bfloat16
dot = functools.partial(jnp.dot, preferred_element_type=F32)


def iota(shape, dim):
    return lax.broadcasted_iota(jnp.int32, shape, dim)


def line_pairs(count, shift):
    return [(i, i + 1) for i in range(shift, count - 1, 2)]


def swaps(counts, axis, shift):
    depth_count, count_x, count_y = counts
    index = lambda d, x, y: (d * count_x + x) * count_y + y
    pairs = []
    for x in range(count_x):
        for y in range(count_y):
            ends = [p for p in line_pairs(counts[axis], shift) if (x, y)[axis - 1] in p]
            if not ends:
                pairs += [
                    (index(d, x, y), index(d + 1, x, y)) for d in range(0, depth_count - 1, 2)
                ]
            elif (x, y)[axis - 1] == ends[0][0]:
                other = (ends[0][1], y) if axis == 1 else (x, ends[0][1])
                pairs += [(index(d, x, y), index(d, *other)) for d in range(depth_count)]
    return pairs + [(b, a) for a, b in pairs]


class Place:
    def __init__(self):
        self.depth = lax.axis_index("depth")
        self.half, self.has_x = self.sides("sx", 1)
        self.group, self.has_y = self.sides("sy", 0)

    def sides(self, axis, shift):
        at, last = lax.axis_index(axis), lax.axis_size(axis) - 1
        parity = lax.rem(at + shift, 2)
        upper, lower = at < last, at > 0
        order = (1 - parity, parity)
        either = lambda side: jnp.where(side == 1, upper.astype(jnp.int32), lower.astype(jnp.int32))
        return order, [either(side) == 1 for side in order]


def group_rows(place, rim, g):
    return pl.ds(pl.multiple_of(place.group[g] * rim, rim), rim)


def half_rows(place, rim, h):
    return pl.ds(place.half[h] * rim, rim)


def first_kernel(rim, density, *refs):
    place = Place()
    tables, held, coarse, refs = refs[:7], refs[7], refs[8:12], refs[12:]
    mx, my, table, signs, order_map, *local_tables, padded, sems = refs
    copies = []
    for i, (src, dst) in enumerate(zip(tables, local_tables)):
        copies.append(pltpu.make_async_copy(src, dst, sems.at[4 + i]))
    parts = []
    for g in range(2):
        for h in range(2):
            rows = density.at[half_rows(place, rim, h), group_rows(place, rim, g), :]
            parts.append(pltpu.make_async_copy(rows, held.at[g, h], sems.at[2 * g + h]))
    for copy in copies + parts:
        copy.start()
    for copy in copies:
        copy.wait()
    taps, *local_tables = local_tables
    padded[...] = jnp.zeros(padded.shape, F32)
    padded[0:2, 0:taps.shape[1]] = taps[...].astype(F32)
    mx[...], my[...] = blur_matrices(rim, place, padded[...])
    look_up(rim, place, *local_tables, table, signs, order_map)
    for g in range(2):
        for h in range(2):
            parts[2 * g + h].wait()
            coarse[2 * g + h][...] = held[g, h].astype(BF16)


def toeplitz(taps, rim):
    return pltpu.roll(jnp.broadcast_to(taps, (rim, 128)), 0, 1, stride=1, stride_axis=0)


def blur_matrices(rim, place, taps):
    size = rim * rim
    wide = 3 * size
    shift = rim.bit_length() - 1
    pick = lambda mask: jnp.where(mask, 1.0, 0.0).astype(BF16)
    row_hi = pick(iota((size, rim), 0) >> shift == iota((size, rim), 1))
    row_lo = pick(iota((size, rim), 0) & (rim - 1) == iota((size, rim), 1))
    col = iota((128, wide), 1)
    src = iota((128, wide), 0)
    k, j, b = col >> 2 * shift, col >> shift & (rim - 1), col & (rim - 1)
    k_x = jnp.where(place.half[0] == 1, k, 2 - k)
    k_y = jnp.where(place.group[0] == 1, k, 2 - k)
    tx = toeplitz(taps[0:1], rim).astype(BF16)
    ty = toeplitz(taps[1:2] * 0.5, rim).astype(BF16)
    full_x = dot(row_hi, dot(tx, pick(k_x * rim + j == src)).astype(BF16))
    full_y = dot(row_lo, dot(ty, pick(k_y * rim + b == src)).astype(BF16))
    r, c = iota((size, size), 0), iota((size, size), 1)
    same_x = r & (rim - 1) == c & (rim - 1)
    same_y = r >> shift == c >> shift
    parts = []
    for full, same in ((full_x, same_x), (full_y, same_y)):
        blocks = [
            jnp.where(same, full[:, n * size:(n + 1) * size], 0.0).astype(BF16) for n in range(3)
        ]
        parts.append(jnp.concatenate(blocks, axis=1))
    return parts


def look_up(
    rim, place, centre, width, colour, opacity, brick_tf, view_order, table, signs, order_map
):
    wide = width[...]
    rows = [centre[...], (-LOG2E) / (wide * wide), opacity[...] * (-LOG2E)]
    rows += [colour[c] * 0.5 for c in range(3)]
    rows = jnp.concatenate(rows, axis=0)
    which = iota(rows.shape, 1)
    n = 0
    for g in range(2):
        for h in range(2):
            bricks = brick_tf[place.half[h]]
            bricks = jnp.where(place.group[g] == 0, bricks[0:1], bricks[1:2])
            for bz in range(bricks.shape[1]):
                mine = jnp.where(which == bricks[:, bz:bz + 1], rows, 0.0)
                mine = jnp.sum(mine, axis=1, keepdims=True)
                table[n] = jnp.broadcast_to(mine, table.shape[1:])
                n += 1
            orders = view_order[...]
            orders = jnp.where(place.half[h] == 0, orders[0:1], orders[1:2])
            order = jnp.where(place.group[g] == 0, orders[:, 0:1], orders[:, 1:2])
            signs[g, h] = jnp.broadcast_to(1 - 2 * order, signs.shape[2:])
    block, shape = order_map.shape[1], order_map.shape[1:]
    for n in range(order_map.shape[0]):
        brick = n * block // rim
        orders = view_order[brick:brick + 1]
        order_map[n] = jnp.where(
            iota(shape, 1) < rim,
            jnp.broadcast_to(orders[:, 0:1], shape),
            jnp.broadcast_to(orders[:, 1:2], shape),
        )


def cells_kernel(rim, bumps, g, held, table, signs, shaded, total, optical_s, emitted_s):
    place = Place()
    rows_z = held.shape[4]
    depth = 128
    bricks = rows_z // depth
    lane = iota((rim, 128), 1)
    for h in range(2):
        cells = held.at[g, h]
        for bz in range(bricks):
            zs = slice(bz * depth, (bz + 1) * depth)
            at = (2 * g + h) * bricks + bz
            row = lambda i: jnp.broadcast_to(table[at, i:i + 1, :], (8, depth))[None]
            cen = [row(j) for j in range(bumps)]
            neg = [row(bumps + j) for j in range(bumps)]
            opa = [row(2 * bumps + j) for j in range(bumps)]
            col = [[row((3 + c) * bumps + j) for c in range(3)] for j in range(bumps)]
            for x in range(rim):
                d = cells[x, :, zs].reshape(rim // 8, 8, depth)
                opt, em = None, [None] * 3
                for j in range(bumps):
                    w = d - cen[j]
                    b = jnp.exp2((w * w) * neg[j])
                    opt = opa[j] * b if opt is None else opt + opa[j] * b
                    for c in range(3):
                        em[c] = col[j][c] * b if em[c] is None else em[c] + col[j][c] * b
                rows = slice(x * rim, (x + 1) * rim)
                optical_s[h, rows, zs] = opt.reshape(rim, depth)
                for c in range(3):
                    emitted_s[c, h, rows, zs] = em[c].reshape(rim, depth)
        behind = iota((rows_z, rows_z), 1) - iota((rows_z, rows_z), 0)
        sign = jnp.broadcast_to(signs[g, h][0:1, 0:1], (rows_z, rows_z))
        tri = jnp.where(behind * sign > 0, 1.0, 0.0).astype(BF16)
        opt = optical_s[h]
        hi = opt.astype(BF16)
        lo = (opt - hi.astype(F32)).astype(BF16)
        ahead = dot(hi, tri) + dot(lo, tri)
        weight = jnp.exp2(ahead) * (1.0 - jnp.exp2(opt))
        for c in range(3):
            shaded[c, h] = (weight * emitted_s[c, h]).reshape(rim, rim, rows_z)
        part = rays(opt.reshape(rim, rim, rows_z), place.half[h] * rim, lane)
        total[...] = part if h == 0 else total[...] + part


def rays(cells, first_lane, lane):
    folded = cells[:, :, :128]
    for z in range(128, cells.shape[2], 128):
        folded = folded + cells[:, :, z:z + 128]
    summed = jnp.sum(folded, axis=2, keepdims=True)
    acc = jnp.zeros(lane.shape, F32)
    for x in range(cells.shape[0]):
        acc = jnp.where(lane == first_lane + x, summed[x], acc)
    return acc


def blur_x(place, rim, mx, h, near, halo):
    flat = lambda cells: cells.reshape(rim * rim, cells.shape[-1])
    edge = flat(halo)
    edge = jnp.where(place.has_x[h], edge, jnp.zeros_like(edge))
    own = [flat(near[1]), flat(near[0])]
    blocks = own + [edge] if h == 0 else [edge] + own
    return dot(mx[...], jnp.concatenate(blocks, axis=0)).astype(BF16)


def lit(place, rim, occlusion, shaded, h):
    rows_z = occlusion.shape[1]
    lane = iota((rim, 128), 1)
    shade = (1.0 - jnp.tanh(occlusion)).reshape(rim, rim, rows_z)
    return [rays(shade * shaded[c, h], place.half[h] * rim, lane) for c in range(3)]


def strip_kernel(rim, h, mx, near0, near1, halo, out):
    across = blur_x(Place(), rim, mx, h, [near0[...], near1[...]], halo[...])
    out[...] = across.reshape(out.shape)


def own_kernel(rim, early, strip0, halo1, strip1, halo0, mx, my, near0, near1, *refs):
    place = Place()
    size = rim * rim
    across = [
        blur_x(place, rim, mx, h, [near0[...], near1[...]], halo[...])
        for h, halo in enumerate((halo0, halo1))
    ]
    if early:
        shaded, out, partial = refs
    else:
        partial, *others = refs
    for h, strip in enumerate((strip0, strip1)):
        cells = jnp.concatenate([across[h], strip[...].reshape(size, strip.shape[2])], axis=0)
        partial[0, h] = dot(my[:, :2 * size], cells)
        other = dot(my[:, size:], cells)
        if not early:
            others[h][...] = across[h].reshape(strip.shape)
            partial[1, h] = other
            continue
        for c, part in enumerate(lit(place, rim, other, shaded, h)):
            out[c] = part if h == 0 else out[c] + part


def late(rim, g, my, partial, halo0, halo1, shaded):
    place = Place()
    size = rim * rim
    block = my[:, 2 * size:] if g == 0 else my[:, :size]
    occlusion = []
    for h, halo in enumerate((halo0, halo1)):
        cells = halo[...].reshape(size, halo.shape[2])
        cells = jnp.where(place.has_y[g], cells, jnp.zeros_like(cells))
        occlusion.append(partial[g, h] + dot(block, cells))
    lights = [lit(place, rim, occlusion[h], shaded, h) for h in range(2)]
    return [a + b for a, b in zip(*lights)]


def late_kernel(rim, g, *refs):
    *refs, out = refs
    for c, part in enumerate(late(rim, g, *refs)):
        out[c] = part


def last_kernel(rim, depth_count, *refs):
    refs, (light_e, total0, total1, kept, given, img) = refs[:5], refs[5:]
    place = Place()
    rows = 2 * rim
    at_s, at_e = group_rows(place, rim, 0), group_rows(place, rim, 1)
    for c, part in enumerate(late(rim, 0, *refs)):
        img[c, at_s, :] = part
        img[c, at_e, :] = light_e[c]
    img[3, at_s, :] = jnp.exp2(total0[...])
    img[3, at_e, :] = jnp.exp2(total1[...])
    for c in range(4):
        img[4 + c, :, 0:rows] = img[c].T[:rows, :]
    block = rows // depth_count
    bit = place.depth & 1
    for n in range(depth_count // 2):
        for out, b in ((kept, bit), (given, 1 - bit)):
            out[n] = img[4:8, pl.ds(pl.multiple_of((2 * n + b) * block, block), block), 0:rows]


def merge_kernel(level, order_map, kept, theirs, *outs):
    me = lax.axis_index("depth")
    bit = me >> level & 1
    low = me & (2 << level) - 1
    merged = []
    for n in range(kept.shape[0]):
        mine = (bit == order_map[(n << level + 1) + low])[None]
        front = jnp.where(mine, kept[n], theirs[n])
        back = jnp.where(mine, theirs[n], kept[n])
        merged.append((front[:3] + front[3:] * back[:3], front[3:] * back[3:]))
    if len(merged) == 1:
        colour, through = merged[0]
        outs[0][...] = jnp.concatenate([colour, 1.0 - through]).reshape(outs[0].shape)
        return
    up = me >> level + 1 & 1
    for n in range(len(merged) // 2):
        even, odd = (jnp.concatenate(merged[2 * n + i]) for i in range(2))
        outs[0][n] = jnp.where(up == 1, odd, even)
        outs[1][n] = jnp.where(up == 1, even, odd)


def call(kernel, name, ins, outs, scratch=(), limit=16 * MIB, **more):
    return pl.pallas_call(
        kernel,
        out_shape=outs,
        in_specs=ins,
        out_specs=jax.tree.map(lambda _: VMEM, outs),
        scratch_shapes=list(scratch),
        compiler_params=pltpu.CompilerParams(vmem_limit_bytes=limit),
        name=name,
        **more,
    )


def per_device(
    density, kernel_taps, tf_centre, tf_width, tf_color, tf_opacity, brick_tf, view_order
):
    rows_x, rows_y, rows_z = density.shape
    rim = (kernel_taps.shape[1] - 1) // 2
    bumps = tf_centre.shape[1]
    size = rim * rim
    axes = ("depth", "sx", "sy")
    counts = tuple(lax.axis_size(axis) for axis in axes)
    depth_count, count_y = counts[0], counts[2]
    struct = jax.ShapeDtypeStruct
    block = rows_x // depth_count
    rounds = sum(1 for shift in range(2) if line_pairs(count_y, shift))

    def swap(piece, axis, shift):
        return lax.ppermute(piece, axes, swaps(counts, axis, shift))

    in_hbm = lambda array: pltpu.with_memory_space_constraint(array, pltpu.HBM)
    tables = (
        kernel_taps, tf_centre.T, tf_width.T, tf_color.T, tf_opacity.T, brick_tf, view_order
    )
    piece = struct((rim, rim, rows_z), BF16)
    bricks = rows_z // 128
    held, *refs = call(
        functools.partial(first_kernel, rim),
        "first",
        [HBM] * (1 + len(tables)),
        [struct((2, 2, rim, rim, rows_z), F32)]
        + [piece] * 4
        + [struct((size, 3 * size), BF16)] * 2
        + [struct((4 * bricks, 6 * bumps, 128), F32), struct((2, 2, 8, 128), jnp.int32)]
        + [struct((depth_count, block, rows_y), jnp.int32)],
        [pltpu.VMEM(t.shape, t.dtype) for t in tables]
        + [pltpu.VMEM((8, 128), F32), pltpu.SemaphoreType.DMA((4 + len(tables),))],
    )(in_hbm(density), *[in_hbm(t) for t in tables])
    coarse, (mx, my, table, signs, order_map) = [refs[0:2], refs[2:4]], refs[4:]
    halo_x = [[swap(coarse[g][h], 1, 1 - h) for h in range(2)] for g in range(2)]
    strips, halo_y = [], []
    for h in range(2):
        strip = call(functools.partial(strip_kernel, rim, h), f"strip{h}", [VMEM] * 4, piece)(
            mx, *coarse[0], halo_x[0][h]
        )
        strips.append(strip)
        halo_y.append(swap(strip, 2, 0))
    table, first = lax.optimization_barrier((table, strips[0]))
    strips[0] = first
    shaded, total = [None, None], [None, None]
    for g in (1, 0):
        shaded[g], total[g] = call(
            functools.partial(cells_kernel, rim, bumps, g),
            f"cells{g}",
            [VMEM] * 3,
            [struct((3, 2, rim, rim, rows_z), F32), struct((rim, 128), F32)],
            [pltpu.VMEM((2, size, rows_z), F32), pltpu.VMEM((3, 2, size, rows_z), F32)],
            cost_estimate=pl.CostEstimate(
                flops=density.size * (100000 if g == 0 else 1),
                bytes_accessed=density.size,
                transcendentals=density.size * 3,
            ),
        )(held, table, signs)

    early = rounds < 2
    colours = struct((3, rim, 128), F32)
    unlit = struct((2 - early, 2, size, rows_z), F32)
    results = call(
        functools.partial(own_kernel, rim, early),
        "own",
        [VMEM] * (9 if early else 8),
        [colours, unlit] if early else [unlit, piece, piece],
    )(
        strips[0], halo_x[1][1], strips[1], halo_x[1][0], mx, my, *coarse[1], *([shaded[1]] if early else [])
    )
    if early:
        light, partial = results
    else:
        partial, *others = results
        light = call(functools.partial(late_kernel, rim, 1), "late", [VMEM] * 5, colours)(
            my, partial, *[swap(strip, 2, 1) for strip in others], shaded[1]
        )
    kept, given = call(
        functools.partial(last_kernel, rim, depth_count),
        "last",
        [VMEM] * 8,
        [struct((depth_count // 2, 4, block, rows_y), F32)] * 2,
        [pltpu.VMEM((8, rows_y, 128), F32)],
    )(my, partial, *halo_y, shaded[0], light, *total)
    level = 0
    while True:
        theirs = lax.ppermute(given, "depth", [(i, i ^ 1 << level) for i in range(depth_count)])
        left = kept.shape[0] // 2
        outs = [struct((left, 4, block, rows_y), F32)] * 2
        merged = call(
            functools.partial(merge_kernel, level),
            f"merge{level}",
            [VMEM] * 3,
            outs if left else struct((4, 1, 1, block, rows_y), F32),
            limit=2 * MIB,
        )(order_map, kept, theirs)
        if not left:
            return merged
        kept, given = merged
        level += 1


def solution(mesh):
    return jax.shard_map(
        per_device,
        mesh=mesh,
        in_specs=(
            P("sx", "sy", "depth"),
            P(),
            P(),
            P(),
            P(),
            P(),
            P("sx", "sy", "depth"),
            P("sx", "sy"),
        ),
        out_specs=P(None, "sx", "depth", None, "sy"),
        check_vma=False,
    )
```

```python
import functools
import math
import jax
import jax.numpy as jnp
from jax import lax
from jax.experimental import pallas as pl
from jax.experimental.pallas import tpu as pltpu
from jax.sharding import PartitionSpec as P

LOG2E = math.log2(math.e)
VMEM = pl.BlockSpec(memory_space=pltpu.VMEM)
HBM = pl.BlockSpec(memory_space=pltpu.HBM)
MIB = 1024 * 1024
F32, BF16 = jnp.float32, jnp.bfloat16
dot = functools.partial(jnp.dot, preferred_element_type=F32)


def iota(shape, dim):
    return lax.broadcasted_iota(jnp.int32, shape, dim)


def line_pairs(count, shift):
    return [(i, i + 1) for i in range(shift, count - 1, 2)]


def swaps(counts, axis, shift):
    depth_count, count_x, count_y = counts
    index = lambda d, x, y: (d * count_x + x) * count_y + y
    pairs = []
    for x in range(count_x):
        for y in range(count_y):
            ends = [p for p in line_pairs(counts[axis], shift) if (x, y)[axis - 1] in p]
            if not ends:
                pairs += [
                    (index(d, x, y), index(d + 1, x, y)) for d in range(0, depth_count - 1, 2)
                ]
            elif (x, y)[axis - 1] == ends[0][0]:
                other = (ends[0][1], y) if axis == 1 else (x, ends[0][1])
                pairs += [(index(d, x, y), index(d, *other)) for d in range(depth_count)]
    return pairs + [(b, a) for a, b in pairs]


class Place:
    def __init__(self):
        self.depth = lax.axis_index("depth")
        self.half, self.has_x = self.sides("sx", 0)
        self.group, self.has_y = self.sides("sy", 0)

    def sides(self, axis, shift):
        at, last = lax.axis_index(axis), lax.axis_size(axis) - 1
        parity = lax.rem(at + shift, 2)
        upper, lower = at < last, at > 0
        order = (1 - parity, parity)
        either = lambda side: jnp.where(side == 1, upper.astype(jnp.int32), lower.astype(jnp.int32))
        return order, [either(side) == 1 for side in order]


def group_rows(place, rim, g):
    return pl.ds(pl.multiple_of(place.group[g] * rim, rim), rim)


def half_rows(place, rim, h):
    return pl.ds(place.half[h] * rim, rim)


def first_kernel(rim, density, *refs):
    place = Place()
    tables, held, coarse, refs = refs[:7], refs[7], refs[8:12], refs[12:]
    mx, my, table, signs, order_map, *local_tables, padded, sems = refs
    copies = []
    for i, (src, dst) in enumerate(zip(tables, local_tables)):
        copies.append(pltpu.make_async_copy(src, dst, sems.at[4 + i]))
    parts = []
    for g in range(2):
        for h in range(2):
            rows = density.at[half_rows(place, rim, h), group_rows(place, rim, g), :]
            parts.append(pltpu.make_async_copy(rows, held.at[g, h], sems.at[2 * g + h]))
    for copy in copies + parts:
        copy.start()
    for copy in copies:
        copy.wait()
    taps, *local_tables = local_tables
    padded[...] = jnp.zeros(padded.shape, F32)
    padded[0:2, 0:taps.shape[1]] = taps[...].astype(F32)
    mx[...], my[...] = blur_matrices(rim, place, padded[...])
    look_up(rim, place, *local_tables, table, signs, order_map)
    for g in range(2):
        for h in range(2):
            parts[2 * g + h].wait()
            coarse[2 * g + h][...] = held[g, h].astype(BF16)


def toeplitz(taps, rim):
    return pltpu.roll(jnp.broadcast_to(taps, (rim, 128)), 0, 1, stride=1, stride_axis=0)


def blur_matrices(rim, place, taps):
    size = rim * rim
    wide = 3 * size
    shift = rim.bit_length() - 1
    pick = lambda mask: jnp.where(mask, 1.0, 0.0).astype(BF16)
    row_hi = pick(iota((size, rim), 0) >> shift == iota((size, rim), 1))
    row_lo = pick(iota((size, rim), 0) & (rim - 1) == iota((size, rim), 1))
    col = iota((128, wide), 1)
    src = iota((128, wide), 0)
    k, j, b = col >> 2 * shift, col >> shift & (rim - 1), col & (rim - 1)
    k_x = jnp.where(place.half[0] == 1, k, 2 - k)
    k_y = jnp.where(place.group[0] == 1, k, 2 - k)
    tx = toeplitz(taps[0:1], rim).astype(BF16)
    ty = toeplitz(taps[1:2] * 0.5, rim).astype(BF16)
    full_x = dot(row_hi, dot(tx, pick(k_x * rim + j == src)).astype(BF16))
    full_y = dot(row_lo, dot(ty, pick(k_y * rim + b == src)).astype(BF16))
    r, c = iota((size, size), 0), iota((size, size), 1)
    same_x = r & (rim - 1) == c & (rim - 1)
    same_y = r >> shift == c >> shift
    parts = []
    for full, same in ((full_x, same_x), (full_y, same_y)):
        blocks = [
            jnp.where(same, full[:, n * size:(n + 1) * size], 0.0).astype(BF16) for n in range(3)
        ]
        parts.append(jnp.concatenate(blocks, axis=1))
    return parts


def look_up(
    rim, place, centre, width, colour, opacity, brick_tf, view_order, table, signs, order_map
):
    wide = width[...]
    rows = [centre[...], (-LOG2E) / (wide * wide), opacity[...] * (-LOG2E)]
    rows += [colour[c] * 0.5 for c in range(3)]
    rows = jnp.concatenate(rows, axis=0)
    which = iota(rows.shape, 1)
    n = 0
    for g in range(2):
        for h in range(2):
            bricks = brick_tf[place.half[h]]
            bricks = jnp.where(place.group[g] == 0, bricks[0:1], bricks[1:2])
            for bz in range(bricks.shape[1]):
                mine = jnp.where(which == bricks[:, bz:bz + 1], rows, 0.0)
                mine = jnp.sum(mine, axis=1, keepdims=True)
                table[n] = jnp.broadcast_to(mine, table.shape[1:])
                n += 1
            orders = view_order[...]
            orders = jnp.where(place.half[h] == 0, orders[0:1], orders[1:2])
            order = jnp.where(place.group[g] == 0, orders[:, 0:1], orders[:, 1:2])
            signs[g, h] = jnp.broadcast_to(1 - 2 * order, signs.shape[2:])
    block, shape = order_map.shape[1], order_map.shape[1:]
    for n in range(order_map.shape[0]):
        brick = n * block // rim
        orders = view_order[brick:brick + 1]
        order_map[n] = jnp.where(
            iota(shape, 1) < rim,
            jnp.broadcast_to(orders[:, 0:1], shape),
            jnp.broadcast_to(orders[:, 1:2], shape),
        )


def cells_kernel(rim, bumps, g, held, table, signs, shaded, total, optical_s, emitted_s):
    place = Place()
    rows_z = held.shape[4]
    depth = 128
    bricks = rows_z // depth
    lane = iota((rim, 128), 1)
    for h in range(2):
        cells = held.at[g, h]
        for bz in range(bricks):
            zs = slice(bz * depth, (bz + 1) * depth)
            at = (2 * g + h) * bricks + bz
            row = lambda i: jnp.broadcast_to(table[at, i:i + 1, :], (8, depth))[None]
            cen = [row(j) for j in range(bumps)]
            neg = [row(bumps + j) for j in range(bumps)]
            opa = [row(2 * bumps + j) for j in range(bumps)]
            col = [[row((3 + c) * bumps + j) for c in range(3)] for j in range(bumps)]
            for x in range(rim):
                d = cells[x, :, zs].reshape(rim // 8, 8, depth)
                opt, em = None, [None] * 3
                for j in range(bumps):
                    w = d - cen[j]
                    b = jnp.exp2((w * w) * neg[j])
                    opt = opa[j] * b if opt is None else opt + opa[j] * b
                    for c in range(3):
                        em[c] = col[j][c] * b if em[c] is None else em[c] + col[j][c] * b
                rows = slice(x * rim, (x + 1) * rim)
                optical_s[h, rows, zs] = opt.reshape(rim, depth)
                for c in range(3):
                    emitted_s[c, h, rows, zs] = em[c].reshape(rim, depth)
        behind = iota((rows_z, rows_z), 1) - iota((rows_z, rows_z), 0)
        sign = jnp.broadcast_to(signs[g, h][0:1, 0:1], (rows_z, rows_z))
        tri = jnp.where(behind * sign > 0, 1.0, 0.0).astype(BF16)
        opt = optical_s[h]
        hi = opt.astype(BF16)
        lo = (opt - hi.astype(F32)).astype(BF16)
        ahead = dot(hi, tri) + dot(lo, tri)
        weight = jnp.exp2(ahead) * (1.0 - jnp.exp2(opt))
        for c in range(3):
            shaded[c, h] = (weight * emitted_s[c, h]).reshape(rim, rim, rows_z)
        part = rays(opt.reshape(rim, rim, rows_z), place.half[h] * rim, lane)
        total[...] = part if h == 0 else total[...] + part


def rays(cells, first_lane, lane):
    folded = cells[:, :, :128]
    for z in range(128, cells.shape[2], 128):
        folded = folded + cells[:, :, z:z + 128]
    summed = jnp.sum(folded, axis=2, keepdims=True)
    acc = jnp.zeros(lane.shape, F32)
    for x in range(cells.shape[0]):
        acc = jnp.where(lane == first_lane + x, summed[x], acc)
    return acc


def blur_x(place, rim, mx, h, near, halo):
    flat = lambda cells: cells.reshape(rim * rim, cells.shape[-1])
    edge = flat(halo)
    edge = jnp.where(place.has_x[h], edge, jnp.zeros_like(edge))
    own = [flat(near[1]), flat(near[0])]
    blocks = own + [edge] if h == 0 else [edge] + own
    return dot(mx[...], jnp.concatenate(blocks, axis=0)).astype(BF16)


def lit(place, rim, occlusion, shaded, h):
    rows_z = occlusion.shape[1]
    lane = iota((rim, 128), 1)
    shade = (1.0 - jnp.tanh(occlusion)).reshape(rim, rim, rows_z)
    return [rays(shade * shaded[c, h], place.half[h] * rim, lane) for c in range(3)]


def strip_kernel(rim, h, mx, near0, near1, halo, out):
    across = blur_x(Place(), rim, mx, h, [near0[...], near1[...]], halo[...])
    out[...] = across.reshape(out.shape)


def own_kernel(rim, early, strip0, halo0, strip1, halo1, mx, my, near0, near1, *refs):
    place = Place()
    size = rim * rim
    across = [
        blur_x(place, rim, mx, h, [near0[...], near1[...]], halo[...])
        for h, halo in enumerate((halo0, halo1))
    ]
    if early:
        shaded, out, partial = refs
    else:
        partial, *others = refs
    for h, strip in enumerate((strip0, strip1)):
        cells = jnp.concatenate([across[h], strip[...].reshape(size, strip.shape[2])], axis=0)
        partial[0, h] = dot(my[:, :2 * size], cells)
        other = dot(my[:, size:], cells)
        if not early:
            others[h][...] = across[h].reshape(strip.shape)
            partial[1, h] = other
            continue
        for c, part in enumerate(lit(place, rim, other, shaded, h)):
            out[c] = part if h == 0 else out[c] + part


def late(rim, g, my, partial, halo0, halo1, shaded):
    place = Place()
    size = rim * rim
    block = my[:, 2 * size:] if g == 0 else my[:, :size]
    occlusion = []
    for h, halo in enumerate((halo0, halo1)):
        cells = halo[...].reshape(size, halo.shape[2])
        cells = jnp.where(place.has_y[g], cells, jnp.zeros_like(cells))
        occlusion.append(partial[g, h] + dot(block, cells))
    lights = [lit(place, rim, occlusion[h], shaded, h) for h in range(2)]
    return [a + b for a, b in zip(*lights)]


def late_kernel(rim, g, *refs):
    *refs, out = refs
    for c, part in enumerate(late(rim, g, *refs)):
        out[c] = part


def last_kernel(rim, depth_count, *refs):
    refs, (light_e, total0, total1, kept, given, img) = refs[:5], refs[5:]
    place = Place()
    rows = 2 * rim
    at_s, at_e = group_rows(place, rim, 0), group_rows(place, rim, 1)
    for c, part in enumerate(late(rim, 0, *refs)):
        img[c, at_s, :] = part
        img[c, at_e, :] = light_e[c]
    img[3, at_s, :] = jnp.exp2(total0[...])
    img[3, at_e, :] = jnp.exp2(total1[...])
    for c in range(4):
        img[4 + c, :, 0:rows] = img[c].T[:rows, :]
    block = rows // depth_count
    bit = place.depth & 1
    for n in range(depth_count // 2):
        for out, b in ((kept, bit), (given, 1 - bit)):
            out[n] = img[4:8, pl.ds(pl.multiple_of((2 * n + b) * block, block), block), 0:rows]


def merge_kernel(level, order_map, kept, theirs, *outs):
    me = lax.axis_index("depth")
    bit = me >> level & 1
    low = me & (2 << level) - 1
    merged = []
    for n in range(kept.shape[0]):
        mine = (bit == order_map[(n << level + 1) + low])[None]
        front = jnp.where(mine, kept[n], theirs[n])
        back = jnp.where(mine, theirs[n], kept[n])
        merged.append((front[:3] + front[3:] * back[:3], front[3:] * back[3:]))
    if len(merged) == 1:
        colour, through = merged[0]
        outs[0][...] = jnp.concatenate([colour, 1.0 - through]).reshape(outs[0].shape)
        return
    up = me >> level + 1 & 1
    for n in range(len(merged) // 2):
        even, odd = (jnp.concatenate(merged[2 * n + i]) for i in range(2))
        outs[0][n] = jnp.where(up == 1, odd, even)
        outs[1][n] = jnp.where(up == 1, even, odd)


def call(kernel, name, ins, outs, scratch=(), limit=16 * MIB, **more):
    return pl.pallas_call(
        kernel,
        out_shape=outs,
        in_specs=ins,
        out_specs=jax.tree.map(lambda _: VMEM, outs),
        scratch_shapes=list(scratch),
        compiler_params=pltpu.CompilerParams(vmem_limit_bytes=limit),
        name=name,
        **more,
    )


def per_device(
    density, kernel_taps, tf_centre, tf_width, tf_color, tf_opacity, brick_tf, view_order
):
    rows_x, rows_y, rows_z = density.shape
    rim = (kernel_taps.shape[1] - 1) // 2
    bumps = tf_centre.shape[1]
    size = rim * rim
    axes = ("depth", "sx", "sy")
    counts = tuple(lax.axis_size(axis) for axis in axes)
    depth_count, count_y = counts[0], counts[2]
    struct = jax.ShapeDtypeStruct
    block = rows_x // depth_count
    rounds = sum(1 for shift in range(2) if line_pairs(count_y, shift))

    def swap(piece, axis, shift):
        return lax.ppermute(piece, axes, swaps(counts, axis, shift))

    in_hbm = lambda array: pltpu.with_memory_space_constraint(array, pltpu.HBM)
    tables = (
        kernel_taps, tf_centre.T, tf_width.T, tf_color.T, tf_opacity.T, brick_tf, view_order
    )
    piece = struct((rim, rim, rows_z), BF16)
    bricks = rows_z // 128
    held, *refs = call(
        functools.partial(first_kernel, rim),
        "first",
        [HBM] * (1 + len(tables)),
        [struct((2, 2, rim, rim, rows_z), F32)]
        + [piece] * 4
        + [struct((size, 3 * size), BF16)] * 2
        + [struct((4 * bricks, 6 * bumps, 128), F32), struct((2, 2, 8, 128), jnp.int32)]
        + [struct((depth_count, block, rows_y), jnp.int32)],
        [pltpu.VMEM(t.shape, t.dtype) for t in tables]
        + [pltpu.VMEM((8, 128), F32), pltpu.SemaphoreType.DMA((4 + len(tables),))],
    )(in_hbm(density), *[in_hbm(t) for t in tables])
    coarse, (mx, my, table, signs, order_map) = [refs[0:2], refs[2:4]], refs[4:]
    halo_x = [[swap(coarse[g][h], 1, h) for h in range(2)] for g in range(2)]
    strips, halo_y = [], []
    for h in range(2):
        strip = call(functools.partial(strip_kernel, rim, h), f"strip{h}", [VMEM] * 4, piece)(
            mx, *coarse[0], halo_x[0][h]
        )
        strips.append(strip)
        halo_y.append(swap(strip, 2, 0))
    table, first = lax.optimization_barrier((table, strips[0]))
    strips[0] = first
    shaded, total = [None, None], [None, None]
    for g in (1, 0):
        shaded[g], total[g] = call(
            functools.partial(cells_kernel, rim, bumps, g),
            f"cells{g}",
            [VMEM] * 3,
            [struct((3, 2, rim, rim, rows_z), F32), struct((rim, 128), F32)],
            [pltpu.VMEM((2, size, rows_z), F32), pltpu.VMEM((3, 2, size, rows_z), F32)],
            cost_estimate=pl.CostEstimate(
                flops=density.size * (100000 if g == 0 else 1),
                bytes_accessed=density.size,
                transcendentals=density.size * 3,
            ),
        )(held, table, signs)

    early = rounds < 2
    colours = struct((3, rim, 128), F32)
    unlit = struct((2 - early, 2, size, rows_z), F32)
    results = call(
        functools.partial(own_kernel, rim, early),
        "own",
        [VMEM] * (9 if early else 8),
        [colours, unlit] if early else [unlit, piece, piece],
    )(
        strips[0], halo_x[1][0], strips[1], halo_x[1][1], mx, my, *coarse[1], *([shaded[1]] if early else [])
    )
    if early:
        light, partial = results
    else:
        partial, *others = results
        light = call(functools.partial(late_kernel, rim, 1), "late", [VMEM] * 5, colours)(
            my, partial, *[swap(strip, 2, 1) for strip in others], shaded[1]
        )
    kept, given = call(
        functools.partial(last_kernel, rim, depth_count),
        "last",
        [VMEM] * 8,
        [struct((depth_count // 2, 4, block, rows_y), F32)] * 2,
        [pltpu.VMEM((8, rows_y, 128), F32)],
    )(my, partial, *halo_y, shaded[0], light, *total)
    level = 0
    while True:
        theirs = lax.ppermute(given, "depth", [(i, i ^ 1 << level) for i in range(depth_count)])
        left = kept.shape[0] // 2
        outs = [struct((left, 4, block, rows_y), F32)] * 2
        merged = call(
            functools.partial(merge_kernel, level),
            f"merge{level}",
            [VMEM] * 3,
            outs if left else struct((4, 1, 1, block, rows_y), F32),
            limit=2 * MIB,
        )(order_map, kept, theirs)
        if not left:
            return merged
        kept, given = merged
        level += 1


def solution(mesh):
    return jax.shard_map(
        per_device,
        mesh=mesh,
        in_specs=(
            P("sx", "sy", "depth"),
            P(),
            P(),
            P(),
            P(),
            P(),
            P("sx", "sy", "depth"),
            P("sx", "sy"),
        ),
        out_specs=P(None, "sx", "depth", None, "sy"),
        check_vma=False,
    )
```

```python
import functools
import math
import jax
import jax.numpy as jnp
from jax import lax
from jax.experimental import pallas as pl
from jax.experimental.pallas import tpu as pltpu
from jax.sharding import PartitionSpec as P

LOG2E = math.log2(math.e)
VMEM = pl.BlockSpec(memory_space=pltpu.VMEM)
HBM = pl.BlockSpec(memory_space=pltpu.HBM)
MIB = 1024 * 1024
F32, BF16 = jnp.float32, jnp.bfloat16
dot = functools.partial(jnp.dot, preferred_element_type=F32)


def iota(shape, dim):
    return lax.broadcasted_iota(jnp.int32, shape, dim)


def line_pairs(count, shift):
    return [(i, i + 1) for i in range(shift, count - 1, 2)]


def swaps(counts, x_round, y_round):
    depth_count, count_x, count_y = counts
    index = lambda d, x, y: (d * count_x + x) * count_y + y
    stay = lambda count: [(i, i) for i in range(count)]
    pairs_x = stay(count_x) if x_round is None else line_pairs(count_x, x_round)
    pairs_y = stay(count_y) if y_round is None else line_pairs(count_y, y_round)
    ends = {((a, c), (b, e)) for a, b in pairs_x for c, e in pairs_y}
    if x_round is not None and y_round is not None:
        ends |= {((a, e), (b, c)) for a, b in pairs_x for c, e in pairs_y}
    used = {end for pair in ends for end in pair}
    pairs = []
    for d in range(depth_count):
        pairs += [(index(d, *a), index(d, *b)) for a, b in sorted(ends)]
    for x in range(count_x):
        for y in range(count_y):
            if (x, y) not in used:
                pairs += [
                    (index(d, x, y), index(d + 1, x, y)) for d in range(0, depth_count - 1, 2)
                ]
    return pairs + [(b, a) for a, b in pairs]


class Place:
    def __init__(self):
        self.depth = lax.axis_index("depth")
        self.half, self.has_x = self.sides("sx")
        self.group, self.has_y = self.sides("sy")

    def sides(self, axis):
        at, last = lax.axis_index(axis), lax.axis_size(axis) - 1
        parity = lax.rem(at, 2)
        upper, lower = at < last, at > 0
        order = (1 - parity, parity)
        either = lambda side: jnp.where(side == 1, upper.astype(jnp.int32), lower.astype(jnp.int32))
        return order, [either(side) == 1 for side in order]


def group_rows(place, rim, g):
    return pl.ds(pl.multiple_of(place.group[g] * rim, rim), rim)


def half_rows(place, rim, h):
    return pl.ds(place.half[h] * rim, rim)


def first_kernel(rim, rounds, density, *refs):
    place = Place()
    n_tables = (len(refs) - 4 - 2 * rounds) // 2
    tables, refs = refs[:n_tables], refs[n_tables:]
    held, xs, refs = refs[0], refs[1:3], refs[3:]
    strips, refs = refs[:2 * rounds], refs[2 * rounds:]
    tables_out, sems = refs[:n_tables], refs[n_tables]
    copies = []
    for g in range(2):
        for h in range(2):
            rows = density.at[half_rows(place, rim, h), group_rows(place, rim, g), :]
            copies.append(pltpu.make_async_copy(rows, held.at[g, h], sems.at[2 * g + h]))
    for i, (src, dst) in enumerate(zip(tables, tables_out)):
        copies.append(pltpu.make_async_copy(src, dst, sems.at[4 + i]))
    for copy in copies:
        copy.start()
    for g in range(2):
        for h in range(2):
            copies[2 * g + h].wait()
            coarse = held[g, h].astype(BF16)
            xs[h][g] = coarse
            if g < rounds:
                strips[2 * g + h][...] = coarse
    for copy in copies[4:]:
        copy.wait()


def toeplitz(taps, rim):
    return pltpu.roll(jnp.broadcast_to(taps, (rim, 128)), 0, 1, stride=1, stride_axis=0)


def blur_matrices(rim, place, taps):
    size = rim * rim
    wide = 3 * size
    shift = rim.bit_length() - 1
    pick = lambda mask: jnp.where(mask, 1.0, 0.0).astype(BF16)
    row_hi = pick(iota((size, rim), 0) >> shift == iota((size, rim), 1))
    row_lo = pick(iota((size, rim), 0) & (rim - 1) == iota((size, rim), 1))
    col = iota((128, wide), 1)
    src = iota((128, wide), 0)
    k, j, b = col >> 2 * shift, col >> shift & (rim - 1), col & (rim - 1)
    k_x = jnp.where(place.half[0] == 1, k, 2 - k)
    k_y = jnp.where(place.group[0] == 1, k, 2 - k)
    tx = toeplitz(taps[0:1], rim).astype(BF16)
    ty = toeplitz(taps[1:2] * 0.5, rim).astype(BF16)
    full_x = dot(row_hi, dot(tx, pick(k_x * rim + j == src)).astype(BF16))
    full_y = dot(row_lo, dot(ty, pick(k_y * rim + b == src)).astype(BF16))
    r, c = iota((size, size), 0), iota((size, size), 1)
    same_x = r & (rim - 1) == c & (rim - 1)
    same_y = r >> shift == c >> shift
    parts = []
    for full, same in ((full_x, same_x), (full_y, same_y)):
        blocks = [
            jnp.where(same, full[:, n * size:(n + 1) * size], 0.0).astype(BF16) for n in range(3)
        ]
        parts.append(jnp.concatenate(blocks, axis=1))
    return parts


def matrices_kernel(rim, taps, mx, my, padded):
    padded[...] = jnp.zeros(padded.shape, F32)
    padded[0:2, 0:taps.shape[1]] = taps[...]
    mx[...], my[...] = blur_matrices(rim, Place(), padded[...])


def prepare_kernel(
    rim, centre, width, colour, opacity, brick_tf, view_order, table, signs, order_map
):
    place = Place()
    wide = width[...]
    rows = [centre[...], (-LOG2E) / (wide * wide), opacity[...] * (-LOG2E)]
    rows += [colour[c] * 0.5 for c in range(3)]
    rows = jnp.concatenate(rows, axis=0)
    which = iota(rows.shape, 1)
    n = 0
    for g in range(2):
        for h in range(2):
            bricks = brick_tf[place.half[h]]
            bricks = jnp.where(place.group[g] == 0, bricks[0:1], bricks[1:2])
            for bz in range(bricks.shape[1]):
                mine = jnp.where(which == bricks[:, bz:bz + 1], rows, 0.0)
                mine = jnp.sum(mine, axis=1, keepdims=True)
                table[n] = jnp.broadcast_to(mine, table.shape[1:])
                n += 1
            orders = view_order[...]
            orders = jnp.where(place.half[h] == 0, orders[0:1], orders[1:2])
            order = jnp.where(place.group[g] == 0, orders[:, 0:1], orders[:, 1:2])
            signs[g, h] = jnp.broadcast_to(1 - 2 * order, signs.shape[2:])
    block, shape = order_map.shape[1], order_map.shape[1:]
    for n in range(order_map.shape[0]):
        brick = n * block // rim
        orders = view_order[brick:brick + 1]
        order_map[n] = jnp.where(
            iota(shape, 1) < rim,
            jnp.broadcast_to(orders[:, 0:1], shape),
            jnp.broadcast_to(orders[:, 1:2], shape),
        )


def cells_kernel(rim, bumps, g, held, table, signs, shaded, total, optical_s, emitted_s):
    place = Place()
    rows_z = held.shape[4]
    depth = 128
    bricks = rows_z // depth
    lane = iota((rim, 128), 1)
    for h in range(2):
        cells = held.at[g, h]
        for bz in range(bricks):
            zs = slice(bz * depth, (bz + 1) * depth)
            at = (2 * g + h) * bricks + bz
            row = lambda i: jnp.broadcast_to(table[at, i:i + 1, :], (8, depth))[None]
            cen = [row(j) for j in range(bumps)]
            neg = [row(bumps + j) for j in range(bumps)]
            opa = [row(2 * bumps + j) for j in range(bumps)]
            col = [[row((3 + c) * bumps + j) for c in range(3)] for j in range(bumps)]
            for x in range(rim):
                d = cells[x, :, zs].reshape(rim // 8, 8, depth)
                opt, em = None, [None] * 3
                for j in range(bumps):
                    w = d - cen[j]
                    b = jnp.exp2((w * w) * neg[j])
                    opt = opa[j] * b if opt is None else opt + opa[j] * b
                    for c in range(3):
                        em[c] = col[j][c] * b if em[c] is None else em[c] + col[j][c] * b
                rows = slice(x * rim, (x + 1) * rim)
                optical_s[h, rows, zs] = opt.reshape(rim, depth)
                for c in range(3):
                    emitted_s[c, h, rows, zs] = em[c].reshape(rim, depth)
        behind = iota((rows_z, rows_z), 1) - iota((rows_z, rows_z), 0)
        sign = jnp.broadcast_to(signs[g, h][0:1, 0:1], (rows_z, rows_z))
        tri = jnp.where(behind * sign > 0, 1.0, 0.0).astype(BF16)
        opt = optical_s[h]
        hi = opt.astype(BF16)
        lo = (opt - hi.astype(F32)).astype(BF16)
        ahead = dot(hi, tri) + dot(lo, tri)
        weight = jnp.exp2(ahead) * (1.0 - jnp.exp2(opt))
        for c in range(3):
            shaded[c, h] = (weight * emitted_s[c, h]).reshape(rim, rim, rows_z)
        part = rays(opt.reshape(rim, rim, rows_z), place.half[h] * rim, lane)
        total[...] = part if h == 0 else total[...] + part


def rays(cells, first_lane, lane):
    folded = cells[:, :, :128]
    for z in range(128, cells.shape[2], 128):
        folded = folded + cells[:, :, z:z + 128]
    summed = jnp.sum(folded, axis=2, keepdims=True)
    acc = jnp.zeros(lane.shape, F32)
    for x in range(cells.shape[0]):
        acc = jnp.where(lane == first_lane + x, summed[x], acc)
    return acc


def blur_x(place, rim, mx, h, near, halo):
    flat = lambda cells: cells.reshape(rim * rim, cells.shape[-1])
    edge = flat(halo)
    edge = jnp.where(place.has_x[h], edge, jnp.zeros_like(edge))
    own = [flat(near[1]), flat(near[0])]
    blocks = own + [edge] if h == 0 else [edge] + own
    return dot(mx[...], jnp.concatenate(blocks, axis=0)).astype(BF16)


def lit(place, rim, occlusion, shaded, h):
    rows_z = occlusion.shape[1]
    lane = iota((rim, 128), 1)
    shade = (1.0 - jnp.tanh(occlusion)).reshape(rim, rim, rows_z)
    return [rays(shade * shaded[c, h], place.half[h] * rim, lane) for c in range(3)]


def own_kernel(rim, early, mx, my, xs0, xs1, halo0, halo1, *refs):
    place = Place()
    size = rim * rim
    if early:
        shaded, out, partial = refs
    else:
        partial, = refs
    halos = (halo0, halo1)
    across = [
        [blur_x(place, rim, mx, h, [xs0[g], xs1[g]], halos[h][g]) for h in range(2)]
        for g in range(2)
    ]
    for h in range(2):
        cells = jnp.concatenate([across[1][h], across[0][h]], axis=0)
        partial[0, h] = dot(my[:, :2 * size], cells)
        other = dot(my[:, size:], cells)
        if not early:
            partial[1, h] = other
            continue
        for c, part in enumerate(lit(place, rim, other, shaded, h)):
            out[c] = part if h == 0 else out[c] + part


def late(rim, g, mx, my, near0, partial, near1, halo0, halo1, shaded):
    place = Place()
    size = rim * rim
    block = my[:, 2 * size:] if g == 0 else my[:, :size]
    across = [
        blur_x(place, rim, mx, h, [near0[...], near1[...]], halo[...])
        for h, halo in enumerate((halo0, halo1))
    ]
    across = [jnp.where(place.has_y[g], cells, jnp.zeros_like(cells)) for cells in across]
    occlusion = [partial[g, h] + dot(block, across[h]) for h in range(2)]
    lights = [lit(place, rim, occlusion[h], shaded, h) for h in range(2)]
    return [a + b for a, b in zip(*lights)]


def late_kernel(rim, g, *refs):
    *refs, out = refs
    for c, part in enumerate(late(rim, g, *refs)):
        out[c] = part


def last_kernel(rim, depth_count, *refs):
    refs, (light_e, total0, total1, kept, given, img) = refs[:8], refs[8:]
    place = Place()
    rows = 2 * rim
    at_s, at_e = group_rows(place, rim, 0), group_rows(place, rim, 1)
    for c, part in enumerate(late(rim, 0, *refs)):
        img[c, at_s, :] = part
        img[c, at_e, :] = light_e[c]
    img[3, at_s, :] = jnp.exp2(total0[...])
    img[3, at_e, :] = jnp.exp2(total1[...])
    for c in range(4):
        img[4 + c, :, 0:rows] = img[c].T[:rows, :]
    block = rows // depth_count
    bit = place.depth & 1
    for n in range(depth_count // 2):
        for out, b in ((kept, bit), (given, 1 - bit)):
            out[n] = img[4:8, pl.ds(pl.multiple_of((2 * n + b) * block, block), block), 0:rows]


def merge_kernel(level, order_map, kept, theirs, *outs):
    me = lax.axis_index("depth")
    bit = me >> level & 1
    low = me & (2 << level) - 1
    merged = []
    for n in range(kept.shape[0]):
        mine = (bit == order_map[(n << level + 1) + low])[None]
        front = jnp.where(mine, kept[n], theirs[n])
        back = jnp.where(mine, theirs[n], kept[n])
        merged.append((front[:3] + front[3:] * back[:3], front[3:] * back[3:]))
    if len(merged) == 1:
        colour, through = merged[0]
        outs[0][...] = jnp.concatenate([colour, 1.0 - through]).reshape(outs[0].shape)
        return
    up = me >> level + 1 & 1
    for n in range(len(merged) // 2):
        even, odd = (jnp.concatenate(merged[2 * n + i]) for i in range(2))
        outs[0][n] = jnp.where(up == 1, odd, even)
        outs[1][n] = jnp.where(up == 1, even, odd)


def call(kernel, name, ins, outs, scratch=(), limit=16 * MIB, **more):
    return pl.pallas_call(
        kernel,
        out_shape=outs,
        in_specs=ins,
        out_specs=jax.tree.map(lambda _: VMEM, outs),
        scratch_shapes=list(scratch),
        compiler_params=pltpu.CompilerParams(vmem_limit_bytes=limit),
        name=name,
        **more,
    )


def per_device(
    density, kernel_taps, tf_centre, tf_width, tf_color, tf_opacity, brick_tf, view_order
):
    rows_x, rows_y, rows_z = density.shape
    rim = (kernel_taps.shape[1] - 1) // 2
    bumps = tf_centre.shape[1]
    size = rim * rim
    axes = ("depth", "sx", "sy")
    counts = tuple(lax.axis_size(axis) for axis in axes)
    depth_count, count_y = counts[0], counts[2]
    struct = jax.ShapeDtypeStruct
    block = rows_x // depth_count
    rounds = sum(1 for shift in range(2) if line_pairs(count_y, shift))

    def swap(piece, x_round, y_round):
        return lax.ppermute(piece, axes, swaps(counts, x_round, y_round))

    in_hbm = lambda array: pltpu.with_memory_space_constraint(array, pltpu.HBM)
    tables = (tf_centre.T, tf_width.T, tf_color.T, tf_opacity.T, brick_tf, view_order)
    piece = struct((rim, rim, rows_z), BF16)
    both = struct((2, rim, rim, rows_z), BF16)
    held, xs0, xs1, *refs = call(
        functools.partial(first_kernel, rim, rounds),
        "first",
        [HBM] * (1 + len(tables)),
        [struct((2, 2, rim, rim, rows_z), F32), both, both]
        + [piece] * (2 * rounds)
        + [struct(t.shape, t.dtype) for t in tables],
        [pltpu.SemaphoreType.DMA((4 + len(tables),))],
    )(in_hbm(density), *[in_hbm(t) for t in tables])
    strips, tables = refs[:2 * rounds], refs[2 * rounds:]
    near = [[swap(strips[2 * r], None, r), None] for r in range(rounds)]

    bricks = rows_z // 128
    table, signs, order_map = call(
        functools.partial(prepare_kernel, rim),
        "prepare",
        [VMEM] * len(tables),
        [struct((4 * bricks, 6 * bumps, 128), F32), struct((2, 2, 8, 128), jnp.int32)]
        + [struct((depth_count, block, rows_y), jnp.int32)],
    )(*tables)
    halo_x = [swap(cells, h, None) for h, cells in enumerate((xs0, xs1))]
    mx, my = call(
        functools.partial(matrices_kernel, rim),
        "matrices",
        [VMEM],
        [struct((size, 3 * size), BF16)] * 2,
        [pltpu.VMEM((8, 128), F32)],
    )(kernel_taps.astype(F32))
    shaded, total = [None, None], [None, None]
    for g in (1, 0):
        shaded[g], total[g] = call(
            functools.partial(cells_kernel, rim, bumps, g),
            f"cells{g}",
            [VMEM] * 3,
            [struct((3, 2, rim, rim, rows_z), F32), struct((rim, 128), F32)],
            [pltpu.VMEM((2, size, rows_z), F32), pltpu.VMEM((3, 2, size, rows_z), F32)],
            cost_estimate=pl.CostEstimate(
                flops=density.size * (100000 if g == 0 else 1),
                bytes_accessed=density.size * (10000 if g == 0 else 1),
                transcendentals=density.size * 3,
            ),
        )(held, table, signs)

    corner = [[None, None] for r in range(rounds)]
    for r in range(rounds):
        near[r][1] = swap(strips[2 * r + 1], None, r)
        strip, arrived, total[1] = lax.optimization_barrier(
            (strips[2 * r + 1], near[r][0], total[1])
        )
        corner[r] = [swap(arrived, 0, None), swap(strip, 1, r)]

    early = rounds < 2
    colours = struct((3, rim, 128), F32)
    unlit = struct((2 - early, 2, size, rows_z), F32)
    results = call(
        functools.partial(own_kernel, rim, early),
        "own",
        [VMEM] * (7 if early else 6),
        [colours, unlit] if early else [unlit],
    )(mx, my, xs0, xs1, *halo_x, *([shaded[1]] if early else []))
    partial = results[-1]
    if early:
        light = results[0]
    else:
        light = call(functools.partial(late_kernel, rim, 1), "late", [VMEM] * 8, colours)(
            mx, my, near[1][0], partial, near[1][1], *corner[1], shaded[1]
        )
    kept, given = call(
        functools.partial(last_kernel, rim, depth_count),
        "last",
        [VMEM] * 11,
        [struct((depth_count // 2, 4, block, rows_y), F32)] * 2,
        [pltpu.VMEM((8, rows_y, 128), F32)],
    )(mx, my, near[0][0], partial, near[0][1], *corner[0], shaded[0], light, *total)
    level = 0
    while True:
        theirs = lax.ppermute(given, "depth", [(i, i ^ 1 << level) for i in range(depth_count)])
        left = kept.shape[0] // 2
        outs = [struct((left, 4, block, rows_y), F32)] * 2
        merged = call(
            functools.partial(merge_kernel, level),
            f"merge{level}",
            [VMEM] * 3,
            outs if left else struct((4, 1, 1, block, rows_y), F32),
            limit=2 * MIB,
        )(order_map, kept, theirs)
        if not left:
            return merged
        kept, given = merged
        level += 1


def solution(mesh):
    return jax.shard_map(
        per_device,
        mesh=mesh,
        in_specs=(
            P("sx", "sy", "depth"),
            P(),
            P(),
            P(),
            P(),
            P(),
            P("sx", "sy", "depth"),
            P("sx", "sy"),
        ),
        out_specs=P(None, "sx", "depth", None, "sy"),
        check_vma=False,
    )
```

```python
import functools
import math
import jax
import jax.numpy as jnp
from jax import lax
from jax.experimental import pallas as pl
from jax.experimental.pallas import tpu as pltpu
from jax.sharding import PartitionSpec as P

LOG2E = math.log2(math.e)
VMEM = pl.BlockSpec(memory_space=pltpu.VMEM)
HBM = pl.BlockSpec(memory_space=pltpu.HBM)
MIB = 1024 * 1024
F32, BF16 = jnp.float32, jnp.bfloat16
dot = functools.partial(jnp.dot, preferred_element_type=F32)


def iota(shape, dim):
    return lax.broadcasted_iota(jnp.int32, shape, dim)


def line_pairs(count, shift):
    return [(i, i + 1) for i in range(shift, count - 1, 2)]


def swaps(counts, x_round, y_round):
    depth_count, count_x, count_y = counts
    index = lambda d, x, y: (d * count_x + x) * count_y + y
    stay = lambda count: [(i, i) for i in range(count)]
    pairs_x = stay(count_x) if x_round is None else line_pairs(count_x, x_round)
    pairs_y = stay(count_y) if y_round is None else line_pairs(count_y, y_round)
    ends = {((a, c), (b, e)) for a, b in pairs_x for c, e in pairs_y}
    if x_round is not None and y_round is not None:
        ends |= {((a, e), (b, c)) for a, b in pairs_x for c, e in pairs_y}
    used = {end for pair in ends for end in pair}
    pairs = []
    for d in range(depth_count):
        pairs += [(index(d, *a), index(d, *b)) for a, b in sorted(ends)]
    for x in range(count_x):
        for y in range(count_y):
            if (x, y) not in used:
                pairs += [
                    (index(d, x, y), index(d + 1, x, y)) for d in range(0, depth_count - 1, 2)
                ]
    return pairs + [(b, a) for a, b in pairs]


class Place:
    def __init__(self):
        self.depth = lax.axis_index("depth")
        self.half, self.has_x = self.sides("sx")
        self.group, self.has_y = self.sides("sy")

    def sides(self, axis):
        at, last = lax.axis_index(axis), lax.axis_size(axis) - 1
        parity = lax.rem(at, 2)
        upper, lower = at < last, at > 0
        order = (1 - parity, parity)
        either = lambda side: jnp.where(side == 1, upper.astype(jnp.int32), lower.astype(jnp.int32))
        return order, [either(side) == 1 for side in order]


def group_rows(place, rim, g):
    return pl.ds(pl.multiple_of(place.group[g] * rim, rim), rim)


def half_rows(place, rim, h):
    return pl.ds(place.half[h] * rim, rim)


def first_kernel(rim, rounds, density, *refs):
    place = Place()
    n_tables = (len(refs) - 4 - 2 * rounds) // 2
    tables, refs = refs[:n_tables], refs[n_tables:]
    held, xs, refs = refs[0], refs[1:3], refs[3:]
    strips, refs = refs[:2 * rounds], refs[2 * rounds:]
    tables_out, sems = refs[:n_tables], refs[n_tables]
    copies = []
    for g in range(2):
        for h in range(2):
            rows = density.at[half_rows(place, rim, h), group_rows(place, rim, g), :]
            copies.append(pltpu.make_async_copy(rows, held.at[g, h], sems.at[2 * g + h]))
    for i, (src, dst) in enumerate(zip(tables, tables_out)):
        copies.append(pltpu.make_async_copy(src, dst, sems.at[4 + i]))
    for copy in copies:
        copy.start()
    for g in range(2):
        for h in range(2):
            copies[2 * g + h].wait()
            coarse = held[g, h].astype(BF16)
            xs[h][g] = coarse
            if g < rounds:
                strips[2 * g + h][...] = coarse
    for copy in copies[4:]:
        copy.wait()


def toeplitz(taps, rim):
    return pltpu.roll(jnp.broadcast_to(taps, (rim, 128)), 0, 1, stride=1, stride_axis=0)


def blur_matrices(rim, place, taps):
    size = rim * rim
    wide = 3 * size
    shift = rim.bit_length() - 1
    pick = lambda mask: jnp.where(mask, 1.0, 0.0).astype(BF16)
    row_hi = pick(iota((size, rim), 0) >> shift == iota((size, rim), 1))
    row_lo = pick(iota((size, rim), 0) & (rim - 1) == iota((size, rim), 1))
    col = iota((128, wide), 1)
    src = iota((128, wide), 0)
    k, j, b = col >> 2 * shift, col >> shift & (rim - 1), col & (rim - 1)
    k_x = jnp.where(place.half[0] == 1, k, 2 - k)
    k_y = jnp.where(place.group[0] == 1, k, 2 - k)
    tx = toeplitz(taps[0:1], rim).astype(BF16)
    ty = toeplitz(taps[1:2] * 0.5, rim).astype(BF16)
    full_x = dot(row_hi, dot(tx, pick(k_x * rim + j == src)).astype(BF16))
    full_y = dot(row_lo, dot(ty, pick(k_y * rim + b == src)).astype(BF16))
    r, c = iota((size, size), 0), iota((size, size), 1)
    same_x = r & (rim - 1) == c & (rim - 1)
    same_y = r >> shift == c >> shift
    parts = []
    for full, same in ((full_x, same_x), (full_y, same_y)):
        blocks = [
            jnp.where(same, full[:, n * size:(n + 1) * size], 0.0).astype(BF16) for n in range(3)
        ]
        parts.append(jnp.concatenate(blocks, axis=1))
    return parts


def matrices_kernel(rim, taps, mx, my, padded):
    padded[...] = jnp.zeros(padded.shape, F32)
    padded[0:2, 0:taps.shape[1]] = taps[...]
    mx[...], my[...] = blur_matrices(rim, Place(), padded[...])


def prepare_kernel(
    rim, centre, width, colour, opacity, brick_tf, view_order, table, signs, order_map
):
    place = Place()
    wide = width[...]
    rows = [centre[...], (-LOG2E) / (wide * wide), opacity[...] * (-LOG2E)]
    rows += [colour[c] * 0.5 for c in range(3)]
    rows = jnp.concatenate(rows, axis=0)
    which = iota(rows.shape, 1)
    n = 0
    for g in range(2):
        for h in range(2):
            bricks = brick_tf[place.half[h]]
            bricks = jnp.where(place.group[g] == 0, bricks[0:1], bricks[1:2])
            for bz in range(bricks.shape[1]):
                mine = jnp.where(which == bricks[:, bz:bz + 1], rows, 0.0)
                mine = jnp.sum(mine, axis=1, keepdims=True)
                table[n] = jnp.broadcast_to(mine, table.shape[1:])
                n += 1
            orders = view_order[...]
            orders = jnp.where(place.half[h] == 0, orders[0:1], orders[1:2])
            order = jnp.where(place.group[g] == 0, orders[:, 0:1], orders[:, 1:2])
            signs[g, h] = jnp.broadcast_to(1 - 2 * order, signs.shape[2:])
    block, shape = order_map.shape[1], order_map.shape[1:]
    for n in range(order_map.shape[0]):
        brick = n * block // rim
        orders = view_order[brick:brick + 1]
        order_map[n] = jnp.where(
            iota(shape, 1) < rim,
            jnp.broadcast_to(orders[:, 0:1], shape),
            jnp.broadcast_to(orders[:, 1:2], shape),
        )


def cells_kernel(rim, bumps, g, held, table, signs, shaded, total, optical_s, emitted_s):
    place = Place()
    rows_z = held.shape[4]
    depth = 128
    bricks = rows_z // depth
    lane = iota((rim, 128), 1)
    for h in range(2):
        cells = held.at[g, h]
        for bz in range(bricks):
            zs = slice(bz * depth, (bz + 1) * depth)
            at = (2 * g + h) * bricks + bz
            row = lambda i: jnp.broadcast_to(table[at, i:i + 1, :], (8, depth))[None]
            cen = [row(j) for j in range(bumps)]
            neg = [row(bumps + j) for j in range(bumps)]
            opa = [row(2 * bumps + j) for j in range(bumps)]
            col = [[row((3 + c) * bumps + j) for c in range(3)] for j in range(bumps)]
            for x in range(rim):
                d = cells[x, :, zs].reshape(rim // 8, 8, depth)
                opt, em = None, [None] * 3
                for j in range(bumps):
                    w = d - cen[j]
                    b = jnp.exp2((w * w) * neg[j])
                    opt = opa[j] * b if opt is None else opt + opa[j] * b
                    for c in range(3):
                        em[c] = col[j][c] * b if em[c] is None else em[c] + col[j][c] * b
                rows = slice(x * rim, (x + 1) * rim)
                optical_s[h, rows, zs] = opt.reshape(rim, depth)
                for c in range(3):
                    emitted_s[c, h, rows, zs] = em[c].reshape(rim, depth)
        behind = iota((rows_z, rows_z), 1) - iota((rows_z, rows_z), 0)
        sign = jnp.broadcast_to(signs[g, h][0:1, 0:1], (rows_z, rows_z))
        tri = jnp.where(behind * sign > 0, 1.0, 0.0).astype(BF16)
        opt = optical_s[h]
        hi = opt.astype(BF16)
        lo = (opt - hi.astype(F32)).astype(BF16)
        ahead = dot(hi, tri) + dot(lo, tri)
        weight = jnp.exp2(ahead) * (1.0 - jnp.exp2(opt))
        for c in range(3):
            shaded[c, h] = (weight * emitted_s[c, h]).reshape(rim, rim, rows_z)
        part = rays(opt.reshape(rim, rim, rows_z), place.half[h] * rim, lane)
        total[...] = part if h == 0 else total[...] + part


def rays(cells, first_lane, lane):
    folded = cells[:, :, :128]
    for z in range(128, cells.shape[2], 128):
        folded = folded + cells[:, :, z:z + 128]
    summed = jnp.sum(folded, axis=2, keepdims=True)
    acc = jnp.zeros(lane.shape, F32)
    for x in range(cells.shape[0]):
        acc = jnp.where(lane == first_lane + x, summed[x], acc)
    return acc


def blur_x(place, rim, mx, h, near, halo):
    flat = lambda cells: cells.reshape(rim * rim, cells.shape[-1])
    edge = flat(halo)
    edge = jnp.where(place.has_x[h], edge, jnp.zeros_like(edge))
    own = [flat(near[1]), flat(near[0])]
    blocks = own + [edge] if h == 0 else [edge] + own
    return dot(mx[...], jnp.concatenate(blocks, axis=0)).astype(BF16)


def lit(place, rim, occlusion, shaded, h):
    rows_z = occlusion.shape[1]
    lane = iota((rim, 128), 1)
    shade = (1.0 - jnp.tanh(occlusion)).reshape(rim, rim, rows_z)
    return [rays(shade * shaded[c, h], place.half[h] * rim, lane) for c in range(3)]


def own_kernel(rim, early, mx, my, xs0, xs1, halo0, halo1, *refs):
    place = Place()
    size = rim * rim
    if early:
        shaded, out, partial = refs
    else:
        partial, = refs
    halos = (halo0, halo1)
    across = [
        [blur_x(place, rim, mx, h, [xs0[g], xs1[g]], halos[h][g]) for h in range(2)]
        for g in range(2)
    ]
    for h in range(2):
        cells = jnp.concatenate([across[1][h], across[0][h]], axis=0)
        partial[0, h] = dot(my[:, :2 * size], cells)
        other = dot(my[:, size:], cells)
        if not early:
            partial[1, h] = other
            continue
        for c, part in enumerate(lit(place, rim, other, shaded, h)):
            out[c] = part if h == 0 else out[c] + part


def near_kernel(rim, mx, near0, order, near1, out):
    size = rim * rim
    cells = jnp.concatenate([r[...].reshape(size, r.shape[2]) for r in (near1, near0)], axis=0)
    out[0] = dot(mx[:, :2 * size], cells)
    out[1] = dot(mx[:, size:], cells)


def late(rim, g, mx, my, blurred, partial, corner0, corner1, shaded):
    place = Place()
    size = rim * rim
    block = my[:, 2 * size:] if g == 0 else my[:, :size]
    across = []
    for h, corner in enumerate((corner0, corner1)):
        edge = corner[...].reshape(size, corner.shape[2])
        edge = jnp.where(place.has_x[h], edge, jnp.zeros_like(edge))
        beside = mx[:, 2 * size:] if h == 0 else mx[:, :size]
        cells = (blurred[h] + dot(beside, edge)).astype(BF16)
        across.append(jnp.where(place.has_y[g], cells, jnp.zeros_like(cells)))
    occlusion = [partial[g, h] + dot(block, across[h]) for h in range(2)]
    lights = [lit(place, rim, occlusion[h], shaded, h) for h in range(2)]
    return [a + b for a, b in zip(*lights)]


def late_kernel(rim, g, *refs):
    *refs, out = refs
    for c, part in enumerate(late(rim, g, *refs)):
        out[c] = part


def last_kernel(rim, depth_count, *refs):
    refs, (light_e, total0, total1, kept, given, img) = refs[:7], refs[7:]
    place = Place()
    rows = 2 * rim
    at_s, at_e = group_rows(place, rim, 0), group_rows(place, rim, 1)
    for c, part in enumerate(late(rim, 0, *refs)):
        img[c, at_s, :] = part
        img[c, at_e, :] = light_e[c]
    img[3, at_s, :] = jnp.exp2(total0[...])
    img[3, at_e, :] = jnp.exp2(total1[...])
    for c in range(4):
        img[4 + c, :, 0:rows] = img[c].T[:rows, :]
    block = rows // depth_count
    bit = place.depth & 1
    for n in range(depth_count // 2):
        for out, b in ((kept, bit), (given, 1 - bit)):
            out[n] = img[4:8, pl.ds(pl.multiple_of((2 * n + b) * block, block), block), 0:rows]


def merge_kernel(level, order_map, kept, theirs, *outs):
    me = lax.axis_index("depth")
    bit = me >> level & 1
    low = me & (2 << level) - 1
    merged = []
    for n in range(kept.shape[0]):
        mine = (bit == order_map[(n << level + 1) + low])[None]
        front = jnp.where(mine, kept[n], theirs[n])
        back = jnp.where(mine, theirs[n], kept[n])
        merged.append((front[:3] + front[3:] * back[:3], front[3:] * back[3:]))
    if len(merged) == 1:
        colour, through = merged[0]
        outs[0][...] = jnp.concatenate([colour, 1.0 - through]).reshape(outs[0].shape)
        return
    up = me >> level + 1 & 1
    for n in range(len(merged) // 2):
        even, odd = (jnp.concatenate(merged[2 * n + i]) for i in range(2))
        outs[0][n] = jnp.where(up == 1, odd, even)
        outs[1][n] = jnp.where(up == 1, even, odd)


def call(kernel, name, ins, outs, scratch=(), limit=16 * MIB, **more):
    return pl.pallas_call(
        kernel,
        out_shape=outs,
        in_specs=ins,
        out_specs=jax.tree.map(lambda _: VMEM, outs),
        scratch_shapes=list(scratch),
        compiler_params=pltpu.CompilerParams(vmem_limit_bytes=limit),
        name=name,
        **more,
    )


def per_device(
    density, kernel_taps, tf_centre, tf_width, tf_color, tf_opacity, brick_tf, view_order
):
    rows_x, rows_y, rows_z = density.shape
    rim = (kernel_taps.shape[1] - 1) // 2
    bumps = tf_centre.shape[1]
    size = rim * rim
    axes = ("depth", "sx", "sy")
    counts = tuple(lax.axis_size(axis) for axis in axes)
    depth_count, count_y = counts[0], counts[2]
    struct = jax.ShapeDtypeStruct
    block = rows_x // depth_count
    rounds = sum(1 for shift in range(2) if line_pairs(count_y, shift))

    def swap(piece, x_round, y_round):
        return lax.ppermute(piece, axes, swaps(counts, x_round, y_round))

    in_hbm = lambda array: pltpu.with_memory_space_constraint(array, pltpu.HBM)
    tables = (tf_centre.T, tf_width.T, tf_color.T, tf_opacity.T, brick_tf, view_order)
    piece = struct((rim, rim, rows_z), BF16)
    both = struct((2, rim, rim, rows_z), BF16)
    held, xs0, xs1, *refs = call(
        functools.partial(first_kernel, rim, rounds),
        "first",
        [HBM] * (1 + len(tables)),
        [struct((2, 2, rim, rim, rows_z), F32), both, both]
        + [piece] * (2 * rounds)
        + [struct(t.shape, t.dtype) for t in tables],
        [pltpu.SemaphoreType.DMA((4 + len(tables),))],
    )(in_hbm(density), *[in_hbm(t) for t in tables])
    strips, tables = refs[:2 * rounds], refs[2 * rounds:]
    near = [[swap(strips[2 * r], None, r), None] for r in range(rounds)]

    bricks = rows_z // 128
    table, signs, order_map = call(
        functools.partial(prepare_kernel, rim),
        "prepare",
        [VMEM] * len(tables),
        [struct((4 * bricks, 6 * bumps, 128), F32), struct((2, 2, 8, 128), jnp.int32)]
        + [struct((depth_count, block, rows_y), jnp.int32)],
    )(*tables)
    halo_x = [swap(cells, h, None) for h, cells in enumerate((xs0, xs1))]
    mx, my = call(
        functools.partial(matrices_kernel, rim),
        "matrices",
        [VMEM],
        [struct((size, 3 * size), BF16)] * 2,
        [pltpu.VMEM((8, 128), F32)],
    )(kernel_taps.astype(F32))
    shaded, total = [None, None], [None, None]
    for g in (1, 0):
        shaded[g], total[g] = call(
            functools.partial(cells_kernel, rim, bumps, g),
            f"cells{g}",
            [VMEM] * 3,
            [struct((3, 2, rim, rim, rows_z), F32), struct((rim, 128), F32)],
            [pltpu.VMEM((2, size, rows_z), F32), pltpu.VMEM((3, 2, size, rows_z), F32)],
            cost_estimate=pl.CostEstimate(
                flops=density.size * (100000 if g == 0 else 1),
                bytes_accessed=density.size * (10000 if g == 0 else 1),
                transcendentals=density.size * 3,
            ),
        )(held, table, signs)

    corner = [[None, None] for r in range(rounds)]
    for r in range(rounds):
        near[r][1] = swap(strips[2 * r + 1], None, r)
        strip, arrived, total[1] = lax.optimization_barrier(
            (strips[2 * r + 1], near[r][0], total[1])
        )
        corner[r] = [swap(arrived, 0, None), swap(strip, 1, r)]

    early = rounds < 2
    colours = struct((3, rim, 128), F32)
    unlit = struct((2 - early, 2, size, rows_z), F32)
    results = call(
        functools.partial(own_kernel, rim, early),
        "own",
        [VMEM] * (7 if early else 6),
        [colours, unlit] if early else [unlit],
    )(mx, my, xs0, xs1, *halo_x, *([shaded[1]] if early else []))
    partial = results[-1]
    blurred = [
        call(
            functools.partial(near_kernel, rim),
            f"near{r}",
            [VMEM] * 4,
            struct((2, size, rows_z), F32),
        )(mx, near[r][0], partial, near[r][1])
        for r in range(rounds)
    ]
    if early:
        light = results[0]
    else:
        light = call(functools.partial(late_kernel, rim, 1), "late", [VMEM] * 7, colours)(
            mx, my, blurred[1], partial, *corner[1], shaded[1]
        )
    kept, given = call(
        functools.partial(last_kernel, rim, depth_count),
        "last",
        [VMEM] * 10,
        [struct((depth_count // 2, 4, block, rows_y), F32)] * 2,
        [pltpu.VMEM((8, rows_y, 128), F32)],
    )(mx, my, blurred[0], partial, *corner[0], shaded[0], light, *total)
    level = 0
    while True:
        theirs = lax.ppermute(given, "depth", [(i, i ^ 1 << level) for i in range(depth_count)])
        left = kept.shape[0] // 2
        outs = [struct((left, 4, block, rows_y), F32)] * 2
        merged = call(
            functools.partial(merge_kernel, level),
            f"merge{level}",
            [VMEM] * 3,
            outs if left else struct((4, 1, 1, block, rows_y), F32),
            limit=2 * MIB,
        )(order_map, kept, theirs)
        if not left:
            return merged
        kept, given = merged
        level += 1


def solution(mesh):
    return jax.shard_map(
        per_device,
        mesh=mesh,
        in_specs=(
            P("sx", "sy", "depth"),
            P(),
            P(),
            P(),
            P(),
            P(),
            P("sx", "sy", "depth"),
            P("sx", "sy"),
        ),
        out_specs=P(None, "sx", "depth", None, "sy"),
        check_vma=False,
    )
```

```python
import functools
import math
import jax
import jax.numpy as jnp
from jax import lax
from jax.experimental import pallas as pl
from jax.experimental.pallas import tpu as pltpu
from jax.sharding import PartitionSpec as P

LOG2E = math.log2(math.e)
VMEM = pl.BlockSpec(memory_space=pltpu.VMEM)
HBM = pl.BlockSpec(memory_space=pltpu.HBM)
MIB = 1024 * 1024
F32, BF16 = jnp.float32, jnp.bfloat16
dot = functools.partial(jnp.dot, preferred_element_type=F32)


def iota(shape, dim):
    return lax.broadcasted_iota(jnp.int32, shape, dim)


def line_pairs(count, shift):
    return [(i, i + 1) for i in range(shift, count - 1, 2)]


def swaps(counts, x_round, y_round):
    depth_count, count_x, count_y = counts
    index = lambda d, x, y: (d * count_x + x) * count_y + y
    stay = lambda count: [(i, i) for i in range(count)]
    pairs_x = stay(count_x) if x_round is None else line_pairs(count_x, x_round)
    pairs_y = stay(count_y) if y_round is None else line_pairs(count_y, y_round)
    ends = {((a, c), (b, e)) for a, b in pairs_x for c, e in pairs_y}
    if x_round is not None and y_round is not None:
        ends |= {((a, e), (b, c)) for a, b in pairs_x for c, e in pairs_y}
    used = {end for pair in ends for end in pair}
    pairs = []
    for d in range(depth_count):
        pairs += [(index(d, *a), index(d, *b)) for a, b in sorted(ends)]
    for x in range(count_x):
        for y in range(count_y):
            if (x, y) not in used:
                pairs += [
                    (index(d, x, y), index(d + 1, x, y)) for d in range(0, depth_count - 1, 2)
                ]
    return pairs + [(b, a) for a, b in pairs]


class Place:
    def __init__(self):
        self.depth = lax.axis_index("depth")
        self.half, self.has_x = self.sides("sx")
        self.group, self.has_y = self.sides("sy")

    def sides(self, axis):
        at, last = lax.axis_index(axis), lax.axis_size(axis) - 1
        parity = lax.rem(at, 2)
        upper, lower = at < last, at > 0
        order = (1 - parity, parity)
        either = lambda side: jnp.where(side == 1, upper.astype(jnp.int32), lower.astype(jnp.int32))
        return order, [either(side) == 1 for side in order]


def group_rows(place, rim, g):
    return pl.ds(pl.multiple_of(place.group[g] * rim, rim), rim)


def half_rows(place, rim, h):
    return pl.ds(place.half[h] * rim, rim)


def first_kernel(rim, rounds, density, *refs):
    place = Place()
    n_tables = (len(refs) - 7 - 2 * rounds) // 2
    tables, refs = refs[:n_tables], refs[n_tables:]
    held, xs, refs = refs[0], refs[1:3], refs[3:]
    strips, refs = refs[:2 * rounds], refs[2 * rounds:]
    looked_up, local_tables, sems = refs[:3], refs[3:-1], refs[-1]
    copies = []
    for g in range(2):
        for h in range(2):
            rows = density.at[half_rows(place, rim, h), group_rows(place, rim, g), :]
            copies.append(pltpu.make_async_copy(rows, held.at[g, h], sems.at[2 * g + h]))
    for i, (src, dst) in enumerate(zip(tables, local_tables)):
        copies.append(pltpu.make_async_copy(src, dst, sems.at[4 + i]))
    for copy in copies[4:] + copies[:4]:
        copy.start()
    for copy in copies[4:]:
        copy.wait()
    look_up(rim, place, *local_tables, *looked_up)
    for g in range(2):
        for h in range(2):
            copies[2 * g + h].wait()
            coarse = held[g, h].astype(BF16)
            xs[h][g] = coarse
            if g < rounds:
                strips[2 * g + h][...] = coarse


def toeplitz(taps, rim):
    return pltpu.roll(jnp.broadcast_to(taps, (rim, 128)), 0, 1, stride=1, stride_axis=0)


def blur_matrices(rim, place, taps):
    size = rim * rim
    wide = 3 * size
    shift = rim.bit_length() - 1
    pick = lambda mask: jnp.where(mask, 1.0, 0.0).astype(BF16)
    row_hi = pick(iota((size, rim), 0) >> shift == iota((size, rim), 1))
    row_lo = pick(iota((size, rim), 0) & (rim - 1) == iota((size, rim), 1))
    col = iota((128, wide), 1)
    src = iota((128, wide), 0)
    k, j, b = col >> 2 * shift, col >> shift & (rim - 1), col & (rim - 1)
    k_x = jnp.where(place.half[0] == 1, k, 2 - k)
    k_y = jnp.where(place.group[0] == 1, k, 2 - k)
    tx = toeplitz(taps[0:1], rim).astype(BF16)
    ty = toeplitz(taps[1:2] * 0.5, rim).astype(BF16)
    full_x = dot(row_hi, dot(tx, pick(k_x * rim + j == src)).astype(BF16))
    full_y = dot(row_lo, dot(ty, pick(k_y * rim + b == src)).astype(BF16))
    r, c = iota((size, size), 0), iota((size, size), 1)
    same_x = r & (rim - 1) == c & (rim - 1)
    same_y = r >> shift == c >> shift
    parts = []
    for full, same in ((full_x, same_x), (full_y, same_y)):
        blocks = [
            jnp.where(same, full[:, n * size:(n + 1) * size], 0.0).astype(BF16) for n in range(3)
        ]
        parts.append(jnp.concatenate(blocks, axis=1))
    return parts


def matrices_kernel(rim, taps, mx, my, padded):
    padded[...] = jnp.zeros(padded.shape, F32)
    padded[0:2, 0:taps.shape[1]] = taps[...]
    mx[...], my[...] = blur_matrices(rim, Place(), padded[...])


def look_up(
    rim, place, centre, width, colour, opacity, brick_tf, view_order, table, signs, order_map
):
    wide = width[...]
    rows = [centre[...], (-LOG2E) / (wide * wide), opacity[...] * (-LOG2E)]
    rows += [colour[c] * 0.5 for c in range(3)]
    rows = jnp.concatenate(rows, axis=0)
    which = iota(rows.shape, 1)
    n = 0
    for g in range(2):
        for h in range(2):
            bricks = brick_tf[place.half[h]]
            bricks = jnp.where(place.group[g] == 0, bricks[0:1], bricks[1:2])
            for bz in range(bricks.shape[1]):
                mine = jnp.where(which == bricks[:, bz:bz + 1], rows, 0.0)
                mine = jnp.sum(mine, axis=1, keepdims=True)
                table[n] = jnp.broadcast_to(mine, table.shape[1:])
                n += 1
            orders = view_order[...]
            orders = jnp.where(place.half[h] == 0, orders[0:1], orders[1:2])
            order = jnp.where(place.group[g] == 0, orders[:, 0:1], orders[:, 1:2])
            signs[g, h] = jnp.broadcast_to(1 - 2 * order, signs.shape[2:])
    block, shape = order_map.shape[1], order_map.shape[1:]
    for n in range(order_map.shape[0]):
        brick = n * block // rim
        orders = view_order[brick:brick + 1]
        order_map[n] = jnp.where(
            iota(shape, 1) < rim,
            jnp.broadcast_to(orders[:, 0:1], shape),
            jnp.broadcast_to(orders[:, 1:2], shape),
        )


def cells_kernel(rim, bumps, g, held, table, signs, shaded, total, optical_s, emitted_s):
    place = Place()
    rows_z = held.shape[4]
    depth = 128
    bricks = rows_z // depth
    lane = iota((rim, 128), 1)
    for h in range(2):
        cells = held.at[g, h]
        for bz in range(bricks):
            zs = slice(bz * depth, (bz + 1) * depth)
            at = (2 * g + h) * bricks + bz
            row = lambda i: jnp.broadcast_to(table[at, i:i + 1, :], (8, depth))[None]
            cen = [row(j) for j in range(bumps)]
            neg = [row(bumps + j) for j in range(bumps)]
            opa = [row(2 * bumps + j) for j in range(bumps)]
            col = [[row((3 + c) * bumps + j) for c in range(3)] for j in range(bumps)]
            for x in range(rim):
                d = cells[x, :, zs].reshape(rim // 8, 8, depth)
                opt, em = None, [None] * 3
                for j in range(bumps):
                    w = d - cen[j]
                    b = jnp.exp2((w * w) * neg[j])
                    opt = opa[j] * b if opt is None else opt + opa[j] * b
                    for c in range(3):
                        em[c] = col[j][c] * b if em[c] is None else em[c] + col[j][c] * b
                rows = slice(x * rim, (x + 1) * rim)
                optical_s[h, rows, zs] = opt.reshape(rim, depth)
                for c in range(3):
                    emitted_s[c, h, rows, zs] = em[c].reshape(rim, depth)
        behind = iota((rows_z, rows_z), 1) - iota((rows_z, rows_z), 0)
        sign = jnp.broadcast_to(signs[g, h][0:1, 0:1], (rows_z, rows_z))
        tri = jnp.where(behind * sign > 0, 1.0, 0.0).astype(BF16)
        opt = optical_s[h]
        hi = opt.astype(BF16)
        lo = (opt - hi.astype(F32)).astype(BF16)
        ahead = dot(hi, tri) + dot(lo, tri)
        weight = jnp.exp2(ahead) * (1.0 - jnp.exp2(opt))
        for c in range(3):
            shaded[c, h] = (weight * emitted_s[c, h]).reshape(rim, rim, rows_z)
        part = rays(opt.reshape(rim, rim, rows_z), place.half[h] * rim, lane)
        total[...] = part if h == 0 else total[...] + part


def rays(cells, first_lane, lane):
    folded = cells[:, :, :128]
    for z in range(128, cells.shape[2], 128):
        folded = folded + cells[:, :, z:z + 128]
    summed = jnp.sum(folded, axis=2, keepdims=True)
    acc = jnp.zeros(lane.shape, F32)
    for x in range(cells.shape[0]):
        acc = jnp.where(lane == first_lane + x, summed[x], acc)
    return acc


def blur_x(place, rim, mx, h, near, halo):
    flat = lambda cells: cells.reshape(rim * rim, cells.shape[-1])
    edge = flat(halo)
    edge = jnp.where(place.has_x[h], edge, jnp.zeros_like(edge))
    own = [flat(near[1]), flat(near[0])]
    blocks = own + [edge] if h == 0 else [edge] + own
    return dot(mx[...], jnp.concatenate(blocks, axis=0)).astype(BF16)


def lit(place, rim, occlusion, shaded, h):
    rows_z = occlusion.shape[1]
    lane = iota((rim, 128), 1)
    shade = (1.0 - jnp.tanh(occlusion)).reshape(rim, rim, rows_z)
    return [rays(shade * shaded[c, h], place.half[h] * rim, lane) for c in range(3)]


def own_kernel(rim, early, mx, my, xs0, xs1, halo0, halo1, *refs):
    place = Place()
    size = rim * rim
    if early:
        shaded, out, partial = refs
    else:
        partial, = refs
    halos = (halo0, halo1)
    across = [
        [blur_x(place, rim, mx, h, [xs0[g], xs1[g]], halos[h][g]) for h in range(2)]
        for g in range(2)
    ]
    for h in range(2):
        cells = jnp.concatenate([across[1][h], across[0][h]], axis=0)
        partial[0, h] = dot(my[:, :2 * size], cells)
        other = dot(my[:, size:], cells)
        if not early:
            partial[1, h] = other
            continue
        for c, part in enumerate(lit(place, rim, other, shaded, h)):
            out[c] = part if h == 0 else out[c] + part


def near_kernel(rim, mx, near0, order, near1, out):
    size = rim * rim
    cells = jnp.concatenate([r[...].reshape(size, r.shape[2]) for r in (near1, near0)], axis=0)
    out[0] = dot(mx[:, :2 * size], cells)
    out[1] = dot(mx[:, size:], cells)


def late(rim, g, mx, my, blurred, partial, corner0, corner1, shaded):
    place = Place()
    size = rim * rim
    block = my[:, 2 * size:] if g == 0 else my[:, :size]
    across = []
    for h, corner in enumerate((corner0, corner1)):
        edge = corner[...].reshape(size, corner.shape[2])
        edge = jnp.where(place.has_x[h], edge, jnp.zeros_like(edge))
        beside = mx[:, 2 * size:] if h == 0 else mx[:, :size]
        cells = (blurred[h] + dot(beside, edge)).astype(BF16)
        across.append(jnp.where(place.has_y[g], cells, jnp.zeros_like(cells)))
    occlusion = [partial[g, h] + dot(block, across[h]) for h in range(2)]
    lights = [lit(place, rim, occlusion[h], shaded, h) for h in range(2)]
    return [a + b for a, b in zip(*lights)]


def late_kernel(rim, g, *refs):
    *refs, out = refs
    for c, part in enumerate(late(rim, g, *refs)):
        out[c] = part


def last_kernel(rim, depth_count, *refs):
    refs, (light_e, total0, total1, kept, given, img) = refs[:7], refs[7:]
    place = Place()
    rows = 2 * rim
    at_s, at_e = group_rows(place, rim, 0), group_rows(place, rim, 1)
    for c, part in enumerate(late(rim, 0, *refs)):
        img[c, at_s, :] = part
        img[c, at_e, :] = light_e[c]
    img[3, at_s, :] = jnp.exp2(total0[...])
    img[3, at_e, :] = jnp.exp2(total1[...])
    for c in range(4):
        img[4 + c, :, 0:rows] = img[c].T[:rows, :]
    block = rows // depth_count
    bit = place.depth & 1
    for n in range(depth_count // 2):
        for out, b in ((kept, bit), (given, 1 - bit)):
            out[n] = img[4:8, pl.ds(pl.multiple_of((2 * n + b) * block, block), block), 0:rows]


def merge_kernel(level, order_map, kept, theirs, *outs):
    me = lax.axis_index("depth")
    bit = me >> level & 1
    low = me & (2 << level) - 1
    merged = []
    for n in range(kept.shape[0]):
        mine = (bit == order_map[(n << level + 1) + low])[None]
        front = jnp.where(mine, kept[n], theirs[n])
        back = jnp.where(mine, theirs[n], kept[n])
        merged.append((front[:3] + front[3:] * back[:3], front[3:] * back[3:]))
    if len(merged) == 1:
        colour, through = merged[0]
        outs[0][...] = jnp.concatenate([colour, 1.0 - through]).reshape(outs[0].shape)
        return
    up = me >> level + 1 & 1
    for n in range(len(merged) // 2):
        even, odd = (jnp.concatenate(merged[2 * n + i]) for i in range(2))
        outs[0][n] = jnp.where(up == 1, odd, even)
        outs[1][n] = jnp.where(up == 1, even, odd)


def call(kernel, name, ins, outs, scratch=(), limit=16 * MIB, **more):
    return pl.pallas_call(
        kernel,
        out_shape=outs,
        in_specs=ins,
        out_specs=jax.tree.map(lambda _: VMEM, outs),
        scratch_shapes=list(scratch),
        compiler_params=pltpu.CompilerParams(vmem_limit_bytes=limit),
        name=name,
        **more,
    )


def per_device(
    density, kernel_taps, tf_centre, tf_width, tf_color, tf_opacity, brick_tf, view_order
):
    rows_x, rows_y, rows_z = density.shape
    rim = (kernel_taps.shape[1] - 1) // 2
    bumps = tf_centre.shape[1]
    size = rim * rim
    axes = ("depth", "sx", "sy")
    counts = tuple(lax.axis_size(axis) for axis in axes)
    depth_count, count_y = counts[0], counts[2]
    struct = jax.ShapeDtypeStruct
    block = rows_x // depth_count
    rounds = sum(1 for shift in range(2) if line_pairs(count_y, shift))

    def swap(piece, x_round, y_round):
        return lax.ppermute(piece, axes, swaps(counts, x_round, y_round))

    in_hbm = lambda array: pltpu.with_memory_space_constraint(array, pltpu.HBM)
    tables = (tf_centre.T, tf_width.T, tf_color.T, tf_opacity.T, brick_tf, view_order)
    piece = struct((rim, rim, rows_z), BF16)
    both = struct((2, rim, rim, rows_z), BF16)
    bricks = rows_z // 128
    held, xs0, xs1, *refs = call(
        functools.partial(first_kernel, rim, rounds),
        "first",
        [HBM] * (1 + len(tables)),
        [struct((2, 2, rim, rim, rows_z), F32), both, both]
        + [piece] * (2 * rounds)
        + [struct((4 * bricks, 6 * bumps, 128), F32), struct((2, 2, 8, 128), jnp.int32)]
        + [struct((depth_count, block, rows_y), jnp.int32)],
        [pltpu.VMEM(t.shape, t.dtype) for t in tables]
        + [pltpu.SemaphoreType.DMA((4 + len(tables),))],
    )(in_hbm(density), *[in_hbm(t) for t in tables])
    strips, (table, signs, order_map) = refs[:2 * rounds], refs[2 * rounds:]
    near = [[swap(strips[2 * r], None, r), None] for r in range(rounds)]

    halo_x = [swap(cells, h, None) for h, cells in enumerate((xs0, xs1))]
    mx, my = call(
        functools.partial(matrices_kernel, rim),
        "matrices",
        [VMEM],
        [struct((size, 3 * size), BF16)] * 2,
        [pltpu.VMEM((8, 128), F32)],
    )(kernel_taps.astype(F32))
    shaded, total = [None, None], [None, None]
    for g in (1, 0):
        shaded[g], total[g] = call(
            functools.partial(cells_kernel, rim, bumps, g),
            f"cells{g}",
            [VMEM] * 3,
            [struct((3, 2, rim, rim, rows_z), F32), struct((rim, 128), F32)],
            [pltpu.VMEM((2, size, rows_z), F32), pltpu.VMEM((3, 2, size, rows_z), F32)],
            cost_estimate=pl.CostEstimate(
                flops=density.size * (100000 if g == 0 else 1),
                bytes_accessed=density.size * (10000 if g == 0 else 1),
                transcendentals=density.size * 3,
            ),
        )(held, table, signs)

    corner = [[None, None] for r in range(rounds)]
    for r in range(rounds):
        near[r][1] = swap(strips[2 * r + 1], None, r)
        strip, arrived, total[1] = lax.optimization_barrier(
            (strips[2 * r + 1], near[r][0], total[1])
        )
        corner[r] = [swap(arrived, 0, None), swap(strip, 1, r)]

    early = rounds < 2
    colours = struct((3, rim, 128), F32)
    unlit = struct((2 - early, 2, size, rows_z), F32)
    results = call(
        functools.partial(own_kernel, rim, early),
        "own",
        [VMEM] * (7 if early else 6),
        [colours, unlit] if early else [unlit],
    )(mx, my, xs0, xs1, *halo_x, *([shaded[1]] if early else []))
    partial = results[-1]
    blurred = [
        call(
            functools.partial(near_kernel, rim),
            f"near{r}",
            [VMEM] * 4,
            struct((2, size, rows_z), F32),
        )(mx, near[r][0], partial, near[r][1])
        for r in range(rounds)
    ]
    if early:
        light = results[0]
    else:
        light = call(functools.partial(late_kernel, rim, 1), "late", [VMEM] * 7, colours)(
            mx, my, blurred[1], partial, *corner[1], shaded[1]
        )
    kept, given = call(
        functools.partial(last_kernel, rim, depth_count),
        "last",
        [VMEM] * 10,
        [struct((depth_count // 2, 4, block, rows_y), F32)] * 2,
        [pltpu.VMEM((8, rows_y, 128), F32)],
    )(mx, my, blurred[0], partial, *corner[0], shaded[0], light, *total)
    level = 0
    while True:
        theirs = lax.ppermute(given, "depth", [(i, i ^ 1 << level) for i in range(depth_count)])
        left = kept.shape[0] // 2
        outs = [struct((left, 4, block, rows_y), F32)] * 2
        merged = call(
            functools.partial(merge_kernel, level),
            f"merge{level}",
            [VMEM] * 3,
            outs if left else struct((4, 1, 1, block, rows_y), F32),
            limit=2 * MIB,
        )(order_map, kept, theirs)
        if not left:
            return merged
        kept, given = merged
        level += 1


def solution(mesh):
    return jax.shard_map(
        per_device,
        mesh=mesh,
        in_specs=(
            P("sx", "sy", "depth"),
            P(),
            P(),
            P(),
            P(),
            P(),
            P("sx", "sy", "depth"),
            P("sx", "sy"),
        ),
        out_specs=P(None, "sx", "depth", None, "sy"),
        check_vma=False,
    )
```

```python
import functools
import math
import jax
import jax.numpy as jnp
from jax import lax
from jax.experimental import pallas as pl
from jax.experimental.pallas import tpu as pltpu
from jax.sharding import PartitionSpec as P

LOG2E = math.log2(math.e)
VMEM = pl.BlockSpec(memory_space=pltpu.VMEM)
HBM = pl.BlockSpec(memory_space=pltpu.HBM)
MIB = 1024 * 1024
F32, BF16 = jnp.float32, jnp.bfloat16
dot = functools.partial(jnp.dot, preferred_element_type=F32)


def iota(shape, dim):
    return lax.broadcasted_iota(jnp.int32, shape, dim)


def line_pairs(count, shift):
    return [(i, i + 1) for i in range(shift, count - 1, 2)]


def swaps(counts, x_round, y_round):
    depth_count, count_x, count_y = counts
    index = lambda d, x, y: (d * count_x + x) * count_y + y
    stay = lambda count: [(i, i) for i in range(count)]
    pairs_x = stay(count_x) if x_round is None else line_pairs(count_x, x_round)
    pairs_y = stay(count_y) if y_round is None else line_pairs(count_y, y_round)
    ends = {((a, c), (b, e)) for a, b in pairs_x for c, e in pairs_y}
    if x_round is not None and y_round is not None:
        ends |= {((a, e), (b, c)) for a, b in pairs_x for c, e in pairs_y}
    used = {end for pair in ends for end in pair}
    pairs = []
    for d in range(depth_count):
        pairs += [(index(d, *a), index(d, *b)) for a, b in sorted(ends)]
    for x in range(count_x):
        for y in range(count_y):
            if (x, y) not in used:
                pairs += [
                    (index(d, x, y), index(d + 1, x, y)) for d in range(0, depth_count - 1, 2)
                ]
    return pairs + [(b, a) for a, b in pairs]


class Place:
    def __init__(self):
        self.depth = lax.axis_index("depth")
        self.half, self.has_x = self.sides("sx")
        self.group, self.has_y = self.sides("sy")

    def sides(self, axis):
        at, last = lax.axis_index(axis), lax.axis_size(axis) - 1
        parity = lax.rem(at, 2)
        upper, lower = at < last, at > 0
        order = (1 - parity, parity)
        either = lambda side: jnp.where(side == 1, upper.astype(jnp.int32), lower.astype(jnp.int32))
        return order, [either(side) == 1 for side in order]


def group_rows(place, rim, g):
    return pl.ds(pl.multiple_of(place.group[g] * rim, rim), rim)


def half_rows(place, rim, h):
    return pl.ds(place.half[h] * rim, rim)


def first_kernel(rim, rounds, density, *refs):
    place = Place()
    n_tables = (len(refs) - 7 - 2 * rounds) // 2
    tables, refs = refs[:n_tables], refs[n_tables:]
    held, xs, refs = refs[0], refs[1:3], refs[3:]
    strips, refs = refs[:2 * rounds], refs[2 * rounds:]
    looked_up, local_tables, sems = refs[:3], refs[3:-1], refs[-1]
    copies = []
    for g in range(2):
        for h in range(2):
            rows = density.at[half_rows(place, rim, h), group_rows(place, rim, g), :]
            copies.append(pltpu.make_async_copy(rows, held.at[g, h], sems.at[2 * g + h]))
    for i, (src, dst) in enumerate(zip(tables, local_tables)):
        copies.append(pltpu.make_async_copy(src, dst, sems.at[4 + i]))
    for copy in copies[4:] + copies[:4]:
        copy.start()
    for copy in copies[4:]:
        copy.wait()
    look_up(rim, place, *local_tables, *looked_up)
    for g in range(2):
        for h in range(2):
            copies[2 * g + h].wait()
            coarse = held[g, h].astype(BF16)
            xs[h][g] = coarse
            if g < rounds:
                strips[2 * g + h][...] = coarse


def toeplitz(taps, rim):
    return pltpu.roll(jnp.broadcast_to(taps, (rim, 128)), 0, 1, stride=1, stride_axis=0)


def blur_matrices(rim, place, taps):
    size = rim * rim
    wide = 3 * size
    shift = rim.bit_length() - 1
    pick = lambda mask: jnp.where(mask, 1.0, 0.0).astype(BF16)
    row_hi = pick(iota((size, rim), 0) >> shift == iota((size, rim), 1))
    row_lo = pick(iota((size, rim), 0) & (rim - 1) == iota((size, rim), 1))
    col = iota((128, wide), 1)
    src = iota((128, wide), 0)
    k, j, b = col >> 2 * shift, col >> shift & (rim - 1), col & (rim - 1)
    k_x = jnp.where(place.half[0] == 1, k, 2 - k)
    k_y = jnp.where(place.group[0] == 1, k, 2 - k)
    tx = toeplitz(taps[0:1], rim).astype(BF16)
    ty = toeplitz(taps[1:2] * 0.5, rim).astype(BF16)
    full_x = dot(row_hi, dot(tx, pick(k_x * rim + j == src)).astype(BF16))
    full_y = dot(row_lo, dot(ty, pick(k_y * rim + b == src)).astype(BF16))
    r, c = iota((size, size), 0), iota((size, size), 1)
    same_x = r & (rim - 1) == c & (rim - 1)
    same_y = r >> shift == c >> shift
    parts = []
    for full, same in ((full_x, same_x), (full_y, same_y)):
        blocks = [
            jnp.where(same, full[:, n * size:(n + 1) * size], 0.0).astype(BF16) for n in range(3)
        ]
        parts.append(jnp.concatenate(blocks, axis=1))
    return parts


def matrices_kernel(rim, taps, mx, my, padded):
    padded[...] = jnp.zeros(padded.shape, F32)
    padded[0:2, 0:taps.shape[1]] = taps[...]
    mx[...], my[...] = blur_matrices(rim, Place(), padded[...])


def look_up(
    rim, place, centre, width, colour, opacity, brick_tf, view_order, table, signs, order_map
):
    wide = width[...]
    rows = [centre[...], (-LOG2E) / (wide * wide), opacity[...] * (-LOG2E)]
    rows += [colour[c] * 0.5 for c in range(3)]
    rows = jnp.concatenate(rows, axis=0)
    which = iota(rows.shape, 1)
    n = 0
    for g in range(2):
        for h in range(2):
            bricks = brick_tf[place.half[h]]
            bricks = jnp.where(place.group[g] == 0, bricks[0:1], bricks[1:2])
            for bz in range(bricks.shape[1]):
                mine = jnp.where(which == bricks[:, bz:bz + 1], rows, 0.0)
                mine = jnp.sum(mine, axis=1, keepdims=True)
                table[n] = jnp.broadcast_to(mine, table.shape[1:])
                n += 1
            orders = view_order[...]
            orders = jnp.where(place.half[h] == 0, orders[0:1], orders[1:2])
            order = jnp.where(place.group[g] == 0, orders[:, 0:1], orders[:, 1:2])
            signs[g, h] = jnp.broadcast_to(1 - 2 * order, signs.shape[2:])
    block, shape = order_map.shape[1], order_map.shape[1:]
    for n in range(order_map.shape[0]):
        brick = n * block // rim
        orders = view_order[brick:brick + 1]
        order_map[n] = jnp.where(
            iota(shape, 1) < rim,
            jnp.broadcast_to(orders[:, 0:1], shape),
            jnp.broadcast_to(orders[:, 1:2], shape),
        )


def cells_kernel(rim, bumps, g, held, table, signs, shaded, total, optical_s, emitted_s):
    place = Place()
    rows_z = held.shape[4]
    depth = 128
    bricks = rows_z // depth
    lane = iota((rim, 128), 1)
    for h in range(2):
        cells = held.at[g, h]
        for bz in range(bricks):
            zs = slice(bz * depth, (bz + 1) * depth)
            at = (2 * g + h) * bricks + bz
            row = lambda i: jnp.broadcast_to(table[at, i:i + 1, :], (8, depth))[None]
            cen = [row(j) for j in range(bumps)]
            neg = [row(bumps + j) for j in range(bumps)]
            opa = [row(2 * bumps + j) for j in range(bumps)]
            col = [[row((3 + c) * bumps + j) for c in range(3)] for j in range(bumps)]
            for x in range(rim):
                d = cells[x, :, zs].reshape(rim // 8, 8, depth)
                opt, em = None, [None] * 3
                for j in range(bumps):
                    w = d - cen[j]
                    b = jnp.exp2((w * w) * neg[j])
                    opt = opa[j] * b if opt is None else opt + opa[j] * b
                    for c in range(3):
                        em[c] = col[j][c] * b if em[c] is None else em[c] + col[j][c] * b
                rows = slice(x * rim, (x + 1) * rim)
                optical_s[h, rows, zs] = opt.reshape(rim, depth)
                for c in range(3):
                    emitted_s[c, h, rows, zs] = em[c].reshape(rim, depth)
        behind = iota((rows_z, rows_z), 1) - iota((rows_z, rows_z), 0)
        sign = jnp.broadcast_to(signs[g, h][0:1, 0:1], (rows_z, rows_z))
        tri = jnp.where(behind * sign > 0, 1.0, 0.0).astype(BF16)
        opt = optical_s[h]
        hi = opt.astype(BF16)
        lo = (opt - hi.astype(F32)).astype(BF16)
        ahead = dot(hi, tri) + dot(lo, tri)
        weight = jnp.exp2(ahead) * (1.0 - jnp.exp2(opt))
        for c in range(3):
            shaded[c, h] = (weight * emitted_s[c, h]).reshape(rim, rim, rows_z)
        part = rays(opt.reshape(rim, rim, rows_z), place.half[h] * rim, lane)
        total[...] = part if h == 0 else total[...] + part


def rays(cells, first_lane, lane):
    folded = cells[:, :, :128]
    for z in range(128, cells.shape[2], 128):
        folded = folded + cells[:, :, z:z + 128]
    summed = jnp.sum(folded, axis=2, keepdims=True)
    acc = jnp.zeros(lane.shape, F32)
    for x in range(cells.shape[0]):
        acc = jnp.where(lane == first_lane + x, summed[x], acc)
    return acc


def blur_x(place, rim, mx, h, near, halo):
    flat = lambda cells: cells.reshape(rim * rim, cells.shape[-1])
    edge = flat(halo)
    edge = jnp.where(place.has_x[h], edge, jnp.zeros_like(edge))
    own = [flat(near[1]), flat(near[0])]
    blocks = own + [edge] if h == 0 else [edge] + own
    return dot(mx[...], jnp.concatenate(blocks, axis=0)).astype(BF16)


def lit(place, rim, occlusion, shaded, h):
    rows_z = occlusion.shape[1]
    lane = iota((rim, 128), 1)
    shade = (1.0 - jnp.tanh(occlusion)).reshape(rim, rim, rows_z)
    return [rays(shade * shaded[c, h], place.half[h] * rim, lane) for c in range(3)]


def own_kernel(rim, early, mx, my, xs0, xs1, halo0, halo1, *refs):
    place = Place()
    size = rim * rim
    if early:
        shaded, out, partial = refs
    else:
        partial, = refs
    halos = (halo0, halo1)
    across = [
        [blur_x(place, rim, mx, h, [xs0[g], xs1[g]], halos[h][g]) for h in range(2)]
        for g in range(2)
    ]
    for h in range(2):
        cells = jnp.concatenate([across[1][h], across[0][h]], axis=0)
        partial[0, h] = dot(my[:, :2 * size], cells)
        other = dot(my[:, size:], cells)
        if not early:
            partial[1, h] = other
            continue
        for c, part in enumerate(lit(place, rim, other, shaded, h)):
            out[c] = part if h == 0 else out[c] + part


def near_kernel(rim, mx, near0, order, near1, out):
    size = rim * rim
    cells = jnp.concatenate([r[...].reshape(size, r.shape[2]) for r in (near1, near0)], axis=0)
    out[0] = dot(mx[:, :2 * size], cells)
    out[1] = dot(mx[:, size:], cells)


def late(rim, g, mx, my, blurred, partial, corner0, corner1, shaded):
    place = Place()
    size = rim * rim
    block = my[:, 2 * size:] if g == 0 else my[:, :size]
    across = []
    for h, corner in enumerate((corner0, corner1)):
        edge = corner[...].reshape(size, corner.shape[2])
        edge = jnp.where(place.has_x[h], edge, jnp.zeros_like(edge))
        beside = mx[:, 2 * size:] if h == 0 else mx[:, :size]
        cells = (blurred[h] + dot(beside, edge)).astype(BF16)
        across.append(jnp.where(place.has_y[g], cells, jnp.zeros_like(cells)))
    occlusion = [partial[g, h] + dot(block, across[h]) for h in range(2)]
    lights = [lit(place, rim, occlusion[h], shaded, h) for h in range(2)]
    return [a + b for a, b in zip(*lights)]


def late_kernel(rim, g, *refs):
    *refs, out = refs
    for c, part in enumerate(late(rim, g, *refs)):
        out[c] = part


def last_kernel(rim, depth_count, *refs):
    refs, (light_e, total0, total1, kept, given, img) = refs[:7], refs[7:]
    place = Place()
    rows = 2 * rim
    at_s, at_e = group_rows(place, rim, 0), group_rows(place, rim, 1)
    for c, part in enumerate(late(rim, 0, *refs)):
        img[c, at_s, :] = part
        img[c, at_e, :] = light_e[c]
    img[3, at_s, :] = jnp.exp2(total0[...])
    img[3, at_e, :] = jnp.exp2(total1[...])
    for c in range(4):
        img[4 + c, :, 0:rows] = img[c].T[:rows, :]
    block = rows // depth_count
    bit = place.depth & 1
    for n in range(depth_count // 2):
        for out, b in ((kept, bit), (given, 1 - bit)):
            out[n] = img[4:8, pl.ds(pl.multiple_of((2 * n + b) * block, block), block), 0:rows]


def merge_kernel(level, order_map, kept, theirs, *outs):
    me = lax.axis_index("depth")
    bit = me >> level & 1
    low = me & (2 << level) - 1
    merged = []
    for n in range(kept.shape[0]):
        mine = (bit == order_map[(n << level + 1) + low])[None]
        front = jnp.where(mine, kept[n], theirs[n])
        back = jnp.where(mine, theirs[n], kept[n])
        merged.append((front[:3] + front[3:] * back[:3], front[3:] * back[3:]))
    if len(merged) == 1:
        colour, through = merged[0]
        outs[0][...] = jnp.concatenate([colour, 1.0 - through]).reshape(outs[0].shape)
        return
    up = me >> level + 1 & 1
    for n in range(len(merged) // 2):
        even, odd = (jnp.concatenate(merged[2 * n + i]) for i in range(2))
        outs[0][n] = jnp.where(up == 1, odd, even)
        outs[1][n] = jnp.where(up == 1, even, odd)


def call(kernel, name, ins, outs, scratch=(), limit=16 * MIB, **more):
    return pl.pallas_call(
        kernel,
        out_shape=outs,
        in_specs=ins,
        out_specs=jax.tree.map(lambda _: VMEM, outs),
        scratch_shapes=list(scratch),
        compiler_params=pltpu.CompilerParams(vmem_limit_bytes=limit),
        name=name,
        **more,
    )


def per_device(
    density, kernel_taps, tf_centre, tf_width, tf_color, tf_opacity, brick_tf, view_order
):
    rows_x, rows_y, rows_z = density.shape
    rim = (kernel_taps.shape[1] - 1) // 2
    bumps = tf_centre.shape[1]
    size = rim * rim
    axes = ("depth", "sx", "sy")
    counts = tuple(lax.axis_size(axis) for axis in axes)
    depth_count, count_y = counts[0], counts[2]
    struct = jax.ShapeDtypeStruct
    block = rows_x // depth_count
    rounds = sum(1 for shift in range(2) if line_pairs(count_y, shift))

    def swap(piece, x_round, y_round):
        return lax.ppermute(piece, axes, swaps(counts, x_round, y_round))

    in_hbm = lambda array: pltpu.with_memory_space_constraint(array, pltpu.HBM)
    tables = (tf_centre.T, tf_width.T, tf_color.T, tf_opacity.T, brick_tf, view_order)
    piece = struct((rim, rim, rows_z), BF16)
    both = struct((2, rim, rim, rows_z), BF16)
    bricks = rows_z // 128
    held, xs0, xs1, *refs = call(
        functools.partial(first_kernel, rim, rounds),
        "first",
        [HBM] * (1 + len(tables)),
        [struct((2, 2, rim, rim, rows_z), F32), both, both]
        + [piece] * (2 * rounds)
        + [struct((4 * bricks, 6 * bumps, 128), F32), struct((2, 2, 8, 128), jnp.int32)]
        + [struct((depth_count, block, rows_y), jnp.int32)],
        [pltpu.VMEM(t.shape, t.dtype) for t in tables]
        + [pltpu.SemaphoreType.DMA((4 + len(tables),))],
    )(in_hbm(density), *[in_hbm(t) for t in tables])
    strips, (table, signs, order_map) = refs[:2 * rounds], refs[2 * rounds:]
    near = [[swap(strips[2 * r], None, r), None] for r in range(rounds)]

    halo_x = [swap(cells, h, None) for h, cells in enumerate((xs0, xs1))]
    mx, my = call(
        functools.partial(matrices_kernel, rim),
        "matrices",
        [VMEM],
        [struct((size, 3 * size), BF16)] * 2,
        [pltpu.VMEM((8, 128), F32)],
    )(kernel_taps.astype(F32))
    shaded, total = [None, None], [None, None]
    for g in (1, 0):
        shaded[g], total[g] = call(
            functools.partial(cells_kernel, rim, bumps, g),
            f"cells{g}",
            [VMEM] * 3,
            [struct((3, 2, rim, rim, rows_z), F32), struct((rim, 128), F32)],
            [pltpu.VMEM((2, size, rows_z), F32), pltpu.VMEM((3, 2, size, rows_z), F32)],
            cost_estimate=pl.CostEstimate(
                flops=density.size * (100000 if g == 0 else 1),
                bytes_accessed=density.size * (10000 if g == 0 else 1),
                transcendentals=density.size * 3,
            ),
        )(held, table, signs)

    corner = [[None, None] for r in range(rounds)]
    for r in range(rounds):
        near[r][1] = swap(strips[2 * r + 1], None, r)
        strip, arrived, mx, total[1] = lax.optimization_barrier(
            (strips[2 * r + 1], near[r][0], mx, total[1])
        )
        corner[r] = [swap(arrived, 0, None), swap(strip, 1, r)]

    early = rounds < 2
    colours = struct((3, rim, 128), F32)
    unlit = struct((2 - early, 2, size, rows_z), F32)
    results = call(
        functools.partial(own_kernel, rim, early),
        "own",
        [VMEM] * (7 if early else 6),
        [colours, unlit] if early else [unlit],
    )(mx, my, xs0, xs1, *halo_x, *([shaded[1]] if early else []))
    partial = results[-1]
    blurred = [
        call(
            functools.partial(near_kernel, rim),
            f"near{r}",
            [VMEM] * 4,
            struct((2, size, rows_z), F32),
        )(mx, near[r][0], partial, near[r][1])
        for r in range(rounds)
    ]
    if early:
        light = results[0]
    else:
        light = call(functools.partial(late_kernel, rim, 1), "late", [VMEM] * 7, colours)(
            mx, my, blurred[1], partial, *corner[1], shaded[1]
        )
    kept, given = call(
        functools.partial(last_kernel, rim, depth_count),
        "last",
        [VMEM] * 10,
        [struct((depth_count // 2, 4, block, rows_y), F32)] * 2,
        [pltpu.VMEM((8, rows_y, 128), F32)],
    )(mx, my, blurred[0], partial, *corner[0], shaded[0], light, *total)
    level = 0
    while True:
        theirs = lax.ppermute(given, "depth", [(i, i ^ 1 << level) for i in range(depth_count)])
        left = kept.shape[0] // 2
        outs = [struct((left, 4, block, rows_y), F32)] * 2
        merged = call(
            functools.partial(merge_kernel, level),
            f"merge{level}",
            [VMEM] * 3,
            outs if left else struct((4, 1, 1, block, rows_y), F32),
            limit=2 * MIB,
        )(order_map, kept, theirs)
        if not left:
            return merged
        kept, given = merged
        level += 1


def solution(mesh):
    return jax.shard_map(
        per_device,
        mesh=mesh,
        in_specs=(
            P("sx", "sy", "depth"),
            P(),
            P(),
            P(),
            P(),
            P(),
            P("sx", "sy", "depth"),
            P("sx", "sy"),
        ),
        out_specs=P(None, "sx", "depth", None, "sy"),
        check_vma=False,
    )
```

```python
import functools
import math
import jax
import jax.numpy as jnp
from jax import lax
from jax.experimental import pallas as pl
from jax.experimental.pallas import tpu as pltpu
from jax.sharding import PartitionSpec as P

LOG2E = math.log2(math.e)
VMEM = pl.BlockSpec(memory_space=pltpu.VMEM)
HBM = pl.BlockSpec(memory_space=pltpu.HBM)
MIB = 1024 * 1024
F32, BF16 = jnp.float32, jnp.bfloat16
dot = functools.partial(jnp.dot, preferred_element_type=F32)


def iota(shape, dim):
    return lax.broadcasted_iota(jnp.int32, shape, dim)


def line_pairs(count, shift):
    return [(i, i + 1) for i in range(shift, count - 1, 2)]


def swaps(counts, x_round, y_round):
    depth_count, count_x, count_y = counts
    index = lambda d, x, y: (d * count_x + x) * count_y + y
    stay = lambda count: [(i, i) for i in range(count)]
    pairs_x = stay(count_x) if x_round is None else line_pairs(count_x, x_round)
    pairs_y = stay(count_y) if y_round is None else line_pairs(count_y, y_round)
    ends = {((a, c), (b, e)) for a, b in pairs_x for c, e in pairs_y}
    if x_round is not None and y_round is not None:
        ends |= {((a, e), (b, c)) for a, b in pairs_x for c, e in pairs_y}
    used = {end for pair in ends for end in pair}
    pairs = []
    for d in range(depth_count):
        pairs += [(index(d, *a), index(d, *b)) for a, b in sorted(ends)]
    for x in range(count_x):
        for y in range(count_y):
            if (x, y) not in used:
                pairs += [
                    (index(d, x, y), index(d + 1, x, y)) for d in range(0, depth_count - 1, 2)
                ]
    return pairs + [(b, a) for a, b in pairs]


class Place:
    def __init__(self):
        self.depth = lax.axis_index("depth")
        self.half, self.has_x = self.sides("sx")
        self.group, self.has_y = self.sides("sy")

    def sides(self, axis):
        at, last = lax.axis_index(axis), lax.axis_size(axis) - 1
        parity = lax.rem(at, 2)
        upper, lower = at < last, at > 0
        order = (1 - parity, parity)
        either = lambda side: jnp.where(side == 1, upper.astype(jnp.int32), lower.astype(jnp.int32))
        return order, [either(side) == 1 for side in order]


def group_rows(place, rim, g):
    return pl.ds(pl.multiple_of(place.group[g] * rim, rim), rim)


def half_rows(place, rim, h):
    return pl.ds(place.half[h] * rim, rim)


def first_kernel(rim, rounds, density, *refs):
    place = Place()
    n_tables = (len(refs) - 7 - 2 * rounds) // 2
    tables, refs = refs[:n_tables], refs[n_tables:]
    held, xs, refs = refs[0], refs[1:3], refs[3:]
    strips, refs = refs[:2 * rounds], refs[2 * rounds:]
    looked_up, local_tables, sems = refs[:3], refs[3:-1], refs[-1]
    copies = []
    for g in range(2):
        for h in range(2):
            rows = density.at[half_rows(place, rim, h), group_rows(place, rim, g), :]
            copies.append(pltpu.make_async_copy(rows, held.at[g, h], sems.at[2 * g + h]))
    for i, (src, dst) in enumerate(zip(tables, local_tables)):
        copies.append(pltpu.make_async_copy(src, dst, sems.at[4 + i]))
    for copy in copies:
        copy.start()
    for copy in copies[4:]:
        copy.wait()
    look_up(rim, place, *local_tables, *looked_up)
    for g in range(2):
        for h in range(2):
            copies[2 * g + h].wait()
            coarse = held[g, h].astype(BF16)
            xs[h][g] = coarse
            if g < rounds:
                strips[2 * g + h][...] = coarse


def toeplitz(taps, rim):
    return pltpu.roll(jnp.broadcast_to(taps, (rim, 128)), 0, 1, stride=1, stride_axis=0)


def blur_matrices(rim, place, taps):
    size = rim * rim
    wide = 3 * size
    shift = rim.bit_length() - 1
    pick = lambda mask: jnp.where(mask, 1.0, 0.0).astype(BF16)
    row_hi = pick(iota((size, rim), 0) >> shift == iota((size, rim), 1))
    row_lo = pick(iota((size, rim), 0) & (rim - 1) == iota((size, rim), 1))
    col = iota((128, wide), 1)
    src = iota((128, wide), 0)
    k, j, b = col >> 2 * shift, col >> shift & (rim - 1), col & (rim - 1)
    k_x = jnp.where(place.half[0] == 1, k, 2 - k)
    k_y = jnp.where(place.group[0] == 1, k, 2 - k)
    tx = toeplitz(taps[0:1], rim).astype(BF16)
    ty = toeplitz(taps[1:2] * 0.5, rim).astype(BF16)
    full_x = dot(row_hi, dot(tx, pick(k_x * rim + j == src)).astype(BF16))
    full_y = dot(row_lo, dot(ty, pick(k_y * rim + b == src)).astype(BF16))
    r, c = iota((size, size), 0), iota((size, size), 1)
    same_x = r & (rim - 1) == c & (rim - 1)
    same_y = r >> shift == c >> shift
    parts = []
    for full, same in ((full_x, same_x), (full_y, same_y)):
        blocks = [
            jnp.where(same, full[:, n * size:(n + 1) * size], 0.0).astype(BF16) for n in range(3)
        ]
        parts.append(jnp.concatenate(blocks, axis=1))
    return parts


def matrices_kernel(rim, taps, mx, my, padded):
    padded[...] = jnp.zeros(padded.shape, F32)
    padded[0:2, 0:taps.shape[1]] = taps[...]
    mx[...], my[...] = blur_matrices(rim, Place(), padded[...])


def look_up(
    rim, place, centre, width, colour, opacity, brick_tf, view_order, table, signs, order_map
):
    wide = width[...]
    rows = [centre[...], (-LOG2E) / (wide * wide), opacity[...] * (-LOG2E)]
    rows += [colour[c] * 0.5 for c in range(3)]
    rows = jnp.concatenate(rows, axis=0)
    which = iota(rows.shape, 1)
    n = 0
    for g in range(2):
        for h in range(2):
            bricks = brick_tf[place.half[h]]
            bricks = jnp.where(place.group[g] == 0, bricks[0:1], bricks[1:2])
            for bz in range(bricks.shape[1]):
                mine = jnp.where(which == bricks[:, bz:bz + 1], rows, 0.0)
                mine = jnp.sum(mine, axis=1, keepdims=True)
                table[n] = jnp.broadcast_to(mine, table.shape[1:])
                n += 1
            orders = view_order[...]
            orders = jnp.where(place.half[h] == 0, orders[0:1], orders[1:2])
            order = jnp.where(place.group[g] == 0, orders[:, 0:1], orders[:, 1:2])
            signs[g, h] = jnp.broadcast_to(1 - 2 * order, signs.shape[2:])
    block, shape = order_map.shape[1], order_map.shape[1:]
    for n in range(order_map.shape[0]):
        brick = n * block // rim
        orders = view_order[brick:brick + 1]
        order_map[n] = jnp.where(
            iota(shape, 1) < rim,
            jnp.broadcast_to(orders[:, 0:1], shape),
            jnp.broadcast_to(orders[:, 1:2], shape),
        )


def cells_kernel(rim, bumps, g, held, table, signs, shaded, total, optical_s, emitted_s):
    place = Place()
    rows_z = held.shape[4]
    depth = 128
    bricks = rows_z // depth
    lane = iota((rim, 128), 1)
    for h in range(2):
        cells = held.at[g, h]
        for bz in range(bricks):
            zs = slice(bz * depth, (bz + 1) * depth)
            at = (2 * g + h) * bricks + bz
            row = lambda i: jnp.broadcast_to(table[at, i:i + 1, :], (8, depth))[None]
            cen = [row(j) for j in range(bumps)]
            neg = [row(bumps + j) for j in range(bumps)]
            opa = [row(2 * bumps + j) for j in range(bumps)]
            col = [[row((3 + c) * bumps + j) for c in range(3)] for j in range(bumps)]
            for x in range(rim):
                d = cells[x, :, zs].reshape(rim // 8, 8, depth)
                opt, em = None, [None] * 3
                for j in range(bumps):
                    w = d - cen[j]
                    b = jnp.exp2((w * w) * neg[j])
                    opt = opa[j] * b if opt is None else opt + opa[j] * b
                    for c in range(3):
                        em[c] = col[j][c] * b if em[c] is None else em[c] + col[j][c] * b
                rows = slice(x * rim, (x + 1) * rim)
                optical_s[h, rows, zs] = opt.reshape(rim, depth)
                for c in range(3):
                    emitted_s[c, h, rows, zs] = em[c].reshape(rim, depth)
        behind = iota((rows_z, rows_z), 1) - iota((rows_z, rows_z), 0)
        sign = jnp.broadcast_to(signs[g, h][0:1, 0:1], (rows_z, rows_z))
        tri = jnp.where(behind * sign > 0, 1.0, 0.0).astype(BF16)
        opt = optical_s[h]
        hi = opt.astype(BF16)
        lo = (opt - hi.astype(F32)).astype(BF16)
        ahead = dot(hi, tri) + dot(lo, tri)
        weight = jnp.exp2(ahead) * (1.0 - jnp.exp2(opt))
        for c in range(3):
            shaded[c, h] = (weight * emitted_s[c, h]).reshape(rim, rim, rows_z)
        part = rays(opt.reshape(rim, rim, rows_z), place.half[h] * rim, lane)
        total[...] = part if h == 0 else total[...] + part


def rays(cells, first_lane, lane):
    folded = cells[:, :, :128]
    for z in range(128, cells.shape[2], 128):
        folded = folded + cells[:, :, z:z + 128]
    summed = jnp.sum(folded, axis=2, keepdims=True)
    acc = jnp.zeros(lane.shape, F32)
    for x in range(cells.shape[0]):
        acc = jnp.where(lane == first_lane + x, summed[x], acc)
    return acc


def blur_x(place, rim, mx, h, near, halo):
    flat = lambda cells: cells.reshape(rim * rim, cells.shape[-1])
    edge = flat(halo)
    edge = jnp.where(place.has_x[h], edge, jnp.zeros_like(edge))
    own = [flat(near[1]), flat(near[0])]
    blocks = own + [edge] if h == 0 else [edge] + own
    return dot(mx[...], jnp.concatenate(blocks, axis=0)).astype(BF16)


def lit(place, rim, occlusion, shaded, h):
    rows_z = occlusion.shape[1]
    lane = iota((rim, 128), 1)
    shade = (1.0 - jnp.tanh(occlusion)).reshape(rim, rim, rows_z)
    return [rays(shade * shaded[c, h], place.half[h] * rim, lane) for c in range(3)]


def own_kernel(rim, early, mx, my, xs0, xs1, halo0, halo1, *refs):
    place = Place()
    size = rim * rim
    if early:
        shaded, out, partial = refs
    else:
        partial, = refs
    halos = (halo0, halo1)
    across = [
        [blur_x(place, rim, mx, h, [xs0[g], xs1[g]], halos[h][g]) for h in range(2)]
        for g in range(2)
    ]
    for h in range(2):
        cells = jnp.concatenate([across[1][h], across[0][h]], axis=0)
        partial[0, h] = dot(my[:, :2 * size], cells)
        other = dot(my[:, size:], cells)
        if not early:
            partial[1, h] = other
            continue
        for c, part in enumerate(lit(place, rim, other, shaded, h)):
            out[c] = part if h == 0 else out[c] + part


def near_kernel(rim, mx, near0, order, near1, out):
    size = rim * rim
    cells = jnp.concatenate([r[...].reshape(size, r.shape[2]) for r in (near1, near0)], axis=0)
    out[0] = dot(mx[:, :2 * size], cells)
    out[1] = dot(mx[:, size:], cells)


def late(rim, g, mx, my, blurred, partial, corner0, corner1, shaded):
    place = Place()
    size = rim * rim
    block = my[:, 2 * size:] if g == 0 else my[:, :size]
    across = []
    for h, corner in enumerate((corner0, corner1)):
        edge = corner[...].reshape(size, corner.shape[2])
        edge = jnp.where(place.has_x[h], edge, jnp.zeros_like(edge))
        beside = mx[:, 2 * size:] if h == 0 else mx[:, :size]
        cells = (blurred[h] + dot(beside, edge)).astype(BF16)
        across.append(jnp.where(place.has_y[g], cells, jnp.zeros_like(cells)))
    occlusion = [partial[g, h] + dot(block, across[h]) for h in range(2)]
    lights = [lit(place, rim, occlusion[h], shaded, h) for h in range(2)]
    return [a + b for a, b in zip(*lights)]


def late_kernel(rim, g, *refs):
    *refs, out = refs
    for c, part in enumerate(late(rim, g, *refs)):
        out[c] = part


def last_kernel(rim, depth_count, *refs):
    refs, (light_e, total0, total1, kept, given, img) = refs[:7], refs[7:]
    place = Place()
    rows = 2 * rim
    at_s, at_e = group_rows(place, rim, 0), group_rows(place, rim, 1)
    for c, part in enumerate(late(rim, 0, *refs)):
        img[c, at_s, :] = part
        img[c, at_e, :] = light_e[c]
    img[3, at_s, :] = jnp.exp2(total0[...])
    img[3, at_e, :] = jnp.exp2(total1[...])
    for c in range(4):
        img[4 + c, :, 0:rows] = img[c].T[:rows, :]
    block = rows // depth_count
    bit = place.depth & 1
    for n in range(depth_count // 2):
        for out, b in ((kept, bit), (given, 1 - bit)):
            out[n] = img[4:8, pl.ds(pl.multiple_of((2 * n + b) * block, block), block), 0:rows]


def merge_kernel(level, order_map, kept, theirs, *outs):
    me = lax.axis_index("depth")
    bit = me >> level & 1
    low = me & (2 << level) - 1
    merged = []
    for n in range(kept.shape[0]):
        mine = (bit == order_map[(n << level + 1) + low])[None]
        front = jnp.where(mine, kept[n], theirs[n])
        back = jnp.where(mine, theirs[n], kept[n])
        merged.append((front[:3] + front[3:] * back[:3], front[3:] * back[3:]))
    if len(merged) == 1:
        colour, through = merged[0]
        outs[0][...] = jnp.concatenate([colour, 1.0 - through]).reshape(outs[0].shape)
        return
    up = me >> level + 1 & 1
    for n in range(len(merged) // 2):
        even, odd = (jnp.concatenate(merged[2 * n + i]) for i in range(2))
        outs[0][n] = jnp.where(up == 1, odd, even)
        outs[1][n] = jnp.where(up == 1, even, odd)


def call(kernel, name, ins, outs, scratch=(), limit=16 * MIB, **more):
    return pl.pallas_call(
        kernel,
        out_shape=outs,
        in_specs=ins,
        out_specs=jax.tree.map(lambda _: VMEM, outs),
        scratch_shapes=list(scratch),
        compiler_params=pltpu.CompilerParams(vmem_limit_bytes=limit),
        name=name,
        **more,
    )


def per_device(
    density, kernel_taps, tf_centre, tf_width, tf_color, tf_opacity, brick_tf, view_order
):
    rows_x, rows_y, rows_z = density.shape
    rim = (kernel_taps.shape[1] - 1) // 2
    bumps = tf_centre.shape[1]
    size = rim * rim
    axes = ("depth", "sx", "sy")
    counts = tuple(lax.axis_size(axis) for axis in axes)
    depth_count, count_y = counts[0], counts[2]
    struct = jax.ShapeDtypeStruct
    block = rows_x // depth_count
    rounds = sum(1 for shift in range(2) if line_pairs(count_y, shift))

    def swap(piece, x_round, y_round):
        return lax.ppermute(piece, axes, swaps(counts, x_round, y_round))

    in_hbm = lambda array: pltpu.with_memory_space_constraint(array, pltpu.HBM)
    tables = (tf_centre.T, tf_width.T, tf_color.T, tf_opacity.T, brick_tf, view_order)
    piece = struct((rim, rim, rows_z), BF16)
    both = struct((2, rim, rim, rows_z), BF16)
    bricks = rows_z // 128
    held, xs0, xs1, *refs = call(
        functools.partial(first_kernel, rim, rounds),
        "first",
        [HBM] * (1 + len(tables)),
        [struct((2, 2, rim, rim, rows_z), F32), both, both]
        + [piece] * (2 * rounds)
        + [struct((4 * bricks, 6 * bumps, 128), F32), struct((2, 2, 8, 128), jnp.int32)]
        + [struct((depth_count, block, rows_y), jnp.int32)],
        [pltpu.VMEM(t.shape, t.dtype) for t in tables]
        + [pltpu.SemaphoreType.DMA((4 + len(tables),))],
    )(in_hbm(density), *[in_hbm(t) for t in tables])
    strips, (table, signs, order_map) = refs[:2 * rounds], refs[2 * rounds:]
    near = [[swap(strips[2 * r], None, r), None] for r in range(rounds)]

    halo_x = [swap(cells, h, None) for h, cells in enumerate((xs0, xs1))]
    mx, my = call(
        functools.partial(matrices_kernel, rim),
        "matrices",
        [VMEM],
        [struct((size, 3 * size), BF16)] * 2,
        [pltpu.VMEM((8, 128), F32)],
    )(kernel_taps.astype(F32))
    shaded, total = [None, None], [None, None]
    for g in (1, 0):
        shaded[g], total[g] = call(
            functools.partial(cells_kernel, rim, bumps, g),
            f"cells{g}",
            [VMEM] * 3,
            [struct((3, 2, rim, rim, rows_z), F32), struct((rim, 128), F32)],
            [pltpu.VMEM((2, size, rows_z), F32), pltpu.VMEM((3, 2, size, rows_z), F32)],
            cost_estimate=pl.CostEstimate(
                flops=density.size * (100000 if g == 0 else 1),
                bytes_accessed=density.size * (10000 if g == 0 else 1),
                transcendentals=density.size * 3,
            ),
        )(held, table, signs)

    corner = [[None, None] for r in range(rounds)]
    for r in range(rounds):
        near[r][1] = swap(strips[2 * r + 1], None, r)
        strip, arrived, mx, total[1] = lax.optimization_barrier(
            (strips[2 * r + 1], near[r][0], mx, total[1])
        )
        corner[r] = [swap(arrived, 0, None), swap(strip, 1, r)]

    early = rounds < 2
    colours = struct((3, rim, 128), F32)
    unlit = struct((2 - early, 2, size, rows_z), F32)
    results = call(
        functools.partial(own_kernel, rim, early),
        "own",
        [VMEM] * (7 if early else 6),
        [colours, unlit] if early else [unlit],
    )(mx, my, xs0, xs1, *halo_x, *([shaded[1]] if early else []))
    partial = results[-1]
    blurred = [
        call(
            functools.partial(near_kernel, rim),
            f"near{r}",
            [VMEM] * 4,
            struct((2, size, rows_z), F32),
        )(mx, near[r][0], partial, near[r][1])
        for r in range(rounds)
    ]
    if early:
        light = results[0]
    else:
        light = call(functools.partial(late_kernel, rim, 1), "late", [VMEM] * 7, colours)(
            mx, my, blurred[1], partial, *corner[1], shaded[1]
        )
    kept, given = call(
        functools.partial(last_kernel, rim, depth_count),
        "last",
        [VMEM] * 10,
        [struct((depth_count // 2, 4, block, rows_y), F32)] * 2,
        [pltpu.VMEM((8, rows_y, 128), F32)],
    )(mx, my, blurred[0], partial, *corner[0], shaded[0], light, *total)
    level = 0
    while True:
        theirs = lax.ppermute(given, "depth", [(i, i ^ 1 << level) for i in range(depth_count)])
        left = kept.shape[0] // 2
        outs = [struct((left, 4, block, rows_y), F32)] * 2
        merged = call(
            functools.partial(merge_kernel, level),
            f"merge{level}",
            [VMEM] * 3,
            outs if left else struct((4, 1, 1, block, rows_y), F32),
            limit=2 * MIB,
        )(order_map, kept, theirs)
        if not left:
            return merged
        kept, given = merged
        level += 1


def solution(mesh):
    return jax.shard_map(
        per_device,
        mesh=mesh,
        in_specs=(
            P("sx", "sy", "depth"),
            P(),
            P(),
            P(),
            P(),
            P(),
            P("sx", "sy", "depth"),
            P("sx", "sy"),
        ),
        out_specs=P(None, "sx", "depth", None, "sy"),
        check_vma=False,
    )
```
